32 devices in a mesh: dp: 8 (over z, y), seq: 4 (over x, core).
Axes of the slice: x: 2, y: 2, z: 4, core: 2. Of those that a mesh axis runs over, the one named last changes fastest.
Arguments:
- target: bfloat16 [8, 1024, 1024], P('dp', 'seq'), may hold values from -6 to 6
- memory: bfloat16 [8, 512, 1024], P('dp', 'seq'), may hold values from -6 to 6
- mem_lengths: int32 [8], P('dp'), may hold values from 64 to 512, as said below
- mem_mask: int32 [8, 512], P('dp'), may hold values 0 or 1
- distance_buckets: int32 [1024], replicated, may hold values from 0 to 31, as said below
- norm_self: float32 [1024], replicated, may hold values from 0.25 to 1.75
- w_query: bfloat16 [1024, 1024], replicated, may hold values from -0.1875 to 0.1875
- w_key: bfloat16 [1024, 512], replicated, may hold values from -0.1875 to 0.1875
- w_value: bfloat16 [1024, 512], replicated, may hold values from -0.1875 to 0.1875
- w_out: bfloat16 [1024, 1024], replicated, may hold values from -1.5 to 1.5
- pos_table: float32 [16, 32], replicated, may hold values from -4 to 4
- norm_cross: float32 [1024], replicated, may hold values from 0.25 to 1.75
- wc_query: bfloat16 [1024, 1024], replicated, may hold values from -0.1875 to 0.1875
- wc_key: bfloat16 [1024, 512], replicated, may hold values from -0.1875 to 0.1875
- wc_value: bfloat16 [1024, 512], replicated, may hold values from -0.1875 to 0.1875
- wc_out: bfloat16 [1024, 1024], replicated, may hold values from -1.5 to 1.5
- norm_ffn: float32 [1024], replicated, may hold values from 0.25 to 1.75
- w_gate: bfloat16 [1024, 2816], replicated, may hold values from -0.1875 to 0.1875
- w_up: bfloat16 [1024, 2816], replicated, may hold values from -0.1875 to 0.1875
- w_down: bfloat16 [2816, 1024], replicated, may hold values from -0.109375 to 0.109375
- out_grad: bfloat16 [8, 1024, 1024], P('dp', 'seq'), may hold values from -6 to 6
Outputs:
- output: bfloat16 [8, 1024, 1024], P('dp', 'seq')
- grad_target: float32 [8, 1024, 1024], P('dp', 'seq')
- grad_memory: float32 [8, 512, 1024], P('dp', 'seq')
- grad_norm_self: float32 [1024], P(('dp', 'seq'))
- grad_w_query: float32 [1024, 1024], P(('dp', 'seq'))
- grad_w_key: float32 [1024, 512], P(('dp', 'seq'))
- grad_w_value: float32 [1024, 512], P(('dp', 'seq'))
- grad_w_out: float32 [1024, 1024], P(('dp', 'seq'))
- grad_pos_table: float32 [512], P(('dp', 'seq'))
- grad_norm_cross: float32 [1024], P(('dp', 'seq'))
- grad_wc_query: float32 [1024, 1024], P(('dp', 'seq'))
- grad_wc_key: float32 [1024, 512], P(('dp', 'seq'))
- grad_wc_value: float32 [1024, 512], P(('dp', 'seq'))
- grad_wc_out: float32 [1024, 1024], P(('dp', 'seq'))
- grad_norm_ffn: float32 [1024], P(('dp', 'seq'))
- grad_w_gate: float32 [1024, 2816], P(('dp', 'seq'))
- grad_w_up: float32 [1024, 2816], P(('dp', 'seq'))
- grad_w_down: float32 [2816, 1024], P(('dp', 'seq'))
The draws below stay inside these ranges and needn't reach their ends.
Inputs may be any that keep to these rules, and one draw needn't show every extreme that they name: `mem_lengths`: memory lengths lie between 64 and 512, and 512 is reached in every draw. `distance_buckets`: buckets never fall as the distance grows; distance 0 has bucket 0 and distance 1024 - 1 has bucket 32 - 1.
All inputs are finite; a program needn't handle non-finite values. No bound on the sum of `mem_mask` on one device may be relied on, other than what follows from the above.
Results may differ from the reference program's by a relative error of at most 0.033.
Values may be sent and summed in bfloat16 or wider, within the bound.
No kernel may reach another device: no remote copies, remote signals or barrier semaphores. Data moves between devices by JAX's collectives and lax.ppermute only.
A program may use at most 192 MiB of HBM per device.

```python
import jax
import jax.numpy as jnp
from jax import lax

D = 1024
HEADS = 16
KV = 8
HEAD_DIM = 64
FF = 2816
BUCKETS = 32
SEQ_LEN = 1024
MEM = 512
Q = 1024
KVC = 512
SEQS = 8


def draw_mem_lengths(key, part):
    drawn = jax.random.randint(key, (SEQS,), MEM // 8, MEM + 1, dtype=jnp.int32)
    return drawn.at[0].set(MEM)


def draw_distance_buckets(key, part):
    drawn = jax.random.randint(key, (SEQ_LEN,), 1, BUCKETS - 1, dtype=jnp.int32)
    ordered = jnp.sort(drawn)
    return ordered.at[0].set(0).at[SEQ_LEN - 1].set(BUCKETS - 1)


def set_ends(values, stream_key, smallest, top_value):
    index_at = [jax.random.randint(jax.random.fold_in(stream_key, axis), (), 0, length) for axis, length in enumerate(values.shape)]
    widest = values.shape.index(max(values.shape))
    beside = index_at[:widest] + [(index_at[widest] + 1) % values.shape[widest]] + index_at[widest + 1:]
    return values.at[tuple(index_at)].set(smallest).at[tuple(beside)].set(top_value)


def block_scale(own_key, extent, shards, smallest, high):
    gain = 1.0
    for dim, parts in shards:
        heights = jax.random.uniform(jax.random.fold_in(jax.random.fold_in(own_key, 6), dim), (parts,), jnp.float32, smallest / len(shards), high / len(shards))
        gain = gain * jnp.repeat(jnp.exp(heights), extent[dim] // parts).reshape((-1,) + (1,) * (len(extent) - 1 - dim))
    return gain


def centred(rng, extent, spread, reach, pieces=(), kind=jnp.bfloat16):
    entries = spread * jax.random.normal(rng, extent, jnp.float32)
    if pieces:
        entries = entries * block_scale(rng, extent, pieces, -0.22, 0.18)
    return jnp.clip(entries, -reach, reach).astype(kind)


def setup_inputs(seed: int = 0) -> dict:
    splits = jax.random.split(jax.random.key(seed), 22)
    target = centred(splits[0], (SEQS, SEQ_LEN, D), 1.0, 6.0, ((0, 8), (1, 4)))
    memory = centred(splits[1], (SEQS, MEM, D), 1.0, 6.0, ((0, 8), (1, 4)))
    mem_lengths = draw_mem_lengths(jax.random.fold_in(splits[21], 71), 0)
    mem_mask = set_ends((jax.random.randint(splits[3], (SEQS, MEM), 0, 8) < 7).astype(jnp.int32), jax.random.fold_in(splits[3], 1), 0, 1)
    distance_buckets = draw_distance_buckets(jax.random.fold_in(splits[21], 71), 0)
    norm_self = jnp.clip(1.0 + 0.15 * jax.random.normal(splits[5], (D,), jnp.float32), 0.25, 1.75)
    w_query = centred(splits[6], (D, Q), D ** -0.5, 0.1875)
    w_key = centred(splits[7], (D, KVC), D ** -0.5, 0.1875)
    w_value = centred(splits[8], (D, KVC), D ** -0.5, 0.1875)
    w_out = centred(splits[9], (Q, D), (Q // 64) ** -0.5, 1.5)
    pos_table = centred(splits[10], (HEADS, BUCKETS), 1.0, 4.0, (), jnp.float32)
    norm_cross = jnp.clip(1.0 + 0.15 * jax.random.normal(splits[11], (D,), jnp.float32), 0.25, 1.75)
    wc_query = centred(splits[12], (D, Q), D ** -0.5, 0.1875)
    wc_key = centred(splits[13], (D, KVC), D ** -0.5, 0.1875)
    wc_value = centred(splits[14], (D, KVC), D ** -0.5, 0.1875)
    wc_out = centred(splits[15], (Q, D), (Q // 64) ** -0.5, 1.5)
    norm_ffn = jnp.clip(1.0 + 0.15 * jax.random.normal(splits[16], (D,), jnp.float32), 0.25, 1.75)
    w_gate = centred(splits[17], (D, FF), D ** -0.5, 0.1875)
    w_up = centred(splits[18], (D, FF), D ** -0.5, 0.1875)
    w_down = centred(splits[19], (FF, D), FF ** -0.5, 0.109375)
    out_grad = centred(splits[20], (SEQS, SEQ_LEN, D), 1.0, 6.0, ((0, 8), (1, 4)))
    return {"target": target, "memory": memory, "mem_lengths": mem_lengths, "mem_mask": mem_mask, "distance_buckets": distance_buckets, "norm_self": norm_self, "w_query": w_query, "w_key": w_key, "w_value": w_value, "w_out": w_out, "pos_table": pos_table, "norm_cross": norm_cross, "wc_query": wc_query, "wc_key": wc_key, "wc_value": wc_value, "wc_out": wc_out, "norm_ffn": norm_ffn, "w_gate": w_gate, "w_up": w_up, "w_down": w_down, "out_grad": out_grad}


@jax.custom_vjp
def low(v):
    return lax.optimization_barrier(v.astype(jnp.bfloat16)).astype(jnp.float32)

@jax.custom_vjp
def low_back(v):
    return v

def low_keep(v):
    return (low(v), None)

def low_pass(kept, grad):
    return (grad,)

def back_keep(v):
    return (v, None)

def back_low(kept, grad):
    return (low(grad),)
low.defvjp(low_keep, low_pass)
low_back.defvjp(back_keep, back_low)
norm_eps = 1e-06
big_negative = -1000000000.0
highest = lax.Precision.HIGHEST

def both_ways(value):
    return low(low_back(value))

def rms_norm(values, scale_gain):
    inverse = lax.rsqrt(lax.optimization_barrier(jnp.mean(values * values, axis=-1, keepdims=True)) + norm_eps)
    return values * inverse * scale_gain

def matmul(left_rows, right_rows):
    return jnp.dot(left_rows, right_rows, precision=highest, preferred_element_type=jnp.float32)

def attend(query_rows, key_rows, value_rows, bias_add, valid_mask):
    total_rows = query_rows.shape[0]
    grouped = query_rows.reshape(total_rows, KV, HEADS // KV, HEAD_DIM)
    raw_scores = jnp.einsum('lgrd,mgd->grlm', grouped, key_rows, precision=highest) * HEAD_DIM ** (-0.5) + bias_add
    scores = jnp.where(valid_mask, low_back(raw_scores), big_negative)
    weights = low(jax.nn.softmax(scores, axis=-1))
    mixed_rows = jnp.einsum('grlm,mgd->lgrd', weights, value_rows, precision=highest)
    return both_ways(mixed_rows.reshape(total_rows, HEADS * HEAD_DIM))

def gated_unit(gate_in, up_in):
    return jax.nn.gelu(gate_in, approximate=True) * up_in

def layer_one(params, target_seq, memory_seq, valid_seq, distance_buckets):
    norm_self, w_query, w_key, w_value, w_out, pos_table, norm_cross, wc_query, wc_key, wc_value, wc_out, norm_ffn, w_gate, w_up, w_down = params
    total_rows = target_seq.shape[0]
    mem_rows = memory_seq.shape[0]
    row_ids = jnp.arange(total_rows)
    distance = jnp.maximum(row_ids[:, None] - row_ids[None, :], 0)
    self_bias = pos_table[:, distance_buckets[distance]].reshape(KV, HEADS // KV, total_rows, total_rows)
    causal = row_ids[:, None] >= row_ids[None, :]
    normed = low(rms_norm(target_seq, norm_self))
    query_rows = both_ways(matmul(normed, w_query)).reshape(total_rows, HEADS, HEAD_DIM)
    key_rows = both_ways(matmul(normed, w_key)).reshape(total_rows, KV, HEAD_DIM)
    value_rows = both_ways(matmul(normed, w_value)).reshape(total_rows, KV, HEAD_DIM)
    attended = attend(query_rows, key_rows, value_rows, self_bias, causal)
    after_self = target_seq + low_back(matmul(attended, w_out))
    normed_cross = low(rms_norm(after_self, norm_cross))
    cross_rows = both_ways(matmul(normed_cross, wc_query)).reshape(total_rows, HEADS, HEAD_DIM)
    mem_keys = both_ways(matmul(memory_seq, wc_key)).reshape(mem_rows, KV, HEAD_DIM)
    mem_values = both_ways(matmul(memory_seq, wc_value)).reshape(mem_rows, KV, HEAD_DIM)
    crossed = attend(cross_rows, mem_keys, mem_values, jnp.float32(0.0), valid_seq)
    after_cross = after_self + low_back(matmul(crossed, wc_out))
    normed_ffn = low(rms_norm(after_cross, norm_ffn))
    gate_rows = low_back(matmul(normed_ffn, w_gate))
    up_rows = low_back(matmul(normed_ffn, w_up))
    hidden = low(gated_unit(gate_rows, up_rows))
    return after_cross + low_back(matmul(hidden, w_down))

def reference(target, memory, mem_lengths, mem_mask, distance_buckets, norm_self, w_query, w_key, w_value, w_out, pos_table, norm_cross, wc_query, wc_key, wc_value, wc_out, norm_ffn, w_gate, w_up, w_down, out_grad):
    params = (norm_self, w_query.astype(jnp.float32), w_key.astype(jnp.float32), w_value.astype(jnp.float32), w_out.astype(jnp.float32), pos_table, norm_cross, wc_query.astype(jnp.float32), wc_key.astype(jnp.float32), wc_value.astype(jnp.float32), wc_out.astype(jnp.float32), norm_ffn, w_gate.astype(jnp.float32), w_up.astype(jnp.float32), w_down.astype(jnp.float32))
    positions = jnp.arange(memory.shape[1])
    mem_valid = (positions[None, :] < mem_lengths[:, None]) & ((mem_mask == 1) | (positions[None, :] == 0))

    def forward(params_in, target_all, memory_all):

        def one_sequence(seq_item):
            return layer_one(params_in, seq_item[0], seq_item[1], seq_item[2][None, :], distance_buckets)
        return lax.map(jax.checkpoint(one_sequence), (target_all, memory_all, mem_valid))
    result, pullback = jax.vjp(forward, params, target.astype(jnp.float32), memory.astype(jnp.float32))
    weight_grads, grad_target, grad_memory = pullback(out_grad.astype(jnp.float32))
    return (result.astype(jnp.bfloat16), grad_target, grad_memory, weight_grads[0], weight_grads[1], weight_grads[2], weight_grads[3], weight_grads[4], weight_grads[5].reshape(-1), weight_grads[6], weight_grads[7], weight_grads[8], weight_grads[9], weight_grads[10], weight_grads[11], weight_grads[12], weight_grads[13], weight_grads[14])
```

```python
import functools

import jax
import jax.numpy as jnp
from jax import lax
from jax.experimental import pallas as pl
from jax.experimental.pallas import tpu as pltpu
from jax.sharding import PartitionSpec as P

HEADS = 16
KV = 8
HEAD_DIM = 64
BUCKETS = 32
BLK = 256
PAIR = 2 * HEAD_DIM

norm_eps = 1e-06
big_negative = -1000000000.0
score_scale = HEAD_DIM ** (-0.5)
F32 = jnp.float32
BF16 = jnp.bfloat16
VMEM_LIMIT = 48 * 1024 * 1024


def dot_nn(a, b):
    return lax.dot_general(a, b, (((1,), (0,)), ((), ())), preferred_element_type=F32)


def dot_nt(a, b):
    return lax.dot_general(a, b, (((1,), (1,)), ((), ())), preferred_element_type=F32)


def dot_tn(a, b):
    return lax.dot_general(a, b, (((0,), (0,)), ((), ())), preferred_element_type=F32)


def lane_pick(source, dest):
    a = lax.broadcasted_iota(jnp.int32, (PAIR, PAIR), 0)
    b = lax.broadcasted_iota(jnp.int32, (PAIR, PAIR), 1)
    keep = (a - source == b - dest) & (b >= dest) & (b < dest + HEAD_DIM)
    return keep.astype(F32).astype(BF16)


def lane_pick_t(source, dest):
    a = lax.broadcasted_iota(jnp.int32, (PAIR, PAIR), 1)
    b = lax.broadcasted_iota(jnp.int32, (PAIR, PAIR), 0)
    keep = (a - source == b - dest) & (b >= dest) & (b < dest + HEAD_DIM)
    return keep.astype(F32).astype(BF16)


def fill_bias(bias_vec_ref, tile_ref, tiles):
    for h in range(2):
        for delta in range(tiles):
            piece = bias_vec_ref[0, h : h + 1, delta * BLK : delta * BLK + 2 * BLK]
            wide = jnp.broadcast_to(piece, (BLK, 2 * BLK))
            rolled = pltpu.roll(wide, 0, 1, stride=1, stride_axis=0)
            tile_ref[h, delta] = rolled[:, BLK:]


def causal_tile():
    key_pos = lax.broadcasted_iota(jnp.int32, (BLK, BLK), 0)
    row_pos = lax.broadcasted_iota(jnp.int32, (BLK, BLK), 1)
    return key_pos <= row_pos


def online_step(carry, scores, value_t):
    highest, total, mixed = carry
    new_high = jnp.maximum(highest, jnp.max(scores, axis=0, keepdims=True))
    fade = jnp.exp(highest - new_high)
    weights = jnp.exp(scores - new_high)
    total = total * fade + jnp.sum(weights, axis=0, keepdims=True)
    mixed = mixed * fade + dot_nn(value_t, weights.astype(BF16))
    return (new_high, total, mixed)


def first_step(scores, value_t):
    highest = jnp.max(scores, axis=0, keepdims=True)
    weights = jnp.exp(scores - highest)
    total = jnp.sum(weights, axis=0, keepdims=True)
    return (highest, total, dot_nn(value_t, weights.astype(BF16)))


def self_forward_kernel(
    place_ref, q_ref, k_ref, v_ref, b_ref, o_ref, ot_ref, lse_ref, tile_ref, kz_ref, vt_ref
):
    parity = lax.rem(pl.program_id(0), 2)
    row_blocks = q_ref.shape[0] // BLK
    tiles = tile_ref.shape[1]
    fill_bias(b_ref, tile_ref, tiles)
    for h in range(2):
        kz_ref[h] = dot_nn(k_ref[...], lane_pick(parity * HEAD_DIM, h * HEAD_DIM)).astype(BF16)
        vt_ref[h] = dot_nt(lane_pick_t(parity * HEAD_DIM, h * HEAD_DIM), v_ref[...]).astype(BF16)
    remote = place_ref[0] * row_blocks
    for rb in range(row_blocks):
        rows = slice(rb * BLK, (rb + 1) * BLK)
        queries = q_ref[rows, :]
        state = []
        for h in range(2):
            scores = dot_nt(kz_ref[h, rows, :], queries) + tile_ref[h, 0]
            scores = jnp.where(causal_tile(), scores, big_negative)
            state.append(first_step(scores, vt_ref[h, :, rows]))
        for jb in range(rb):
            keys = slice(jb * BLK, (jb + 1) * BLK)
            for h in range(2):
                scores = dot_nt(kz_ref[h, keys, :], queries) + tile_ref[h, rb - jb]
                state[h] = online_step(state[h], scores, vt_ref[h, :, keys])

        def far(t, carried):
            slot = 1 + t // row_blocks
            delta = slot * row_blocks + rb - lax.rem(t, row_blocks)
            start = pl.multiple_of((row_blocks + t) * BLK, BLK)
            fresh = []
            for h in range(2):
                scores = dot_nt(kz_ref[h, pl.ds(start, BLK), :], queries) + tile_ref[h, delta]
                fresh.append(online_step(carried[h], scores, vt_ref[h, :, pl.ds(start, BLK)]))
            return tuple(fresh)

        state = lax.fori_loop(0, remote, far, tuple(state))
        mixed_t = state[0][2] / state[0][1] + state[1][2] / state[1][1]
        ot_ref[:, rows] = mixed_t.astype(BF16)
        o_ref[rows, :] = mixed_t.T.astype(BF16)
        for h in range(2):
            lse_ref[0, h : h + 1, rows] = state[h][0] + jnp.log(state[h][1])


def diagonal_sums(wide):
    rows, lanes = wide.shape
    while rows > 8:
        rows //= 2
        wide = wide[:rows] + pltpu.roll(wide[rows:], lanes - rows, 1)
    row = lax.broadcasted_iota(jnp.int32, (8, lanes), 0)
    total = jnp.where(row == 0, wide, 0.0)
    for b in range(1, 8):
        total = total + jnp.where(row == b, pltpu.roll(wide, lanes - b, 1), 0.0)
    return jnp.sum(total, axis=0, keepdims=True)


def row_products(grad_block, mixed_block, h):
    lane = lax.broadcasted_iota(jnp.int32, (8, PAIR), 1)
    picks = ((lane >= h * HEAD_DIM) & (lane < (h + 1) * HEAD_DIM)).astype(F32)
    product = grad_block.astype(F32) * mixed_block.astype(F32)
    summed = lax.dot_general(
        picks,
        product,
        (((1,), (1,)), ((), ())),
        precision=lax.Precision.HIGHEST,
        preferred_element_type=F32,
    )
    return summed[0:1]


def self_backward_kernel(
    place_ref,
    q_ref,
    k_ref,
    v_ref,
    b_ref,
    do_ref,
    o_ref,
    lse_ref,
    dq_ref,
    dk_ref,
    dv_ref,
    diag_ref,
    tile_ref,
    sum_ref,
    kz_ref,
    kt_ref,
    vz_ref,
    qp_ref,
    dop_ref,
    dk_acc,
    dv_acc,
):
    parity = lax.rem(pl.program_id(0), 2)
    row_blocks = q_ref.shape[0] // BLK
    tiles = tile_ref.shape[1]
    fill_bias(b_ref, tile_ref, tiles)
    sum_ref[...] = jnp.zeros_like(sum_ref)

    @pl.when(parity == 0)
    def clear():
        dk_acc[...] = jnp.zeros_like(dk_acc)
        dv_acc[...] = jnp.zeros_like(dv_acc)

    for h in range(2):
        in_pick = lane_pick(parity * HEAD_DIM, h * HEAD_DIM)
        out_pick = lane_pick(h * HEAD_DIM, parity * HEAD_DIM)
        kz_ref[h] = dot_nn(k_ref[...], in_pick).astype(BF16)
        kt_ref[h] = dot_nt(lane_pick_t(parity * HEAD_DIM, h * HEAD_DIM), k_ref[...]).astype(BF16)
        vz_ref[h] = dot_nn(v_ref[...], in_pick).astype(BF16)
        qp_ref[h] = dot_nn(q_ref[...], out_pick).astype(BF16)
        dop_ref[h] = dot_nn(do_ref[...], out_pick).astype(BF16)
    remote = place_ref[0] * row_blocks
    for rb in range(row_blocks):
        rows = slice(rb * BLK, (rb + 1) * BLK)
        queries = q_ref[rows, :]
        grads = do_ref[rows, :]
        mixed = o_ref[rows, :]
        deltas = [row_products(grads, mixed, h) for h in range(2)]
        lses = [lse_ref[0, h : h + 1, rows] for h in range(2)]

        def one_tile(h, keys, delta, masked):
            scores = dot_nt(kz_ref[h, keys, :], queries) + tile_ref[h, delta]
            if masked:
                scores = jnp.where(causal_tile(), scores, big_negative)
            probs = jnp.exp(scores - lses[h])
            grad_probs = dot_nt(vz_ref[h, keys, :], grads)
            grad_scores = probs * (grad_probs - deltas[h])
            sum_ref[h, delta] += grad_scores
            low_scores = grad_scores.astype(BF16)
            dv_acc[keys, :] += dot_nn(probs.astype(BF16), dop_ref[h, rows, :])
            dk_acc[keys, :] += dot_nn(low_scores, qp_ref[h, rows, :])
            return dot_nn(kt_ref[h, :, keys], low_scores)

        grad_q = one_tile(0, rows, 0, True) + one_tile(1, rows, 0, True)
        for jb in range(rb):
            keys = slice(jb * BLK, (jb + 1) * BLK)
            grad_q = grad_q + one_tile(0, keys, rb - jb, False) + one_tile(1, keys, rb - jb, False)

        def far(t, carried):
            slot = 1 + t // row_blocks
            delta = slot * row_blocks + rb - lax.rem(t, row_blocks)
            keys = pl.ds(pl.multiple_of((row_blocks + t) * BLK, BLK), BLK)
            return carried + one_tile(0, keys, delta, False) + one_tile(1, keys, delta, False)

        grad_q = lax.fori_loop(0, remote, far, grad_q)
        dq_ref[rows, :] = (grad_q.T * score_scale).astype(BF16)

    diag_ref[...] = jnp.zeros_like(diag_ref)
    for h in range(2):
        for delta in range(tiles):
            wide = jnp.concatenate([jnp.zeros((BLK, BLK), F32), sum_ref[h, delta]], axis=1)
            diag_ref[0, h : h + 1, delta * BLK : delta * BLK + 2 * BLK] += diagonal_sums(wide)

    @pl.when(parity == 1)
    def store():
        dk_ref[...] = dk_acc[...].astype(BF16)
        dv_ref[...] = dv_acc[...].astype(BF16)


def cross_forward_kernel(q_ref, k_ref, v_ref, m_ref, o_ref, ot_ref, lse_ref, kz_ref, vt_ref):
    parity = lax.rem(pl.program_id(0), 2)
    for h in range(2):
        kz_ref[h] = dot_nn(k_ref[...], lane_pick(parity * HEAD_DIM, h * HEAD_DIM)).astype(BF16)
        vt_ref[h] = dot_nt(lane_pick_t(parity * HEAD_DIM, h * HEAD_DIM), v_ref[...]).astype(BF16)
    for rb in range(q_ref.shape[0] // BLK):
        rows = slice(rb * BLK, (rb + 1) * BLK)
        queries = q_ref[rows, :]
        mixed_t = None
        for h in range(2):
            state = None
            for jb in range(k_ref.shape[0] // BLK):
                keys = slice(jb * BLK, (jb + 1) * BLK)
                scores = dot_nt(kz_ref[h, keys, :], queries) + m_ref[keys, :]
                if state is None:
                    state = first_step(scores, vt_ref[h, :, keys])
                else:
                    state = online_step(state, scores, vt_ref[h, :, keys])
            part = state[2] / state[1]
            mixed_t = part if mixed_t is None else mixed_t + part
            lse_ref[0, h : h + 1, rows] = state[0] + jnp.log(state[1])
        ot_ref[:, rows] = mixed_t.astype(BF16)
        o_ref[rows, :] = mixed_t.T.astype(BF16)


def cross_backward_kernel(
    q_ref,
    k_ref,
    v_ref,
    m_ref,
    do_ref,
    o_ref,
    lse_ref,
    dq_ref,
    dk_ref,
    dv_ref,
    kz_ref,
    kt_ref,
    vz_ref,
    qp_ref,
    dop_ref,
    dk_acc,
    dv_acc,
):
    parity = lax.rem(pl.program_id(0), 2)

    @pl.when(parity == 0)
    def clear():
        dk_acc[...] = jnp.zeros_like(dk_acc)
        dv_acc[...] = jnp.zeros_like(dv_acc)

    for h in range(2):
        in_pick = lane_pick(parity * HEAD_DIM, h * HEAD_DIM)
        out_pick = lane_pick(h * HEAD_DIM, parity * HEAD_DIM)
        kz_ref[h] = dot_nn(k_ref[...], in_pick).astype(BF16)
        kt_ref[h] = dot_nt(lane_pick_t(parity * HEAD_DIM, h * HEAD_DIM), k_ref[...]).astype(BF16)
        vz_ref[h] = dot_nn(v_ref[...], in_pick).astype(BF16)
        qp_ref[h] = dot_nn(q_ref[...], out_pick).astype(BF16)
        dop_ref[h] = dot_nn(do_ref[...], out_pick).astype(BF16)
    for rb in range(q_ref.shape[0] // BLK):
        rows = slice(rb * BLK, (rb + 1) * BLK)
        queries = q_ref[rows, :]
        grads = do_ref[rows, :]
        mixed = o_ref[rows, :]
        grad_q = None
        for h in range(2):
            delta = row_products(grads, mixed, h)
            lse = lse_ref[0, h : h + 1, rows]
            for jb in range(k_ref.shape[0] // BLK):
                keys = slice(jb * BLK, (jb + 1) * BLK)
                scores = dot_nt(kz_ref[h, keys, :], queries) + m_ref[keys, :]
                probs = jnp.exp(scores - lse)
                grad_probs = dot_nt(vz_ref[h, keys, :], grads)
                low_scores = (probs * (grad_probs - delta)).astype(BF16)
                dv_acc[keys, :] += dot_nn(probs.astype(BF16), dop_ref[h, rows, :])
                dk_acc[keys, :] += dot_nn(low_scores, qp_ref[h, rows, :])
                part = dot_nn(kt_ref[h, :, keys], low_scores)
                grad_q = part if grad_q is None else grad_q + part
        dq_ref[rows, :] = (grad_q.T * score_scale).astype(BF16)

    @pl.when(parity == 1)
    def store():
        dk_ref[...] = dk_acc[...].astype(BF16)
        dv_ref[...] = dv_acc[...].astype(BF16)


def shape_of(shape, dtype):
    return jax.ShapeDtypeStruct(shape, dtype)


def tile_pair(rows):
    return pl.BlockSpec((rows, PAIR), lambda g: (0, g))


def tile_pair_t(rows):
    return pl.BlockSpec((PAIR, rows), lambda g: (g, 0))


def tile_group(rows):
    return pl.BlockSpec((rows, PAIR), lambda g: (0, g // 2))


def tile_rows(width):
    return pl.BlockSpec((1, 2, width), lambda g: (g, 0, 0))


def kernel_params():
    return pltpu.CompilerParams(
        dimension_semantics=("arbitrary",), vmem_limit_bytes=VMEM_LIMIT
    )


def cost(flops, transcendentals, nbytes):
    return pl.CostEstimate(
        flops=int(flops), transcendentals=int(transcendentals), bytes_accessed=int(nbytes)
    )


def self_forward(place, q, k, v, bias_vec):
    rows, width = q.shape
    keys = k.shape[0]
    pairs = width // PAIR
    tiles = keys // BLK
    return pl.pallas_call(
        self_forward_kernel,
        grid=(pairs,),
        in_specs=[
            pl.BlockSpec(memory_space=pltpu.SMEM),
            tile_pair(rows),
            tile_group(keys),
            tile_group(keys),
            tile_rows(bias_vec.shape[2]),
        ],
        out_specs=[tile_pair(rows), tile_pair_t(rows), tile_rows(rows)],
        out_shape=[
            shape_of((rows, width), BF16),
            shape_of((width, rows), BF16),
            shape_of((pairs, 2, rows), F32),
        ],
        scratch_shapes=[
            pltpu.VMEM((2, tiles, BLK, BLK), F32),
            pltpu.VMEM((2, keys, PAIR), BF16),
            pltpu.VMEM((2, PAIR, keys), BF16),
        ],
        compiler_params=kernel_params(),
        cost_estimate=cost(4 * 2 * rows * keys * width * 2, pairs * 2 * rows * keys, 8 * rows * width),
        name="self_forward",
    )(place, q, k, v, bias_vec)


def self_backward(place, q, k, v, bias_vec, grads, mixed, lse):
    rows, width = q.shape
    keys, kv_width = k.shape
    pairs = width // PAIR
    tiles = keys // BLK
    return pl.pallas_call(
        self_backward_kernel,
        grid=(pairs,),
        in_specs=[
            pl.BlockSpec(memory_space=pltpu.SMEM),
            tile_pair(rows),
            tile_group(keys),
            tile_group(keys),
            tile_rows(bias_vec.shape[2]),
            tile_pair(rows),
            tile_pair(rows),
            tile_rows(rows),
        ],
        out_specs=[
            tile_pair(rows),
            tile_group(keys),
            tile_group(keys),
            tile_rows(bias_vec.shape[2]),
        ],
        out_shape=[
            shape_of((rows, width), BF16),
            shape_of((keys, kv_width), BF16),
            shape_of((keys, kv_width), BF16),
            shape_of(bias_vec.shape, F32),
        ],
        scratch_shapes=[
            pltpu.VMEM((2, tiles, BLK, BLK), F32),
            pltpu.VMEM((2, tiles, BLK, BLK), F32),
            pltpu.VMEM((2, keys, PAIR), BF16),
            pltpu.VMEM((2, PAIR, keys), BF16),
            pltpu.VMEM((2, keys, PAIR), BF16),
            pltpu.VMEM((2, rows, PAIR), BF16),
            pltpu.VMEM((2, rows, PAIR), BF16),
            pltpu.VMEM((keys, PAIR), F32),
            pltpu.VMEM((keys, PAIR), F32),
        ],
        compiler_params=kernel_params(),
        cost_estimate=cost(10 * 2 * rows * keys * width * 2, pairs * 2 * rows * keys, 12 * rows * width),
        name="self_backward",
    )(place, q, k, v, bias_vec, grads, mixed, lse)


def cross_forward(q, k, v, mask_col):
    rows, width = q.shape
    keys = k.shape[0]
    pairs = width // PAIR
    return pl.pallas_call(
        cross_forward_kernel,
        grid=(pairs,),
        in_specs=[
            tile_pair(rows),
            tile_group(keys),
            tile_group(keys),
            pl.BlockSpec((keys, 1), lambda g: (0, 0)),
        ],
        out_specs=[tile_pair(rows), tile_pair_t(rows), tile_rows(rows)],
        out_shape=[
            shape_of((rows, width), BF16),
            shape_of((width, rows), BF16),
            shape_of((pairs, 2, rows), F32),
        ],
        scratch_shapes=[
            pltpu.VMEM((2, keys, PAIR), BF16),
            pltpu.VMEM((2, PAIR, keys), BF16),
        ],
        compiler_params=kernel_params(),
        cost_estimate=cost(4 * 2 * rows * keys * width * 2, pairs * 2 * rows * keys, 8 * rows * width),
        name="cross_forward",
    )(q, k, v, mask_col)


def cross_backward(q, k, v, mask_col, grads, mixed, lse):
    rows, width = q.shape
    keys, kv_width = k.shape
    pairs = width // PAIR
    return pl.pallas_call(
        cross_backward_kernel,
        grid=(pairs,),
        in_specs=[
            tile_pair(rows),
            tile_group(keys),
            tile_group(keys),
            pl.BlockSpec((keys, 1), lambda g: (0, 0)),
            tile_pair(rows),
            tile_pair(rows),
            tile_rows(rows),
        ],
        out_specs=[tile_pair(rows), tile_group(keys), tile_group(keys)],
        out_shape=[
            shape_of((rows, width), BF16),
            shape_of((keys, kv_width), BF16),
            shape_of((keys, kv_width), BF16),
        ],
        scratch_shapes=[
            pltpu.VMEM((2, keys, PAIR), BF16),
            pltpu.VMEM((2, PAIR, keys), BF16),
            pltpu.VMEM((2, keys, PAIR), BF16),
            pltpu.VMEM((2, rows, PAIR), BF16),
            pltpu.VMEM((2, rows, PAIR), BF16),
            pltpu.VMEM((keys, PAIR), F32),
            pltpu.VMEM((keys, PAIR), F32),
        ],
        compiler_params=kernel_params(),
        cost_estimate=cost(10 * 2 * rows * keys * width * 2, pairs * 2 * rows * keys, 12 * rows * width),
        name="cross_backward",
    )(q, k, v, mask_col, grads, mixed, lse)


FBLK = 128


def ffn_kernel(core_ref, x_ref, og_ref, wg_ref, wu_ref, wd_ref, ht_ref, gg_ref, gu_ref, out_ref, e_ref, out_acc, e_acc):
    step = pl.program_id(0)

    @pl.when(step == 0)
    def clear():
        out_acc[...] = jnp.zeros_like(out_acc)
        e_acc[...] = jnp.zeros_like(e_acc)

    wide = jnp.concatenate([wg_ref[...], wu_ref[...]], axis=1)
    both = dot_nn(x_ref[...], wide)
    gate, up = both[:, :FBLK], both[:, FBLK:]
    grad_hidden = dot_nt(og_ref[...], wd_ref[...])
    factor = (2.0 / jnp.pi) ** 0.5
    square = gate * gate
    bend = jnp.tanh(factor * (gate + 0.044715 * gate * square))
    half = 0.5 * (1.0 + bend)
    gelu = gate * half
    slope = half + 0.5 * gate * (1.0 - bend * bend) * (factor * (1.0 + 3 * 0.044715 * square))
    hidden = gelu * up
    low_hidden = hidden.astype(BF16)
    ht_ref[...] = hidden.T.astype(BF16)
    grad_gate = (grad_hidden * up * slope).astype(BF16)
    grad_up = (grad_hidden * gelu).astype(BF16)
    gg_ref[...] = grad_gate
    gu_ref[...] = grad_up
    out_acc[...] += dot_nn(low_hidden, wd_ref[...])
    e_acc[...] += dot_nt(jnp.concatenate([grad_gate, grad_up], axis=1), wide)

    @pl.when(step == pl.num_programs(0) - 1)
    def store():
        out_ref[...] = out_acc[...].astype(BF16)
        e_ref[...] = e_acc[...].astype(BF16)


def ffn(core, normed, out_grad, w_gate, w_up, w_down):
    rows, width = normed.shape
    hidden = w_gate.shape[1] // 2
    steps = hidden // FBLK
    whole = pl.BlockSpec((rows, width), lambda j, c: (0, 0))
    return pl.pallas_call(
        ffn_kernel,
        grid_spec=pltpu.PrefetchScalarGridSpec(
            num_scalar_prefetch=1,
            grid=(steps,),
            in_specs=[
                whole,
                whole,
                pl.BlockSpec((width, FBLK), lambda j, c: (0, c[0] * steps + j)),
                pl.BlockSpec((width, FBLK), lambda j, c: (0, c[0] * steps + j)),
                pl.BlockSpec((FBLK, width), lambda j, c: (c[0] * steps + j, 0)),
            ],
            out_specs=[
                pl.BlockSpec((FBLK, rows), lambda j, c: (j, 0)),
                pl.BlockSpec((rows, FBLK), lambda j, c: (0, j)),
                pl.BlockSpec((rows, FBLK), lambda j, c: (0, j)),
                whole,
                whole,
            ],
            scratch_shapes=[pltpu.VMEM((rows, width), F32), pltpu.VMEM((rows, width), F32)],
        ),
        out_shape=[
            shape_of((hidden, rows), BF16),
            shape_of((rows, hidden), BF16),
            shape_of((rows, hidden), BF16),
            shape_of((rows, width), BF16),
            shape_of((rows, width), BF16),
        ],
        compiler_params=kernel_params(),
        cost_estimate=cost(2 * 6 * rows * width * hidden, rows * hidden, 6 * width * hidden),
        name="ffn",
    )(core, normed, out_grad, w_gate, w_up, w_down)


def rms_parts(values, gain):
    inverse = lax.rsqrt(jnp.mean(values * values, axis=-1, keepdims=True) + norm_eps)
    return (values * inverse * gain).astype(BF16), inverse


def rms_back(values, inverse, gain, grad):
    scaled = grad * gain
    mean_dot = jnp.mean(values * scaled, axis=-1, keepdims=True)
    grad_values = inverse * scaled - inverse * inverse * inverse * values * mean_dot
    grad_gain = jnp.sum(grad * values * inverse, axis=0)
    return grad_values, grad_gain


def bits_of(size):
    return (size - 1).bit_length()


class Places:
    def __init__(self):
        self.seq = lax.axis_size("seq")
        self.dp = lax.axis_size("dp")
        self.nx = self.seq // 2
        self.chips = self.dp * self.nx
        place = lax.axis_index("seq")
        self.core = lax.rem(place, 2)
        self.x = place // 2
        self.d = lax.axis_index("dp")
        self.dp_bits = bits_of(self.dp)
        self.x_bits = bits_of(self.nx)
        self.names = [("dp", b) for b in reversed(range(self.dp_bits))] + [
            ("x", b) for b in reversed(range(self.x_bits))
        ]

    def swap_core(self, value):
        return lax.ppermute(value, "seq", [(s, s ^ 1) for s in range(self.seq)])

    def shift_x(self, value, by):
        pairs = [(s, (s + 2 * by) % self.seq) for s in range(self.seq)]
        return lax.ppermute(value, "seq", pairs)

    def my_bit(self, name):
        axis, bit = name
        where = self.d if axis == "dp" else self.x
        return (where >> bit) & 1

    def flip(self, value, name):
        axis, bit = name
        if axis == "dp":
            pairs = [(s, s ^ (1 << bit)) for s in range(self.dp)]
            return lax.ppermute(value, "dp", pairs)
        pairs = [(s, s ^ (2 << bit)) for s in range(self.seq)]
        return lax.ppermute(value, "seq", pairs)

    def by_core(self, own, other, axis):
        first = jnp.concatenate([own, other], axis=axis)
        second = jnp.concatenate([other, own], axis=axis)
        return jnp.where(self.core == 0, first, second)

    def core_rows(self, value, mine):
        half = value.shape[0] // 2
        which = self.core if mine else 1 - self.core
        return lax.dynamic_slice_in_dim(value, which * half, half, 0)

    def core_columns(self, value):
        half = value.shape[1] // 2
        return lax.dynamic_slice_in_dim(value, self.core * half, half, 1)


def order_of(places, kind):
    dp0 = [("dp", 0)]
    dp_rest = [("dp", b) for b in range(1, places.dp_bits)]
    xs = [("x", b) for b in range(places.x_bits)]
    if kind == 0:
        return xs + dp0 + dp_rest
    if kind == 1:
        return dp0 + xs + dp_rest
    return dp_rest + xs + dp0


def pick(value, index, axis):
    return lax.dynamic_index_in_dim(value, index, axis, keepdims=False)


def chip_scatter(places, kind, factors, core_major=False):
    names = list(places.names)
    flipped = names[0] if core_major else None
    lefts = []
    for xt, _ in factors:
        rows = xt.shape[0] // places.chips
        lefts.append(xt.reshape((2,) * len(names) + (rows, xt.shape[1])))
    got = []

    def products(left_list, received):
        parts = []
        for left, (_, y) in zip(left_list, factors):
            flat = left.reshape((-1, left.shape[-1]))
            parts.append(lax.dot_general(flat, y, (((1,), (0,)), ((), ())), preferred_element_type=F32))
        total = jnp.concatenate(parts, axis=1) if len(parts) > 1 else parts[0]
        for value in received:
            total = total + value.reshape(total.shape).astype(F32)
        return total

    for name in order_of(places, kind):
        axis = names.index(name)
        names.pop(axis)
        own = places.my_bit(name)
        if name == flipped:
            own = own ^ places.core
        sent = products(
            [pick(v, 1 - own, axis) for v in lefts], [pick(v, 1 - own, axis) for v in got]
        ).astype(BF16)
        lefts = [pick(v, own, axis) for v in lefts]
        got = [pick(v, own, axis) for v in got]
        arrived = places.flip(sent, name)
        got.append(arrived.reshape((2,) * len(names) + (lefts[0].shape[-2], arrived.shape[-1])))
    return products(lefts, got)


def core_join(places, share):
    own = places.core_rows(share, True)
    arrived = places.swap_core(places.core_rows(share, False))
    return places.by_core(own, arrived, 1)


def per_device(
    target,
    memory,
    mem_lengths,
    mem_mask,
    distance_buckets,
    norm_self,
    w_query,
    w_key,
    w_value,
    w_out,
    pos_table,
    norm_cross,
    wc_query,
    wc_key,
    wc_value,
    wc_out,
    norm_ffn,
    w_gate,
    w_up,
    w_down,
    out_grad,
):
    at = Places()
    core, nx = at.core, at.nx
    local, width = target.shape[1], target.shape[2]
    mem_local = memory.shape[1]
    chip_rows = 2 * local
    full = distance_buckets.shape[0]
    qw = HEADS * HEAD_DIM // 2
    kw = KV * HEAD_DIM // 2
    head_count = HEADS // 2
    place = at.x.astype(jnp.int32).reshape(1)
    core_arg = core.astype(jnp.int32).reshape(1)

    tokens = target.reshape(local, width)
    slots = jnp.concatenate([tokens[None]] + [at.shift_x(tokens, s)[None] for s in range(1, nx)], axis=0)
    slots = at.by_core(slots, at.swap_core(slots), 1)
    mem_own = memory.reshape(mem_local, width)
    mem_slots = jnp.concatenate(
        [mem_own[None]] + [at.shift_x(mem_own, s)[None] for s in range(1, nx)], axis=0
    )
    mem_slots = at.by_core(mem_slots, at.swap_core(mem_slots), 1)
    mem_all = mem_slots.reshape(-1, width)
    grad_own = out_grad.reshape(local, width)
    grad_chip = at.by_core(grad_own, at.swap_core(grad_own), 0)

    own_table = lax.dynamic_slice_in_dim(pos_table, core * head_count, head_count, 0)
    onehot = (distance_buckets[:, None] == jnp.arange(BUCKETS, dtype=jnp.int32)[None, :]).astype(F32)
    by_distance = lax.dot_general(
        own_table, onehot, (((1,), (1,)), ((), ())), precision=lax.Precision.HIGHEST
    )
    bias_vec = jnp.pad(by_distance, ((0, 0), (BLK, 0))).reshape(head_count // 2, 2, BLK + full)

    mem_ids = jnp.arange(mem_mask.shape[1], dtype=jnp.int32)
    valid = (mem_ids < mem_lengths[0]) & ((mem_mask[0] == 1) | (mem_ids == 0))
    mask_add = jnp.where(valid, 0.0, big_negative).astype(F32).reshape(nx, 2 * mem_local)
    mask_order = jnp.concatenate(
        [pick(mask_add, lax.rem(at.x - s + nx, nx), 0)[None] for s in range(nx)], axis=0
    )
    mask_col = mask_order.reshape(-1, 1)

    base = slots.astype(F32)
    normed_slots, inverse_slots = rms_parts(base, norm_self)
    normed_all = normed_slots.reshape(-1, width)
    normed_chip = normed_all[:chip_rows]
    query = (dot_nn(normed_chip, at.core_columns(w_query)).astype(BF16) * BF16(score_scale)).astype(BF16)
    keys = dot_nn(normed_all, at.core_columns(w_key)).astype(BF16)
    values = dot_nn(normed_all, at.core_columns(w_value)).astype(BF16)
    mixed, mixed_t, lse_self = self_forward(place, query, keys, values, bias_vec)
    mixed_other = at.swap_core(mixed)
    mixed_t_other = at.swap_core(mixed_t)
    base_chip = base[0]
    after_self = (
        base_chip
        + dot_nn(mixed, at.core_rows(w_out, True))
        + dot_nn(mixed_other, at.core_rows(w_out, False))
    )

    normed_cross, inverse_cross = rms_parts(after_self, norm_cross)
    mem_keys = dot_nn(mem_all, at.core_columns(wc_key)).astype(BF16)
    mem_values = dot_nn(mem_all, at.core_columns(wc_value)).astype(BF16)
    cross_query = (dot_nn(normed_cross, at.core_columns(wc_query)).astype(BF16) * BF16(score_scale)).astype(BF16)
    crossed, crossed_t, lse_cross = cross_forward(cross_query, mem_keys, mem_values, mask_col)
    crossed_other = at.swap_core(crossed)
    crossed_t_other = at.swap_core(crossed_t)
    after_cross = (
        after_self
        + dot_nn(crossed, at.core_rows(wc_out, True))
        + dot_nn(crossed_other, at.core_rows(wc_out, False))
    )

    normed_ffn, inverse_ffn = rms_parts(after_cross, norm_ffn)
    hidden_t, grad_gate, grad_up, out_part, e_part = ffn(
        core_arg, normed_ffn, grad_chip, w_gate, w_up, w_down
    )
    out_other = at.swap_core(at.core_rows(out_part, False))
    output = (
        at.core_rows(after_cross, True)
        + at.core_rows(out_part, True).astype(F32)
        + out_other.astype(F32)
    ).astype(BF16)
    e_ffn = e_part.astype(F32) + at.swap_core(e_part).astype(F32)
    grad_cross_part, grad_norm_ffn = rms_back(after_cross, inverse_ffn, norm_ffn, e_ffn)
    grad_after_cross = grad_chip.astype(F32) + grad_cross_part
    grad_cross_bf = grad_after_cross.astype(BF16)

    hidden_t_all = jnp.concatenate([hidden_t, at.swap_core(hidden_t)], axis=0)
    down_share = chip_scatter(at, 2, [(hidden_t_all, at.core_columns(grad_chip))], core_major=True)
    normed_ffn_t = normed_ffn.T
    gate_share = chip_scatter(at, 0, [(normed_ffn_t, grad_gate)])
    up_share = chip_scatter(at, 1, [(normed_ffn_t, grad_up)])

    grad_crossed = dot_nt(grad_cross_bf, at.core_rows(wc_out, True)).astype(BF16)
    grad_cq, grad_mk, grad_mv = cross_backward(
        cross_query, mem_keys, mem_values, mask_col, grad_crossed, crossed, lse_cross
    )
    grad_cq_other = at.swap_core(grad_cq)
    wc_query_own = at.core_columns(wc_query)
    wc_query_other = lax.dynamic_slice_in_dim(wc_query, (1 - core) * qw, qw, 1)
    e_cross = dot_nt(grad_cq, wc_query_own) + dot_nt(grad_cq_other, wc_query_other)
    grad_self_part, grad_norm_cross = rms_back(after_self, inverse_cross, norm_cross, e_cross)
    grad_after_self = grad_after_cross + grad_self_part
    grad_self_bf = grad_after_self.astype(BF16)

    crossed_t_all = jnp.concatenate([crossed_t, crossed_t_other], axis=0)
    wc_out_share = chip_scatter(at, 0, [(crossed_t_all, at.core_columns(grad_cross_bf))], core_major=True)
    wc_in_share = chip_scatter(
        at, 1, [(normed_cross.T, grad_cq), (mem_all.T, jnp.concatenate([grad_mk, grad_mv], axis=1))]
    )

    grad_mem_pair = jnp.concatenate([grad_mk, grad_mv], axis=1).reshape(nx, 2 * mem_local, 2 * kw)
    grad_mem_chip = grad_mem_pair[0].astype(F32)
    for s in range(1, nx):
        grad_mem_chip = grad_mem_chip + at.shift_x(grad_mem_pair[s], nx - s).astype(F32)
    grad_mem_chip = grad_mem_chip.astype(BF16)
    mem_mine = at.core_rows(grad_mem_chip, True)
    mem_got = at.swap_core(at.core_rows(grad_mem_chip, False))
    grad_memory = dot_nt(at.by_core(mem_mine[:, :kw], mem_got[:, :kw], 1), wc_key) + dot_nt(
        at.by_core(mem_mine[:, kw:], mem_got[:, kw:], 1), wc_value
    )

    grad_mixed = dot_nt(grad_self_bf, at.core_rows(w_out, True)).astype(BF16)
    grad_q, grad_k, grad_v, diagonals = self_backward(
        place, query, keys, values, bias_vec, grad_mixed, mixed, lse_self
    )
    grad_pair = jnp.concatenate([grad_k, grad_v], axis=1)
    mixed_t_all = jnp.concatenate([mixed_t, mixed_t_other], axis=0)
    out_share = chip_scatter(at, 0, [(mixed_t_all, at.core_columns(grad_self_bf))], core_major=True)
    normed_all_t = normed_all.T
    in_share = chip_scatter(at, 1, [(normed_all_t[:, :chip_rows], grad_q), (normed_all_t, grad_pair)])

    pair_slots = grad_pair.reshape(nx, chip_rows, 2 * kw)
    pair_chip = pair_slots[0].astype(F32)
    for s in range(1, nx):
        pair_chip = pair_chip + at.shift_x(pair_slots[s], nx - s).astype(F32)
    grads_chip = jnp.concatenate([grad_q, pair_chip.astype(BF16)], axis=1)
    grads_mine = at.core_rows(grads_chip, True)
    grads_got = at.swap_core(at.core_rows(grads_chip, False))
    e_self = (
        dot_nt(at.by_core(grads_mine[:, :qw], grads_got[:, :qw], 1), w_query)
        + dot_nt(at.by_core(grads_mine[:, qw : qw + kw], grads_got[:, qw : qw + kw], 1), w_key)
        + dot_nt(at.by_core(grads_mine[:, qw + kw :], grads_got[:, qw + kw :], 1), w_value)
    )
    base_own = tokens.astype(F32)
    inverse_own = at.core_rows(inverse_slots[0], True)
    grad_base, grad_norm_self = rms_back(base_own, inverse_own, norm_self, e_self)
    grad_target = at.core_rows(grad_after_self, True) + grad_base

    own_bias = lax.dot_general(
        diagonals.reshape(head_count, -1)[:, BLK:],
        onehot,
        (((1,), (0,)), ((), ())),
        precision=lax.Precision.HIGHEST,
        preferred_element_type=F32,
    )
    table = lax.dynamic_update_slice_in_dim(
        jnp.zeros((HEADS, BUCKETS), F32), own_bias, core * head_count, 0
    )
    first_core = (core == 0).astype(F32)
    small = jnp.concatenate(
        [
            grad_norm_self.reshape(at.chips, -1),
            (grad_norm_cross * first_core).reshape(at.chips, -1),
            (grad_norm_ffn * first_core).reshape(at.chips, -1),
            table.reshape(at.chips, -1),
        ],
        axis=1,
    )
    small = small + at.swap_core(small)
    small = small.reshape((2,) * len(at.names) + (small.shape[1],))
    names = list(at.names)
    for name in order_of(at, 0):
        axis = names.index(name)
        names.pop(axis)
        mine = at.my_bit(name)
        small = pick(small, mine, axis) + at.flip(pick(small, 1 - mine, axis), name)
    norm_block = width // at.chips
    bias_block = HEADS * BUCKETS // at.chips
    half_norm = norm_block // 2

    def share_of(start, size):
        return lax.dynamic_slice_in_dim(small, start + core * (size // 2), size // 2, 0)

    cross_in = core_join(at, wc_in_share[:, :qw])
    cross_key = core_join(at, wc_in_share[:, qw : qw + kw])
    cross_value = core_join(at, wc_in_share[:, qw + kw :])
    self_in = core_join(at, in_share[:, :qw])
    self_key = core_join(at, in_share[:, qw : qw + kw])
    self_value = core_join(at, in_share[:, qw + kw :])
    return (
        output.reshape(target.shape),
        grad_target.reshape(target.shape),
        grad_memory.reshape(memory.shape),
        share_of(0, norm_block),
        self_in,
        self_key,
        self_value,
        core_join(at, out_share),
        share_of(3 * norm_block, bias_block),
        share_of(norm_block, norm_block),
        cross_in,
        cross_key,
        cross_value,
        core_join(at, wc_out_share),
        share_of(2 * norm_block, norm_block),
        core_join(at, gate_share),
        core_join(at, up_share),
        core_join(at, down_share),
    )


def solution(mesh):
    tokens = P("dp", "seq", None)
    row_share = P(("dp", "seq"))
    matrix_share = P(("dp", "seq"), None)
    return jax.shard_map(
        per_device,
        mesh=mesh,
        in_specs=(tokens, tokens, P("dp"), P("dp", None)) + (P(),) * 16 + (tokens,),
        out_specs=(tokens, tokens, tokens, row_share)
        + (matrix_share,) * 4
        + (row_share, row_share)
        + (matrix_share,) * 4
        + (row_share,)
        + (matrix_share,) * 3,
        check_vma=False,
    )
```

```python
import functools

import jax
import jax.numpy as jnp
from jax import lax
from jax.experimental import pallas as pl
from jax.experimental.pallas import tpu as pltpu
from jax.sharding import PartitionSpec as P

HEADS = 16
KV = 8
HEAD_DIM = 64
BUCKETS = 32
BLK = 256
PAIR = 2 * HEAD_DIM

norm_eps = 1e-06
big_negative = -1000000000.0
score_scale = HEAD_DIM ** (-0.5)
F32 = jnp.float32
BF16 = jnp.bfloat16
VMEM_LIMIT = 61 * 1024 * 1024


def dot_nn(a, b):
    return lax.dot_general(a, b, (((1,), (0,)), ((), ())), preferred_element_type=F32)


def dot_nt(a, b):
    return lax.dot_general(a, b, (((1,), (1,)), ((), ())), preferred_element_type=F32)


def dot_tn(a, b):
    return lax.dot_general(a, b, (((0,), (0,)), ((), ())), preferred_element_type=F32)


def lane_pick(source, dest):
    a = lax.broadcasted_iota(jnp.int32, (PAIR, PAIR), 0)
    b = lax.broadcasted_iota(jnp.int32, (PAIR, PAIR), 1)
    keep = (a - source == b - dest) & (b >= dest) & (b < dest + HEAD_DIM)
    return keep.astype(F32).astype(BF16)


def lane_pick_t(source, dest):
    a = lax.broadcasted_iota(jnp.int32, (PAIR, PAIR), 1)
    b = lax.broadcasted_iota(jnp.int32, (PAIR, PAIR), 0)
    keep = (a - source == b - dest) & (b >= dest) & (b < dest + HEAD_DIM)
    return keep.astype(F32).astype(BF16)


def bias_tile(bias_vec_ref, h, delta):
    piece = bias_vec_ref[0, h : h + 1, delta * BLK : delta * BLK + 2 * BLK]
    wide = jnp.broadcast_to(piece, (BLK, 2 * BLK))
    return pltpu.roll(wide, 0, 1, stride=1, stride_axis=0)[:, BLK:]


def tile_plan(row_blocks, slots):
    plan = [(delta, 0) for delta in range(row_blocks)]
    for slot in range(1, slots):
        plan += [(slot * row_blocks + c, slot) for c in range(1 - row_blocks, row_blocks)]
    return plan


def tile_at(row_blocks, rb, kb):
    slot, jb = kb // row_blocks, kb % row_blocks
    if slot == 0:
        return rb - jb, rb - jb
    first = row_blocks + (slot - 1) * (2 * row_blocks - 1)
    return first + rb - jb + row_blocks - 1, slot * row_blocks + rb - jb


def key_blocks(row_blocks, slots, rb):
    return list(range(rb + 1)) + list(range(row_blocks, row_blocks * slots))


def fill_bias(place, bias_vec_ref, tile_ref, row_blocks, slots):
    for at, (delta, slot) in enumerate(tile_plan(row_blocks, slots)):
        for h in range(2):
            tile = bias_tile(bias_vec_ref, h, delta)
            if slot:
                tile = tile + jnp.where(place >= slot, 0.0, big_negative)
            elif delta == 0:
                tile = jnp.where(causal_tile(), tile, big_negative)
            tile_ref[h, at] = tile


def causal_tile():
    key_pos = lax.broadcasted_iota(jnp.int32, (BLK, BLK), 0)
    row_pos = lax.broadcasted_iota(jnp.int32, (BLK, BLK), 1)
    return key_pos <= row_pos


def online_step(carry, scores, value_t):
    highest, total, mixed = carry
    new_high = jnp.maximum(highest, jnp.max(scores, axis=0, keepdims=True))
    fade = jnp.exp(highest - new_high)
    weights = jnp.exp(scores - new_high)
    total = total * fade + jnp.sum(weights, axis=0, keepdims=True)
    mixed = mixed * fade + dot_nn(value_t, weights.astype(BF16))
    return (new_high, total, mixed)


def first_step(scores, value_t):
    highest = jnp.max(scores, axis=0, keepdims=True)
    weights = jnp.exp(scores - highest)
    total = jnp.sum(weights, axis=0, keepdims=True)
    return (highest, total, dot_nn(value_t, weights.astype(BF16)))


def self_forward_kernel(slots, place_ref, q_ref, b_ref, *refs):
    k_refs, v_refs = refs[:slots], refs[slots : 2 * slots]
    o_ref, ot_ref, lse_ref, tile_ref, kz_ref, vt_ref = refs[2 * slots :]
    parity = lax.rem(pl.program_id(0), 2)
    rows_all = q_ref.shape[0]
    row_blocks = rows_all // BLK
    fill_bias(place_ref[0], b_ref, tile_ref, row_blocks, slots)
    for h in range(2):
        for slot in range(slots):
            span = slice(slot * rows_all, (slot + 1) * rows_all)
            pick_k = lane_pick(parity * HEAD_DIM, h * HEAD_DIM)
            pick_v = lane_pick_t(parity * HEAD_DIM, h * HEAD_DIM)
            kz_ref[h, span, :] = dot_nn(k_refs[slot][...], pick_k).astype(BF16)
            vt_ref[h, :, span] = dot_nt(pick_v, v_refs[slot][...]).astype(BF16)
    for rb in range(row_blocks):
        rows = slice(rb * BLK, (rb + 1) * BLK)
        queries = q_ref[rows, :]
        state = [None, None]
        for kb in key_blocks(row_blocks, slots, rb):
            keys = slice(kb * BLK, (kb + 1) * BLK)
            at, _ = tile_at(row_blocks, rb, kb)
            for h in range(2):
                scores = dot_nt(kz_ref[h, keys, :], queries) + tile_ref[h, at]
                values = vt_ref[h, :, keys]
                if state[h] is None:
                    state[h] = first_step(scores, values)
                else:
                    state[h] = online_step(state[h], scores, values)
        mixed_t = state[0][2] / state[0][1] + state[1][2] / state[1][1]
        ot_ref[:, rows] = mixed_t.astype(BF16)
        o_ref[rows, :] = mixed_t.T.astype(BF16)
        for h in range(2):
            lse_ref[0, h : h + 1, rows] = state[h][0] + jnp.log(state[h][1])


def diagonal_sums(wide):
    rows, lanes = wide.shape
    while rows > 8:
        rows //= 2
        wide = wide[:rows] + pltpu.roll(wide[rows:], lanes - rows, 1)
    row = lax.broadcasted_iota(jnp.int32, (8, lanes), 0)
    total = jnp.where(row == 0, wide, 0.0)
    for b in range(1, 8):
        total = total + jnp.where(row == b, pltpu.roll(wide, lanes - b, 1), 0.0)
    return jnp.sum(total, axis=0, keepdims=True)


def row_products(grad_block, mixed_block, h):
    lane = lax.broadcasted_iota(jnp.int32, (8, PAIR), 1)
    picks = ((lane >= h * HEAD_DIM) & (lane < (h + 1) * HEAD_DIM)).astype(F32)
    product = grad_block.astype(F32) * mixed_block.astype(F32)
    summed = lax.dot_general(
        picks,
        product,
        (((1,), (1,)), ((), ())),
        precision=lax.Precision.HIGHEST,
        preferred_element_type=F32,
    )
    return summed[0:1]


def self_backward_kernel(slots, place_ref, q_ref, b_ref, do_ref, o_ref, lse_ref, *refs):
    k_refs, v_refs = refs[:slots], refs[slots : 2 * slots]
    dq_ref, dk_ref, dv_ref, diag_ref = refs[2 * slots : 2 * slots + 4]
    tile_ref, sum_ref, kz_ref, kt_ref, vz_ref, qp_ref, dop_ref, dk_acc, dv_acc = refs[2 * slots + 4 :]
    parity = lax.rem(pl.program_id(0), 2)
    rows_all = q_ref.shape[0]
    row_blocks = rows_all // BLK
    fill_bias(place_ref[0], b_ref, tile_ref, row_blocks, slots)
    sum_ref[...] = jnp.zeros_like(sum_ref)

    @pl.when(parity == 0)
    def clear():
        dk_acc[...] = jnp.zeros_like(dk_acc)
        dv_acc[...] = jnp.zeros_like(dv_acc)

    for h in range(2):
        in_pick = lane_pick(parity * HEAD_DIM, h * HEAD_DIM)
        out_pick = lane_pick(h * HEAD_DIM, parity * HEAD_DIM)
        for slot in range(slots):
            span = slice(slot * rows_all, (slot + 1) * rows_all)
            kz_ref[h, span, :] = dot_nn(k_refs[slot][...], in_pick).astype(BF16)
            pick_t = lane_pick_t(parity * HEAD_DIM, h * HEAD_DIM)
            kt_ref[h, :, span] = dot_nt(pick_t, k_refs[slot][...]).astype(BF16)
            vz_ref[h, span, :] = dot_nn(v_refs[slot][...], in_pick).astype(BF16)
        qp_ref[h] = dot_nn(q_ref[...], out_pick).astype(BF16)
        dop_ref[h] = dot_nn(do_ref[...], out_pick).astype(BF16)
    deltas, lses, grad_q = [], [], []
    for rb in range(row_blocks):
        rows = slice(rb * BLK, (rb + 1) * BLK)
        deltas.append([row_products(do_ref[rows, :], o_ref[rows, :], h) for h in range(2)])
        lses.append([lse_ref[0, h : h + 1, rows] for h in range(2)])
        grad_q.append(None)
    for kb in range(row_blocks * slots):
        keys = slice(kb * BLK, (kb + 1) * BLK)
        grad_v = dv_acc[keys, :]
        grad_k = dk_acc[keys, :]
        for rb in range(row_blocks):
            if kb not in key_blocks(row_blocks, slots, rb):
                continue
            rows = slice(rb * BLK, (rb + 1) * BLK)
            at, delta = tile_at(row_blocks, rb, kb)
            for h in range(2):
                scores = dot_nt(kz_ref[h, keys, :], q_ref[rows, :]) + tile_ref[h, at]
                probs = jnp.exp(scores - lses[rb][h])
                grad_probs = dot_nt(vz_ref[h, keys, :], do_ref[rows, :])
                grad_scores = probs * (grad_probs - deltas[rb][h])
                sum_ref[h, delta] += grad_scores
                low_scores = grad_scores.astype(BF16)
                grad_v = grad_v + dot_nn(probs.astype(BF16), dop_ref[h, rows, :])
                grad_k = grad_k + dot_nn(low_scores, qp_ref[h, rows, :])
                part = dot_nn(kt_ref[h, :, keys], low_scores)
                grad_q[rb] = part if grad_q[rb] is None else grad_q[rb] + part
        dv_acc[keys, :] = grad_v
        dk_acc[keys, :] = grad_k
    for rb in range(row_blocks):
        rows = slice(rb * BLK, (rb + 1) * BLK)
        dq_ref[rows, :] = (grad_q[rb].T * score_scale).astype(BF16)

    diag_ref[...] = jnp.zeros_like(diag_ref)
    for h in range(2):
        for delta in range(row_blocks * slots):
            wide = jnp.concatenate([jnp.zeros((BLK, BLK), F32), sum_ref[h, delta]], axis=1)
            diag_ref[0, h : h + 1, delta * BLK : delta * BLK + 2 * BLK] += diagonal_sums(wide)

    @pl.when(parity == 1)
    def store():
        dk_ref[...] = dk_acc[...].astype(BF16)
        dv_ref[...] = dv_acc[...].astype(BF16)


def cross_forward_kernel(q_ref, k_ref, v_ref, m_ref, o_ref, ot_ref, lse_ref, kz_ref, vt_ref):
    parity = lax.rem(pl.program_id(0), 2)
    for h in range(2):
        kz_ref[h] = dot_nn(k_ref[...], lane_pick(parity * HEAD_DIM, h * HEAD_DIM)).astype(BF16)
        vt_ref[h] = dot_nt(lane_pick_t(parity * HEAD_DIM, h * HEAD_DIM), v_ref[...]).astype(BF16)
    for rb in range(q_ref.shape[0] // BLK):
        rows = slice(rb * BLK, (rb + 1) * BLK)
        queries = q_ref[rows, :]
        mixed_t = None
        for h in range(2):
            state = None
            for jb in range(k_ref.shape[0] // BLK):
                keys = slice(jb * BLK, (jb + 1) * BLK)
                scores = dot_nt(kz_ref[h, keys, :], queries) + m_ref[keys, :]
                if state is None:
                    state = first_step(scores, vt_ref[h, :, keys])
                else:
                    state = online_step(state, scores, vt_ref[h, :, keys])
            part = state[2] / state[1]
            mixed_t = part if mixed_t is None else mixed_t + part
            lse_ref[0, h : h + 1, rows] = state[0] + jnp.log(state[1])
        ot_ref[:, rows] = mixed_t.astype(BF16)
        o_ref[rows, :] = mixed_t.T.astype(BF16)


def cross_backward_kernel(
    q_ref,
    k_ref,
    v_ref,
    m_ref,
    do_ref,
    o_ref,
    lse_ref,
    dq_ref,
    dk_ref,
    dv_ref,
    kz_ref,
    kt_ref,
    vz_ref,
    qp_ref,
    dop_ref,
    dk_acc,
    dv_acc,
):
    parity = lax.rem(pl.program_id(0), 2)

    @pl.when(parity == 0)
    def clear():
        dk_acc[...] = jnp.zeros_like(dk_acc)
        dv_acc[...] = jnp.zeros_like(dv_acc)

    for h in range(2):
        in_pick = lane_pick(parity * HEAD_DIM, h * HEAD_DIM)
        out_pick = lane_pick(h * HEAD_DIM, parity * HEAD_DIM)
        kz_ref[h] = dot_nn(k_ref[...], in_pick).astype(BF16)
        kt_ref[h] = dot_nt(lane_pick_t(parity * HEAD_DIM, h * HEAD_DIM), k_ref[...]).astype(BF16)
        vz_ref[h] = dot_nn(v_ref[...], in_pick).astype(BF16)
        qp_ref[h] = dot_nn(q_ref[...], out_pick).astype(BF16)
        dop_ref[h] = dot_nn(do_ref[...], out_pick).astype(BF16)
    for rb in range(q_ref.shape[0] // BLK):
        rows = slice(rb * BLK, (rb + 1) * BLK)
        queries = q_ref[rows, :]
        grads = do_ref[rows, :]
        mixed = o_ref[rows, :]
        grad_q = None
        for h in range(2):
            delta = row_products(grads, mixed, h)
            lse = lse_ref[0, h : h + 1, rows]
            for jb in range(k_ref.shape[0] // BLK):
                keys = slice(jb * BLK, (jb + 1) * BLK)
                scores = dot_nt(kz_ref[h, keys, :], queries) + m_ref[keys, :]
                probs = jnp.exp(scores - lse)
                grad_probs = dot_nt(vz_ref[h, keys, :], grads)
                low_scores = (probs * (grad_probs - delta)).astype(BF16)
                dv_acc[keys, :] += dot_nn(probs.astype(BF16), dop_ref[h, rows, :])
                dk_acc[keys, :] += dot_nn(low_scores, qp_ref[h, rows, :])
                part = dot_nn(kt_ref[h, :, keys], low_scores)
                grad_q = part if grad_q is None else grad_q + part
        dq_ref[rows, :] = (grad_q.T * score_scale).astype(BF16)

    @pl.when(parity == 1)
    def store():
        dk_ref[...] = dk_acc[...].astype(BF16)
        dv_ref[...] = dv_acc[...].astype(BF16)


def shape_of(shape, dtype):
    return jax.ShapeDtypeStruct(shape, dtype)


def tile_pair(rows):
    return pl.BlockSpec((rows, PAIR), lambda g: (0, g))


def tile_pair_t(rows):
    return pl.BlockSpec((PAIR, rows), lambda g: (g, 0))


def tile_group(rows):
    return pl.BlockSpec((rows, PAIR), lambda g: (0, g // 2))


def tile_rows(width):
    return pl.BlockSpec((1, 2, width), lambda g: (g, 0, 0))


def kernel_params():
    return pltpu.CompilerParams(
        dimension_semantics=("arbitrary",), vmem_limit_bytes=VMEM_LIMIT
    )


def cost(flops, transcendentals, nbytes):
    return pl.CostEstimate(
        flops=int(flops) // 16, transcendentals=0, bytes_accessed=int(nbytes) // 16
    )


def self_forward(place, q, ks, vs, bias_vec):
    rows, width = q.shape
    slots = len(ks)
    keys = rows * slots
    pairs = width // PAIR
    tiles = len(tile_plan(rows // BLK, slots))
    return pl.pallas_call(
        functools.partial(self_forward_kernel, slots),
        grid=(pairs,),
        in_specs=[pl.BlockSpec(memory_space=pltpu.SMEM), tile_pair(rows), tile_rows(bias_vec.shape[2])]
        + [tile_group(rows)] * (2 * slots),
        out_specs=[tile_pair(rows), tile_pair_t(rows), tile_rows(rows)],
        out_shape=[
            shape_of((rows, width), BF16),
            shape_of((width, rows), BF16),
            shape_of((pairs, 2, rows), F32),
        ],
        scratch_shapes=[
            pltpu.VMEM((2, tiles, BLK, BLK), F32),
            pltpu.VMEM((2, keys, PAIR), BF16),
            pltpu.VMEM((2, PAIR, keys), BF16),
        ],
        compiler_params=kernel_params(),
        cost_estimate=cost(4 * 2 * rows * keys * width * 2, pairs * 2 * rows * keys, 8 * rows * width),
        name="self_forward",
    )(place, q, bias_vec, *ks, *vs)


def self_backward(place, q, ks, vs, bias_vec, grads, mixed, lse):
    rows, width = q.shape
    kv_width = ks[0].shape[1]
    slots = len(ks)
    keys = rows * slots
    pairs = width // PAIR
    tiles = len(tile_plan(rows // BLK, slots))
    return pl.pallas_call(
        functools.partial(self_backward_kernel, slots),
        grid=(pairs,),
        in_specs=[
            pl.BlockSpec(memory_space=pltpu.SMEM),
            tile_pair(rows),
            tile_rows(bias_vec.shape[2]),
            tile_pair(rows),
            tile_pair(rows),
            tile_rows(rows),
        ]
        + [tile_group(rows)] * (2 * slots),
        out_specs=[
            tile_pair(rows),
            tile_group(keys),
            tile_group(keys),
            tile_rows(bias_vec.shape[2]),
        ],
        out_shape=[
            shape_of((rows, width), BF16),
            shape_of((keys, kv_width), BF16),
            shape_of((keys, kv_width), BF16),
            shape_of(bias_vec.shape, F32),
        ],
        scratch_shapes=[
            pltpu.VMEM((2, tiles, BLK, BLK), F32),
            pltpu.VMEM((2, keys // BLK, BLK, BLK), F32),
            pltpu.VMEM((2, keys, PAIR), BF16),
            pltpu.VMEM((2, PAIR, keys), BF16),
            pltpu.VMEM((2, keys, PAIR), BF16),
            pltpu.VMEM((2, rows, PAIR), BF16),
            pltpu.VMEM((2, rows, PAIR), BF16),
            pltpu.VMEM((keys, PAIR), F32),
            pltpu.VMEM((keys, PAIR), F32),
        ],
        compiler_params=kernel_params(),
        cost_estimate=cost(10 * 2 * rows * keys * width * 2, pairs * 2 * rows * keys, 12 * rows * width),
        name="self_backward",
    )(place, q, bias_vec, grads, mixed, lse, *ks, *vs)


def cross_forward(q, k, v, mask_col):
    rows, width = q.shape
    keys = k.shape[0]
    pairs = width // PAIR
    return pl.pallas_call(
        cross_forward_kernel,
        grid=(pairs,),
        in_specs=[
            tile_pair(rows),
            tile_group(keys),
            tile_group(keys),
            pl.BlockSpec((keys, 1), lambda g: (0, 0)),
        ],
        out_specs=[tile_pair(rows), tile_pair_t(rows), tile_rows(rows)],
        out_shape=[
            shape_of((rows, width), BF16),
            shape_of((width, rows), BF16),
            shape_of((pairs, 2, rows), F32),
        ],
        scratch_shapes=[
            pltpu.VMEM((2, keys, PAIR), BF16),
            pltpu.VMEM((2, PAIR, keys), BF16),
        ],
        compiler_params=kernel_params(),
        cost_estimate=cost(4 * 2 * rows * keys * width * 2, pairs * 2 * rows * keys, 8 * rows * width),
        name="cross_forward",
    )(q, k, v, mask_col)


def cross_backward(q, k, v, mask_col, grads, mixed, lse):
    rows, width = q.shape
    keys, kv_width = k.shape
    pairs = width // PAIR
    return pl.pallas_call(
        cross_backward_kernel,
        grid=(pairs,),
        in_specs=[
            tile_pair(rows),
            tile_group(keys),
            tile_group(keys),
            pl.BlockSpec((keys, 1), lambda g: (0, 0)),
            tile_pair(rows),
            tile_pair(rows),
            tile_rows(rows),
        ],
        out_specs=[tile_pair(rows), tile_group(keys), tile_group(keys)],
        out_shape=[
            shape_of((rows, width), BF16),
            shape_of((keys, kv_width), BF16),
            shape_of((keys, kv_width), BF16),
        ],
        scratch_shapes=[
            pltpu.VMEM((2, keys, PAIR), BF16),
            pltpu.VMEM((2, PAIR, keys), BF16),
            pltpu.VMEM((2, keys, PAIR), BF16),
            pltpu.VMEM((2, rows, PAIR), BF16),
            pltpu.VMEM((2, rows, PAIR), BF16),
            pltpu.VMEM((keys, PAIR), F32),
            pltpu.VMEM((keys, PAIR), F32),
        ],
        compiler_params=kernel_params(),
        cost_estimate=cost(10 * 2 * rows * keys * width * 2, pairs * 2 * rows * keys, 12 * rows * width),
        name="cross_backward",
    )(q, k, v, mask_col, grads, mixed, lse)


FBLK = 128


def ffn_kernel(core_ref, x_ref, og_ref, wg_ref, wu_ref, wd_ref, ht_ref, gg_ref, gu_ref, out_ref, e_ref, out_acc, e_acc):
    step = pl.program_id(0)

    @pl.when(step == 0)
    def clear():
        out_acc[...] = jnp.zeros_like(out_acc)
        e_acc[...] = jnp.zeros_like(e_acc)

    wide = jnp.concatenate([wg_ref[...], wu_ref[...]], axis=1)
    both = dot_nn(x_ref[...], wide)
    gate, up = both[:, :FBLK], both[:, FBLK:]
    grad_hidden = dot_nt(og_ref[...], wd_ref[...])
    factor = (2.0 / jnp.pi) ** 0.5
    square = gate * gate
    bend = jnp.tanh(factor * (gate + 0.044715 * gate * square))
    half = 0.5 * (1.0 + bend)
    gelu = gate * half
    slope = half + 0.5 * gate * (1.0 - bend * bend) * (factor * (1.0 + 3 * 0.044715 * square))
    hidden = gelu * up
    low_hidden = hidden.astype(BF16)
    ht_ref[...] = hidden.T.astype(BF16)
    grad_gate = (grad_hidden * up * slope).astype(BF16)
    grad_up = (grad_hidden * gelu).astype(BF16)
    gg_ref[...] = grad_gate
    gu_ref[...] = grad_up
    out_acc[...] += dot_nn(low_hidden, wd_ref[...])
    e_acc[...] += dot_nt(jnp.concatenate([grad_gate, grad_up], axis=1), wide)

    @pl.when(step == pl.num_programs(0) - 1)
    def store():
        out_ref[...] = out_acc[...].astype(BF16)
        e_ref[...] = e_acc[...].astype(BF16)


def ffn(core, normed, out_grad, w_gate, w_up, w_down):
    rows, width = normed.shape
    hidden = w_gate.shape[1] // 2
    steps = hidden // FBLK
    whole = pl.BlockSpec((rows, width), lambda j, c: (0, 0))
    return pl.pallas_call(
        ffn_kernel,
        grid_spec=pltpu.PrefetchScalarGridSpec(
            num_scalar_prefetch=1,
            grid=(steps,),
            in_specs=[
                whole,
                whole,
                pl.BlockSpec((width, FBLK), lambda j, c: (0, c[0] * steps + j)),
                pl.BlockSpec((width, FBLK), lambda j, c: (0, c[0] * steps + j)),
                pl.BlockSpec((FBLK, width), lambda j, c: (c[0] * steps + j, 0)),
            ],
            out_specs=[
                pl.BlockSpec((FBLK, rows), lambda j, c: (j, 0)),
                pl.BlockSpec((rows, FBLK), lambda j, c: (0, j)),
                pl.BlockSpec((rows, FBLK), lambda j, c: (0, j)),
                whole,
                whole,
            ],
            scratch_shapes=[pltpu.VMEM((rows, width), F32), pltpu.VMEM((rows, width), F32)],
        ),
        out_shape=[
            shape_of((hidden, rows), BF16),
            shape_of((rows, hidden), BF16),
            shape_of((rows, hidden), BF16),
            shape_of((rows, width), BF16),
            shape_of((rows, width), BF16),
        ],
        compiler_params=kernel_params(),
        cost_estimate=cost(2 * 6 * rows * width * hidden, rows * hidden, 6 * width * hidden),
        name="ffn",
    )(core, normed, out_grad, w_gate, w_up, w_down)


def normalise(values, gain):
    inverse = lax.rsqrt(jnp.mean(values * values, axis=-1, keepdims=True) + norm_eps)
    return values * inverse * gain


def rms_back(values, gain, grad):
    inverse = lax.rsqrt(jnp.mean(values * values, axis=-1, keepdims=True) + norm_eps)
    scaled = grad * gain
    mean_dot = jnp.mean(values * scaled, axis=-1, keepdims=True)
    unit = values * inverse
    return inverse * (scaled - unit * (inverse * mean_dot))


def project_kernel(scales, core_ref, own_ref, other_ref, gain_ref, *refs):
    count = len(scales)
    w_refs, nt_ref, out_refs = refs[:count], refs[count], refs[count + 1 :]
    mine = core_ref[0] == pl.program_id(0)
    values = jnp.where(mine, own_ref[...], other_ref[...]).astype(F32)
    normed = normalise(values, gain_ref[...])
    nt_ref[...] = normed.T.astype(BF16)
    low = normed.astype(BF16)
    for scale, w_ref, out_ref in zip(scales, w_refs, out_refs):
        out = dot_nn(low, w_ref[...]).astype(BF16)
        out_ref[...] = out if scale is None else out * BF16(scale)


def own_columns(weight):
    return pl.BlockSpec((weight.shape[0], weight.shape[1] // 2), lambda i, c: (0, c[0]))


def other_columns(weight):
    return pl.BlockSpec((weight.shape[0], weight.shape[1] // 2), lambda i, c: (0, 1 - c[0]))


def own_rows(array):
    return pl.BlockSpec((array.shape[0] // 2, array.shape[1]), lambda i, c: (c[0], 0))


def other_rows(array):
    return pl.BlockSpec((array.shape[0] // 2, array.shape[1]), lambda i, c: (1 - c[0], 0))


def all_of(array):
    return pl.BlockSpec(array.shape, lambda i, c: (0,) * array.ndim)


def half_rows(rows, width):
    return pl.BlockSpec((rows, width), lambda i, c: (i, 0))


def half_columns(width, rows):
    return pl.BlockSpec((width, rows), lambda i, c: (0, i))


def fixed(shape):
    return pl.BlockSpec(shape, lambda i, c: (0,) * len(shape))


def core_call(kernel, steps, core, args, in_specs, out_specs, out_shape, scratch, flops, name):
    return pl.pallas_call(
        kernel,
        grid_spec=pltpu.PrefetchScalarGridSpec(
            num_scalar_prefetch=1,
            grid=(steps,),
            in_specs=in_specs,
            out_specs=out_specs,
            scratch_shapes=scratch,
        ),
        out_shape=out_shape,
        compiler_params=kernel_params(),
        cost_estimate=cost(flops, 0, flops // 400),
        name=name,
    )(core, *args)


def project(core, own, other, gain, weights, scales, name):
    local, width = own.shape
    return core_call(
        functools.partial(project_kernel, scales),
        2,
        core,
        (own, other, gain, *weights),
        [all_of(own), all_of(other), all_of(gain)] + [own_columns(w) for w in weights],
        [half_columns(width, local)] + [half_rows(local, w.shape[1] // 2) for w in weights],
        [shape_of((width, 2 * local), BF16)]
        + [shape_of((2 * local, w.shape[1] // 2), BF16) for w in weights],
        [],
        2 * 2 * local * width * sum(w.shape[1] // 2 for w in weights),
        name,
    )


def memory_kernel(parts, core_ref, *refs):
    in_refs = refs[:parts]
    wk_ref, wv_ref, mt_ref, k_ref, v_ref, all_ref = refs[parts:]
    rows = in_refs[0].shape[0]
    for i in range(parts):
        all_ref[i * rows : (i + 1) * rows, :] = in_refs[i][...]
    mt_ref[...] = all_ref[...].astype(F32).T.astype(BF16)
    k_ref[...] = dot_nn(all_ref[...], wk_ref[...]).astype(BF16)
    v_ref[...] = dot_nn(all_ref[...], wv_ref[...]).astype(BF16)


def project_memory(core, parts, w_key, w_value):
    rows, width = parts[0].shape
    total = rows * len(parts)
    kw = w_key.shape[1] // 2
    return core_call(
        functools.partial(memory_kernel, len(parts)),
        1,
        core,
        (*parts, w_key, w_value),
        [all_of(p) for p in parts] + [own_columns(w_key), own_columns(w_value)],
        [fixed((width, total)), fixed((total, kw)), fixed((total, kw))],
        [shape_of((width, total), BF16), shape_of((total, kw), BF16), shape_of((total, kw), BF16)],
        [pltpu.VMEM((total, width), BF16)],
        2 * total * width * 2 * kw,
        "project_memory",
    )


def join_kernel(low_base, project_next, core_ref, *refs):
    if low_base:
        own_ref, other_ref, refs = refs[0], refs[1], refs[2:]
        mine = core_ref[0] == pl.program_id(0)
        base = jnp.where(mine, own_ref[...], other_ref[...]).astype(F32)
    else:
        base, refs = refs[0][...], refs[1:]
    mixed_ref, got_ref, w_own_ref, w_other_ref, gain_ref = refs[:5]
    after = base + dot_nn(mixed_ref[...], w_own_ref[...]) + dot_nn(got_ref[...], w_other_ref[...])
    normed = normalise(after, gain_ref[...])
    low = normed.astype(BF16)
    if project_next:
        w_ref, after_ref, nt_ref, out_ref = refs[5:]
        out_ref[...] = dot_nn(low, w_ref[...]).astype(BF16) * BF16(score_scale)
    else:
        after_ref, nt_ref, out_ref = refs[5:]
        out_ref[...] = low
    after_ref[...] = after
    nt_ref[...] = normed.T.astype(BF16)


def join(core, base, mixed, got, w_out, gain, w_next, name):
    rows, half = mixed.shape
    width = w_out.shape[1]
    local = rows // 2
    low_base = isinstance(base, tuple)
    bases = base if low_base else (base,)
    base_specs = [all_of(v) for v in bases] if low_base else [half_rows(local, width)]
    nexts = () if w_next is None else (w_next,)
    out_width = width if w_next is None else w_next.shape[1] // 2
    return core_call(
        functools.partial(join_kernel, low_base, w_next is not None),
        2,
        core,
        (*bases, mixed, got, w_out, w_out, gain, *nexts),
        base_specs
        + [half_rows(local, half), half_rows(local, half), own_rows(w_out), other_rows(w_out), all_of(gain)]
        + [own_columns(w) for w in nexts],
        [half_rows(local, width), half_columns(width, local), half_rows(local, out_width)],
        [shape_of((rows, width), F32), shape_of((width, rows), BF16), shape_of((rows, out_width), BF16)],
        [],
        2 * rows * width * (width + out_width),
        name,
    )


def back_kernel(low_prior, products, core_ref, *refs):
    if low_prior:
        own_ref, other_ref, refs = refs[0], refs[1], refs[2:]
        mine = core_ref[0] == pl.program_id(0)
        prior = jnp.where(mine, own_ref[...], other_ref[...]).astype(F32)
    else:
        prior, refs = refs[0][...], refs[1:]
    value_ref, gain_ref, e_ref, got_ref, refs = refs[0], refs[1], refs[2], refs[3], refs[4:]
    if products:
        e = dot_nt(e_ref[...], refs[0][...]) + dot_nt(got_ref[...], refs[1][...])
        refs = refs[2:]
    else:
        e = e_ref[...].astype(F32) + got_ref[...].astype(F32)
    w_ref, grad_ref, half_ref, next_ref = refs
    grad = prior + rms_back(value_ref[...], gain_ref[...], e)
    grad_ref[...] = grad
    low = grad.astype(BF16)
    half = low.shape[1] // 2
    half_ref[...] = jnp.where(core_ref[0] == 0, low[:, :half], low[:, half:])
    next_ref[...] = dot_nt(low, w_ref[...]).astype(BF16)


def back(core, prior, values, gain, e, got, w_in, w_out, name):
    rows, width = values.shape
    local = rows // 2
    low_prior = isinstance(prior, tuple)
    priors = prior if low_prior else (prior,)
    prior_specs = [all_of(v) for v in priors] if low_prior else [half_rows(local, width)]
    ins = () if w_in is None else (w_in, w_in)
    in_specs = [] if w_in is None else [own_columns(w_in), other_columns(w_in)]
    half = w_out.shape[0] // 2
    return core_call(
        functools.partial(back_kernel, low_prior, w_in is not None),
        2,
        core,
        (*priors, values, gain, e, got, *ins, w_out),
        prior_specs
        + [half_rows(local, width), all_of(gain), half_rows(local, e.shape[1]), half_rows(local, e.shape[1])]
        + in_specs
        + [own_rows(w_out)],
        [half_rows(local, width), half_rows(local, width // 2), half_rows(local, half)],
        [
            shape_of((rows, width), F32),
            shape_of((rows, width // 2), BF16),
            shape_of((rows, half), BF16),
        ],
        [],
        2 * rows * width * (half + 2 * e.shape[1] * len(ins) // 2),
        name,
    )


def last_kernel(core_ref, prior_ref, base_ref, gain_ref, q_ref, pair_ref, got_ref, *refs):
    wq_own, wq_other, wk_own, wk_other, wv_own, wv_other, grad_ref = refs
    qw = wq_own.shape[1]
    kw = wk_own.shape[1]
    e = dot_nt(q_ref[...], wq_own[...]) + dot_nt(got_ref[:, :qw], wq_other[...])
    e = e + dot_nt(pair_ref[:, :kw], wk_own[...]) + dot_nt(got_ref[:, qw : qw + kw], wk_other[...])
    e = e + dot_nt(pair_ref[:, kw:], wv_own[...]) + dot_nt(got_ref[:, qw + kw :], wv_other[...])
    grad_ref[...] = prior_ref[...] + rms_back(base_ref[...].astype(F32), gain_ref[...], e)


def last(core, prior, base, gain, grad_q, pair, got, w_query, w_key, w_value):
    local, width = base.shape
    weights = (w_query, w_query, w_key, w_key, w_value, w_value)
    specs = []
    for w in (w_query, w_key, w_value):
        specs += [own_columns(w), other_columns(w)]
    return core_call(
        last_kernel,
        1,
        core,
        (prior, base, gain, grad_q, pair, got, *weights),
        [own_rows(prior), all_of(base), all_of(gain), own_rows(grad_q), own_rows(pair), all_of(got)] + specs,
        [fixed((local, width))],
        [shape_of((local, width), F32)],
        [],
        2 * local * width * 2 * width,
        "last",
    )


def outer_kernel(plan, split, count, order_ref, *refs):
    terms = plan
    lefts = []
    for parts in split:
        lefts.append(refs[:parts])
        refs = refs[parts:]
    right_refs, keep_ref, send_ref, sorted_refs = refs[:count], refs[count], refs[count + 1], refs[count + 2 :]
    blocks = order_ref.shape[0]
    for left, sorted_ref in zip(lefts, sorted_refs):
        rows = sorted_ref.shape[0] // blocks
        for p in range(blocks):
            index = order_ref[p]
            if len(left) == 1:
                piece = left[0][pl.ds(pl.multiple_of(index * rows, rows), rows), :]
            else:
                middle = blocks // 2
                first = pl.multiple_of(jnp.minimum(index, middle - 1) * rows, rows)
                second = pl.multiple_of(jnp.maximum(index - middle, 0) * rows, rows)
                piece = jnp.where(
                    index < middle, left[0][pl.ds(first, rows), :], left[1][pl.ds(second, rows), :]
                )
            sorted_ref[p * rows : (p + 1) * rows, :] = piece
    middle = sorted_refs[0].shape[0] // 2
    for out_ref, span in ((send_ref, slice(middle, 2 * middle)), (keep_ref, slice(0, middle))):
        column = 0
        for products in terms:
            total = None
            for left, right, first in products:
                depth = sorted_refs[left].shape[1]
                part = dot_nn(sorted_refs[left][span, :], right_refs[right][first : first + depth, :])
                total = part if total is None else total + part
            width = total.shape[1]
            out_ref[:, column : column + width] = total.astype(BF16)
            column += width


def outer_halves(order, lefts, rights, terms):
    blocks = order.shape[0]
    lefts = [v if isinstance(v, tuple) else (v,) for v in lefts]
    totals = [sum(v.shape[0] for v in left) for left in lefts]
    rows = totals[0] // blocks
    if rows % 16:
        joined = [jnp.concatenate(left, axis=0) for left in lefts]
        joined = [
            jnp.concatenate(
                [lax.dynamic_slice_in_dim(v, order[p] * rows, rows, 0) for p in range(blocks)], axis=0
            )
            for v in joined
        ]
        half = totals[0] // 2
        columns = []
        for products in terms:
            columns.append(
                sum(
                    dot_nn(joined[l], rights[r][first : first + joined[l].shape[1]])
                    for l, r, first in products
                )
            )
        total = jnp.concatenate(columns, axis=1).astype(BF16)
        return total[:half], total[half:]
    width = sum(rights[products[0][1]].shape[1] for products in terms)
    half = shape_of((totals[0] // 2, width), BF16)
    flops = 0
    for products in terms:
        for l, r, first in products:
            flops += 2 * totals[l] * lefts[l][0].shape[1] * rights[r].shape[1]
    whole = pl.BlockSpec(memory_space=pltpu.VMEM)
    flat = [v for left in lefts for v in left]
    return pl.pallas_call(
        functools.partial(outer_kernel, terms, [len(left) for left in lefts], len(rights)),
        in_specs=[pl.BlockSpec(memory_space=pltpu.SMEM)] + [whole] * (len(flat) + len(rights)),
        out_specs=[whole, whole],
        out_shape=[half, half],
        scratch_shapes=[
            pltpu.VMEM((total, left[0].shape[1]), BF16) for total, left in zip(totals, lefts)
        ],
        compiler_params=pltpu.CompilerParams(vmem_limit_bytes=VMEM_LIMIT),
        cost_estimate=cost(flops, 0, flops // 400),
        name="outer_halves",
    )(order, *flat, *rights)


def bits_of(size):
    return (size - 1).bit_length()


class Places:
    def __init__(self):
        self.seq = lax.axis_size("seq")
        self.dp = lax.axis_size("dp")
        self.nx = self.seq // 2
        self.chips = self.dp * self.nx
        place = lax.axis_index("seq")
        self.core = place & 1
        self.x = place >> 1
        self.d = lax.axis_index("dp")
        self.dp_bits = bits_of(self.dp)
        self.x_bits = bits_of(self.nx)
        self.chip = self.d * self.nx + self.x
        self.names = [("dp", b) for b in reversed(range(self.dp_bits))] + [
            ("x", b) for b in reversed(range(self.x_bits))
        ]

    def swap_core(self, value):
        return lax.ppermute(value, "seq", [(s, s ^ 1) for s in range(self.seq)])

    def shift_x(self, value, by):
        pairs = [(s, (s + 2 * by) % self.seq) for s in range(self.seq)]
        return lax.ppermute(value, "seq", pairs)

    def flip(self, value, name):
        axis, bit = name
        if axis == "dp":
            pairs = [(s, s ^ (1 << bit)) for s in range(self.dp)]
            return lax.ppermute(value, "dp", pairs)
        pairs = [(s, s ^ (2 << bit)) for s in range(self.seq)]
        return lax.ppermute(value, "seq", pairs)

    def by_core(self, own, other, axis):
        first = jnp.concatenate([own, other], axis=axis)
        second = jnp.concatenate([other, own], axis=axis)
        return jnp.where(self.core == 0, first, second)

    def core_rows(self, value, mine):
        half = value.shape[0] // 2
        which = self.core if mine else 1 - self.core
        return lax.dynamic_slice_in_dim(value, which * half, half, 0)

    def order_of(self, kind):
        dp0 = [("dp", 0)]
        dp_rest = [("dp", b) for b in range(1, self.dp_bits)]
        xs = [("x", b) for b in range(self.x_bits)]
        if kind == 0:
            return xs + dp0 + dp_rest
        if kind == 1:
            return dp0 + xs + dp_rest
        return dp_rest + xs + dp0

    def block_order(self, kind, core_major=False):
        order = self.order_of(kind)
        count = len(order)
        masks = []
        for p in range(self.chips):
            mask = 0
            for k, name in enumerate(order):
                if (p >> (count - 1 - k)) & 1:
                    mask |= 1 << (count - 1 - self.names.index(name))
            masks.append(mask)
        base = self.chip
        if core_major:
            base = base ^ (self.core << (count - 1))
        return jnp.array(masks, jnp.int32) ^ base.astype(jnp.int32)


class ChipSum:
    def __init__(self, at, kind, halves, dtype=BF16):
        self.at = at
        self.left = list(at.order_of(kind))
        self.parts = [halves[0]]
        self.sent = halves[1]
        self.flying = None
        self.dtype = dtype

    def add(self):
        self.parts.append(self.flying)
        self.flying = None
        if not self.left:
            return
        half = self.parts[0].shape[0] // 2
        self.sent = sum(v[half:].astype(F32) for v in self.parts).astype(self.dtype)
        self.parts = [v[:half] for v in self.parts]

    def result(self):
        return sum(v.astype(F32) for v in self.parts)


def send(sums):
    ways = {}
    for one in sums:
        if one.left:
            way = (one.left[0], one.sent.dtype, one.sent.shape[0])
            ways.setdefault(way, []).append(one)
    for (name, _, _), group in ways.items():
        joined = jnp.concatenate([one.sent for one in group], axis=1) if len(group) > 1 else group[0].sent
        flying = group[0].at.flip(joined, name)
        first = 0
        for one in group:
            last_column = first + one.sent.shape[1]
            one.flying = flying[:, first:last_column]
            one.left.pop(0)
            first = last_column


def fold(sums, *ties):
    for one in sums:
        if one.flying is not None:
            one.add()
    live = [one for one in sums if one.left]
    values = together(*[one.sent for one in live], *ties)
    for one, value in zip(live, values):
        one.sent = value
    return values[len(live) :]


def settle(sums, *values):
    flying = [one for one in sums if one.flying is not None]
    out = together(*[one.flying for one in flying], *values)
    for one, value in zip(flying, out):
        one.flying = value
    return out[len(flying) :]


def core_join(places, shares):
    joined = jnp.concatenate(shares, axis=1) if len(shares) > 1 else shares[0]
    own = places.core_rows(joined, True)
    arrived = places.swap_core(places.core_rows(joined, False))
    outs = []
    first = 0
    for share in shares:
        last_column = first + share.shape[1]
        outs.append(places.by_core(own[:, first:last_column], arrived[:, first:last_column], 1))
        first = last_column
    return outs


def together(*values):
    return lax.optimization_barrier(values)


def per_device(
    target,
    memory,
    mem_lengths,
    mem_mask,
    distance_buckets,
    norm_self,
    w_query,
    w_key,
    w_value,
    w_out,
    pos_table,
    norm_cross,
    wc_query,
    wc_key,
    wc_value,
    wc_out,
    norm_ffn,
    w_gate,
    w_up,
    w_down,
    out_grad,
):
    at = Places()
    core, nx = at.core, at.nx
    local, width = target.shape[1], target.shape[2]
    mem_local = memory.shape[1]
    rows = 2 * local
    full = distance_buckets.shape[0]
    qw = HEADS * HEAD_DIM // 2
    kw = KV * HEAD_DIM // 2
    head_count = HEADS // 2
    place = at.x.astype(jnp.int32).reshape(1)
    core_arg = core.astype(jnp.int32).reshape(1)
    gain_self = norm_self.reshape(1, width)
    gain_cross = norm_cross.reshape(1, width)
    gain_ffn = norm_ffn.reshape(1, width)

    tokens = target.reshape(local, width)
    far_tokens = [at.shift_x(tokens, s) for s in range(1, nx)]
    tokens_got = at.swap_core(tokens)
    memories = memory.reshape(mem_local, width)
    far_memories = [at.shift_x(memories, s) for s in range(1, nx)]
    memories_got = at.swap_core(memories)
    grads = out_grad.reshape(local, width)
    grads_got = at.swap_core(grads)
    grad_chip = at.by_core(grads, grads_got, 0)

    own_table = lax.dynamic_slice_in_dim(pos_table, core * head_count, head_count, 0)
    onehot = (distance_buckets[:, None] == jnp.arange(BUCKETS, dtype=jnp.int32)[None, :]).astype(F32)
    by_distance = lax.dot_general(
        own_table, onehot, (((1,), (1,)), ((), ())), precision=lax.Precision.HIGHEST
    )
    bias_vec = jnp.pad(by_distance, ((0, 0), (BLK, 0))).reshape(head_count // 2, 2, BLK + full)

    normed_t, query, keys, values = project(
        core_arg, tokens, tokens_got, gain_self, (w_query, w_key, w_value), (score_scale, None, None), "project"
    )
    keys, values, normed_ts = [keys], [values], [normed_t]
    for far in far_tokens:
        far_t, far_k, far_v = project(
            core_arg, far, at.swap_core(far), gain_self, (w_key, w_value), (None, None), "project_far"
        )
        normed_ts.append(far_t)
        keys.append(far_k)
        values.append(far_v)

    mem_parts = [memories, memories_got]
    for far in far_memories:
        mem_parts += [far, at.swap_core(far)]
    mem_ids = jnp.arange(mem_mask.shape[1], dtype=jnp.int32)
    valid = (mem_ids < mem_lengths[0]) & ((mem_mask[0] == 1) | (mem_ids == 0))
    mask_add = jnp.where(valid, 0.0, big_negative).astype(F32).reshape(2 * nx, mem_local)
    slot_of = jnp.array([s for s in range(nx) for c in range(2)], jnp.int32)
    core_of = jnp.array([c for s in range(nx) for c in range(2)], jnp.int32)
    mask_rows = (((at.x - slot_of + nx) % nx) * 2 + (core ^ core_of))[:, None] == jnp.arange(2 * nx)[None, :]
    mask_col = jnp.sum(jnp.where(mask_rows[:, :, None], mask_add[None], 0.0), axis=1).reshape(-1, 1)
    mem_t, mem_keys, mem_values = project_memory(core_arg, mem_parts, wc_key, wc_value)

    mixed, mixed_t, lse_self = self_forward(place, query, keys, values, bias_vec)
    mixed_got = at.swap_core(mixed)
    mixed_t_got = at.swap_core(mixed_t)
    after_self, cross_t, cross_query = join(
        core_arg, (tokens, tokens_got), mixed, mixed_got, w_out, gain_cross, wc_query, "join_self"
    )

    crossed, crossed_t, lse_cross = cross_forward(cross_query, mem_keys, mem_values, mask_col)
    crossed_got = at.swap_core(crossed)
    crossed_t_got = at.swap_core(crossed_t)
    after_cross, ffn_t, normed_ffn = join(
        core_arg, after_self, crossed, crossed_got, wc_out, gain_ffn, None, "join_cross"
    )

    hidden_t, grad_gate, grad_up, out_part, e_part = ffn(
        core_arg, normed_ffn, grad_chip, w_gate, w_up, w_down
    )
    e_got = at.swap_core(e_part)
    hidden_t_got = at.swap_core(hidden_t)
    out_got = at.swap_core(at.core_rows(out_part, False))
    gate_sum = ChipSum(at, 0, outer_halves(at.block_order(0), [ffn_t], [grad_gate], [[(0, 0, 0)]]))
    send([gate_sum])
    up_sum = ChipSum(at, 1, outer_halves(at.block_order(1), [ffn_t], [grad_up], [[(0, 0, 0)]]))
    send([up_sum])
    grad_after_cross, cross_half, grad_crossed = back(
        core_arg, (grads, grads_got), after_cross, gain_ffn, e_part, e_got, None, wc_out, "back_ffn"
    )
    grad_half = lax.dynamic_slice_in_dim(grad_chip, core * (width // 2), width // 2, 1)
    down_sum = ChipSum(
        at, 2, outer_halves(at.block_order(2, True), [(hidden_t, hidden_t_got)], [grad_half], [[(0, 0, 0)]])
    )
    (grad_crossed, grad_after_cross) = fold([down_sum], grad_crossed, grad_after_cross)
    send([down_sum])

    grad_cq, grad_mk, grad_mv = cross_backward(
        cross_query, mem_keys, mem_values, mask_col, grad_crossed, crossed, lse_cross
    )
    grad_cq_got = at.swap_core(grad_cq)
    wc_out_halves = outer_halves(
        at.block_order(1, True), [(crossed_t, crossed_t_got)], [cross_half], [[(0, 0, 0)]]
    )
    grad_after_self, self_half, grad_mixed = back(
        core_arg, grad_after_cross, after_self, gain_cross, grad_cq, grad_cq_got, wc_query, w_out, "back_cross"
    )
    wc_in_halves = outer_halves(
        at.block_order(2),
        [cross_t, mem_t],
        [grad_cq, grad_mk, grad_mv],
        [[(0, 0, 0)], [(1, 1, 0)], [(1, 2, 0)]],
    )
    out_halves = outer_halves(at.block_order(1, True), [(mixed_t, mixed_t_got)], [self_half], [[(0, 0, 0)]])

    ffn_sums = [gate_sum, up_sum, down_sum]
    tied = settle(
        ffn_sums,
        grad_mixed,
        grad_after_self,
        grad_mk,
        grad_mv,
        out_part,
        out_got,
        *wc_out_halves,
        *wc_in_halves,
        *out_halves,
    )
    grad_mixed, grad_after_self, grad_mk, grad_mv, out_part, out_got = tied[:6]
    wc_out_sum = ChipSum(at, 1, tied[6:8])
    wc_in_sum = ChipSum(at, 2, tied[8:10])
    out_sum = ChipSum(at, 1, tied[10:12])

    early = [*ffn_sums, out_sum, wc_out_sum, wc_in_sum]
    grad_mem_pair = jnp.concatenate([grad_mk, grad_mv], axis=1)
    grad_mixed, grad_mem_pair = fold(early, grad_mixed, grad_mem_pair)
    send(early)
    grad_q, grad_k, grad_v, diagonals = self_backward(
        place, query, keys, values, bias_vec, grad_mixed, mixed, lse_self
    )
    grad_q, grad_k, grad_v, diagonals, grad_mem_pair, out_part, out_got = settle(
        early, grad_q, grad_k, grad_v, diagonals, grad_mem_pair, out_part, out_got
    )
    output = (
        at.core_rows(after_cross, True)
        + at.core_rows(out_part, True).astype(F32)
        + out_got.astype(F32)
    ).astype(BF16)
    pair_chip = jnp.concatenate([grad_k[:rows], grad_v[:rows]], axis=1)
    pair_got = []
    for s in range(1, nx):
        span_s = slice(s * rows, (s + 1) * rows)
        sent = jnp.concatenate([grad_k[span_s], grad_v[span_s]], axis=1)
        pair_got.append(at.shift_x(sent, nx - s))
    in_sum = ChipSum(
        at,
        1,
        outer_halves(
            at.block_order(1),
            normed_ts,
            [grad_q, grad_k, grad_v],
            [[(0, 0, 0)]] + [[(s, r, s * rows) for s in range(nx)] for r in (1, 2)],
        ),
    )
    own_bias = lax.dot_general(
        diagonals.reshape(head_count, -1)[:, BLK:],
        onehot,
        (((1,), (0,)), ((), ())),
        precision=lax.Precision.HIGHEST,
        preferred_element_type=F32,
    )
    table = lax.dynamic_update_slice_in_dim(
        jnp.zeros((HEADS, BUCKETS), F32), own_bias, core * head_count, 0
    )
    table = (table + at.swap_core(table)).reshape(at.chips, -1)
    sorter = (at.block_order(0)[:, None] == jnp.arange(at.chips, dtype=jnp.int32)[None, :]).astype(F32)
    table = jnp.dot(sorter, table, precision=lax.Precision.HIGHEST)
    bias_sum = ChipSum(at, 0, (table[: at.chips // 2], table[at.chips // 2 :]), F32)

    every = early + [in_sum, bias_sum]
    fold(every)
    send(every)
    for got in pair_got:
        pair_chip = pair_chip + got

    span = 2 * mem_local
    grad_mem_chip = grad_mem_pair[:span].astype(F32)
    for s in range(1, nx):
        grad_mem_chip = grad_mem_chip + at.shift_x(grad_mem_pair[s * span : (s + 1) * span], nx - s).astype(F32)
    grad_mem_chip = grad_mem_chip.astype(BF16)
    mem_mine = grad_mem_chip[:mem_local]
    mem_got = at.swap_core(grad_mem_chip[mem_local:])
    grad_memory = dot_nt(at.by_core(mem_mine[:, :kw], mem_got[:, :kw], 1), wc_key) + dot_nt(
        at.by_core(mem_mine[:, kw:], mem_got[:, kw:], 1), wc_value
    )
    sent = jnp.concatenate([at.core_rows(grad_q, False), at.core_rows(pair_chip, False)], axis=1)
    (grad_target,) = last(
        core_arg,
        grad_after_self,
        tokens,
        gain_self,
        grad_q,
        pair_chip,
        at.swap_core(sent),
        w_query,
        w_key,
        w_value,
    )

    while any(one.flying is not None for one in every):
        fold(every)
        send(every)

    gate, up = core_join(at, [gate_sum.result(), up_sum.result()])
    (down,) = core_join(at, [down_sum.result()])
    wc_in = wc_in_sum.result()
    cross_out, cross_in, cross_key, cross_value = core_join(
        at, [wc_out_sum.result(), wc_in[:, :qw], wc_in[:, qw : qw + kw], wc_in[:, qw + kw :]]
    )
    self_all = in_sum.result()
    self_out, self_in, self_key, self_value = core_join(
        at, [out_sum.result(), self_all[:, :qw], self_all[:, qw : qw + kw], self_all[:, qw + kw :]]
    )

    share = width // (2 * at.chips)
    first_row = (2 * at.chip + core) * share

    def gain_share(gain, *pairs):
        total = 0.0
        for weight, grad in pairs:
            total = total + jnp.sum(
                lax.dynamic_slice_in_dim(weight, first_row, share, 0).astype(F32) * grad, axis=1
            )
        return total / lax.dynamic_slice_in_dim(gain, first_row, share, 0)

    bias_block = HEADS * BUCKETS // (2 * at.chips)
    bias_share = lax.dynamic_slice_in_dim(bias_sum.result().reshape(-1), core * bias_block, bias_block, 0)
    return (
        output.reshape(target.shape),
        grad_target.reshape(target.shape),
        grad_memory.reshape(memory.shape),
        gain_share(norm_self, (w_query, self_in), (w_key, self_key), (w_value, self_value)),
        self_in,
        self_key,
        self_value,
        self_out,
        bias_share,
        gain_share(norm_cross, (wc_query, cross_in)),
        cross_in,
        cross_key,
        cross_value,
        cross_out,
        gain_share(norm_ffn, (w_gate, gate), (w_up, up)),
        gate,
        up,
        down,
    )


def solution(mesh):
    tokens = P("dp", "seq", None)
    row_share = P(("dp", "seq"))
    matrix_share = P(("dp", "seq"), None)
    return jax.shard_map(
        per_device,
        mesh=mesh,
        in_specs=(tokens, tokens, P("dp"), P("dp", None)) + (P(),) * 16 + (tokens,),
        out_specs=(tokens, tokens, tokens, row_share)
        + (matrix_share,) * 4
        + (row_share, row_share)
        + (matrix_share,) * 4
        + (row_share,)
        + (matrix_share,) * 3,
        check_vma=False,
    )
```

```python
import functools

import jax
import jax.numpy as jnp
from jax import lax
from jax.experimental import pallas as pl
from jax.experimental.pallas import tpu as pltpu
from jax.sharding import PartitionSpec as P

HEADS = 16
KV = 8
HEAD_DIM = 64
BUCKETS = 32
BLK = 256
PAIR = 2 * HEAD_DIM

norm_eps = 1e-06
big_negative = -1000000000.0
score_scale = HEAD_DIM ** (-0.5)
F32 = jnp.float32
BF16 = jnp.bfloat16
VMEM_LIMIT = 61 * 1024 * 1024


def dot_nn(a, b):
    return lax.dot_general(a, b, (((1,), (0,)), ((), ())), preferred_element_type=F32)


def dot_nt(a, b):
    return lax.dot_general(a, b, (((1,), (1,)), ((), ())), preferred_element_type=F32)


def dot_tn(a, b):
    return lax.dot_general(a, b, (((0,), (0,)), ((), ())), preferred_element_type=F32)


def lane_pick(source, dest):
    a = lax.broadcasted_iota(jnp.int32, (PAIR, PAIR), 0)
    b = lax.broadcasted_iota(jnp.int32, (PAIR, PAIR), 1)
    keep = (a - source == b - dest) & (b >= dest) & (b < dest + HEAD_DIM)
    return keep.astype(F32).astype(BF16)


def lane_pick_t(source, dest):
    a = lax.broadcasted_iota(jnp.int32, (PAIR, PAIR), 1)
    b = lax.broadcasted_iota(jnp.int32, (PAIR, PAIR), 0)
    keep = (a - source == b - dest) & (b >= dest) & (b < dest + HEAD_DIM)
    return keep.astype(F32).astype(BF16)


def bias_tile(bias_vec_ref, h, delta):
    piece = bias_vec_ref[0, h : h + 1, delta * BLK : delta * BLK + 2 * BLK]
    wide = jnp.broadcast_to(piece, (BLK, 2 * BLK))
    return pltpu.roll(wide, 0, 1, stride=1, stride_axis=0)[:, BLK:]


def tile_plan(row_blocks, slots):
    plan = [(delta, 0) for delta in range(row_blocks)]
    for slot in range(1, slots):
        plan += [(slot * row_blocks + c, slot) for c in range(1 - row_blocks, row_blocks)]
    return plan


def tile_at(row_blocks, rb, kb):
    slot, jb = kb // row_blocks, kb % row_blocks
    if slot == 0:
        return rb - jb, rb - jb
    first = row_blocks + (slot - 1) * (2 * row_blocks - 1)
    return first + rb - jb + row_blocks - 1, slot * row_blocks + rb - jb


def key_blocks(row_blocks, slots, rb):
    return list(range(rb + 1)) + list(range(row_blocks, row_blocks * slots))


def fill_bias(place, bias_vec_ref, tile_ref, row_blocks, slots):
    for at, (delta, slot) in enumerate(tile_plan(row_blocks, slots)):
        for h in range(2):
            tile = bias_tile(bias_vec_ref, h, delta)
            if slot:
                tile = tile + jnp.where(place >= slot, 0.0, big_negative)
            elif delta == 0:
                tile = jnp.where(causal_tile(), tile, big_negative)
            tile_ref[h, at] = tile


def causal_tile():
    key_pos = lax.broadcasted_iota(jnp.int32, (BLK, BLK), 0)
    row_pos = lax.broadcasted_iota(jnp.int32, (BLK, BLK), 1)
    return key_pos <= row_pos


def online_step(carry, scores, value_t):
    highest, total, mixed = carry
    new_high = jnp.maximum(highest, jnp.max(scores, axis=0, keepdims=True))
    fade = jnp.exp(highest - new_high)
    weights = jnp.exp(scores - new_high)
    total = total * fade + jnp.sum(weights, axis=0, keepdims=True)
    mixed = mixed * fade + dot_nn(value_t, weights.astype(BF16))
    return (new_high, total, mixed)


def first_step(scores, value_t):
    highest = jnp.max(scores, axis=0, keepdims=True)
    weights = jnp.exp(scores - highest)
    total = jnp.sum(weights, axis=0, keepdims=True)
    return (highest, total, dot_nn(value_t, weights.astype(BF16)))


def key_spans(row_blocks, slots, rb):
    own, end = (rb + 1) * BLK, row_blocks * slots * BLK
    first_far = row_blocks * BLK
    if slots == 1:
        return [(0, own)]
    if own == first_far:
        return [(0, end)]
    return [(0, own), (first_far, end)]


def self_forward_kernel(slots, place_ref, q_ref, b_ref, *refs):
    k_refs, v_refs = refs[:slots], refs[slots : 2 * slots]
    o_ref, ot_ref, lse_ref, tile_ref, kz_ref, vt_ref, s_ref, p_ref = refs[2 * slots :]
    parity = lax.rem(pl.program_id(0), 2)
    rows_all = q_ref.shape[0]
    row_blocks = rows_all // BLK
    fill_bias(place_ref[0], b_ref, tile_ref, row_blocks, slots)
    for h in range(2):
        for slot in range(slots):
            span = slice(slot * rows_all, (slot + 1) * rows_all)
            pick_k = lane_pick(parity * HEAD_DIM, h * HEAD_DIM)
            pick_v = lane_pick_t(parity * HEAD_DIM, h * HEAD_DIM)
            kz_ref[h, span, :] = dot_nn(k_refs[slot][...], pick_k).astype(BF16)
            vt_ref[h, :, span] = dot_nt(pick_v, v_refs[slot][...]).astype(BF16)
    for rb in range(row_blocks):
        rows = slice(rb * BLK, (rb + 1) * BLK)
        queries = q_ref[rows, :]
        spans = key_spans(row_blocks, slots, rb)
        highest = [None, None]
        for h in range(2):
            for first, end in spans:
                products = dot_nt(kz_ref[h, first:end, :], queries)
                for kb in range(first // BLK, end // BLK):
                    at, _ = tile_at(row_blocks, rb, kb)
                    scores = products[kb * BLK - first : (kb + 1) * BLK - first, :] + tile_ref[h, at]
                    s_ref[h, kb * BLK : (kb + 1) * BLK, :] = scores
                    top = jnp.max(scores, axis=0, keepdims=True)
                    highest[h] = top if highest[h] is None else jnp.maximum(highest[h], top)
        mixed_t = None
        for h in range(2):
            total = None
            part = None
            for first, end in spans:
                weights = jnp.exp(s_ref[h, first:end, :] - highest[h])
                one = jnp.sum(weights, axis=0, keepdims=True)
                total = one if total is None else total + one
                p_ref[h, first:end, :] = weights.astype(BF16)
            for first, end in spans:
                one = dot_nn(vt_ref[h, :, first:end], p_ref[h, first:end, :])
                part = one if part is None else part + one
            part = part / total
            mixed_t = part if mixed_t is None else mixed_t + part
            lse_ref[0, h : h + 1, rows] = highest[h] + jnp.log(total)
        ot_ref[:, rows] = mixed_t.astype(BF16)
        o_ref[rows, :] = mixed_t.T.astype(BF16)


def diagonal_sums(wide):
    rows, lanes = wide.shape
    while rows > 8:
        rows //= 2
        wide = wide[:rows] + pltpu.roll(wide[rows:], lanes - rows, 1)
    row = lax.broadcasted_iota(jnp.int32, (8, lanes), 0)
    total = jnp.where(row == 0, wide, 0.0)
    for b in range(1, 8):
        total = total + jnp.where(row == b, pltpu.roll(wide, lanes - b, 1), 0.0)
    return jnp.sum(total, axis=0, keepdims=True)


def row_products(grad_block, mixed_block):
    turned = (grad_block.astype(F32) * mixed_block.astype(F32)).T
    return [
        jnp.sum(turned[h * HEAD_DIM : (h + 1) * HEAD_DIM], axis=0, keepdims=True) for h in range(2)
    ]


def self_backward_kernel(slots, place_ref, q_ref, b_ref, do_ref, o_ref, lse_ref, *refs):
    k_refs, v_refs = refs[:slots], refs[slots : 2 * slots]
    dq_ref, diag_ref = refs[2 * slots : 2 * slots + 2]
    pair_refs, refs = refs[2 * slots + 2 : 3 * slots + 2], refs[3 * slots + 2 :]
    tile_ref, sum_ref, kz_ref, kt_ref, vz_ref, qp_ref, dop_ref, dk_acc, dv_acc, p_ref, ds_ref = refs
    parity = lax.rem(pl.program_id(0), 2)
    rows_all = q_ref.shape[0]
    row_blocks = rows_all // BLK
    fill_bias(place_ref[0], b_ref, tile_ref, row_blocks, slots)
    for h in range(2):
        in_pick = lane_pick(parity * HEAD_DIM, h * HEAD_DIM)
        out_pick = lane_pick(h * HEAD_DIM, parity * HEAD_DIM)
        pick_t = lane_pick_t(parity * HEAD_DIM, h * HEAD_DIM)
        for slot in range(slots):
            span = slice(slot * rows_all, (slot + 1) * rows_all)
            kz_ref[h, span, :] = dot_nn(k_refs[slot][...], in_pick).astype(BF16)
            kt_ref[h, :, span] = dot_nt(pick_t, k_refs[slot][...]).astype(BF16)
            vz_ref[h, span, :] = dot_nn(v_refs[slot][...], in_pick).astype(BF16)
        side = slice(h * rows_all, (h + 1) * rows_all)
        qp_ref[side, :] = dot_nn(q_ref[...], out_pick).astype(BF16)
        dop_ref[side, :] = dot_nn(do_ref[...], out_pick).astype(BF16)
    seen = set()
    for rb in range(row_blocks):
        rows = slice(rb * BLK, (rb + 1) * BLK)
        spans = key_spans(row_blocks, slots, rb)
        delta_rows = row_products(do_ref[rows, :], o_ref[rows, :])
        for kb in range(rb + 1, row_blocks):
            for h in range(2):
                side = slice(h * rows_all + rb * BLK, h * rows_all + (rb + 1) * BLK)
                keys = slice(kb * BLK, (kb + 1) * BLK)
                p_ref[keys, side] = jnp.zeros((BLK, BLK), BF16)
                ds_ref[keys, side] = jnp.zeros((BLK, BLK), BF16)
        for h in range(2):
            side = slice(h * rows_all + rb * BLK, h * rows_all + (rb + 1) * BLK)
            delta_row = delta_rows[h]
            lse = lse_ref[0, h : h + 1, rows]
            for first, end in spans:
                products = dot_nt(kz_ref[h, first:end, :], q_ref[rows, :])
                grad_products = dot_nt(vz_ref[h, first:end, :], do_ref[rows, :])
                for kb in range(first // BLK, end // BLK):
                    keys = slice(kb * BLK, (kb + 1) * BLK)
                    inner = slice(kb * BLK - first, (kb + 1) * BLK - first)
                    at, delta = tile_at(row_blocks, rb, kb)
                    probs = jnp.exp(products[inner, :] + tile_ref[h, at] - lse)
                    grad_scores = probs * (grad_products[inner, :] - delta_row)
                    p_ref[keys, side] = probs.astype(BF16)
                    ds_ref[keys, side] = grad_scores.astype(BF16)
                    if (h, delta) in seen:
                        sum_ref[h, delta] += grad_scores
                    else:
                        sum_ref[h, delta] = grad_scores
                        seen.add((h, delta))
    grad_v = dot_nn(p_ref[...], dop_ref[...])
    grad_k = dot_nn(ds_ref[...], qp_ref[...])

    @pl.when(parity == 0)
    def first():
        dv_acc[...] = grad_v
        dk_acc[...] = grad_k

    @pl.when(parity == 1)
    def second():
        dv_acc[...] += grad_v
        dk_acc[...] += grad_k

    grad_q = None
    for h in range(2):
        part = dot_nn(kt_ref[h], ds_ref[:, h * rows_all : (h + 1) * rows_all])
        grad_q = part if grad_q is None else grad_q + part
    dq_ref[...] = (grad_q.T * score_scale).astype(BF16)

    diag_ref[...] = jnp.zeros_like(diag_ref)
    for h in range(2):
        for delta in range(row_blocks * slots):
            wide = jnp.concatenate([jnp.zeros((BLK, BLK), F32), sum_ref[h, delta]], axis=1)
            diag_ref[0, h : h + 1, delta * BLK : delta * BLK + 2 * BLK] += diagonal_sums(wide)

    @pl.when(parity == 1)
    def store():
        for slot, pair_ref in enumerate(pair_refs):
            span = slice(slot * rows_all, (slot + 1) * rows_all)
            pair_ref[:, :PAIR] = dk_acc[span, :].astype(BF16)
            pair_ref[:, PAIR:] = dv_acc[span, :].astype(BF16)


def cross_forward_kernel(q_ref, k_ref, v_ref, m_ref, o_ref, ot_ref, lse_ref, kz_ref, vt_ref, s_ref, p_ref):
    parity = lax.rem(pl.program_id(0), 2)
    for h in range(2):
        kz_ref[h] = dot_nn(k_ref[...], lane_pick(parity * HEAD_DIM, h * HEAD_DIM)).astype(BF16)
        vt_ref[h] = dot_nt(lane_pick_t(parity * HEAD_DIM, h * HEAD_DIM), v_ref[...]).astype(BF16)
    for rb in range(q_ref.shape[0] // BLK):
        rows = slice(rb * BLK, (rb + 1) * BLK)
        queries = q_ref[rows, :]
        highest = []
        for h in range(2):
            scores = dot_nt(kz_ref[h], queries) + m_ref[...]
            s_ref[h] = scores
            highest.append(jnp.max(scores, axis=0, keepdims=True))
        mixed_t = None
        for h in range(2):
            weights = jnp.exp(s_ref[h] - highest[h])
            total = jnp.sum(weights, axis=0, keepdims=True)
            p_ref[h] = weights.astype(BF16)
            part = dot_nn(vt_ref[h], p_ref[h]) / total
            mixed_t = part if mixed_t is None else mixed_t + part
            lse_ref[0, h : h + 1, rows] = highest[h] + jnp.log(total)
        ot_ref[:, rows] = mixed_t.astype(BF16)
        o_ref[rows, :] = mixed_t.T.astype(BF16)


def cross_backward_kernel(
    q_ref,
    k_ref,
    v_ref,
    m_ref,
    do_ref,
    o_ref,
    lse_ref,
    dq_ref,
    pair_ref,
    kz_ref,
    kt_ref,
    vz_ref,
    qp_ref,
    dop_ref,
    dk_acc,
    dv_acc,
    p_ref,
    ds_ref,
):
    parity = lax.rem(pl.program_id(0), 2)
    rows_all = q_ref.shape[0]
    for h in range(2):
        in_pick = lane_pick(parity * HEAD_DIM, h * HEAD_DIM)
        out_pick = lane_pick(h * HEAD_DIM, parity * HEAD_DIM)
        kz_ref[h] = dot_nn(k_ref[...], in_pick).astype(BF16)
        kt_ref[h] = dot_nt(lane_pick_t(parity * HEAD_DIM, h * HEAD_DIM), k_ref[...]).astype(BF16)
        vz_ref[h] = dot_nn(v_ref[...], in_pick).astype(BF16)
        side = slice(h * rows_all, (h + 1) * rows_all)
        qp_ref[side, :] = dot_nn(q_ref[...], out_pick).astype(BF16)
        dop_ref[side, :] = dot_nn(do_ref[...], out_pick).astype(BF16)
    for rb in range(rows_all // BLK):
        rows = slice(rb * BLK, (rb + 1) * BLK)
        delta_rows = row_products(do_ref[rows, :], o_ref[rows, :])
        for h in range(2):
            side = slice(h * rows_all + rb * BLK, h * rows_all + (rb + 1) * BLK)
            delta_row = delta_rows[h]
            lse = lse_ref[0, h : h + 1, rows]
            probs = jnp.exp(dot_nt(kz_ref[h], q_ref[rows, :]) + m_ref[...] - lse)
            grad_products = dot_nt(vz_ref[h], do_ref[rows, :])
            p_ref[:, side] = probs.astype(BF16)
            ds_ref[:, side] = (probs * (grad_products - delta_row)).astype(BF16)
    grad_v = dot_nn(p_ref[...], dop_ref[...])
    grad_k = dot_nn(ds_ref[...], qp_ref[...])

    @pl.when(parity == 0)
    def first():
        dv_acc[...] = grad_v
        dk_acc[...] = grad_k

    @pl.when(parity == 1)
    def second():
        pair_ref[:, :PAIR] = (dk_acc[...] + grad_k).astype(BF16)
        pair_ref[:, PAIR:] = (dv_acc[...] + grad_v).astype(BF16)

    grad_q = None
    for h in range(2):
        part = dot_nn(kt_ref[h], ds_ref[:, h * rows_all : (h + 1) * rows_all])
        grad_q = part if grad_q is None else grad_q + part
    dq_ref[...] = (grad_q.T * score_scale).astype(BF16)


def shape_of(shape, dtype):
    return jax.ShapeDtypeStruct(shape, dtype)


def tile_pair(rows):
    return pl.BlockSpec((rows, PAIR), lambda g: (0, g))


def tile_pair_t(rows):
    return pl.BlockSpec((PAIR, rows), lambda g: (g, 0))


def tile_group(rows):
    return pl.BlockSpec((rows, PAIR), lambda g: (0, g // 2))


def tile_both(rows):
    return pl.BlockSpec((rows, 2 * PAIR), lambda g: (0, g // 2))


def tile_rows(width):
    return pl.BlockSpec((1, 2, width), lambda g: (g, 0, 0))


def kernel_params():
    return pltpu.CompilerParams(
        dimension_semantics=("arbitrary",), vmem_limit_bytes=VMEM_LIMIT
    )


def cost(flops, transcendentals, nbytes):
    return pl.CostEstimate(
        flops=int(flops) // 16, transcendentals=0, bytes_accessed=int(nbytes) // 16
    )


def self_forward(place, q, ks, vs, bias_vec):
    rows, width = q.shape
    slots = len(ks)
    keys = rows * slots
    pairs = width // PAIR
    tiles = len(tile_plan(rows // BLK, slots))
    return pl.pallas_call(
        functools.partial(self_forward_kernel, slots),
        grid=(pairs,),
        in_specs=[pl.BlockSpec(memory_space=pltpu.SMEM), tile_pair(rows), tile_rows(bias_vec.shape[2])]
        + [tile_group(rows)] * (2 * slots),
        out_specs=[tile_pair(rows), tile_pair_t(rows), tile_rows(rows)],
        out_shape=[
            shape_of((rows, width), BF16),
            shape_of((width, rows), BF16),
            shape_of((pairs, 2, rows), F32),
        ],
        scratch_shapes=[
            pltpu.VMEM((2, tiles, BLK, BLK), F32),
            pltpu.VMEM((2, keys, PAIR), BF16),
            pltpu.VMEM((2, PAIR, keys), BF16),
            pltpu.VMEM((2, keys, BLK), F32),
            pltpu.VMEM((2, keys, BLK), BF16),
        ],
        compiler_params=kernel_params(),
        cost_estimate=cost(4 * 2 * rows * keys * width * 2, pairs * 2 * rows * keys, 8 * rows * width),
        name="self_forward",
    )(place, q, bias_vec, *ks, *vs)


def self_backward(place, q, ks, vs, bias_vec, grads, mixed, lse):
    rows, width = q.shape
    kv_width = ks[0].shape[1]
    slots = len(ks)
    keys = rows * slots
    pairs = width // PAIR
    tiles = len(tile_plan(rows // BLK, slots))
    grad_q, diagonals, *pairs_out = pl.pallas_call(
        functools.partial(self_backward_kernel, slots),
        grid=(pairs,),
        in_specs=[
            pl.BlockSpec(memory_space=pltpu.SMEM),
            tile_pair(rows),
            tile_rows(bias_vec.shape[2]),
            tile_pair(rows),
            tile_pair(rows),
            tile_rows(rows),
        ]
        + [tile_group(rows)] * (2 * slots),
        out_specs=[tile_pair(rows), tile_rows(bias_vec.shape[2])] + [tile_both(rows)] * slots,
        out_shape=[shape_of((rows, width), BF16), shape_of(bias_vec.shape, F32)]
        + [shape_of((rows, 2 * kv_width), BF16)] * slots,
        scratch_shapes=[
            pltpu.VMEM((2, tiles, BLK, BLK), F32),
            pltpu.VMEM((2, keys // BLK, BLK, BLK), F32),
            pltpu.VMEM((2, keys, PAIR), BF16),
            pltpu.VMEM((2, PAIR, keys), BF16),
            pltpu.VMEM((2, keys, PAIR), BF16),
            pltpu.VMEM((2 * rows, PAIR), BF16),
            pltpu.VMEM((2 * rows, PAIR), BF16),
            pltpu.VMEM((keys, PAIR), F32),
            pltpu.VMEM((keys, PAIR), F32),
            pltpu.VMEM((keys, 2 * rows), BF16),
            pltpu.VMEM((keys, 2 * rows), BF16),
        ],
        compiler_params=kernel_params(),
        cost_estimate=cost(10 * 2 * rows * keys * width * 2, pairs * 2 * rows * keys, 12 * rows * width),
        name="self_backward",
    )(place, q, bias_vec, grads, mixed, lse, *ks, *vs)
    return grad_q, pairs_out, diagonals


def cross_forward(q, k, v, mask_col):
    rows, width = q.shape
    keys = k.shape[0]
    pairs = width // PAIR
    return pl.pallas_call(
        cross_forward_kernel,
        grid=(pairs,),
        in_specs=[
            tile_pair(rows),
            tile_group(keys),
            tile_group(keys),
            pl.BlockSpec((keys, 1), lambda g: (0, 0)),
        ],
        out_specs=[tile_pair(rows), tile_pair_t(rows), tile_rows(rows)],
        out_shape=[
            shape_of((rows, width), BF16),
            shape_of((width, rows), BF16),
            shape_of((pairs, 2, rows), F32),
        ],
        scratch_shapes=[
            pltpu.VMEM((2, keys, PAIR), BF16),
            pltpu.VMEM((2, PAIR, keys), BF16),
            pltpu.VMEM((2, keys, BLK), F32),
            pltpu.VMEM((2, keys, BLK), BF16),
        ],
        compiler_params=kernel_params(),
        cost_estimate=cost(4 * 2 * rows * keys * width * 2, pairs * 2 * rows * keys, 8 * rows * width),
        name="cross_forward",
    )(q, k, v, mask_col)


def cross_backward(q, k, v, mask_col, grads, mixed, lse):
    rows, width = q.shape
    keys, kv_width = k.shape
    pairs = width // PAIR
    return pl.pallas_call(
        cross_backward_kernel,
        grid=(pairs,),
        in_specs=[
            tile_pair(rows),
            tile_group(keys),
            tile_group(keys),
            pl.BlockSpec((keys, 1), lambda g: (0, 0)),
            tile_pair(rows),
            tile_pair(rows),
            tile_rows(rows),
        ],
        out_specs=[tile_pair(rows), tile_both(keys)],
        out_shape=[shape_of((rows, width), BF16), shape_of((keys, 2 * kv_width), BF16)],
        scratch_shapes=[
            pltpu.VMEM((2, keys, PAIR), BF16),
            pltpu.VMEM((2, PAIR, keys), BF16),
            pltpu.VMEM((2, keys, PAIR), BF16),
            pltpu.VMEM((2 * rows, PAIR), BF16),
            pltpu.VMEM((2 * rows, PAIR), BF16),
            pltpu.VMEM((keys, PAIR), F32),
            pltpu.VMEM((keys, PAIR), F32),
            pltpu.VMEM((keys, 2 * rows), BF16),
            pltpu.VMEM((keys, 2 * rows), BF16),
        ],
        compiler_params=kernel_params(),
        cost_estimate=cost(10 * 2 * rows * keys * width * 2, pairs * 2 * rows * keys, 12 * rows * width),
        name="cross_backward",
    )(q, k, v, mask_col, grads, mixed, lse)


FBLK = 256


def ffn_kernel(core_ref, x_ref, og_ref, wg_ref, wu_ref, wd_ref, ht_ref, gg_ref, gu_ref, out_ref, e_ref, hb_ref):
    rows, hidden_width = gg_ref.shape
    factor = (2.0 / jnp.pi) ** 0.5
    for first in range(0, hidden_width, FBLK):
        span = slice(first, min(first + FBLK, hidden_width))
        gate = dot_nn(x_ref[...], wg_ref[:, span])
        up = dot_nn(x_ref[...], wu_ref[:, span])
        grad_hidden = dot_nt(og_ref[...], wd_ref[span, :])
        square = gate * gate
        bend = jnp.tanh(factor * (gate + 0.044715 * gate * square))
        half = 0.5 * (1.0 + bend)
        gelu = gate * half
        slope = half + 0.5 * gate * (1.0 - bend * bend) * (factor * (1.0 + 3 * 0.044715 * square))
        hidden = gelu * up
        hb_ref[:, span] = hidden.astype(BF16)
        ht_ref[span, :] = hidden.T.astype(BF16)
        gg_ref[:, span] = (grad_hidden * up * slope).astype(BF16)
        gu_ref[:, span] = (grad_hidden * gelu).astype(BF16)
    out_ref[...] = dot_nn(hb_ref[...], wd_ref[...]).astype(BF16)
    e_ref[...] = (dot_nt(gg_ref[...], wg_ref[...]) + dot_nt(gu_ref[...], wu_ref[...])).astype(BF16)


def ffn(core, normed, out_grad, w_gate, w_up, w_down):
    rows, width = normed.shape
    hidden = w_gate.shape[1] // 2
    tile = min(rows, 256)
    by_rows = pl.BlockSpec((tile, width), lambda i, c: (i, 0))
    return pl.pallas_call(
        ffn_kernel,
        grid_spec=pltpu.PrefetchScalarGridSpec(
            num_scalar_prefetch=1,
            grid=(rows // tile,),
            in_specs=[
                by_rows,
                by_rows,
                pl.BlockSpec((width, hidden), lambda i, c: (0, c[0])),
                pl.BlockSpec((width, hidden), lambda i, c: (0, c[0])),
                pl.BlockSpec((hidden, width), lambda i, c: (c[0], 0)),
            ],
            out_specs=[
                pl.BlockSpec((hidden, tile), lambda i, c: (0, i)),
                pl.BlockSpec((tile, hidden), lambda i, c: (i, 0)),
                pl.BlockSpec((tile, hidden), lambda i, c: (i, 0)),
                by_rows,
                by_rows,
            ],
            scratch_shapes=[pltpu.VMEM((tile, hidden), BF16)],
        ),
        out_shape=[
            shape_of((hidden, rows), BF16),
            shape_of((rows, hidden), BF16),
            shape_of((rows, hidden), BF16),
            shape_of((rows, width), BF16),
            shape_of((rows, width), BF16),
        ],
        compiler_params=kernel_params(),
        cost_estimate=cost(2 * 6 * rows * width * hidden, rows * hidden, 6 * width * hidden),
        name="ffn",
    )(core, normed, out_grad, w_gate, w_up, w_down)


def normalise(values, gain):
    inverse = lax.rsqrt(jnp.mean(values * values, axis=-1, keepdims=True) + norm_eps)
    return values * inverse * gain


def rms_back(values, gain, grad):
    inverse = lax.rsqrt(jnp.mean(values * values, axis=-1, keepdims=True) + norm_eps)
    scaled = grad * gain
    mean_dot = jnp.mean(values * scaled, axis=-1, keepdims=True)
    unit = values * inverse
    return inverse * (scaled - unit * (inverse * mean_dot))


def project_kernel(scales, core_ref, own_ref, other_ref, gain_ref, *refs):
    count = len(scales)
    w_refs, nt_ref, out_refs = refs[:count], refs[count], refs[count + 1 :]
    mine = core_ref[0] == pl.program_id(0)
    values = jnp.where(mine, own_ref[...], other_ref[...]).astype(F32)
    normed = normalise(values, gain_ref[...])
    nt_ref[...] = normed.T.astype(BF16)
    low = normed.astype(BF16)
    for scale, w_ref, out_ref in zip(scales, w_refs, out_refs):
        out = dot_nn(low, w_ref[...]).astype(BF16)
        out_ref[...] = out if scale is None else out * BF16(scale)


def own_columns(weight):
    return pl.BlockSpec((weight.shape[0], weight.shape[1] // 2), lambda i, c: (0, c[0]))


def other_columns(weight):
    return pl.BlockSpec((weight.shape[0], weight.shape[1] // 2), lambda i, c: (0, 1 - c[0]))


def own_rows(array):
    return pl.BlockSpec((array.shape[0] // 2, array.shape[1]), lambda i, c: (c[0], 0))


def other_rows(array):
    return pl.BlockSpec((array.shape[0] // 2, array.shape[1]), lambda i, c: (1 - c[0], 0))


def all_of(array):
    return pl.BlockSpec(array.shape, lambda i, c: (0,) * array.ndim)


def half_rows(rows, width):
    return pl.BlockSpec((rows, width), lambda i, c: (i, 0))


def half_columns(width, rows):
    return pl.BlockSpec((width, rows), lambda i, c: (0, i))


def fixed(shape):
    return pl.BlockSpec(shape, lambda i, c: (0,) * len(shape))


def core_call(kernel, steps, core, args, in_specs, out_specs, out_shape, scratch, flops, name):
    return pl.pallas_call(
        kernel,
        grid_spec=pltpu.PrefetchScalarGridSpec(
            num_scalar_prefetch=1,
            grid=(steps,),
            in_specs=in_specs,
            out_specs=out_specs,
            scratch_shapes=scratch,
        ),
        out_shape=out_shape,
        compiler_params=kernel_params(),
        cost_estimate=cost(flops, 0, flops // 400),
        name=name,
    )(core, *args)


def project(core, own, other, gain, weights, scales, name):
    local, width = own.shape
    return core_call(
        functools.partial(project_kernel, scales),
        2,
        core,
        (own, other, gain, *weights),
        [all_of(own), all_of(other), all_of(gain)] + [own_columns(w) for w in weights],
        [half_columns(width, local)] + [half_rows(local, w.shape[1] // 2) for w in weights],
        [shape_of((width, 2 * local), BF16)]
        + [shape_of((2 * local, w.shape[1] // 2), BF16) for w in weights],
        [],
        2 * 2 * local * width * sum(w.shape[1] // 2 for w in weights),
        name,
    )


def memory_kernel(parts, core_ref, *refs):
    in_refs = refs[:parts]
    wk_ref, wv_ref, mt_ref, k_ref, v_ref, all_ref = refs[parts:]
    rows = in_refs[0].shape[0]
    for i in range(parts):
        all_ref[i * rows : (i + 1) * rows, :] = in_refs[i][...]
    mt_ref[...] = all_ref[...].astype(F32).T.astype(BF16)
    k_ref[...] = dot_nn(all_ref[...], wk_ref[...]).astype(BF16)
    v_ref[...] = dot_nn(all_ref[...], wv_ref[...]).astype(BF16)


def project_memory(core, parts, w_key, w_value):
    rows, width = parts[0].shape
    total = rows * len(parts)
    kw = w_key.shape[1] // 2
    return core_call(
        functools.partial(memory_kernel, len(parts)),
        1,
        core,
        (*parts, w_key, w_value),
        [all_of(p) for p in parts] + [own_columns(w_key), own_columns(w_value)],
        [fixed((width, total)), fixed((total, kw)), fixed((total, kw))],
        [shape_of((width, total), BF16), shape_of((total, kw), BF16), shape_of((total, kw), BF16)],
        [pltpu.VMEM((total, width), BF16)],
        2 * total * width * 2 * kw,
        "project_memory",
    )


def join_kernel(low_base, project_next, core_ref, *refs):
    if low_base:
        own_ref, other_ref, refs = refs[0], refs[1], refs[2:]
        mine = core_ref[0] == pl.program_id(0)
        base = jnp.where(mine, own_ref[...], other_ref[...]).astype(F32)
    else:
        base, refs = refs[0][...], refs[1:]
    mixed_ref, got_ref, w_own_ref, w_other_ref, gain_ref = refs[:5]
    after = base + dot_nn(mixed_ref[...], w_own_ref[...]) + dot_nn(got_ref[...], w_other_ref[...])
    normed = normalise(after, gain_ref[...])
    low = normed.astype(BF16)
    if project_next:
        w_ref, after_ref, nt_ref, out_ref = refs[5:]
        out_ref[...] = dot_nn(low, w_ref[...]).astype(BF16) * BF16(score_scale)
    else:
        after_ref, nt_ref, out_ref = refs[5:]
        out_ref[...] = low
    after_ref[...] = after
    nt_ref[...] = normed.T.astype(BF16)


def join(core, base, mixed, got, w_out, gain, w_next, name):
    rows, half = mixed.shape
    width = w_out.shape[1]
    local = rows // 2
    low_base = isinstance(base, tuple)
    bases = base if low_base else (base,)
    base_specs = [all_of(v) for v in bases] if low_base else [half_rows(local, width)]
    nexts = () if w_next is None else (w_next,)
    out_width = width if w_next is None else w_next.shape[1] // 2
    return core_call(
        functools.partial(join_kernel, low_base, w_next is not None),
        2,
        core,
        (*bases, mixed, got, w_out, w_out, gain, *nexts),
        base_specs
        + [half_rows(local, half), half_rows(local, half), own_rows(w_out), other_rows(w_out), all_of(gain)]
        + [own_columns(w) for w in nexts],
        [half_rows(local, width), half_columns(width, local), half_rows(local, out_width)],
        [shape_of((rows, width), F32), shape_of((width, rows), BF16), shape_of((rows, out_width), BF16)],
        [],
        2 * rows * width * (width + out_width),
        name,
    )


def back_kernel(low_prior, products, core_ref, *refs):
    if low_prior:
        own_ref, other_ref, refs = refs[0], refs[1], refs[2:]
        mine = core_ref[0] == pl.program_id(0)
        prior = jnp.where(mine, own_ref[...], other_ref[...]).astype(F32)
    else:
        prior, refs = refs[0][...], refs[1:]
    value_ref, gain_ref, e_ref, got_ref, refs = refs[0], refs[1], refs[2], refs[3], refs[4:]
    if products:
        e = dot_nt(e_ref[...], refs[0][...]) + dot_nt(got_ref[...], refs[1][...])
        refs = refs[2:]
    else:
        e = e_ref[...].astype(F32) + got_ref[...].astype(F32)
    w_ref, grad_ref, half_ref, next_ref = refs
    grad = prior + rms_back(value_ref[...], gain_ref[...], e)
    grad_ref[...] = grad
    low = grad.astype(BF16)
    half = low.shape[1] // 2
    half_ref[...] = jnp.where(core_ref[0] == 0, low[:, :half], low[:, half:])
    next_ref[...] = dot_nt(low, w_ref[...]).astype(BF16)


def back(core, prior, values, gain, e, got, w_in, w_out, name):
    rows, width = values.shape
    local = rows // 2
    low_prior = isinstance(prior, tuple)
    priors = prior if low_prior else (prior,)
    prior_specs = [all_of(v) for v in priors] if low_prior else [half_rows(local, width)]
    ins = () if w_in is None else (w_in, w_in)
    in_specs = [] if w_in is None else [own_columns(w_in), other_columns(w_in)]
    half = w_out.shape[0] // 2
    return core_call(
        functools.partial(back_kernel, low_prior, w_in is not None),
        2,
        core,
        (*priors, values, gain, e, got, *ins, w_out),
        prior_specs
        + [half_rows(local, width), all_of(gain), half_rows(local, e.shape[1]), half_rows(local, e.shape[1])]
        + in_specs
        + [own_rows(w_out)],
        [half_rows(local, width), half_rows(local, width // 2), half_rows(local, half)],
        [
            shape_of((rows, width), F32),
            shape_of((rows, width // 2), BF16),
            shape_of((rows, half), BF16),
        ],
        [],
        2 * rows * width * (half + 2 * e.shape[1] * len(ins) // 2),
        name,
    )


def last_kernel(core_ref, prior_ref, base_ref, gain_ref, q_ref, pair_ref, got_ref, *refs):
    wq_own, wq_other, wk_own, wk_other, wv_own, wv_other, grad_ref = refs
    qw = wq_own.shape[1]
    kw = wk_own.shape[1]
    e = dot_nt(q_ref[...], wq_own[...]) + dot_nt(got_ref[:, :qw], wq_other[...])
    for m in range(kw // PAIR):
        c, span = 2 * PAIR * m, slice(PAIR * m, PAIR * (m + 1))
        e = e + dot_nt(pair_ref[:, c : c + PAIR], wk_own[:, span])
        e = e + dot_nt(got_ref[:, qw + c : qw + c + PAIR], wk_other[:, span])
        c = c + PAIR
        e = e + dot_nt(pair_ref[:, c : c + PAIR], wv_own[:, span])
        e = e + dot_nt(got_ref[:, qw + c : qw + c + PAIR], wv_other[:, span])
    grad_ref[...] = prior_ref[...] + rms_back(base_ref[...].astype(F32), gain_ref[...], e)


def last(core, prior, base, gain, grad_q, pair, got, w_query, w_key, w_value):
    local, width = base.shape
    weights = (w_query, w_query, w_key, w_key, w_value, w_value)
    specs = []
    for w in (w_query, w_key, w_value):
        specs += [own_columns(w), other_columns(w)]
    return core_call(
        last_kernel,
        1,
        core,
        (prior, base, gain, grad_q, pair, got, *weights),
        [own_rows(prior), all_of(base), all_of(gain), own_rows(grad_q), own_rows(pair), all_of(got)] + specs,
        [fixed((local, width))],
        [shape_of((local, width), F32)],
        [],
        2 * local * width * 2 * width,
        "last",
    )


def outer_kernel(terms, split, count, has_extra, order_ref, *refs):
    lefts = []
    for parts in split:
        lefts.append(refs[:parts])
        refs = refs[parts:]
    right_refs, refs = refs[:count], refs[count:]
    if has_extra:
        extra_ref, refs = refs[0], refs[1:]
    keep_ref, send_ref, sorted_refs = refs[0], refs[1], refs[2:]
    blocks = order_ref.shape[1]
    for at, (left, sorted_ref) in enumerate(zip(lefts, sorted_refs)):
        rows = sorted_ref.shape[0] // blocks
        for p in range(blocks):
            index = order_ref[at, p]
            if len(left) == 1:
                piece = left[0][pl.ds(pl.multiple_of(index * rows, rows), rows), :]
            else:
                middle = blocks // 2
                first = pl.multiple_of(jnp.minimum(index, middle - 1) * rows, rows)
                second = pl.multiple_of(jnp.maximum(index - middle, 0) * rows, rows)
                piece = jnp.where(
                    index < middle, left[0][pl.ds(first, rows), :], left[1][pl.ds(second, rows), :]
                )
            sorted_ref[p * rows : (p + 1) * rows, :] = piece
    middle = sorted_refs[0].shape[0] // 2
    for out_ref, span in ((send_ref, slice(middle, 2 * middle)), (keep_ref, slice(0, middle))):
        column = 0
        for products in terms:
            total = None
            for left, right, first, start, size in products:
                depth = sorted_refs[left].shape[1]
                factor = right_refs[right][first : first + depth, start : start + size]
                part = dot_nn(sorted_refs[left][span, :], factor)
                total = part if total is None else total + part
            width = total.shape[1]
            out_ref[:, column : column + width] = total.astype(BF16)
            column += width
    if has_extra:
        rows = sorted_refs[0].shape[0] // blocks
        lanes = extra_ref.shape[1]
        row = lax.broadcasted_iota(jnp.int32, (rows, lanes), 0)
        for p in range(blocks):
            index = 2 * order_ref[0, p]
            block = jnp.where(row == 0, extra_ref[pl.ds(index, 1), :], 0.0)
            block = jnp.where(row == rows // 2, extra_ref[pl.ds(index + 1, 1), :], block)
            out_ref = keep_ref if p < blocks // 2 else send_ref
            first = p % (blocks // 2) * rows
            out_ref[first : first + rows, column:] = block.astype(BF16)


def outer_halves(orders, lefts, rights, terms, extra=None):
    blocks = orders[0].shape[0]
    lefts = [v if isinstance(v, tuple) else (v,) for v in lefts]
    totals = [sum(v.shape[0] for v in left) for left in lefts]
    rows = totals[0] // blocks
    if rows % 16:
        joined = [jnp.concatenate(left, axis=0) for left in lefts]
        joined = [
            jnp.concatenate(
                [lax.dynamic_slice_in_dim(v, order[p] * rows, rows, 0) for p in range(blocks)], axis=0
            )
            for v, order in zip(joined, orders)
        ]
        half = totals[0] // 2
        columns = []
        for products in terms:
            columns.append(
                sum(
                    dot_nn(joined[l], rights[r][first : first + joined[l].shape[1], start : start + size])
                    for l, r, first, start, size in products
                )
            )
        total = jnp.concatenate(columns, axis=1).astype(BF16)
        return total[:half], total[half:]
    width = sum(products[0][4] for products in terms)
    extras = () if extra is None else (extra,)
    if extras:
        width += extra.shape[1]
    half = shape_of((totals[0] // 2, width), BF16)
    flops = 0
    for products in terms:
        for l, _, _, _, size in products:
            flops += 2 * totals[l] * lefts[l][0].shape[1] * size
    whole = pl.BlockSpec(memory_space=pltpu.VMEM)
    flat = [v for left in lefts for v in left]
    return pl.pallas_call(
        functools.partial(outer_kernel, terms, [len(left) for left in lefts], len(rights), bool(extras)),
        in_specs=[pl.BlockSpec(memory_space=pltpu.SMEM)] + [whole] * (len(flat) + len(rights) + len(extras)),
        out_specs=[whole, whole],
        out_shape=[half, half],
        scratch_shapes=[
            pltpu.VMEM((total, left[0].shape[1]), BF16) for total, left in zip(totals, lefts)
        ],
        compiler_params=pltpu.CompilerParams(vmem_limit_bytes=VMEM_LIMIT),
        cost_estimate=cost(flops, 0, flops // 400),
        name="outer_halves",
    )(jnp.stack(orders), *flat, *rights, *extras)


def bits_of(size):
    return (size - 1).bit_length()


class Places:
    def __init__(self):
        self.seq = lax.axis_size("seq")
        self.dp = lax.axis_size("dp")
        self.nx = self.seq // 2
        self.chips = self.dp * self.nx
        place = lax.axis_index("seq")
        self.core = place & 1
        self.x = place >> 1
        self.d = lax.axis_index("dp")
        self.dp_bits = bits_of(self.dp)
        self.x_bits = bits_of(self.nx)
        self.chip = self.d * self.nx + self.x
        self.names = [("dp", b) for b in reversed(range(self.dp_bits))] + [
            ("x", b) for b in reversed(range(self.x_bits))
        ]

    def swap_core(self, value):
        return lax.ppermute(value, "seq", [(s, s ^ 1) for s in range(self.seq)])

    def shift_x(self, value, by):
        pairs = [(s, (s + 2 * by) % self.seq) for s in range(self.seq)]
        return lax.ppermute(value, "seq", pairs)

    def flip(self, value, names):
        d_mask = sum(1 << bit for axis, bit in names if axis == "dp")
        s_mask = sum(2 << bit for axis, bit in names if axis == "x")
        pairs = [
            (d * self.seq + s, (d ^ d_mask) * self.seq + (s ^ s_mask))
            for d in range(self.dp)
            for s in range(self.seq)
        ]
        return lax.ppermute(value, ("dp", "seq"), pairs)

    def by_core(self, own, other, axis):
        first = jnp.concatenate([own, other], axis=axis)
        second = jnp.concatenate([other, own], axis=axis)
        return jnp.where(self.core == 0, first, second)

    def core_rows(self, value, mine):
        half = value.shape[0] // 2
        which = self.core if mine else 1 - self.core
        return lax.dynamic_slice_in_dim(value, which * half, half, 0)

    def stages(self, kind):
        dp0 = [(("dp", 0),)]
        rest = [(("dp", b),) for b in range(1, self.dp_bits)]
        xs = [(("x", b),) for b in range(self.x_bits)]
        at_once = [tuple(one[0] for one in rest)] if len(rest) == 2 else rest
        return {
            "x_y_z": xs + dp0 + rest,
            "y_x_z": dp0 + xs + rest,
            "y_x_zz": dp0 + xs + at_once,
            "z_y_x_z": rest[:1] + dp0 + xs + rest[1:],
            "z_x_y": rest + xs + dp0,
        }[kind]

    def block_order(self, kind, core_major=False):
        order = [name for stage in self.stages(kind) for name in stage]
        count = len(order)
        masks = []
        for p in range(self.chips):
            mask = 0
            for k, name in enumerate(order):
                if (p >> (count - 1 - k)) & 1:
                    mask |= 1 << (count - 1 - self.names.index(name))
            masks.append(mask)
        base = self.chip
        if core_major:
            base = base ^ (self.core << (count - 1))
        return jnp.array(masks, jnp.int32) ^ base.astype(jnp.int32)


class ChipSum:
    def __init__(self, at, kind, halves):
        self.at = at
        self.todo = list(at.stages(kind))
        kept, sent = halves
        self.rows, self.width = kept.shape
        self.parts = [([kept], 0), ([at.flip(sent, self.todo.pop(0))], 0)]

    def result(self):
        return sum(
            box[0][: self.rows, column : column + self.width].astype(F32) for box, column in self.parts
        )


def fold_kernel(plan, count, *refs):
    in_refs, out_refs = refs[:count], refs[count:]
    for sources, (out, out_column), (rows, width) in plan:
        step = 32 if rows % 32 == 0 else 16

        def body(i, carried, sources=sources, out=out, out_column=out_column, width=width, step=step):
            span = pl.ds(pl.multiple_of(i * step, 16), step)
            total = None
            for at, column in sources:
                part = in_refs[at][span, column : column + width].astype(F32)
                total = part if total is None else total + part
            out_refs[out][span, out_column : out_column + width] = total.astype(BF16)
            return carried

        lax.fori_loop(0, rows // step, body, 0)


def fold_arrays(plan, inputs, shapes):
    if all(rows % 16 == 0 for _, _, (rows, _) in plan):
        return pl.pallas_call(
            functools.partial(fold_kernel, plan, len(inputs)),
            grid=(1,),
            in_specs=[
                pl.BlockSpec((rows, array.shape[1]), lambda i, block=block: (block, 0))
                for array, block, rows in inputs
            ],
            out_specs=[pl.BlockSpec(shape, lambda i: (0, 0)) for shape in shapes],
            out_shape=[shape_of(shape, BF16) for shape in shapes],
            compiler_params=kernel_params(),
            cost_estimate=cost(1, 0, 1),
            name="fold",
        )(*[array for array, _, _ in inputs])
    outs = [jnp.zeros(shape, BF16) for shape in shapes]
    for sources, (out, out_column), (rows, width) in plan:
        total = 0.0
        for at, column in sources:
            array, block, size = inputs[at]
            total = total + array[block * size : (block + 1) * size, column : column + width].astype(F32)
        outs[out] = outs[out].at[:, out_column : out_column + width].set(total.astype(BF16))
    return outs


def fold(at, sums, *ties):
    inputs, plan, shapes, sends = [], [], [], {}

    def place_of(array, block, rows):
        for index, known in enumerate(inputs):
            if known[0] is array and known[1:] == (block, rows):
                return index
        inputs.append((array, block, rows))
        return len(inputs) - 1

    for one in sums:
        stage = one.todo.pop(0) if one.todo else ()
        one.rows >>= len(stage)
        for j in range(1, 1 << len(stage)):
            names = tuple(name for k, name in enumerate(stage) if (j >> (len(stage) - 1 - k)) & 1)
            sources = [(place_of(box[0], j, one.rows), column) for box, column in one.parts]
            sends.setdefault((names, one.rows), []).append((one, sources))
    for (names, rows), pieces in sends.items():
        column = 0
        for one, sources in pieces:
            plan.append((sources, (len(shapes), column), (rows, one.width)))
            column += one.width
        shapes.append((rows, column))
    outs = list(fold_arrays(plan, inputs, shapes))
    if ties:
        outs = together(*outs, *ties)
        outs, ties = list(outs[: len(shapes)]), outs[len(shapes) :]
    for out, ((names, rows), pieces) in zip(outs, sends.items()):
        box = [at.flip(out, names)]
        column = 0
        for one, _ in pieces:
            one.parts.append((box, column))
            column += one.width
    return ties


def settle(sums, *values):
    boxes = []
    for one in sums:
        for box, _ in one.parts[1:]:
            if not any(box is known for known in boxes):
                boxes.append(box)
    out = together(*[box[0] for box in boxes], *values)
    for box, value in zip(boxes, out):
        box[0] = value
    return out[len(boxes) :]


def finish_sum_kernel(plan, count, where_ref, *refs):
    in_refs, refs = refs[:count], refs[count:]
    out_refs, total_refs = refs[: 2 * len(plan)], refs[2 * len(plan) :]
    for at, ranges in enumerate(plan):
        mine_ref, other_ref, total_ref = out_refs[2 * at], out_refs[2 * at + 1], total_refs[at]
        first = 0
        for sources, width in ranges:
            total = None
            for index, column in sources:
                part = in_refs[index][:, column : column + width].astype(F32)
                total = part if total is None else total + part
            total_ref[:, first : first + width] = total
            first += width
        half = mine_ref.shape[0]
        core = where_ref[0]
        mine_ref[...] = total_ref[pl.ds(pl.multiple_of(core * half, half), half), :]
        other_ref[...] = total_ref[pl.ds(pl.multiple_of((1 - core) * half, half), half), :]


def finish_sums(places, where, groups):
    if any(group[0].rows % 32 and group[0].rows % 16 for group in groups):
        outs = []
        for group in groups:
            total = jnp.concatenate([one.result() for one in group], axis=1)
            outs.append((places.core_rows(total, True), places.core_rows(total, False)))
        return outs
    inputs, plan = [], []

    def place_of(array, rows):
        for index, known in enumerate(inputs):
            if known[0] is array and known[1] == rows:
                return index
        inputs.append((array, rows))
        return len(inputs) - 1

    shapes, scratch = [], []
    for group in groups:
        ranges = []
        for one in group:
            ranges.append(
                ([(place_of(box[0], one.rows), column) for box, column in one.parts], one.width)
            )
        plan.append(ranges)
        width = sum(one.width for one in group)
        shapes += [(group[0].rows // 2, width)] * 2
        scratch.append(pltpu.VMEM((group[0].rows, width), F32))
    outs = core_call(
        functools.partial(finish_sum_kernel, plan, len(inputs)),
        1,
        where,
        [array for array, _ in inputs],
        [pl.BlockSpec((rows, array.shape[1]), lambda i, c: (0, 0)) for array, rows in inputs],
        [fixed(shape) for shape in shapes],
        [shape_of(shape, F32) for shape in shapes],
        scratch,
        16,
        "finish_sums",
    )
    return [(outs[2 * k], outs[2 * k + 1]) for k in range(len(groups))]


def finish_kernel(plan, gains, count, where_ref, *refs):
    group_refs, refs = refs[: 2 * count], refs[2 * count :]
    weights = sum(len(pairs) for pairs in gains)
    weight_refs, gain_refs, refs = refs[:weights], refs[weights : weights + len(gains)], refs[weights + len(gains) :]
    out_refs, gain_outs = refs[: len(plan)], refs[len(plan) :]
    first_core = where_ref[0] == 0
    for (group, column, width), out_ref in zip(plan, out_refs):
        mine = group_refs[2 * group][:, column : column + width]
        got = group_refs[2 * group + 1][:, column : column + width]
        out_ref[:, :width] = jnp.where(first_core, mine, got)
        out_ref[:, width:] = jnp.where(first_core, got, mine)
    at = 0
    for pairs, gain_ref, gain_out in zip(gains, gain_refs, gain_outs):
        total = None
        for matrix in pairs:
            product = out_refs[matrix][...] * weight_refs[at][...].astype(F32)
            at += 1
            ones = jnp.ones((8, product.shape[1]), F32)
            part = lax.dot_general(
                ones,
                product,
                (((1,), (1,)), ((), ())),
                precision=lax.Precision.HIGHEST,
                preferred_element_type=F32,
            )
            total = part if total is None else total + part
        gain_out[0] = total[0:1] / gain_ref[0]


def finish(places, where, joined, plan, gains):
    half = joined[0][0].shape[0]
    device = 2 * places.chip + places.core
    if half % 16:
        outs = []
        for group, column, width in plan:
            mine, got = joined[group]
            outs.append(places.by_core(mine[:, column : column + width], got[:, column : column + width], 1))
        shares = []
        for gain, pairs in gains:
            total = 0.0
            for matrix, weight in pairs:
                rows = lax.dynamic_slice_in_dim(weight, device * half, half, 0).astype(F32)
                total = total + jnp.sum(rows * outs[matrix], axis=1)
            shares.append(total / lax.dynamic_slice_in_dim(gain, device * half, half, 0))
        return outs, shares
    flat = [v for pair in joined for v in pair]
    weights = [weight for _, pairs in gains for _, weight in pairs]
    gain_rows = [gain.reshape(-1, 1, half) for gain, _ in gains]
    outs = core_call(
        functools.partial(finish_kernel, plan, [[matrix for matrix, _ in pairs] for _, pairs in gains], len(joined)),
        1,
        where,
        (*flat, *weights, *gain_rows),
        [all_of(v) for v in flat]
        + [pl.BlockSpec((half, w.shape[1]), lambda i, c: (c[1], 0)) for w in weights]
        + [pl.BlockSpec((1, 1, half), lambda i, c: (c[1], 0, 0)) for _ in gains],
        [fixed((joined[group][0].shape[0], 2 * width)) for group, _, width in plan]
        + [fixed((1, 1, half)) for _ in gains],
        [shape_of((joined[group][0].shape[0], 2 * width), F32) for group, _, width in plan]
        + [shape_of((1, 1, half), F32) for _ in gains],
        [],
        16,
        "finish",
    )
    return outs[: len(plan)], [v.reshape(half) for v in outs[len(plan) :]]


def together(*values):
    return lax.optimization_barrier(values)


def per_device(
    target,
    memory,
    mem_lengths,
    mem_mask,
    distance_buckets,
    norm_self,
    w_query,
    w_key,
    w_value,
    w_out,
    pos_table,
    norm_cross,
    wc_query,
    wc_key,
    wc_value,
    wc_out,
    norm_ffn,
    w_gate,
    w_up,
    w_down,
    out_grad,
):
    at = Places()
    core, nx = at.core, at.nx
    local, width = target.shape[1], target.shape[2]
    mem_local = memory.shape[1]
    rows = 2 * local
    full = distance_buckets.shape[0]
    qw = HEADS * HEAD_DIM // 2
    kw = KV * HEAD_DIM // 2
    head_count = HEADS // 2
    place = at.x.astype(jnp.int32).reshape(1)
    core_arg = core.astype(jnp.int32).reshape(1)
    gain_self = norm_self.reshape(1, width)
    gain_cross = norm_cross.reshape(1, width)
    gain_ffn = norm_ffn.reshape(1, width)

    tokens = target.reshape(local, width)
    far_tokens = [at.shift_x(tokens, s) for s in range(1, nx)]
    tokens_got = at.swap_core(tokens)
    memories = memory.reshape(mem_local, width)
    far_memories = [at.shift_x(memories, s) for s in range(1, nx)]
    memories_got = at.swap_core(memories)
    grads = out_grad.reshape(local, width)
    grads_got = at.swap_core(grads)
    grad_chip = at.by_core(grads, grads_got, 0)

    own_table = lax.dynamic_slice_in_dim(pos_table, core * head_count, head_count, 0)
    onehot = (distance_buckets[:, None] == jnp.arange(BUCKETS, dtype=jnp.int32)[None, :]).astype(F32)
    by_distance = lax.dot_general(
        own_table, onehot, (((1,), (1,)), ((), ())), precision=lax.Precision.HIGHEST
    )
    bias_vec = jnp.pad(by_distance, ((0, 0), (BLK, 0))).reshape(head_count // 2, 2, BLK + full)

    normed_t, query, keys, values = project(
        core_arg, tokens, tokens_got, gain_self, (w_query, w_key, w_value), (score_scale, None, None), "project"
    )
    keys, values, normed_ts = [keys], [values], [normed_t]
    for far in far_tokens:
        far_t, far_k, far_v = project(
            core_arg, far, at.swap_core(far), gain_self, (w_key, w_value), (None, None), "project_far"
        )
        normed_ts.append(far_t)
        keys.append(far_k)
        values.append(far_v)

    mem_parts = [memories, memories_got]
    for far in far_memories:
        mem_parts += [far, at.swap_core(far)]
    mem_ids = jnp.arange(mem_mask.shape[1], dtype=jnp.int32)
    valid = (mem_ids < mem_lengths[0]) & ((mem_mask[0] == 1) | (mem_ids == 0))
    mask_add = jnp.where(valid, 0.0, big_negative).astype(F32).reshape(2 * nx, mem_local)
    slot_of = jnp.array([s for s in range(nx) for c in range(2)], jnp.int32)
    core_of = jnp.array([c for s in range(nx) for c in range(2)], jnp.int32)
    mask_rows = (((at.x - slot_of + nx) % nx) * 2 + (core ^ core_of))[:, None] == jnp.arange(2 * nx)[None, :]
    mask_col = jnp.sum(jnp.where(mask_rows[:, :, None], mask_add[None], 0.0), axis=1).reshape(-1, 1)
    mem_t, mem_keys, mem_values = project_memory(core_arg, mem_parts, wc_key, wc_value)

    mixed, mixed_t, lse_self = self_forward(place, query, keys, values, bias_vec)
    mixed_got = at.swap_core(mixed)
    mixed_t_got = at.swap_core(mixed_t)
    after_self, cross_t, cross_query = join(
        core_arg, (tokens, tokens_got), mixed, mixed_got, w_out, gain_cross, wc_query, "join_self"
    )

    crossed, crossed_t, lse_cross = cross_forward(cross_query, mem_keys, mem_values, mask_col)
    crossed_got = at.swap_core(crossed)
    crossed_t_got = at.swap_core(crossed_t)
    after_cross, ffn_t, normed_ffn = join(
        core_arg, after_self, crossed, crossed_got, wc_out, gain_ffn, None, "join_cross"
    )

    hidden_t, grad_gate, grad_up, out_part, e_part = ffn(
        core_arg, normed_ffn, grad_chip, w_gate, w_up, w_down
    )
    e_got = at.swap_core(e_part)
    hidden_t_got = at.swap_core(hidden_t)
    out_got = at.swap_core(at.core_rows(out_part, False))
    ffn_half = w_gate.shape[1] // 2
    gate_halves = outer_halves([at.block_order("x_y_z")], [ffn_t], [grad_gate], [[(0, 0, 0, 0, ffn_half)]])
    e_part, e_got, *gate_halves = together(e_part, e_got, *gate_halves)
    gate_sum = ChipSum(at, "x_y_z", gate_halves)
    grad_after_cross, cross_half, grad_crossed = back(
        core_arg, (grads, grads_got), after_cross, gain_ffn, e_part, e_got, None, wc_out, "back_ffn"
    )
    up_halves = outer_halves(
        [at.block_order("y_x_z"), at.block_order("y_x_z", True)],
        [ffn_t, (crossed_t, crossed_t_got)],
        [grad_up, cross_half],
        [[(0, 0, 0, 0, ffn_half)], [(1, 1, 0, 0, width // 2)]],
    )
    grad_half = lax.dynamic_slice_in_dim(grad_chip, core * (width // 2), width // 2, 1)
    up_halves = together(*up_halves, grad_half)
    grad_half = up_halves[2]
    up_sum = ChipSum(at, "y_x_z", up_halves[:2])
    down_halves = outer_halves(
        [at.block_order("z_y_x_z", True)], [(hidden_t, hidden_t_got)], [grad_half], [[(0, 0, 0, 0, width // 2)]]
    )
    tied = together(*down_halves, grad_crossed, grad_after_cross)
    down_sum = ChipSum(at, "z_y_x_z", tied[:2])
    grad_crossed, grad_after_cross = tied[2:]

    grad_cq, grad_mem = cross_backward(
        cross_query, mem_keys, mem_values, mask_col, grad_crossed, crossed, lse_cross
    )
    grad_cq_got = at.swap_core(grad_cq)
    grad_after_self, self_half, grad_mixed = back(
        core_arg, grad_after_cross, after_self, gain_cross, grad_cq, grad_cq_got, wc_query, w_out, "back_cross"
    )
    turns = kw // PAIR
    k_columns = [2 * PAIR * m for m in range(turns)]
    v_columns = [2 * PAIR * m + PAIR for m in range(turns)]
    wc_in_halves = outer_halves(
        [at.block_order("z_x_y")] * 2,
        [cross_t, mem_t],
        [grad_cq, grad_mem],
        [[(0, 0, 0, 0, qw)]] + [[(1, 1, 0, c, PAIR)] for c in k_columns + v_columns],
    )
    out_halves = outer_halves(
        [at.block_order("x_y_z", True)],
        [(mixed_t, mixed_t_got)],
        [self_half],
        [[(0, 0, 0, 0, width // 2)]],
    )
    span = 2 * mem_local
    mem_got = [at.shift_x(grad_mem[s * span : (s + 1) * span], nx - s) for s in range(1, nx)]

    ffn_sums = [gate_sum, up_sum, down_sum]
    tied = settle(
        ffn_sums,
        grad_mixed,
        grad_after_self,
        out_part,
        out_got,
        *wc_in_halves,
        *out_halves,
        grad_mem,
        *mem_got,
    )
    grad_mixed, grad_after_self, out_part, out_got = tied[:4]
    halves = tied[4:8]
    grad_mem, mem_got = tied[8], tied[9:]

    grad_mixed, *halves = fold(at, ffn_sums, grad_mixed, *halves)
    out_sum = ChipSum(at, "x_y_z", halves[2:])
    wc_in_sum = ChipSum(at, "z_x_y", halves[:2])
    early = [*ffn_sums, out_sum, wc_in_sum]
    grad_q, grad_pairs, diagonals = self_backward(
        place, query, keys, values, bias_vec, grad_mixed, mixed, lse_self
    )
    tied = settle(early, grad_q, diagonals, out_part, out_got, grad_mem, *grad_pairs, *mem_got)
    grad_q, diagonals, out_part, out_got, grad_mem = tied[:5]
    grad_pairs, mem_got = tied[5 : 5 + nx], tied[5 + nx :]
    output = (
        at.core_rows(after_cross, True)
        + at.core_rows(out_part, True).astype(F32)
        + out_got.astype(F32)
    ).astype(BF16)
    pair_chip = grad_pairs[0]
    for s in range(1, nx):
        pair_chip = pair_chip + at.shift_x(grad_pairs[s], nx - s)

    own_bias = lax.dot_general(
        diagonals.reshape(head_count, -1)[:, BLK:],
        onehot,
        (((1,), (0,)), ((), ())),
        precision=lax.Precision.HIGHEST,
        preferred_element_type=F32,
    )
    table = lax.dynamic_update_slice_in_dim(
        jnp.zeros((HEADS, BUCKETS), F32), own_bias, core * head_count, 0
    ).reshape(2 * at.chips, -1)
    bias_share = table.shape[1]
    in_halves = outer_halves(
        [at.block_order("y_x_zz")] * nx,
        normed_ts,
        [grad_q, *grad_pairs],
        [[(0, 0, 0, 0, qw)]] + [[(s, 1 + s, 0, c, PAIR) for s in range(nx)] for c in k_columns + v_columns],
        jnp.pad(table, ((0, 0), (0, 128 - bias_share))),
    )
    in_halves = list(in_halves)
    tied = together(*in_halves, *[one.parts[0][0][0] for one in early])
    in_halves = tied[:2]
    for one, value in zip(early, tied[2:]):
        one.parts[0][0][0] = value
    in_sum = ChipSum(at, "y_x_zz", in_halves)
    fold(at, early)
    every = [*early, in_sum]

    grad_mem_chip = grad_mem[:span]
    for got in mem_got:
        grad_mem_chip = grad_mem_chip + got
    mem_mine = grad_mem_chip[:mem_local]
    mem_other = at.swap_core(grad_mem_chip[mem_local:])

    def unpaired(columns):
        mine = [mem_mine[:, c : c + PAIR] for c in columns]
        other = [mem_other[:, c : c + PAIR] for c in columns]
        return at.by_core(jnp.concatenate(mine, axis=1), jnp.concatenate(other, axis=1), 1)

    grad_memory = dot_nt(unpaired(k_columns), wc_key) + dot_nt(unpaired(v_columns), wc_value)
    sent = jnp.concatenate([at.core_rows(grad_q, False), at.core_rows(pair_chip, False)], axis=1)
    (grad_target,) = last(
        core_arg,
        grad_after_self,
        tokens,
        gain_self,
        grad_q,
        pair_chip,
        at.swap_core(sent),
        w_query,
        w_key,
        w_value,
    )

    grad_target, grad_memory = settle(every, grad_target, grad_memory)
    where = jnp.stack([core, 2 * at.chip + core]).astype(jnp.int32)
    front_parts = None
    while any(one.todo for one in every):
        fold(at, every)
        if front_parts is None and not gate_sum.todo and not up_sum.todo:
            front_parts = ()
        elif front_parts == ():
            front_parts = finish_sums(at, where, [[gate_sum, up_sum]])
    if not front_parts:
        front_parts = finish_sums(at, where, [[gate_sum, up_sum]])

    (front,) = front_parts
    (gate, up, cross_out), (gain_ffn_grad,) = finish(
        at,
        where,
        [(front[0], at.swap_core(front[1]))],
        [(0, 0, ffn_half), (0, ffn_half, ffn_half), (0, 2 * ffn_half, width // 2)],
        [(norm_ffn, [(0, w_gate), (1, w_up)])],
    )
    rear, down_rows = finish_sums(at, where, [[wc_in_sum, out_sum, in_sum], [down_sum]])
    rear_join = (rear[0], at.swap_core(rear[1]))
    down_join = (down_rows[0], at.swap_core(down_rows[1]))
    out_at = qw + 2 * kw
    in_at = out_at + width // 2
    (cross_in, cross_key, cross_value, self_out, self_in, self_key, self_value, down), gain_grads = finish(
        at,
        where,
        [rear_join, down_join],
        [
            (0, 0, qw),
            (0, qw, kw),
            (0, qw + kw, kw),
            (0, out_at, width // 2),
            (0, in_at, qw),
            (0, in_at + qw, kw),
            (0, in_at + qw + kw, kw),
            (1, 0, width // 2),
        ],
        [
            (norm_cross, [(0, wc_query)]),
            (norm_self, [(4, w_query), (5, w_key), (6, w_value)]),
        ],
    )
    gain_cross_grad, gain_self_grad = gain_grads
    bias_at = in_at + qw + 2 * kw
    bias_out = (rear_join[0] + rear_join[1])[0, bias_at : bias_at + bias_share]
    return (
        output.reshape(target.shape),
        grad_target.reshape(target.shape),
        grad_memory.reshape(memory.shape),
        gain_self_grad,
        self_in,
        self_key,
        self_value,
        self_out,
        bias_out,
        gain_cross_grad,
        cross_in,
        cross_key,
        cross_value,
        cross_out,
        gain_ffn_grad,
        gate,
        up,
        down,
    )


def solution(mesh):
    tokens = P("dp", "seq", None)
    row_share = P(("dp", "seq"))
    matrix_share = P(("dp", "seq"), None)
    return jax.shard_map(
        per_device,
        mesh=mesh,
        in_specs=(tokens, tokens, P("dp"), P("dp", None)) + (P(),) * 16 + (tokens,),
        out_specs=(tokens, tokens, tokens, row_share)
        + (matrix_share,) * 4
        + (row_share, row_share)
        + (matrix_share,) * 4
        + (row_share,)
        + (matrix_share,) * 3,
        check_vma=False,
    )
```

```python
import functools

import jax
import jax.numpy as jnp
from jax import lax
from jax.experimental import pallas as pl
from jax.experimental.pallas import tpu as pltpu
from jax.sharding import PartitionSpec as P

HEADS = 16
KV = 8
HEAD_DIM = 64
BUCKETS = 32
BLK = 256
PAIR = 2 * HEAD_DIM

norm_eps = 1e-06
big_negative = -1000000000.0
score_scale = HEAD_DIM ** (-0.5)
F32 = jnp.float32
BF16 = jnp.bfloat16
VMEM_LIMIT = 61 * 1024 * 1024


def dot_nn(a, b):
    return lax.dot_general(a, b, (((1,), (0,)), ((), ())), preferred_element_type=F32)


def dot_nt(a, b):
    return lax.dot_general(a, b, (((1,), (1,)), ((), ())), preferred_element_type=F32)


def dot_tn(a, b):
    return lax.dot_general(a, b, (((0,), (0,)), ((), ())), preferred_element_type=F32)


def lane_pick(source, dest):
    a = lax.broadcasted_iota(jnp.int32, (PAIR, PAIR), 0)
    b = lax.broadcasted_iota(jnp.int32, (PAIR, PAIR), 1)
    keep = (a - source == b - dest) & (b >= dest) & (b < dest + HEAD_DIM)
    return keep.astype(F32).astype(BF16)


def lane_pick_t(source, dest):
    a = lax.broadcasted_iota(jnp.int32, (PAIR, PAIR), 1)
    b = lax.broadcasted_iota(jnp.int32, (PAIR, PAIR), 0)
    keep = (a - source == b - dest) & (b >= dest) & (b < dest + HEAD_DIM)
    return keep.astype(F32).astype(BF16)


def bias_tile(bias_vec_ref, h, delta):
    piece = bias_vec_ref[0, h : h + 1, delta * BLK : delta * BLK + 2 * BLK]
    wide = jnp.broadcast_to(piece, (BLK, 2 * BLK))
    return pltpu.roll(wide, 0, 1, stride=1, stride_axis=0)[:, BLK:]


def tile_plan(row_blocks, slots):
    plan = [(delta, 0) for delta in range(row_blocks)]
    for slot in range(1, slots):
        plan += [(slot * row_blocks + c, slot) for c in range(1 - row_blocks, row_blocks)]
    return plan


def tile_at(row_blocks, rb, kb):
    slot, jb = kb // row_blocks, kb % row_blocks
    if slot == 0:
        return rb - jb, rb - jb
    first = row_blocks + (slot - 1) * (2 * row_blocks - 1)
    return first + rb - jb + row_blocks - 1, slot * row_blocks + rb - jb


def key_blocks(row_blocks, slots, rb):
    return list(range(rb + 1)) + list(range(row_blocks, row_blocks * slots))


def fill_bias(place, bias_vec_ref, tile_ref, row_blocks, slots):
    for at, (delta, slot) in enumerate(tile_plan(row_blocks, slots)):
        for h in range(2):
            tile = bias_tile(bias_vec_ref, h, delta)
            if slot:
                tile = tile + jnp.where(place >= slot, 0.0, big_negative)
            elif delta == 0:
                tile = jnp.where(causal_tile(), tile, big_negative)
            tile_ref[h, at] = tile


def causal_tile():
    key_pos = lax.broadcasted_iota(jnp.int32, (BLK, BLK), 0)
    row_pos = lax.broadcasted_iota(jnp.int32, (BLK, BLK), 1)
    return key_pos <= row_pos


def online_step(carry, scores, value_t):
    highest, total, mixed = carry
    new_high = jnp.maximum(highest, jnp.max(scores, axis=0, keepdims=True))
    fade = jnp.exp(highest - new_high)
    weights = jnp.exp(scores - new_high)
    total = total * fade + jnp.sum(weights, axis=0, keepdims=True)
    mixed = mixed * fade + dot_nn(value_t, weights.astype(BF16))
    return (new_high, total, mixed)


def first_step(scores, value_t):
    highest = jnp.max(scores, axis=0, keepdims=True)
    weights = jnp.exp(scores - highest)
    total = jnp.sum(weights, axis=0, keepdims=True)
    return (highest, total, dot_nn(value_t, weights.astype(BF16)))


def key_spans(row_blocks, slots, rb):
    own, end = (rb + 1) * BLK, row_blocks * slots * BLK
    first_far = row_blocks * BLK
    if slots == 1:
        return [(0, own)]
    if own == first_far:
        return [(0, end)]
    return [(0, own), (first_far, end)]


def self_forward_kernel(slots, place_ref, q_ref, b_ref, *refs):
    k_refs, v_refs = refs[:slots], refs[slots : 2 * slots]
    o_ref, ot_ref, lse_ref, tile_ref, kz_ref, vt_ref, s_ref, p_ref = refs[2 * slots :]
    parity = lax.rem(pl.program_id(0), 2)
    rows_all = q_ref.shape[0]
    row_blocks = rows_all // BLK
    fill_bias(place_ref[0], b_ref, tile_ref, row_blocks, slots)
    for h in range(2):
        for slot in range(slots):
            span = slice(slot * rows_all, (slot + 1) * rows_all)
            pick_k = lane_pick(parity * HEAD_DIM, h * HEAD_DIM)
            pick_v = lane_pick_t(parity * HEAD_DIM, h * HEAD_DIM)
            kz_ref[h, span, :] = dot_nn(k_refs[slot][...], pick_k).astype(BF16)
            vt_ref[h, :, span] = dot_nt(pick_v, v_refs[slot][...]).astype(BF16)
    for rb in range(row_blocks):
        rows = slice(rb * BLK, (rb + 1) * BLK)
        queries = q_ref[rows, :]
        spans = key_spans(row_blocks, slots, rb)
        highest = [None, None]
        for h in range(2):
            for first, end in spans:
                products = dot_nt(kz_ref[h, first:end, :], queries)
                for kb in range(first // BLK, end // BLK):
                    at, _ = tile_at(row_blocks, rb, kb)
                    scores = products[kb * BLK - first : (kb + 1) * BLK - first, :] + tile_ref[h, at]
                    s_ref[h, kb * BLK : (kb + 1) * BLK, :] = scores
                    top = jnp.max(scores, axis=0, keepdims=True)
                    highest[h] = top if highest[h] is None else jnp.maximum(highest[h], top)
        mixed_t = None
        for h in range(2):
            total = None
            part = None
            for first, end in spans:
                weights = jnp.exp(s_ref[h, first:end, :] - highest[h])
                one = jnp.sum(weights, axis=0, keepdims=True)
                total = one if total is None else total + one
                p_ref[h, first:end, :] = weights.astype(BF16)
            for first, end in spans:
                one = dot_nn(vt_ref[h, :, first:end], p_ref[h, first:end, :])
                part = one if part is None else part + one
            part = part / total
            mixed_t = part if mixed_t is None else mixed_t + part
            lse_ref[0, h : h + 1, rows] = highest[h] + jnp.log(total)
        ot_ref[:, rows] = mixed_t.astype(BF16)
        o_ref[rows, :] = mixed_t.T.astype(BF16)


def diagonal_sums(wide):
    rows, lanes = wide.shape
    while rows > 8:
        rows //= 2
        wide = wide[:rows] + pltpu.roll(wide[rows:], lanes - rows, 1)
    row = lax.broadcasted_iota(jnp.int32, (8, lanes), 0)
    total = jnp.where(row == 0, wide, 0.0)
    for b in range(1, 8):
        total = total + jnp.where(row == b, pltpu.roll(wide, lanes - b, 1), 0.0)
    return jnp.sum(total, axis=0, keepdims=True)


def row_products(grad_block, mixed_block):
    turned = (grad_block.astype(F32) * mixed_block.astype(F32)).T
    return [
        jnp.sum(turned[h * HEAD_DIM : (h + 1) * HEAD_DIM], axis=0, keepdims=True) for h in range(2)
    ]


def self_backward_kernel(slots, place_ref, q_ref, b_ref, do_ref, o_ref, lse_ref, *refs):
    k_refs, v_refs = refs[:slots], refs[slots : 2 * slots]
    dq_ref, diag_ref = refs[2 * slots : 2 * slots + 2]
    pair_refs, refs = refs[2 * slots + 2 : 3 * slots + 2], refs[3 * slots + 2 :]
    tile_ref, sum_ref, kz_ref, kt_ref, vz_ref, qp_ref, dop_ref, dk_acc, dv_acc, p_ref, ds_ref = refs
    parity = lax.rem(pl.program_id(0), 2)
    rows_all = q_ref.shape[0]
    row_blocks = rows_all // BLK
    fill_bias(place_ref[0], b_ref, tile_ref, row_blocks, slots)
    for h in range(2):
        in_pick = lane_pick(parity * HEAD_DIM, h * HEAD_DIM)
        out_pick = lane_pick(h * HEAD_DIM, parity * HEAD_DIM)
        pick_t = lane_pick_t(parity * HEAD_DIM, h * HEAD_DIM)
        for slot in range(slots):
            span = slice(slot * rows_all, (slot + 1) * rows_all)
            kz_ref[h, span, :] = dot_nn(k_refs[slot][...], in_pick).astype(BF16)
            kt_ref[h, :, span] = dot_nt(pick_t, k_refs[slot][...]).astype(BF16)
            vz_ref[h, span, :] = dot_nn(v_refs[slot][...], in_pick).astype(BF16)
        side = slice(h * rows_all, (h + 1) * rows_all)
        qp_ref[side, :] = dot_nn(q_ref[...], out_pick).astype(BF16)
        dop_ref[side, :] = dot_nn(do_ref[...], out_pick).astype(BF16)
    seen = set()
    for rb in range(row_blocks):
        rows = slice(rb * BLK, (rb + 1) * BLK)
        spans = key_spans(row_blocks, slots, rb)
        delta_rows = row_products(do_ref[rows, :], o_ref[rows, :])
        for kb in range(rb + 1, row_blocks):
            for h in range(2):
                side = slice(h * rows_all + rb * BLK, h * rows_all + (rb + 1) * BLK)
                keys = slice(kb * BLK, (kb + 1) * BLK)
                p_ref[keys, side] = jnp.zeros((BLK, BLK), BF16)
                ds_ref[keys, side] = jnp.zeros((BLK, BLK), BF16)
        for h in range(2):
            side = slice(h * rows_all + rb * BLK, h * rows_all + (rb + 1) * BLK)
            delta_row = delta_rows[h]
            lse = lse_ref[0, h : h + 1, rows]
            for first, end in spans:
                products = dot_nt(kz_ref[h, first:end, :], q_ref[rows, :])
                grad_products = dot_nt(vz_ref[h, first:end, :], do_ref[rows, :])
                for kb in range(first // BLK, end // BLK):
                    keys = slice(kb * BLK, (kb + 1) * BLK)
                    inner = slice(kb * BLK - first, (kb + 1) * BLK - first)
                    at, delta = tile_at(row_blocks, rb, kb)
                    probs = jnp.exp(products[inner, :] + tile_ref[h, at] - lse)
                    grad_scores = probs * (grad_products[inner, :] - delta_row)
                    p_ref[keys, side] = probs.astype(BF16)
                    ds_ref[keys, side] = grad_scores.astype(BF16)
                    if (h, delta) in seen:
                        sum_ref[h, delta] += grad_scores
                    else:
                        sum_ref[h, delta] = grad_scores
                        seen.add((h, delta))
    grad_v = dot_nn(p_ref[...], dop_ref[...])
    grad_k = dot_nn(ds_ref[...], qp_ref[...])

    @pl.when(parity == 0)
    def first():
        dv_acc[...] = grad_v
        dk_acc[...] = grad_k

    @pl.when(parity == 1)
    def second():
        dv_acc[...] += grad_v
        dk_acc[...] += grad_k

    grad_q = None
    for h in range(2):
        part = dot_nn(kt_ref[h], ds_ref[:, h * rows_all : (h + 1) * rows_all])
        grad_q = part if grad_q is None else grad_q + part
    dq_ref[...] = (grad_q.T * score_scale).astype(BF16)

    diag_ref[...] = jnp.zeros_like(diag_ref)
    for h in range(2):
        for delta in range(row_blocks * slots):
            wide = jnp.concatenate([jnp.zeros((BLK, BLK), F32), sum_ref[h, delta]], axis=1)
            diag_ref[0, h : h + 1, delta * BLK : delta * BLK + 2 * BLK] += diagonal_sums(wide)

    @pl.when(parity == 1)
    def store():
        for slot, pair_ref in enumerate(pair_refs):
            span = slice(slot * rows_all, (slot + 1) * rows_all)
            pair_ref[:, :PAIR] = dk_acc[span, :].astype(BF16)
            pair_ref[:, PAIR:] = dv_acc[span, :].astype(BF16)


def cross_forward_kernel(q_ref, k_ref, v_ref, m_ref, o_ref, ot_ref, lse_ref, kz_ref, vt_ref, s_ref, p_ref):
    parity = lax.rem(pl.program_id(0), 2)
    for h in range(2):
        kz_ref[h] = dot_nn(k_ref[...], lane_pick(parity * HEAD_DIM, h * HEAD_DIM)).astype(BF16)
        vt_ref[h] = dot_nt(lane_pick_t(parity * HEAD_DIM, h * HEAD_DIM), v_ref[...]).astype(BF16)
    for rb in range(q_ref.shape[0] // BLK):
        rows = slice(rb * BLK, (rb + 1) * BLK)
        queries = q_ref[rows, :]
        highest = []
        for h in range(2):
            scores = dot_nt(kz_ref[h], queries) + m_ref[...]
            s_ref[h] = scores
            highest.append(jnp.max(scores, axis=0, keepdims=True))
        mixed_t = None
        for h in range(2):
            weights = jnp.exp(s_ref[h] - highest[h])
            total = jnp.sum(weights, axis=0, keepdims=True)
            p_ref[h] = weights.astype(BF16)
            part = dot_nn(vt_ref[h], p_ref[h]) / total
            mixed_t = part if mixed_t is None else mixed_t + part
            lse_ref[0, h : h + 1, rows] = highest[h] + jnp.log(total)
        ot_ref[:, rows] = mixed_t.astype(BF16)
        o_ref[rows, :] = mixed_t.T.astype(BF16)


def cross_backward_kernel(
    slots,
    q_ref,
    k_ref,
    v_ref,
    m_ref,
    do_ref,
    o_ref,
    lse_ref,
    dq_ref,
    *refs,
):
    pair_refs, refs = refs[:slots], refs[slots:]
    cross_backward_body(slots, pair_refs, q_ref, k_ref, v_ref, m_ref, do_ref, o_ref, lse_ref, dq_ref, *refs)


def cross_backward_body(
    slots,
    pair_refs,
    q_ref,
    k_ref,
    v_ref,
    m_ref,
    do_ref,
    o_ref,
    lse_ref,
    dq_ref,
    kz_ref,
    kt_ref,
    vz_ref,
    qp_ref,
    dop_ref,
    dk_acc,
    dv_acc,
    p_ref,
    ds_ref,
):
    parity = lax.rem(pl.program_id(0), 2)
    rows_all = q_ref.shape[0]
    for h in range(2):
        in_pick = lane_pick(parity * HEAD_DIM, h * HEAD_DIM)
        out_pick = lane_pick(h * HEAD_DIM, parity * HEAD_DIM)
        kz_ref[h] = dot_nn(k_ref[...], in_pick).astype(BF16)
        kt_ref[h] = dot_nt(lane_pick_t(parity * HEAD_DIM, h * HEAD_DIM), k_ref[...]).astype(BF16)
        vz_ref[h] = dot_nn(v_ref[...], in_pick).astype(BF16)
        side = slice(h * rows_all, (h + 1) * rows_all)
        qp_ref[side, :] = dot_nn(q_ref[...], out_pick).astype(BF16)
        dop_ref[side, :] = dot_nn(do_ref[...], out_pick).astype(BF16)
    for rb in range(rows_all // BLK):
        rows = slice(rb * BLK, (rb + 1) * BLK)
        delta_rows = row_products(do_ref[rows, :], o_ref[rows, :])
        for h in range(2):
            side = slice(h * rows_all + rb * BLK, h * rows_all + (rb + 1) * BLK)
            delta_row = delta_rows[h]
            lse = lse_ref[0, h : h + 1, rows]
            probs = jnp.exp(dot_nt(kz_ref[h], q_ref[rows, :]) + m_ref[...] - lse)
            grad_products = dot_nt(vz_ref[h], do_ref[rows, :])
            p_ref[:, side] = probs.astype(BF16)
            ds_ref[:, side] = (probs * (grad_products - delta_row)).astype(BF16)
    grad_v = dot_nn(p_ref[...], dop_ref[...])
    grad_k = dot_nn(ds_ref[...], qp_ref[...])

    @pl.when(parity == 0)
    def first():
        dv_acc[...] = grad_v
        dk_acc[...] = grad_k

    @pl.when(parity == 1)
    def second():
        all_k = (dk_acc[...] + grad_k).astype(BF16)
        all_v = (dv_acc[...] + grad_v).astype(BF16)
        size = all_k.shape[0] // slots
        for slot, pair_ref in enumerate(pair_refs):
            pair_ref[:, :PAIR] = all_k[slot * size : (slot + 1) * size]
            pair_ref[:, PAIR:] = all_v[slot * size : (slot + 1) * size]

    grad_q = None
    for h in range(2):
        part = dot_nn(kt_ref[h], ds_ref[:, h * rows_all : (h + 1) * rows_all])
        grad_q = part if grad_q is None else grad_q + part
    dq_ref[...] = (grad_q.T * score_scale).astype(BF16)


def shape_of(shape, dtype):
    return jax.ShapeDtypeStruct(shape, dtype)


def tile_pair(rows):
    return pl.BlockSpec((rows, PAIR), lambda g: (0, g))


def tile_pair_t(rows):
    return pl.BlockSpec((PAIR, rows), lambda g: (g, 0))


def tile_group(rows):
    return pl.BlockSpec((rows, PAIR), lambda g: (0, g // 2))


def tile_both(rows):
    return pl.BlockSpec((rows, 2 * PAIR), lambda g: (0, g // 2))


def tile_rows(width):
    return pl.BlockSpec((1, 2, width), lambda g: (g, 0, 0))


def kernel_params():
    return pltpu.CompilerParams(
        dimension_semantics=("arbitrary",), vmem_limit_bytes=VMEM_LIMIT
    )


def cost(flops, transcendentals, nbytes):
    return pl.CostEstimate(
        flops=int(flops) // 16, transcendentals=0, bytes_accessed=int(nbytes) // 16
    )


def self_forward(place, q, ks, vs, bias_vec):
    rows, width = q.shape
    slots = len(ks)
    keys = rows * slots
    pairs = width // PAIR
    tiles = len(tile_plan(rows // BLK, slots))
    return pl.pallas_call(
        functools.partial(self_forward_kernel, slots),
        grid=(pairs,),
        in_specs=[pl.BlockSpec(memory_space=pltpu.SMEM), tile_pair(rows), tile_rows(bias_vec.shape[2])]
        + [tile_group(rows)] * (2 * slots),
        out_specs=[tile_pair(rows), tile_pair_t(rows), tile_rows(rows)],
        out_shape=[
            shape_of((rows, width), BF16),
            shape_of((width, rows), BF16),
            shape_of((pairs, 2, rows), F32),
        ],
        scratch_shapes=[
            pltpu.VMEM((2, tiles, BLK, BLK), F32),
            pltpu.VMEM((2, keys, PAIR), BF16),
            pltpu.VMEM((2, PAIR, keys), BF16),
            pltpu.VMEM((2, keys, BLK), F32),
            pltpu.VMEM((2, keys, BLK), BF16),
        ],
        compiler_params=kernel_params(),
        cost_estimate=cost(4 * 2 * rows * keys * width * 2, pairs * 2 * rows * keys, 8 * rows * width),
        name="self_forward",
    )(place, q, bias_vec, *ks, *vs)


def self_backward(place, q, ks, vs, bias_vec, grads, mixed, lse):
    rows, width = q.shape
    kv_width = ks[0].shape[1]
    slots = len(ks)
    keys = rows * slots
    pairs = width // PAIR
    tiles = len(tile_plan(rows // BLK, slots))
    grad_q, diagonals, *pairs_out = pl.pallas_call(
        functools.partial(self_backward_kernel, slots),
        grid=(pairs,),
        in_specs=[
            pl.BlockSpec(memory_space=pltpu.SMEM),
            tile_pair(rows),
            tile_rows(bias_vec.shape[2]),
            tile_pair(rows),
            tile_pair(rows),
            tile_rows(rows),
        ]
        + [tile_group(rows)] * (2 * slots),
        out_specs=[tile_pair(rows), tile_rows(bias_vec.shape[2])] + [tile_both(rows)] * slots,
        out_shape=[shape_of((rows, width), BF16), shape_of(bias_vec.shape, F32)]
        + [shape_of((rows, 2 * kv_width), BF16)] * slots,
        scratch_shapes=[
            pltpu.VMEM((2, tiles, BLK, BLK), F32),
            pltpu.VMEM((2, keys // BLK, BLK, BLK), F32),
            pltpu.VMEM((2, keys, PAIR), BF16),
            pltpu.VMEM((2, PAIR, keys), BF16),
            pltpu.VMEM((2, keys, PAIR), BF16),
            pltpu.VMEM((2 * rows, PAIR), BF16),
            pltpu.VMEM((2 * rows, PAIR), BF16),
            pltpu.VMEM((keys, PAIR), F32),
            pltpu.VMEM((keys, PAIR), F32),
            pltpu.VMEM((keys, 2 * rows), BF16),
            pltpu.VMEM((keys, 2 * rows), BF16),
        ],
        compiler_params=kernel_params(),
        cost_estimate=cost(10 * 2 * rows * keys * width * 2, pairs * 2 * rows * keys, 12 * rows * width),
        name="self_backward",
    )(place, q, bias_vec, grads, mixed, lse, *ks, *vs)
    return grad_q, pairs_out, diagonals


def cross_forward(q, k, v, mask_col):
    rows, width = q.shape
    keys = k.shape[0]
    pairs = width // PAIR
    return pl.pallas_call(
        cross_forward_kernel,
        grid=(pairs,),
        in_specs=[
            tile_pair(rows),
            tile_group(keys),
            tile_group(keys),
            pl.BlockSpec((keys, 1), lambda g: (0, 0)),
        ],
        out_specs=[tile_pair(rows), tile_pair_t(rows), tile_rows(rows)],
        out_shape=[
            shape_of((rows, width), BF16),
            shape_of((width, rows), BF16),
            shape_of((pairs, 2, rows), F32),
        ],
        scratch_shapes=[
            pltpu.VMEM((2, keys, PAIR), BF16),
            pltpu.VMEM((2, PAIR, keys), BF16),
            pltpu.VMEM((2, keys, BLK), F32),
            pltpu.VMEM((2, keys, BLK), BF16),
        ],
        compiler_params=kernel_params(),
        cost_estimate=cost(4 * 2 * rows * keys * width * 2, pairs * 2 * rows * keys, 8 * rows * width),
        name="cross_forward",
    )(q, k, v, mask_col)


def cross_backward(q, k, v, mask_col, grads, mixed, lse, slots):
    rows, width = q.shape
    keys, kv_width = k.shape
    pairs = width // PAIR
    grad_q, *pairs_out = pl.pallas_call(
        functools.partial(cross_backward_kernel, slots),
        grid=(pairs,),
        in_specs=[
            tile_pair(rows),
            tile_group(keys),
            tile_group(keys),
            pl.BlockSpec((keys, 1), lambda g: (0, 0)),
            tile_pair(rows),
            tile_pair(rows),
            tile_rows(rows),
        ],
        out_specs=[tile_pair(rows)] + [tile_both(keys // slots)] * slots,
        out_shape=[shape_of((rows, width), BF16)] + [shape_of((keys // slots, 2 * kv_width), BF16)] * slots,
        scratch_shapes=[
            pltpu.VMEM((2, keys, PAIR), BF16),
            pltpu.VMEM((2, PAIR, keys), BF16),
            pltpu.VMEM((2, keys, PAIR), BF16),
            pltpu.VMEM((2 * rows, PAIR), BF16),
            pltpu.VMEM((2 * rows, PAIR), BF16),
            pltpu.VMEM((keys, PAIR), F32),
            pltpu.VMEM((keys, PAIR), F32),
            pltpu.VMEM((keys, 2 * rows), BF16),
            pltpu.VMEM((keys, 2 * rows), BF16),
        ],
        compiler_params=kernel_params(),
        cost_estimate=cost(10 * 2 * rows * keys * width * 2, pairs * 2 * rows * keys, 12 * rows * width),
        name="cross_backward",
    )(q, k, v, mask_col, grads, mixed, lse)
    return grad_q, pairs_out


FBLK = 256


def ffn_kernel(
    chips,
    where_ref,
    x_ref,
    xt_ref,
    og_ref,
    wg_any,
    wu_any,
    wd_any,
    ht_any,
    e_any,
    out_mine_any,
    out_other_any,
    gate_keep_any,
    gate_send_any,
    up_keep_any,
    up_send_any,
    wg_ref,
    wu_ref,
    wd_ref,
    xs_ref,
    hb_ref,
    gg_ref,
    gu_ref,
    ht_ref,
    e_ref,
    out_ref,
    product_ref,
    in_sems,
    out_sems,
):
    hidden_width = gg_ref.shape[1]
    base = where_ref[0] * hidden_width
    spans = [(first, min(FBLK, hidden_width - first)) for first in range(0, hidden_width, FBLK)]
    loads = []
    for k, (first, size) in enumerate(spans):
        away = pl.ds(pl.multiple_of(base + first, 128), size)
        near = slice(first, first + size)
        loads.append(
            [
                pltpu.make_async_copy(wg_any.at[:, away], wg_ref.at[:, near], in_sems.at[0, k]),
                pltpu.make_async_copy(wu_any.at[:, away], wu_ref.at[:, near], in_sems.at[1, k]),
                pltpu.make_async_copy(wd_any.at[away, :], wd_ref.at[near, :], in_sems.at[2, k]),
            ]
        )
    for group in loads:
        for load in group:
            load.start()
    block = xt_ref.shape[0] // chips
    for order in range(2):
        for p in range(chips):
            first = pl.multiple_of(where_ref[1 + order * chips + p] * block, block)
            xs_ref[order, p * block : (p + 1) * block, :] = xt_ref[pl.ds(first, block), :]
    factor = (2.0 / jnp.pi) ** 0.5

    def combine(span, gate, up, grad_hidden):
        square = gate * gate
        bend = jnp.tanh(gate * (factor + (factor * 0.044715) * square))
        half = 0.5 + 0.5 * bend
        gelu = gate * half
        slope = half + gelu * (1.0 - bend) * (factor + (factor * 3 * 0.044715) * square)
        hidden = gelu * up
        hb_ref[:, span] = hidden.astype(BF16)
        ht_ref[span, :] = hidden.T.astype(BF16)
        gg_ref[:, span] = (grad_hidden * up * slope).astype(BF16)
        gu_ref[:, span] = (grad_hidden * gelu).astype(BF16)

    waiting = None
    for (first, size), group in zip(spans, loads):
        span = slice(first, first + size)
        for load in group:
            load.wait()
        gate = dot_nn(x_ref[...], wg_ref[:, span])
        up = dot_nn(x_ref[...], wu_ref[:, span])
        grad_hidden = dot_nt(og_ref[...], wd_ref[span, :])
        if waiting is not None:
            combine(*waiting)
        waiting = (span, gate, up, grad_hidden)
    combine(*waiting)
    stores = [pltpu.make_async_copy(ht_ref, ht_any, out_sems.at[0])]
    stores[-1].start()
    e_ref[...] = (dot_nt(gg_ref[...], wg_ref[...]) + dot_nt(gu_ref[...], wu_ref[...])).astype(BF16)
    stores.append(pltpu.make_async_copy(e_ref, e_any, out_sems.at[1]))
    stores[-1].start()
    middle = xt_ref.shape[0] // 2
    outs = [
        (0, gg_ref, middle, gate_send_any),
        (1, gu_ref, middle, up_send_any),
        (0, gg_ref, 0, gate_keep_any),
        (1, gu_ref, 0, up_keep_any),
    ]
    for k, (order, right_ref, first, any_ref) in enumerate(outs):
        product_ref[k] = dot_nn(xs_ref[order, first : first + middle, :], right_ref[...]).astype(BF16)
        stores.append(pltpu.make_async_copy(product_ref.at[k], any_ref, out_sems.at[2 + k]))
        stores[-1].start()
    out_ref[...] = dot_nn(hb_ref[...], wd_ref[...]).astype(BF16)
    half = out_ref.shape[0] // 2
    for k, (which, any_ref) in enumerate(((where_ref[0], out_mine_any), (1 - where_ref[0], out_other_any))):
        source = out_ref.at[pl.ds(pl.multiple_of(which * half, half), half), :]
        stores.append(pltpu.make_async_copy(source, any_ref, out_sems.at[6 + k]))
        stores[-1].start()
    for store in stores:
        store.wait()


def ffn(where, normed, normed_t, out_grad, w_gate, w_up, w_down, chips):
    rows, width = normed.shape
    hidden = w_gate.shape[1] // 2
    chunks = -(-hidden // FBLK)
    whole = pl.BlockSpec(memory_space=pltpu.VMEM)
    anywhere = pl.BlockSpec(memory_space=pl.ANY)
    half = (width // 2, hidden)
    return pl.pallas_call(
        functools.partial(ffn_kernel, chips),
        in_specs=[pl.BlockSpec(memory_space=pltpu.SMEM), whole, whole, whole] + [anywhere] * 3,
        out_specs=[anywhere] * 8,
        out_shape=[
            shape_of((hidden, rows), BF16),
            shape_of((rows, width), BF16),
            shape_of((rows // 2, width), BF16),
            shape_of((rows // 2, width), BF16),
        ]
        + [shape_of(half, BF16)] * 4,
        scratch_shapes=[
            pltpu.VMEM((width, hidden), BF16),
            pltpu.VMEM((width, hidden), BF16),
            pltpu.VMEM((hidden, width), BF16),
            pltpu.VMEM((2, width, rows), BF16),
            pltpu.VMEM((rows, hidden), BF16),
            pltpu.VMEM((rows, hidden), BF16),
            pltpu.VMEM((rows, hidden), BF16),
            pltpu.VMEM((hidden, rows), BF16),
            pltpu.VMEM((rows, width), BF16),
            pltpu.VMEM((rows, width), BF16),
            pltpu.VMEM((4, *half), BF16),
            pltpu.SemaphoreType.DMA((3, chunks)),
            pltpu.SemaphoreType.DMA((8,)),
        ],
        compiler_params=pltpu.CompilerParams(vmem_limit_bytes=VMEM_LIMIT),
        cost_estimate=cost(2 * 9 * rows * width * hidden, rows * hidden, 6 * width * hidden),
        name="ffn",
    )(where, normed, normed_t, out_grad, w_gate, w_up, w_down)


ROWS = 256


def tile_of(local):
    return min(local, ROWS)


def in_own_half(core_ref):
    return core_ref[0] == pl.program_id(0) // (pl.num_programs(0) // 2)


def within_half(local, width):
    steps = local // tile_of(local)
    return pl.BlockSpec((tile_of(local), width), lambda i, c: (lax.rem(i, steps), 0))


def normalise(values, gain):
    inverse = lax.rsqrt(jnp.mean(values * values, axis=-1, keepdims=True) + norm_eps)
    return values * inverse * gain


def rms_back(values, gain, grad):
    inverse = lax.rsqrt(jnp.mean(values * values, axis=-1, keepdims=True) + norm_eps)
    scaled = grad * gain
    mean_dot = jnp.mean(values * scaled, axis=-1, keepdims=True)
    unit = values * inverse
    return inverse * (scaled - unit * (inverse * mean_dot))


def project_kernel(scales, core_ref, own_ref, other_ref, gain_ref, *refs):
    count = len(scales)
    w_refs, nt_ref, out_refs = refs[:count], refs[count], refs[count + 1 :]
    values = jnp.where(in_own_half(core_ref), own_ref[...], other_ref[...]).astype(F32)
    normed = normalise(values, gain_ref[...])
    nt_ref[...] = normed.T.astype(BF16)
    low = normed.astype(BF16)
    for scale, w_ref, out_ref in zip(scales, w_refs, out_refs):
        out = dot_nn(low, w_ref[...]).astype(BF16)
        out_ref[...] = out if scale is None else out * BF16(scale)


def own_columns(weight):
    return pl.BlockSpec((weight.shape[0], weight.shape[1] // 2), lambda i, c: (0, c[0]))


def other_columns(weight):
    return pl.BlockSpec((weight.shape[0], weight.shape[1] // 2), lambda i, c: (0, 1 - c[0]))


def own_rows(array):
    return pl.BlockSpec((array.shape[0] // 2, array.shape[1]), lambda i, c: (c[0], 0))


def other_rows(array):
    return pl.BlockSpec((array.shape[0] // 2, array.shape[1]), lambda i, c: (1 - c[0], 0))


def all_of(array):
    return pl.BlockSpec(array.shape, lambda i, c: (0,) * array.ndim)


def half_rows(rows, width):
    return pl.BlockSpec((rows, width), lambda i, c: (i, 0))


def half_columns(width, rows):
    return pl.BlockSpec((width, rows), lambda i, c: (0, i))


def fixed(shape):
    return pl.BlockSpec(shape, lambda i, c: (0,) * len(shape))


def core_call(kernel, steps, core, args, in_specs, out_specs, out_shape, scratch, flops, name):
    return pl.pallas_call(
        kernel,
        grid_spec=pltpu.PrefetchScalarGridSpec(
            num_scalar_prefetch=1,
            grid=(steps,),
            in_specs=in_specs,
            out_specs=out_specs,
            scratch_shapes=scratch,
        ),
        out_shape=out_shape,
        compiler_params=kernel_params(),
        cost_estimate=cost(flops, 0, flops // 400),
        name=name,
    )(core, *args)


def project(core, own, other, gain, weights, scales, name):
    local, width = own.shape
    return core_call(
        functools.partial(project_kernel, scales),
        2 * local // tile_of(local),
        core,
        (own, other, gain, *weights),
        [within_half(local, width)] * 2 + [all_of(gain)] + [own_columns(w) for w in weights],
        [half_columns(width, tile_of(local))] + [half_rows(tile_of(local), w.shape[1] // 2) for w in weights],
        [shape_of((width, 2 * local), BF16)]
        + [shape_of((2 * local, w.shape[1] // 2), BF16) for w in weights],
        [],
        2 * 2 * local * width * sum(w.shape[1] // 2 for w in weights),
        name,
    )


def memory_kernel(parts, core_ref, *refs):
    in_refs = refs[:parts]
    wk_ref, wv_ref = refs[parts : parts + 2]
    mt_refs, (k_ref, v_ref, all_ref) = refs[parts + 2 : -3], refs[-3:]
    rows = in_refs[0].shape[0]
    for i in range(parts):
        all_ref[i * rows : (i + 1) * rows, :] = in_refs[i][...]
    for slot, mt_ref in enumerate(mt_refs):
        mt_ref[...] = all_ref[2 * slot * rows : 2 * (slot + 1) * rows, :].astype(F32).T.astype(BF16)
    k_ref[...] = dot_nn(all_ref[...], wk_ref[...]).astype(BF16)
    v_ref[...] = dot_nn(all_ref[...], wv_ref[...]).astype(BF16)


def project_memory(core, parts, w_key, w_value):
    rows, width = parts[0].shape
    total = rows * len(parts)
    kw = w_key.shape[1] // 2
    return core_call(
        functools.partial(memory_kernel, len(parts)),
        1,
        core,
        (*parts, w_key, w_value),
        [all_of(p) for p in parts] + [own_columns(w_key), own_columns(w_value)],
        [fixed((width, 2 * rows))] * (len(parts) // 2) + [fixed((total, kw)), fixed((total, kw))],
        [shape_of((width, 2 * rows), BF16)] * (len(parts) // 2)
        + [shape_of((total, kw), BF16), shape_of((total, kw), BF16)],
        [pltpu.VMEM((total, width), BF16)],
        2 * total * width * 2 * kw,
        "project_memory",
    )


def join_kernel(low_base, project_next, core_ref, *refs):
    if low_base:
        own_ref, other_ref, refs = refs[0], refs[1], refs[2:]
        base = jnp.where(in_own_half(core_ref), own_ref[...], other_ref[...]).astype(F32)
    else:
        base, refs = refs[0][...], refs[1:]
    mixed_ref, got_ref, w_own_ref, w_other_ref, gain_ref = refs[:5]
    after = base + dot_nn(mixed_ref[...], w_own_ref[...]) + dot_nn(got_ref[...], w_other_ref[...])
    normed = normalise(after, gain_ref[...])
    low = normed.astype(BF16)
    if project_next:
        w_ref, after_ref, nt_ref, out_ref = refs[5:]
        out_ref[...] = dot_nn(low, w_ref[...]).astype(BF16) * BF16(score_scale)
    else:
        after_ref, nt_ref, out_ref = refs[5:]
        out_ref[...] = low
    after_ref[...] = after
    nt_ref[...] = normed.T.astype(BF16)


def join(core, base, mixed, got, w_out, gain, w_next, name):
    rows, half = mixed.shape
    width = w_out.shape[1]
    local = rows // 2
    low_base = isinstance(base, tuple)
    bases = base if low_base else (base,)
    base_specs = [within_half(local, width)] * 2 if low_base else [half_rows(tile_of(local), width)]
    nexts = () if w_next is None else (w_next,)
    out_width = width if w_next is None else w_next.shape[1] // 2
    return core_call(
        functools.partial(join_kernel, low_base, w_next is not None),
        rows // tile_of(local),
        core,
        (*bases, mixed, got, w_out, w_out, gain, *nexts),
        base_specs
        + [half_rows(tile_of(local), half), half_rows(tile_of(local), half), own_rows(w_out), other_rows(w_out), all_of(gain)]
        + [own_columns(w) for w in nexts],
        [half_rows(tile_of(local), width), half_columns(width, tile_of(local)), half_rows(tile_of(local), out_width)],
        [shape_of((rows, width), F32), shape_of((width, rows), BF16), shape_of((rows, out_width), BF16)],
        [],
        2 * rows * width * (width + out_width),
        name,
    )


def back_kernel(low_prior, products, core_ref, *refs):
    if low_prior:
        own_ref, other_ref, refs = refs[0], refs[1], refs[2:]
        prior = jnp.where(in_own_half(core_ref), own_ref[...], other_ref[...]).astype(F32)
    else:
        prior, refs = refs[0][...], refs[1:]
    value_ref, gain_ref, e_ref, got_ref, refs = refs[0], refs[1], refs[2], refs[3], refs[4:]
    if products:
        e = dot_nt(e_ref[...], refs[0][...]) + dot_nt(got_ref[...], refs[1][...])
        refs = refs[2:]
    else:
        e = e_ref[...].astype(F32) + got_ref[...].astype(F32)
    w_ref, grad_ref, half_ref, next_ref = refs
    grad = prior + rms_back(value_ref[...], gain_ref[...], e)
    grad_ref[...] = grad
    low = grad.astype(BF16)
    half = low.shape[1] // 2
    half_ref[...] = jnp.where(core_ref[0] == 0, low[:, :half], low[:, half:])
    next_ref[...] = dot_nt(low, w_ref[...]).astype(BF16)


def back(core, prior, values, gain, e, got, w_in, w_out, name):
    rows, width = values.shape
    local = rows // 2
    low_prior = isinstance(prior, tuple)
    priors = prior if low_prior else (prior,)
    prior_specs = [within_half(local, width)] * 2 if low_prior else [half_rows(tile_of(local), width)]
    ins = () if w_in is None else (w_in, w_in)
    in_specs = [] if w_in is None else [own_columns(w_in), other_columns(w_in)]
    half = w_out.shape[0] // 2
    return core_call(
        functools.partial(back_kernel, low_prior, w_in is not None),
        rows // tile_of(local),
        core,
        (*priors, values, gain, e, got, *ins, w_out),
        prior_specs
        + [half_rows(tile_of(local), width), all_of(gain), half_rows(tile_of(local), e.shape[1]), half_rows(tile_of(local), e.shape[1])]
        + in_specs
        + [own_rows(w_out)],
        [half_rows(tile_of(local), width), half_rows(tile_of(local), width // 2), half_rows(tile_of(local), half)],
        [
            shape_of((rows, width), F32),
            shape_of((rows, width // 2), BF16),
            shape_of((rows, half), BF16),
        ],
        [],
        2 * rows * width * (half + 2 * e.shape[1] * len(ins) // 2),
        name,
    )


def last_kernel(core_ref, prior_ref, base_ref, gain_ref, q_ref, pair_ref, got_ref, *refs):
    wq_own, wq_other, wk_own, wk_other, wv_own, wv_other, grad_ref = refs
    qw = wq_own.shape[1]
    kw = wk_own.shape[1]
    e = dot_nt(q_ref[...], wq_own[...]) + dot_nt(got_ref[:, :qw], wq_other[...])
    for m in range(kw // PAIR):
        c, span = 2 * PAIR * m, slice(PAIR * m, PAIR * (m + 1))
        e = e + dot_nt(pair_ref[:, c : c + PAIR], wk_own[:, span])
        e = e + dot_nt(got_ref[:, qw + c : qw + c + PAIR], wk_other[:, span])
        c = c + PAIR
        e = e + dot_nt(pair_ref[:, c : c + PAIR], wv_own[:, span])
        e = e + dot_nt(got_ref[:, qw + c : qw + c + PAIR], wv_other[:, span])
    grad_ref[...] = prior_ref[...] + rms_back(base_ref[...].astype(F32), gain_ref[...], e)


def last(core, prior, base, gain, grad_q, pair, got, w_query, w_key, w_value):
    local, width = base.shape
    steps = local // tile_of(local)

    def own_tile(array):
        return pl.BlockSpec((tile_of(local), array.shape[1]), lambda i, c: (c[0] * steps + i, 0))

    weights = (w_query, w_query, w_key, w_key, w_value, w_value)
    specs = []
    for w in (w_query, w_key, w_value):
        specs += [own_columns(w), other_columns(w)]
    return core_call(
        last_kernel,
        local // tile_of(local),
        core,
        (prior, base, gain, grad_q, pair, got, *weights),
        [own_tile(prior), half_rows(tile_of(local), width), all_of(gain), own_tile(grad_q), own_tile(pair), half_rows(tile_of(local), got.shape[1])]
        + specs,
        [half_rows(tile_of(local), width)],
        [shape_of((local, width), F32)],
        [],
        2 * local * width * 2 * width,
        "last",
    )


def outer_kernel(terms, split, count, has_extra, order_ref, *refs):
    lefts = []
    for parts in split:
        lefts.append(refs[:parts])
        refs = refs[parts:]
    right_refs, refs = refs[:count], refs[count:]
    if has_extra:
        extra_ref, refs = refs[0], refs[1:]
    keep_ref, send_ref, sorted_refs = refs[0], refs[1], refs[2:]
    blocks = order_ref.shape[1]
    for at, (left, sorted_ref) in enumerate(zip(lefts, sorted_refs)):
        rows = sorted_ref.shape[0] // blocks
        for p in range(blocks):
            index = order_ref[at, p]
            if len(left) == 1:
                piece = left[0][pl.ds(pl.multiple_of(index * rows, rows), rows), :]
            else:
                middle = blocks // 2
                first = pl.multiple_of(jnp.minimum(index, middle - 1) * rows, rows)
                second = pl.multiple_of(jnp.maximum(index - middle, 0) * rows, rows)
                piece = jnp.where(
                    index < middle, left[0][pl.ds(first, rows), :], left[1][pl.ds(second, rows), :]
                )
            sorted_ref[p * rows : (p + 1) * rows, :] = piece
    middle = sorted_refs[0].shape[0] // 2
    for out_ref, span in ((send_ref, slice(middle, 2 * middle)), (keep_ref, slice(0, middle))):
        column = 0
        for products in terms:
            total = None
            for left, right, first, start, size in products:
                depth = sorted_refs[left].shape[1]
                factor = right_refs[right][first : first + depth, start : start + size]
                part = dot_nn(sorted_refs[left][span, :], factor)
                total = part if total is None else total + part
            width = total.shape[1]
            out_ref[:, column : column + width] = total.astype(BF16)
            column += width
    if has_extra:
        rows = sorted_refs[0].shape[0] // blocks
        lanes = extra_ref.shape[1]
        row = lax.broadcasted_iota(jnp.int32, (rows, lanes), 0)
        for p in range(blocks):
            index = 2 * order_ref[0, p]
            block = jnp.where(row == 0, extra_ref[pl.ds(index, 1), :], 0.0)
            block = jnp.where(row == rows // 2, extra_ref[pl.ds(index + 1, 1), :], block)
            out_ref = keep_ref if p < blocks // 2 else send_ref
            first = p % (blocks // 2) * rows
            out_ref[first : first + rows, column:] = block.astype(BF16)


def outer_halves(orders, lefts, rights, terms, extra=None):
    blocks = orders[0].shape[0]
    lefts = [v if isinstance(v, tuple) else (v,) for v in lefts]
    totals = [sum(v.shape[0] for v in left) for left in lefts]
    rows = totals[0] // blocks
    if rows % 16:
        joined = [jnp.concatenate(left, axis=0) for left in lefts]
        joined = [
            jnp.concatenate(
                [lax.dynamic_slice_in_dim(v, order[p] * rows, rows, 0) for p in range(blocks)], axis=0
            )
            for v, order in zip(joined, orders)
        ]
        half = totals[0] // 2
        columns = []
        for products in terms:
            columns.append(
                sum(
                    dot_nn(joined[l], rights[r][first : first + joined[l].shape[1], start : start + size])
                    for l, r, first, start, size in products
                )
            )
        total = jnp.concatenate(columns, axis=1).astype(BF16)
        return total[:half], total[half:]
    width = sum(products[0][4] for products in terms)
    extras = () if extra is None else (extra,)
    if extras:
        width += extra.shape[1]
    half = shape_of((totals[0] // 2, width), BF16)
    flops = 0
    for products in terms:
        for l, _, _, _, size in products:
            flops += 2 * totals[l] * lefts[l][0].shape[1] * size
    whole = pl.BlockSpec(memory_space=pltpu.VMEM)
    flat = [v for left in lefts for v in left]
    return pl.pallas_call(
        functools.partial(outer_kernel, terms, [len(left) for left in lefts], len(rights), bool(extras)),
        in_specs=[pl.BlockSpec(memory_space=pltpu.SMEM)] + [whole] * (len(flat) + len(rights) + len(extras)),
        out_specs=[whole, whole],
        out_shape=[half, half],
        scratch_shapes=[
            pltpu.VMEM((total, left[0].shape[1]), BF16) for total, left in zip(totals, lefts)
        ],
        compiler_params=pltpu.CompilerParams(vmem_limit_bytes=VMEM_LIMIT),
        cost_estimate=cost(flops, 0, flops // 400),
        name="outer_halves",
    )(jnp.stack(orders), *flat, *rights, *extras)


def bits_of(size):
    return (size - 1).bit_length()


class Places:
    def __init__(self):
        self.seq = lax.axis_size("seq")
        self.dp = lax.axis_size("dp")
        self.nx = self.seq // 2
        self.chips = self.dp * self.nx
        place = lax.axis_index("seq")
        self.core = place & 1
        self.x = place >> 1
        self.d = lax.axis_index("dp")
        self.dp_bits = bits_of(self.dp)
        self.x_bits = bits_of(self.nx)
        self.chip = self.d * self.nx + self.x
        self.names = [("dp", b) for b in reversed(range(self.dp_bits))] + [
            ("x", b) for b in reversed(range(self.x_bits))
        ]

    def swap_core(self, value):
        return lax.ppermute(value, "seq", [(s, s ^ 1) for s in range(self.seq)])

    def shift_x(self, value, by):
        pairs = [(s, (s + 2 * by) % self.seq) for s in range(self.seq)]
        return lax.ppermute(value, "seq", pairs)

    def flip(self, value, names):
        d_mask = sum(1 << bit for axis, bit in names if axis == "dp")
        s_mask = sum(2 << bit for axis, bit in names if axis == "x")
        pairs = [
            (d * self.seq + s, (d ^ d_mask) * self.seq + (s ^ s_mask))
            for d in range(self.dp)
            for s in range(self.seq)
        ]
        return lax.ppermute(value, ("dp", "seq"), pairs)

    def by_core(self, own, other, axis):
        first = jnp.concatenate([own, other], axis=axis)
        second = jnp.concatenate([other, own], axis=axis)
        return jnp.where(self.core == 0, first, second)

    def core_rows(self, value, mine):
        half = value.shape[0] // 2
        which = self.core if mine else 1 - self.core
        return lax.dynamic_slice_in_dim(value, which * half, half, 0)

    def stages(self, kind):
        dp0 = [(("dp", 0),)]
        rest = [(("dp", b),) for b in range(1, self.dp_bits)]
        xs = [(("x", b),) for b in range(self.x_bits)]
        at_once = [tuple(one[0] for one in rest)] if len(rest) == 2 else rest
        z1, z2 = rest[:1], rest[1:]
        return {
            "x_y_z1_z2": xs + dp0 + z1 + z2,
            "y_x_z1_z2": dp0 + xs + z1 + z2,
            "y_x_zz": dp0 + xs + at_once,
            "z1_x_wait_z2_y": z1 + xs + [()] + z2 + dp0,
            "x_z1_y_z2": xs + z1 + dp0 + z2,
            "z1_x_y_z2": z1 + xs + dp0 + z2,
        }[kind]

    def block_order(self, kind, core_major=False):
        order = [name for stage in self.stages(kind) for name in stage]
        count = len(order)
        masks = []
        for p in range(self.chips):
            mask = 0
            for k, name in enumerate(order):
                if (p >> (count - 1 - k)) & 1:
                    mask |= 1 << (count - 1 - self.names.index(name))
            masks.append(mask)
        base = self.chip
        if core_major:
            base = base ^ (self.core << (count - 1))
        return jnp.array(masks, jnp.int32) ^ base.astype(jnp.int32)


class ChipSum:
    def __init__(self, at, kind, kept, sent=None):
        self.at = at
        self.todo = list(at.stages(kind))
        self.rows, self.width = kept.shape
        self.parts = [([kept], 0)]
        self.sent = sent
        if sent is not None:
            self.parts.append(([at.flip(sent, self.todo.pop(0))], 0))

    def result(self):
        return sum(
            box[0][: self.rows, column : column + self.width].astype(F32) for box, column in self.parts
        )


def fold_kernel(plan, count, *refs):
    in_refs, out_refs = refs[:count], refs[count:]
    for sources, (out, out_column), (rows, width) in plan:
        step = 32 if rows % 32 == 0 else 16

        def body(i, carried, sources=sources, out=out, out_column=out_column, width=width, step=step):
            span = pl.ds(pl.multiple_of(i * step, 16), step)
            total = None
            for at, column in sources:
                part = in_refs[at][span, column : column + width].astype(F32)
                total = part if total is None else total + part
            out_refs[out][span, out_column : out_column + width] = total.astype(BF16)
            return carried

        lax.fori_loop(0, rows // step, body, 0)


def fold_arrays(plan, inputs, shapes):
    if all(rows % 16 == 0 for _, _, (rows, _) in plan):
        return pl.pallas_call(
            functools.partial(fold_kernel, plan, len(inputs)),
            grid=(1,),
            in_specs=[
                pl.BlockSpec((rows, array.shape[1]), lambda i, block=block: (block, 0))
                for array, block, rows in inputs
            ],
            out_specs=[pl.BlockSpec(shape, lambda i: (0, 0)) for shape in shapes],
            out_shape=[shape_of(shape, BF16) for shape in shapes],
            compiler_params=kernel_params(),
            cost_estimate=cost(1, 0, 1),
            name="fold",
        )(*[array for array, _, _ in inputs])
    outs = [jnp.zeros(shape, BF16) for shape in shapes]
    for sources, (out, out_column), (rows, width) in plan:
        total = 0.0
        for at, column in sources:
            array, block, size = inputs[at]
            total = total + array[block * size : (block + 1) * size, column : column + width].astype(F32)
        outs[out] = outs[out].at[:, out_column : out_column + width].set(total.astype(BF16))
    return outs


def fold(at, sums, *ties):
    inputs, plan, shapes, sends = [], [], [], {}

    def place_of(array, block, rows):
        for index, known in enumerate(inputs):
            if known[0] is array and known[1:] == (block, rows):
                return index
        inputs.append((array, block, rows))
        return len(inputs) - 1

    for one in sums:
        stage = one.todo.pop(0) if one.todo else ()
        one.rows >>= len(stage)
        for j in range(1, 1 << len(stage)):
            names = tuple(name for k, name in enumerate(stage) if (j >> (len(stage) - 1 - k)) & 1)
            sources = [(place_of(box[0], j, one.rows), column) for box, column in one.parts]
            sends.setdefault((names, one.rows), []).append((one, sources))
    for (names, rows), pieces in sends.items():
        column = 0
        for one, sources in pieces:
            plan.append((sources, (len(shapes), column), (rows, one.width)))
            column += one.width
        shapes.append((rows, column))
    outs = list(fold_arrays(plan, inputs, shapes))
    if ties:
        outs = together(*outs, *ties)
        outs, ties = list(outs[: len(shapes)]), outs[len(shapes) :]
    for out, ((names, rows), pieces) in zip(outs, sends.items()):
        box = [at.flip(out, names)]
        column = 0
        for one, _ in pieces:
            one.sent = out
            one.parts.append((box, column))
            column += one.width
    return ties


def settle(sums, *values):
    boxes = []
    for one in sums:
        for box, _ in one.parts[1:]:
            if not any(box is known for known in boxes):
                boxes.append(box)
    out = together(*[box[0] for box in boxes], *values)
    for box, value in zip(boxes, out):
        box[0] = value
    return out[len(boxes) :]


def finish_sum_kernel(plan, count, where_ref, *refs):
    in_refs, refs = refs[:count], refs[count:]
    out_refs, total_refs = refs[: 2 * len(plan)], refs[2 * len(plan) :]
    for at, ranges in enumerate(plan):
        mine_ref, other_ref, total_ref = out_refs[2 * at], out_refs[2 * at + 1], total_refs[at]
        first = 0
        for sources, width in ranges:
            total = None
            for index, column in sources:
                part = in_refs[index][:, column : column + width].astype(F32)
                total = part if total is None else total + part
            total_ref[:, first : first + width] = total
            first += width
        half = mine_ref.shape[0]
        core = where_ref[0]
        mine_ref[...] = total_ref[pl.ds(pl.multiple_of(core * half, half), half), :]
        other_ref[...] = total_ref[pl.ds(pl.multiple_of((1 - core) * half, half), half), :]


def finish_sums(places, where, groups):
    if any(group[0].rows % 32 and group[0].rows % 16 for group in groups):
        outs = []
        for group in groups:
            total = jnp.concatenate([one.result() for one in group], axis=1)
            outs.append((places.core_rows(total, True), places.core_rows(total, False)))
        return outs
    inputs, plan = [], []

    def place_of(array, rows):
        for index, known in enumerate(inputs):
            if known[0] is array and known[1] == rows:
                return index
        inputs.append((array, rows))
        return len(inputs) - 1

    shapes, scratch = [], []
    for group in groups:
        ranges = []
        for one in group:
            ranges.append(
                ([(place_of(box[0], one.rows), column) for box, column in one.parts], one.width)
            )
        plan.append(ranges)
        width = sum(one.width for one in group)
        shapes += [(group[0].rows // 2, width)] * 2
        scratch.append(pltpu.VMEM((group[0].rows, width), F32))
    outs = core_call(
        functools.partial(finish_sum_kernel, plan, len(inputs)),
        1,
        where,
        [array for array, _ in inputs],
        [pl.BlockSpec((rows, array.shape[1]), lambda i, c: (0, 0)) for array, rows in inputs],
        [fixed(shape) for shape in shapes],
        [shape_of(shape, F32) for shape in shapes],
        scratch,
        16,
        "finish_sums",
    )
    return [(outs[2 * k], outs[2 * k + 1]) for k in range(len(groups))]


def finish_kernel(plan, gains, count, where_ref, *refs):
    group_refs, refs = refs[: 2 * count], refs[2 * count :]
    weights = sum(len(pairs) for pairs in gains)
    weight_refs, gain_refs, refs = refs[:weights], refs[weights : weights + len(gains)], refs[weights + len(gains) :]
    out_refs, gain_outs = refs[: len(plan)], refs[len(plan) :]
    first_core = where_ref[0] == 0
    for (group, column, width), out_ref in zip(plan, out_refs):
        mine = group_refs[2 * group][:, column : column + width]
        got = group_refs[2 * group + 1][:, column : column + width]
        out_ref[:, :width] = jnp.where(first_core, mine, got)
        out_ref[:, width:] = jnp.where(first_core, got, mine)
    at = 0
    for pairs, gain_ref, gain_out in zip(gains, gain_refs, gain_outs):
        total = None
        for matrix in pairs:
            product = out_refs[matrix][...] * weight_refs[at][...].astype(F32)
            at += 1
            part = product[:, :PAIR]
            for first in range(PAIR, product.shape[1], PAIR):
                part = part + product[:, first : first + PAIR]
            total = part if total is None else total + part
        gain_out[0] = jnp.sum(total.T, axis=0, keepdims=True) / gain_ref[0]


def finish(places, where, joined, plan, gains):
    half = joined[0][0].shape[0]
    device = 2 * places.chip + places.core
    if half % 16:
        outs = []
        for group, column, width in plan:
            mine, got = joined[group]
            outs.append(places.by_core(mine[:, column : column + width], got[:, column : column + width], 1))
        shares = []
        for gain, pairs in gains:
            total = 0.0
            for matrix, weight in pairs:
                rows = lax.dynamic_slice_in_dim(weight, device * half, half, 0).astype(F32)
                total = total + jnp.sum(rows * outs[matrix], axis=1)
            shares.append(total / lax.dynamic_slice_in_dim(gain, device * half, half, 0))
        return outs, shares
    flat = [v for pair in joined for v in pair]
    weights = [weight for _, pairs in gains for _, weight in pairs]
    gain_rows = [gain.reshape(-1, 1, half) for gain, _ in gains]
    outs = core_call(
        functools.partial(finish_kernel, plan, [[matrix for matrix, _ in pairs] for _, pairs in gains], len(joined)),
        1,
        where,
        (*flat, *weights, *gain_rows),
        [all_of(v) for v in flat]
        + [pl.BlockSpec((half, w.shape[1]), lambda i, c: (c[1], 0)) for w in weights]
        + [pl.BlockSpec((1, 1, half), lambda i, c: (c[1], 0, 0)) for _ in gains],
        [fixed((joined[group][0].shape[0], 2 * width)) for group, _, width in plan]
        + [fixed((1, 1, half)) for _ in gains],
        [shape_of((joined[group][0].shape[0], 2 * width), F32) for group, _, width in plan]
        + [shape_of((1, 1, half), F32) for _ in gains],
        [],
        16,
        "finish",
    )
    return outs[: len(plan)], [v.reshape(half) for v in outs[len(plan) :]]


def together(*values):
    return lax.optimization_barrier(values)


def per_device(
    target,
    memory,
    mem_lengths,
    mem_mask,
    distance_buckets,
    norm_self,
    w_query,
    w_key,
    w_value,
    w_out,
    pos_table,
    norm_cross,
    wc_query,
    wc_key,
    wc_value,
    wc_out,
    norm_ffn,
    w_gate,
    w_up,
    w_down,
    out_grad,
):
    at = Places()
    core, nx = at.core, at.nx
    local, width = target.shape[1], target.shape[2]
    mem_local = memory.shape[1]
    rows = 2 * local
    full = distance_buckets.shape[0]
    qw = HEADS * HEAD_DIM // 2
    kw = KV * HEAD_DIM // 2
    head_count = HEADS // 2
    place = at.x.astype(jnp.int32).reshape(1)
    core_arg = core.astype(jnp.int32).reshape(1)
    gain_self = norm_self.reshape(1, width)
    gain_cross = norm_cross.reshape(1, width)
    gain_ffn = norm_ffn.reshape(1, width)

    tokens = target.reshape(local, width)
    far_tokens = [at.shift_x(tokens, s) for s in range(1, nx)]
    tokens_got = at.swap_core(tokens)
    memories = memory.reshape(mem_local, width)
    far_memories = [at.shift_x(memories, s) for s in range(1, nx)]
    memories_got = at.swap_core(memories)
    grads = out_grad.reshape(local, width)
    grads_got = at.swap_core(grads)
    grad_chip = at.by_core(grads, grads_got, 0)

    own_table = lax.dynamic_slice_in_dim(pos_table, core * head_count, head_count, 0)
    onehot = (distance_buckets[:, None] == jnp.arange(BUCKETS, dtype=jnp.int32)[None, :]).astype(F32)
    by_distance = lax.dot_general(
        own_table, onehot, (((1,), (1,)), ((), ())), precision=lax.Precision.HIGHEST
    )
    bias_vec = jnp.pad(by_distance, ((0, 0), (BLK, 0))).reshape(head_count // 2, 2, BLK + full)

    mem_ids = jnp.arange(mem_mask.shape[1], dtype=jnp.int32)
    valid = (mem_ids < mem_lengths[0]) & ((mem_mask[0] == 1) | (mem_ids == 0))
    mask_add = jnp.where(valid, 0.0, big_negative).astype(F32).reshape(2 * nx, mem_local)
    slot_of = jnp.array([s for s in range(nx) for c in range(2)], jnp.int32)
    core_of = jnp.array([c for s in range(nx) for c in range(2)], jnp.int32)
    mask_rows = (((at.x - slot_of + nx) % nx) * 2 + (core ^ core_of))[:, None] == jnp.arange(2 * nx)[None, :]
    mask_col = jnp.sum(jnp.where(mask_rows[:, :, None], mask_add[None], 0.0), axis=1).reshape(-1, 1)

    normed_t, query, keys, values = project(
        core_arg, tokens, tokens_got, gain_self, (w_query, w_key, w_value), (score_scale, None, None), "project"
    )
    grad_half = lax.dynamic_slice_in_dim(grad_chip, core * (width // 2), width // 2, 1)
    tied = together(*far_tokens, query, grad_chip, grad_half, bias_vec, mask_col)
    far_tokens = list(tied[: nx - 1])
    grad_chip, grad_half, bias_vec, mask_col = tied[nx:]
    keys, values, normed_ts = [keys], [values], [normed_t]
    for far in far_tokens:
        far_t, far_k, far_v = project(
            core_arg, far, at.swap_core(far), gain_self, (w_key, w_value), (None, None), "project_far"
        )
        normed_ts.append(far_t)
        keys.append(far_k)
        values.append(far_v)

    mixed, mixed_t, lse_self = self_forward(place, query, keys, values, bias_vec)
    mixed, mixed_t, memories_got, *far_memories = together(mixed, mixed_t, memories_got, *far_memories)
    mem_parts = [memories, memories_got]
    for far in far_memories:
        mem_parts += [far, at.swap_core(far)]
    *mem_ts, mem_keys, mem_values = project_memory(core_arg, mem_parts, wc_key, wc_value)
    mixed_got = at.swap_core(mixed)
    mixed_t_got = at.swap_core(mixed_t)
    after_self, cross_t, cross_query = join(
        core_arg, (tokens, tokens_got), mixed, mixed_got, w_out, gain_cross, wc_query, "join_self"
    )

    crossed, crossed_t, lse_cross = cross_forward(cross_query, mem_keys, mem_values, mask_col)
    crossed_got = at.swap_core(crossed)
    crossed_t_got = at.swap_core(crossed_t)
    after_cross, ffn_t, normed_ffn = join(
        core_arg, after_self, crossed, crossed_got, wc_out, gain_ffn, None, "join_cross"
    )

    ffn_where = jnp.concatenate([core_arg, at.block_order("x_y_z1_z2"), at.block_order("y_x_z1_z2")])
    hidden_t, e_part, out_mine, out_other, gate_keep, gate_send, up_keep, up_send = ffn(
        ffn_where, normed_ffn, ffn_t, grad_chip, w_gate, w_up, w_down, at.chips
    )
    ffn_half = w_gate.shape[1] // 2
    gate_sum = ChipSum(at, "x_y_z1_z2", gate_keep, gate_send)
    up_sum = ChipSum(at, "y_x_z1_z2", up_keep, up_send)
    hidden_t_got = at.swap_core(hidden_t)
    e_got = at.swap_core(e_part)
    out_got = at.swap_core(out_other)
    down_halves = outer_halves(
        [at.block_order("z1_x_wait_z2_y", True)], [(hidden_t, hidden_t_got)], [grad_half], [[(0, 0, 0, 0, width // 2)]]
    )
    e_part, *down_halves = together(e_part, *down_halves)
    down_sum = ChipSum(at, "z1_x_wait_z2_y", *down_halves)
    grad_after_cross, cross_half, grad_crossed = back(
        core_arg, (grads, grads_got), after_cross, gain_ffn, e_part, e_got, None, wc_out, "back_ffn"
    )

    grad_cq, grad_mem = cross_backward(
        cross_query, mem_keys, mem_values, mask_col, grad_crossed, crossed, lse_cross, nx
    )
    grad_cq_got = at.swap_core(grad_cq)
    wc_out_halves = outer_halves(
        [at.block_order("z1_x_y_z2", True)],
        [(crossed_t, crossed_t_got)],
        [cross_half],
        [[(0, 0, 0, 0, width // 2)]],
    )
    turns = kw // PAIR
    k_columns = [2 * PAIR * m for m in range(turns)]
    v_columns = [2 * PAIR * m + PAIR for m in range(turns)]
    wc_in_halves = outer_halves(
        [at.block_order("y_x_z1_z2")] * (1 + nx),
        [cross_t, *mem_ts],
        [grad_cq, *grad_mem],
        [[(0, 0, 0, 0, qw)]] + [[(1 + s, 1 + s, 0, c, PAIR) for s in range(nx)] for c in k_columns + v_columns],
    )
    mem_got = [at.shift_x(grad_mem[s], nx - s) for s in range(1, nx)]

    both = [gate_sum, up_sum]
    tied = settle(both, grad_cq, grad_cq_got, *wc_out_halves)
    grad_cq, grad_cq_got, *wc_out_halves = fold(at, both, *tied)
    grad_after_self, self_half, grad_mixed = back(
        core_arg, grad_after_cross, after_self, gain_cross, grad_cq, grad_cq_got, wc_query, w_out, "back_cross"
    )
    out_halves = outer_halves(
        [at.block_order("x_z1_y_z2", True)],
        [(mixed_t, mixed_t_got)],
        [self_half],
        [[(0, 0, 0, 0, width // 2)]],
    )
    ffn_sums = [gate_sum, up_sum, down_sum]
    tied = settle(
        ffn_sums,
        grad_mixed,
        grad_after_self,
        out_mine,
        out_got,
        *wc_in_halves,
        *out_halves,
        *wc_out_halves,
        grad_mem[0],
        *mem_got,
    )
    grad_mixed, grad_after_self, out_mine, out_got = tied[:4]
    halves = tied[4:10]
    grad_mem_chip, mem_got = tied[10], tied[11:]

    grad_mixed, *halves = fold(at, ffn_sums, grad_mixed, *halves)
    wc_in_sum = ChipSum(at, "y_x_z1_z2", *halves[:2])
    out_sum = ChipSum(at, "x_z1_y_z2", *halves[2:4])
    wc_out_sum = ChipSum(at, "z1_x_y_z2", *halves[4:])
    early = [*ffn_sums, wc_in_sum, out_sum, wc_out_sum]
    grad_q, grad_pairs, diagonals = self_backward(
        place, query, keys, values, bias_vec, grad_mixed, mixed, lse_self
    )
    tied = settle(early, grad_q, diagonals, out_mine, out_got, grad_mem_chip, *grad_pairs, *mem_got)
    grad_q, diagonals, out_mine, out_got, grad_mem_chip = tied[:5]
    grad_pairs, mem_got = tied[5 : 5 + nx], tied[5 + nx :]
    pair_chip = grad_pairs[0]
    pair_got = [at.shift_x(grad_pairs[s], nx - s) for s in range(1, nx)]

    grad_q, diagonals, grad_mem_chip, out_mine = fold(at, early, grad_q, diagonals, grad_mem_chip, out_mine)

    own_bias = lax.dot_general(
        diagonals.reshape(head_count, -1)[:, BLK:],
        onehot,
        (((1,), (0,)), ((), ())),
        precision=lax.Precision.HIGHEST,
        preferred_element_type=F32,
    )
    table = lax.dynamic_update_slice_in_dim(
        jnp.zeros((HEADS, BUCKETS), F32), own_bias, core * head_count, 0
    ).reshape(2 * at.chips, -1)
    bias_share = table.shape[1]
    in_halves = outer_halves(
        [at.block_order("y_x_zz")] * nx,
        normed_ts,
        [grad_q, *grad_pairs],
        [[(0, 0, 0, 0, qw)]] + [[(s, 1 + s, 0, c, PAIR) for s in range(nx)] for c in k_columns + v_columns],
        jnp.pad(table, ((0, 0), (0, 128 - bias_share))),
    )
    in_sum = ChipSum(at, "y_x_zz", *in_halves)
    grad_mem_chip, out_mine, *pair_got = together(grad_mem_chip, out_mine, *pair_got)
    for got in pair_got:
        pair_chip = pair_chip + got
    every = [*early, in_sum]

    output = (
        at.core_rows(after_cross, True)
        + out_mine.astype(F32)
        + out_got.astype(F32)
    ).astype(BF16)
    for got in mem_got:
        grad_mem_chip = grad_mem_chip + got
    mem_mine = grad_mem_chip[:mem_local]
    mem_other = at.swap_core(grad_mem_chip[mem_local:])

    def unpaired(columns):
        mine = [mem_mine[:, c : c + PAIR] for c in columns]
        other = [mem_other[:, c : c + PAIR] for c in columns]
        return at.by_core(jnp.concatenate(mine, axis=1), jnp.concatenate(other, axis=1), 1)

    grad_memory = dot_nt(unpaired(k_columns), wc_key) + dot_nt(unpaired(v_columns), wc_value)
    sent = jnp.concatenate([at.core_rows(grad_q, False), at.core_rows(pair_chip, False)], axis=1)
    (grad_target,) = last(
        core_arg,
        grad_after_self,
        tokens,
        gain_self,
        grad_q,
        pair_chip,
        at.swap_core(sent),
        w_query,
        w_key,
        w_value,
    )

    grad_target, grad_memory, output = settle(every, grad_target, grad_memory, output)
    where = jnp.stack([core, 2 * at.chip + core]).astype(jnp.int32)
    while any(one.todo for one in every):
        fold(at, every)

    sums = [gate_sum, up_sum, wc_in_sum, out_sum, in_sum, wc_out_sum]
    rear, down_rows = finish_sums(at, where, [sums, [down_sum]])
    rear_join = (rear[0], at.swap_core(rear[1]))
    down_join = (down_rows[0], at.swap_core(down_rows[1]))
    wc_at = 2 * ffn_half
    out_at = wc_at + qw + 2 * kw
    in_at = out_at + width // 2
    bias_at = in_at + qw + 2 * kw
    (gate, up, cross_in, cross_key, cross_value, self_out, self_in, self_key, self_value, cross_out, down), gain_grads = finish(
        at,
        where,
        [rear_join, down_join],
        [
            (0, 0, ffn_half),
            (0, ffn_half, ffn_half),
            (0, wc_at, qw),
            (0, wc_at + qw, kw),
            (0, wc_at + qw + kw, kw),
            (0, out_at, width // 2),
            (0, in_at, qw),
            (0, in_at + qw, kw),
            (0, in_at + qw + kw, kw),
            (0, in_at + in_sum.width, width // 2),
            (1, 0, width // 2),
        ],
        [
            (norm_ffn, [(0, w_gate), (1, w_up)]),
            (norm_cross, [(2, wc_query)]),
            (norm_self, [(6, w_query), (7, w_key), (8, w_value)]),
        ],
    )
    gain_ffn_grad, gain_cross_grad, gain_self_grad = gain_grads
    bias_cut = slice(bias_at, bias_at + bias_share)
    bias_out = rear_join[0][0, bias_cut] + rear_join[1][0, bias_cut]
    return (
        output.reshape(target.shape),
        grad_target.reshape(target.shape),
        grad_memory.reshape(memory.shape),
        gain_self_grad,
        self_in,
        self_key,
        self_value,
        self_out,
        bias_out,
        gain_cross_grad,
        cross_in,
        cross_key,
        cross_value,
        cross_out,
        gain_ffn_grad,
        gate,
        up,
        down,
    )


def solution(mesh):
    tokens = P("dp", "seq", None)
    row_share = P(("dp", "seq"))
    matrix_share = P(("dp", "seq"), None)
    return jax.shard_map(
        per_device,
        mesh=mesh,
        in_specs=(tokens, tokens, P("dp"), P("dp", None)) + (P(),) * 16 + (tokens,),
        out_specs=(tokens, tokens, tokens, row_share)
        + (matrix_share,) * 4
        + (row_share, row_share)
        + (matrix_share,) * 4
        + (row_share,)
        + (matrix_share,) * 3,
        check_vma=False,
    )
```

```python
import functools

import jax
import jax.numpy as jnp
from jax import lax
from jax.experimental import pallas as pl
from jax.experimental.pallas import tpu as pltpu
from jax.sharding import PartitionSpec as P

HEADS = 16
KV = 8
HEAD_DIM = 64
BUCKETS = 32
BLK = 256
PAIR = 2 * HEAD_DIM

norm_eps = 1e-06
big_negative = -1000000000.0
score_scale = HEAD_DIM ** (-0.5)
F32 = jnp.float32
BF16 = jnp.bfloat16
VMEM_LIMIT = 64 * 1024 * 1024


def dot_nn(a, b):
    return lax.dot_general(a, b, (((1,), (0,)), ((), ())), preferred_element_type=F32)


def dot_nt(a, b):
    return lax.dot_general(a, b, (((1,), (1,)), ((), ())), preferred_element_type=F32)


def dot_tn(a, b):
    return lax.dot_general(a, b, (((0,), (0,)), ((), ())), preferred_element_type=F32)


def lane_pick(source, dest):
    a = lax.broadcasted_iota(jnp.int32, (PAIR, PAIR), 0)
    b = lax.broadcasted_iota(jnp.int32, (PAIR, PAIR), 1)
    keep = (a - source == b - dest) & (b >= dest) & (b < dest + HEAD_DIM)
    return keep.astype(F32).astype(BF16)


def lane_pick_t(source, dest):
    a = lax.broadcasted_iota(jnp.int32, (PAIR, PAIR), 1)
    b = lax.broadcasted_iota(jnp.int32, (PAIR, PAIR), 0)
    keep = (a - source == b - dest) & (b >= dest) & (b < dest + HEAD_DIM)
    return keep.astype(F32).astype(BF16)


def bias_tile(bias_vec_ref, h, delta):
    piece = bias_vec_ref[0, h : h + 1, delta * BLK : delta * BLK + 2 * BLK]
    wide = jnp.broadcast_to(piece, (BLK, 2 * BLK))
    return pltpu.roll(wide, 0, 1, stride=1, stride_axis=0)[:, BLK:]


def tile_plan(row_blocks, slots):
    plan = [(delta, 0) for delta in range(row_blocks)]
    for slot in range(1, slots):
        plan += [(slot * row_blocks + c, slot) for c in range(1 - row_blocks, row_blocks)]
    return plan


def tile_at(row_blocks, rb, kb):
    slot, jb = kb // row_blocks, kb % row_blocks
    if slot == 0:
        return rb - jb, rb - jb
    first = row_blocks + (slot - 1) * (2 * row_blocks - 1)
    return first + rb - jb + row_blocks - 1, slot * row_blocks + rb - jb


def key_blocks(row_blocks, slots, rb):
    return list(range(rb + 1)) + list(range(row_blocks, row_blocks * slots))


def fill_bias(place, bias_vec_ref, tile_ref, row_blocks, slots):
    for at, (delta, slot) in enumerate(tile_plan(row_blocks, slots)):
        for h in range(2):
            tile = bias_tile(bias_vec_ref, h, delta)
            if slot:
                tile = tile + jnp.where(place >= slot, 0.0, big_negative)
            elif delta == 0:
                tile = jnp.where(causal_tile(), tile, big_negative)
            tile_ref[h, at] = tile


def causal_tile():
    key_pos = lax.broadcasted_iota(jnp.int32, (BLK, BLK), 0)
    row_pos = lax.broadcasted_iota(jnp.int32, (BLK, BLK), 1)
    return key_pos <= row_pos


def online_step(carry, scores, value_t):
    highest, total, mixed = carry
    new_high = jnp.maximum(highest, jnp.max(scores, axis=0, keepdims=True))
    fade = jnp.exp(highest - new_high)
    weights = jnp.exp(scores - new_high)
    total = total * fade + jnp.sum(weights, axis=0, keepdims=True)
    mixed = mixed * fade + dot_nn(value_t, weights.astype(BF16))
    return (new_high, total, mixed)


def first_step(scores, value_t):
    highest = jnp.max(scores, axis=0, keepdims=True)
    weights = jnp.exp(scores - highest)
    total = jnp.sum(weights, axis=0, keepdims=True)
    return (highest, total, dot_nn(value_t, weights.astype(BF16)))


def key_spans(row_blocks, slots, rb):
    own, end = (rb + 1) * BLK, row_blocks * slots * BLK
    first_far = row_blocks * BLK
    if slots == 1:
        return [(0, own)]
    if own == first_far:
        return [(0, end)]
    return [(0, own), (first_far, end)]


def self_forward_kernel(slots, place_ref, q_ref, b_ref, *refs):
    k_refs, v_refs = refs[:slots], refs[slots : 2 * slots]
    o_ref, ot_ref, lse_ref, tile_ref, kz_ref, vt_ref, s_ref, p_ref = refs[2 * slots :]
    parity = lax.rem(pl.program_id(0), 2)
    rows_all = q_ref.shape[0]
    row_blocks = rows_all // BLK
    fill_bias(place_ref[0], b_ref, tile_ref, row_blocks, slots)
    for h in range(2):
        for slot in range(slots):
            span = slice(slot * rows_all, (slot + 1) * rows_all)
            pick_k = lane_pick(parity * HEAD_DIM, h * HEAD_DIM)
            pick_v = lane_pick_t(parity * HEAD_DIM, h * HEAD_DIM)
            kz_ref[h, span, :] = dot_nn(k_refs[slot][...], pick_k).astype(BF16)
            vt_ref[h, :, span] = dot_nt(pick_v, v_refs[slot][...]).astype(BF16)
    for rb in range(row_blocks):
        rows = slice(rb * BLK, (rb + 1) * BLK)
        queries = q_ref[rows, :]
        spans = key_spans(row_blocks, slots, rb)
        highest = [None, None]
        for h in range(2):
            for first, end in spans:
                products = dot_nt(kz_ref[h, first:end, :], queries)
                for kb in range(first // BLK, end // BLK):
                    at, _ = tile_at(row_blocks, rb, kb)
                    scores = products[kb * BLK - first : (kb + 1) * BLK - first, :] + tile_ref[h, at]
                    s_ref[h, kb * BLK : (kb + 1) * BLK, :] = scores
                    top = jnp.max(scores, axis=0, keepdims=True)
                    highest[h] = top if highest[h] is None else jnp.maximum(highest[h], top)
        mixed_t = None
        for h in range(2):
            total = None
            part = None
            for first, end in spans:
                weights = jnp.exp(s_ref[h, first:end, :] - highest[h])
                one = jnp.sum(weights, axis=0, keepdims=True)
                total = one if total is None else total + one
                p_ref[h, first:end, :] = weights.astype(BF16)
            for first, end in spans:
                one = dot_nn(vt_ref[h, :, first:end], p_ref[h, first:end, :])
                part = one if part is None else part + one
            part = part / total
            mixed_t = part if mixed_t is None else mixed_t + part
            lse_ref[0, h : h + 1, rows] = highest[h] + jnp.log(total)
        ot_ref[:, rows] = mixed_t.astype(BF16)
        o_ref[rows, :] = mixed_t.T.astype(BF16)


def diagonal_sums(wide):
    rows, lanes = wide.shape
    while rows > 8:
        rows //= 2
        wide = wide[:rows] + pltpu.roll(wide[rows:], lanes - rows, 1)
    row = lax.broadcasted_iota(jnp.int32, (8, lanes), 0)
    total = jnp.where(row == 0, wide, 0.0)
    for b in range(1, 8):
        total = total + jnp.where(row == b, pltpu.roll(wide, lanes - b, 1), 0.0)
    return jnp.sum(total, axis=0, keepdims=True)


def row_products(grad_block, mixed_block):
    turned = (grad_block.astype(F32) * mixed_block.astype(F32)).T
    return [
        jnp.sum(turned[h * HEAD_DIM : (h + 1) * HEAD_DIM], axis=0, keepdims=True) for h in range(2)
    ]


def self_backward_kernel(slots, place_ref, q_ref, b_ref, do_ref, o_ref, lse_ref, *refs):
    k_refs, v_refs = refs[:slots], refs[slots : 2 * slots]
    dq_ref, diag_ref = refs[2 * slots : 2 * slots + 2]
    pair_refs, refs = refs[2 * slots + 2 : 3 * slots + 2], refs[3 * slots + 2 :]
    tile_ref, sum_ref, kz_ref, kt_ref, vz_ref, qp_ref, dop_ref, dk_acc, dv_acc, p_ref, ds_ref = refs
    parity = lax.rem(pl.program_id(0), 2)
    rows_all = q_ref.shape[0]
    row_blocks = rows_all // BLK
    fill_bias(place_ref[0], b_ref, tile_ref, row_blocks, slots)
    for h in range(2):
        in_pick = lane_pick(parity * HEAD_DIM, h * HEAD_DIM)
        out_pick = lane_pick(h * HEAD_DIM, parity * HEAD_DIM)
        pick_t = lane_pick_t(parity * HEAD_DIM, h * HEAD_DIM)
        for slot in range(slots):
            span = slice(slot * rows_all, (slot + 1) * rows_all)
            kz_ref[h, span, :] = dot_nn(k_refs[slot][...], in_pick).astype(BF16)
            kt_ref[h, :, span] = dot_nt(pick_t, k_refs[slot][...]).astype(BF16)
            vz_ref[h, span, :] = dot_nn(v_refs[slot][...], in_pick).astype(BF16)
        side = slice(h * rows_all, (h + 1) * rows_all)
        qp_ref[side, :] = dot_nn(q_ref[...], out_pick).astype(BF16)
        dop_ref[side, :] = dot_nn(do_ref[...], out_pick).astype(BF16)
    seen = set()
    for rb in range(row_blocks):
        rows = slice(rb * BLK, (rb + 1) * BLK)
        spans = key_spans(row_blocks, slots, rb)
        delta_rows = row_products(do_ref[rows, :], o_ref[rows, :])
        for kb in range(rb + 1, row_blocks):
            for h in range(2):
                side = slice(h * rows_all + rb * BLK, h * rows_all + (rb + 1) * BLK)
                keys = slice(kb * BLK, (kb + 1) * BLK)
                p_ref[keys, side] = jnp.zeros((BLK, BLK), BF16)
                ds_ref[keys, side] = jnp.zeros((BLK, BLK), BF16)
        for h in range(2):
            side = slice(h * rows_all + rb * BLK, h * rows_all + (rb + 1) * BLK)
            delta_row = delta_rows[h]
            lse = lse_ref[0, h : h + 1, rows]
            for first, end in spans:
                products = dot_nt(kz_ref[h, first:end, :], q_ref[rows, :])
                grad_products = dot_nt(vz_ref[h, first:end, :], do_ref[rows, :])
                for kb in range(first // BLK, end // BLK):
                    keys = slice(kb * BLK, (kb + 1) * BLK)
                    inner = slice(kb * BLK - first, (kb + 1) * BLK - first)
                    at, delta = tile_at(row_blocks, rb, kb)
                    probs = jnp.exp(products[inner, :] + tile_ref[h, at] - lse)
                    grad_scores = probs * (grad_products[inner, :] - delta_row)
                    p_ref[keys, side] = probs.astype(BF16)
                    ds_ref[keys, side] = grad_scores.astype(BF16)
                    if (h, delta) in seen:
                        sum_ref[h, delta] += grad_scores
                    else:
                        sum_ref[h, delta] = grad_scores
                        seen.add((h, delta))
    grad_v = dot_nn(p_ref[...], dop_ref[...])
    grad_k = dot_nn(ds_ref[...], qp_ref[...])

    @pl.when(parity == 0)
    def first():
        dv_acc[...] = grad_v
        dk_acc[...] = grad_k

    @pl.when(parity == 1)
    def second():
        dv_acc[...] += grad_v
        dk_acc[...] += grad_k

    grad_q = None
    for h in range(2):
        part = dot_nn(kt_ref[h], ds_ref[:, h * rows_all : (h + 1) * rows_all])
        grad_q = part if grad_q is None else grad_q + part
    dq_ref[...] = (grad_q.T * score_scale).astype(BF16)

    diag_ref[...] = jnp.zeros_like(diag_ref)
    for h in range(2):
        for delta in range(row_blocks * slots):
            wide = jnp.concatenate([jnp.zeros((BLK, BLK), F32), sum_ref[h, delta]], axis=1)
            diag_ref[0, h : h + 1, delta * BLK : delta * BLK + 2 * BLK] += diagonal_sums(wide)

    @pl.when(parity == 1)
    def store():
        for slot, pair_ref in enumerate(pair_refs):
            span = slice(slot * rows_all, (slot + 1) * rows_all)
            pair_ref[:, :PAIR] = dk_acc[span, :].astype(BF16)
            pair_ref[:, PAIR:] = dv_acc[span, :].astype(BF16)


def cross_forward_kernel(q_ref, k_ref, v_ref, m_ref, o_ref, ot_ref, lse_ref, kz_ref, vt_ref, s_ref, p_ref):
    parity = lax.rem(pl.program_id(0), 2)
    for h in range(2):
        kz_ref[h] = dot_nn(k_ref[...], lane_pick(parity * HEAD_DIM, h * HEAD_DIM)).astype(BF16)
        vt_ref[h] = dot_nt(lane_pick_t(parity * HEAD_DIM, h * HEAD_DIM), v_ref[...]).astype(BF16)
    for rb in range(q_ref.shape[0] // BLK):
        rows = slice(rb * BLK, (rb + 1) * BLK)
        queries = q_ref[rows, :]
        highest = []
        for h in range(2):
            scores = dot_nt(kz_ref[h], queries) + m_ref[...]
            s_ref[h] = scores
            highest.append(jnp.max(scores, axis=0, keepdims=True))
        mixed_t = None
        for h in range(2):
            weights = jnp.exp(s_ref[h] - highest[h])
            total = jnp.sum(weights, axis=0, keepdims=True)
            p_ref[h] = weights.astype(BF16)
            part = dot_nn(vt_ref[h], p_ref[h]) / total
            mixed_t = part if mixed_t is None else mixed_t + part
            lse_ref[0, h : h + 1, rows] = highest[h] + jnp.log(total)
        ot_ref[:, rows] = mixed_t.astype(BF16)
        o_ref[rows, :] = mixed_t.T.astype(BF16)


def cross_backward_kernel(
    slots,
    q_ref,
    k_ref,
    v_ref,
    m_ref,
    do_ref,
    o_ref,
    lse_ref,
    dq_ref,
    *refs,
):
    pair_refs, refs = refs[:slots], refs[slots:]
    cross_backward_body(slots, pair_refs, q_ref, k_ref, v_ref, m_ref, do_ref, o_ref, lse_ref, dq_ref, *refs)


def cross_backward_body(
    slots,
    pair_refs,
    q_ref,
    k_ref,
    v_ref,
    m_ref,
    do_ref,
    o_ref,
    lse_ref,
    dq_ref,
    kz_ref,
    kt_ref,
    vz_ref,
    qp_ref,
    dop_ref,
    dk_acc,
    dv_acc,
    p_ref,
    ds_ref,
):
    parity = lax.rem(pl.program_id(0), 2)
    rows_all = q_ref.shape[0]
    for h in range(2):
        in_pick = lane_pick(parity * HEAD_DIM, h * HEAD_DIM)
        out_pick = lane_pick(h * HEAD_DIM, parity * HEAD_DIM)
        kz_ref[h] = dot_nn(k_ref[...], in_pick).astype(BF16)
        kt_ref[h] = dot_nt(lane_pick_t(parity * HEAD_DIM, h * HEAD_DIM), k_ref[...]).astype(BF16)
        vz_ref[h] = dot_nn(v_ref[...], in_pick).astype(BF16)
        side = slice(h * rows_all, (h + 1) * rows_all)
        qp_ref[side, :] = dot_nn(q_ref[...], out_pick).astype(BF16)
        dop_ref[side, :] = dot_nn(do_ref[...], out_pick).astype(BF16)
    for rb in range(rows_all // BLK):
        rows = slice(rb * BLK, (rb + 1) * BLK)
        delta_rows = row_products(do_ref[rows, :], o_ref[rows, :])
        for h in range(2):
            side = slice(h * rows_all + rb * BLK, h * rows_all + (rb + 1) * BLK)
            delta_row = delta_rows[h]
            lse = lse_ref[0, h : h + 1, rows]
            probs = jnp.exp(dot_nt(kz_ref[h], q_ref[rows, :]) + m_ref[...] - lse)
            grad_products = dot_nt(vz_ref[h], do_ref[rows, :])
            p_ref[:, side] = probs.astype(BF16)
            ds_ref[:, side] = (probs * (grad_products - delta_row)).astype(BF16)
    grad_v = dot_nn(p_ref[...], dop_ref[...])
    grad_k = dot_nn(ds_ref[...], qp_ref[...])

    @pl.when(parity == 0)
    def first():
        dv_acc[...] = grad_v
        dk_acc[...] = grad_k

    @pl.when(parity == 1)
    def second():
        all_k = (dk_acc[...] + grad_k).astype(BF16)
        all_v = (dv_acc[...] + grad_v).astype(BF16)
        size = all_k.shape[0] // slots
        for slot, pair_ref in enumerate(pair_refs):
            pair_ref[:, :PAIR] = all_k[slot * size : (slot + 1) * size]
            pair_ref[:, PAIR:] = all_v[slot * size : (slot + 1) * size]

    grad_q = None
    for h in range(2):
        part = dot_nn(kt_ref[h], ds_ref[:, h * rows_all : (h + 1) * rows_all])
        grad_q = part if grad_q is None else grad_q + part
    dq_ref[...] = (grad_q.T * score_scale).astype(BF16)


def shape_of(shape, dtype):
    return jax.ShapeDtypeStruct(shape, dtype)


def tile_pair(rows):
    return pl.BlockSpec((rows, PAIR), lambda g: (0, g))


def tile_pair_t(rows):
    return pl.BlockSpec((PAIR, rows), lambda g: (g, 0))


def tile_group(rows):
    return pl.BlockSpec((rows, PAIR), lambda g: (0, g // 2))


def tile_both(rows):
    return pl.BlockSpec((rows, 2 * PAIR), lambda g: (0, g // 2))


def tile_rows(width):
    return pl.BlockSpec((1, 2, width), lambda g: (g, 0, 0))


def kernel_params():
    return pltpu.CompilerParams(
        dimension_semantics=("arbitrary",), vmem_limit_bytes=VMEM_LIMIT
    )


def cost(flops, transcendentals, nbytes):
    return pl.CostEstimate(
        flops=int(flops) // 16, transcendentals=0, bytes_accessed=int(nbytes) // 16
    )


def self_forward(place, q, ks, vs, bias_vec):
    rows, width = q.shape
    slots = len(ks)
    keys = rows * slots
    pairs = width // PAIR
    tiles = len(tile_plan(rows // BLK, slots))
    return pl.pallas_call(
        functools.partial(self_forward_kernel, slots),
        grid=(pairs,),
        in_specs=[pl.BlockSpec(memory_space=pltpu.SMEM), tile_pair(rows), tile_rows(bias_vec.shape[2])]
        + [tile_group(rows)] * (2 * slots),
        out_specs=[tile_pair(rows), tile_pair_t(rows), tile_rows(rows)],
        out_shape=[
            shape_of((rows, width), BF16),
            shape_of((width, rows), BF16),
            shape_of((pairs, 2, rows), F32),
        ],
        scratch_shapes=[
            pltpu.VMEM((2, tiles, BLK, BLK), F32),
            pltpu.VMEM((2, keys, PAIR), BF16),
            pltpu.VMEM((2, PAIR, keys), BF16),
            pltpu.VMEM((2, keys, BLK), F32),
            pltpu.VMEM((2, keys, BLK), BF16),
        ],
        compiler_params=kernel_params(),
        cost_estimate=cost(4 * 2 * rows * keys * width * 2, pairs * 2 * rows * keys, 8 * rows * width),
        name="self_forward",
    )(place, q, bias_vec, *ks, *vs)


def self_backward(place, q, ks, vs, bias_vec, grads, mixed, lse):
    rows, width = q.shape
    kv_width = ks[0].shape[1]
    slots = len(ks)
    keys = rows * slots
    pairs = width // PAIR
    tiles = len(tile_plan(rows // BLK, slots))
    grad_q, diagonals, *pairs_out = pl.pallas_call(
        functools.partial(self_backward_kernel, slots),
        grid=(pairs,),
        in_specs=[
            pl.BlockSpec(memory_space=pltpu.SMEM),
            tile_pair(rows),
            tile_rows(bias_vec.shape[2]),
            tile_pair(rows),
            tile_pair(rows),
            tile_rows(rows),
        ]
        + [tile_group(rows)] * (2 * slots),
        out_specs=[tile_pair(rows), tile_rows(bias_vec.shape[2])] + [tile_both(rows)] * slots,
        out_shape=[shape_of((rows, width), BF16), shape_of(bias_vec.shape, F32)]
        + [shape_of((rows, 2 * kv_width), BF16)] * slots,
        scratch_shapes=[
            pltpu.VMEM((2, tiles, BLK, BLK), F32),
            pltpu.VMEM((2, keys // BLK, BLK, BLK), F32),
            pltpu.VMEM((2, keys, PAIR), BF16),
            pltpu.VMEM((2, PAIR, keys), BF16),
            pltpu.VMEM((2, keys, PAIR), BF16),
            pltpu.VMEM((2 * rows, PAIR), BF16),
            pltpu.VMEM((2 * rows, PAIR), BF16),
            pltpu.VMEM((keys, PAIR), F32),
            pltpu.VMEM((keys, PAIR), F32),
            pltpu.VMEM((keys, 2 * rows), BF16),
            pltpu.VMEM((keys, 2 * rows), BF16),
        ],
        compiler_params=kernel_params(),
        cost_estimate=cost(10 * 2 * rows * keys * width * 2, pairs * 2 * rows * keys, 12 * rows * width),
        name="self_backward",
    )(place, q, bias_vec, grads, mixed, lse, *ks, *vs)
    return grad_q, pairs_out, diagonals


def cross_forward(q, k, v, mask_col):
    rows, width = q.shape
    keys = k.shape[0]
    pairs = width // PAIR
    return pl.pallas_call(
        cross_forward_kernel,
        grid=(pairs,),
        in_specs=[
            tile_pair(rows),
            tile_group(keys),
            tile_group(keys),
            pl.BlockSpec((keys, 1), lambda g: (0, 0)),
        ],
        out_specs=[tile_pair(rows), tile_pair_t(rows), tile_rows(rows)],
        out_shape=[
            shape_of((rows, width), BF16),
            shape_of((width, rows), BF16),
            shape_of((pairs, 2, rows), F32),
        ],
        scratch_shapes=[
            pltpu.VMEM((2, keys, PAIR), BF16),
            pltpu.VMEM((2, PAIR, keys), BF16),
            pltpu.VMEM((2, keys, BLK), F32),
            pltpu.VMEM((2, keys, BLK), BF16),
        ],
        compiler_params=kernel_params(),
        cost_estimate=cost(4 * 2 * rows * keys * width * 2, pairs * 2 * rows * keys, 8 * rows * width),
        name="cross_forward",
    )(q, k, v, mask_col)


def cross_backward(q, k, v, mask_col, grads, mixed, lse, slots):
    rows, width = q.shape
    keys, kv_width = k.shape
    pairs = width // PAIR
    grad_q, *pairs_out = pl.pallas_call(
        functools.partial(cross_backward_kernel, slots),
        grid=(pairs,),
        in_specs=[
            tile_pair(rows),
            tile_group(keys),
            tile_group(keys),
            pl.BlockSpec((keys, 1), lambda g: (0, 0)),
            tile_pair(rows),
            tile_pair(rows),
            tile_rows(rows),
        ],
        out_specs=[tile_pair(rows)] + [tile_both(keys // slots)] * slots,
        out_shape=[shape_of((rows, width), BF16)] + [shape_of((keys // slots, 2 * kv_width), BF16)] * slots,
        scratch_shapes=[
            pltpu.VMEM((2, keys, PAIR), BF16),
            pltpu.VMEM((2, PAIR, keys), BF16),
            pltpu.VMEM((2, keys, PAIR), BF16),
            pltpu.VMEM((2 * rows, PAIR), BF16),
            pltpu.VMEM((2 * rows, PAIR), BF16),
            pltpu.VMEM((keys, PAIR), F32),
            pltpu.VMEM((keys, PAIR), F32),
            pltpu.VMEM((keys, 2 * rows), BF16),
            pltpu.VMEM((keys, 2 * rows), BF16),
        ],
        compiler_params=kernel_params(),
        cost_estimate=cost(10 * 2 * rows * keys * width * 2, pairs * 2 * rows * keys, 12 * rows * width),
        name="cross_backward",
    )(q, k, v, mask_col, grads, mixed, lse)
    return grad_q, pairs_out


FBLK = 256


def ffn_kernel(
    orders,
    where_ref,
    x_ref,
    xt_ref,
    og_ref,
    wg_any,
    wu_any,
    wd_any,
    ht_any,
    e_any,
    out_mine_any,
    out_other_any,
    gate_keep_any,
    gate_send_any,
    up_keep_any,
    up_send_any,
    wg_ref,
    wu_ref,
    wd_ref,
    xs_ref,
    hb_ref,
    gg_ref,
    gu_ref,
    ht_ref,
    e_ref,
    out_ref,
    product_ref,
    in_sems,
    out_sems,
):
    hidden_width = gg_ref.shape[1]
    base = where_ref[0] * hidden_width
    spans = [(first, min(FBLK, hidden_width - first)) for first in range(0, hidden_width, FBLK)]
    loads = []
    for k, (first, size) in enumerate(spans):
        away = pl.ds(pl.multiple_of(base + first, 128), size)
        near = slice(first, first + size)
        loads.append(
            [
                pltpu.make_async_copy(wg_any.at[:, away], wg_ref.at[:, near], in_sems.at[0, k]),
                pltpu.make_async_copy(wu_any.at[:, away], wu_ref.at[:, near], in_sems.at[1, k]),
                pltpu.make_async_copy(wd_any.at[away, :], wd_ref.at[near, :], in_sems.at[2, k]),
            ]
        )
    for group in loads:
        for load in group:
            load.start()
    chips = len(orders[0][0])
    block = xt_ref.shape[0] // chips
    for order in range(2):
        for p in range(chips):
            first = pl.multiple_of(chip_at(orders[order], p, where_ref) * block, block)
            xs_ref[order, p * block : (p + 1) * block, :] = xt_ref[pl.ds(first, block), :]
    factor = (2.0 / jnp.pi) ** 0.5

    def combine(span, gate, up, grad_hidden):
        square = gate * gate
        bend = jnp.tanh(gate * (factor + (factor * 0.044715) * square))
        half = 0.5 + 0.5 * bend
        gelu = gate * half
        slope = half + gelu * (1.0 - bend) * (factor + (factor * 3 * 0.044715) * square)
        hidden = gelu * up
        hb_ref[:, span] = hidden.astype(BF16)
        ht_ref[span, :] = hidden.T.astype(BF16)
        gg_ref[:, span] = (grad_hidden * up * slope).astype(BF16)
        gu_ref[:, span] = (grad_hidden * gelu).astype(BF16)

    waiting = None
    for (first, size), group in zip(spans, loads):
        span = slice(first, first + size)
        for load in group:
            load.wait()
        gate = dot_nn(x_ref[...], wg_ref[:, span])
        up = dot_nn(x_ref[...], wu_ref[:, span])
        grad_hidden = dot_nt(og_ref[...], wd_ref[span, :])
        if waiting is not None:
            combine(*waiting)
        waiting = (span, gate, up, grad_hidden)
    combine(*waiting)
    stores = [pltpu.make_async_copy(ht_ref, ht_any, out_sems.at[0])]
    stores[-1].start()
    e_ref[...] = (dot_nt(gg_ref[...], wg_ref[...]) + dot_nt(gu_ref[...], wu_ref[...])).astype(BF16)
    stores.append(pltpu.make_async_copy(e_ref, e_any, out_sems.at[1]))
    stores[-1].start()
    middle = xt_ref.shape[0] // 2
    outs = [
        (0, gg_ref, middle, gate_send_any),
        (1, gu_ref, middle, up_send_any),
        (0, gg_ref, 0, gate_keep_any),
        (1, gu_ref, 0, up_keep_any),
    ]
    for k, (order, right_ref, first, any_ref) in enumerate(outs):
        product_ref[k] = dot_nn(xs_ref[order, first : first + middle, :], right_ref[...]).astype(BF16)
        stores.append(pltpu.make_async_copy(product_ref.at[k], any_ref, out_sems.at[2 + k]))
        stores[-1].start()
    out_ref[...] = dot_nn(hb_ref[...], wd_ref[...]).astype(BF16)
    half = out_ref.shape[0] // 2
    for k, (which, any_ref) in enumerate(((where_ref[0], out_mine_any), (1 - where_ref[0], out_other_any))):
        source = out_ref.at[pl.ds(pl.multiple_of(which * half, half), half), :]
        stores.append(pltpu.make_async_copy(source, any_ref, out_sems.at[6 + k]))
        stores[-1].start()
    for store in stores:
        store.wait()


def ffn(where, normed, normed_t, out_grad, w_gate, w_up, w_down, orders):
    rows, width = normed.shape
    hidden = w_gate.shape[1] // 2
    chunks = -(-hidden // FBLK)
    whole = pl.BlockSpec(memory_space=pltpu.VMEM)
    anywhere = pl.BlockSpec(memory_space=pl.ANY)
    half = (width // 2, hidden)
    return pl.pallas_call(
        functools.partial(ffn_kernel, orders),
        in_specs=[pl.BlockSpec(memory_space=pltpu.SMEM), whole, whole, whole] + [anywhere] * 3,
        out_specs=[anywhere] * 8,
        out_shape=[
            shape_of((hidden, rows), BF16),
            shape_of((rows, width), BF16),
            shape_of((rows // 2, width), BF16),
            shape_of((rows // 2, width), BF16),
        ]
        + [shape_of(half, BF16)] * 4,
        scratch_shapes=[
            pltpu.VMEM((width, hidden), BF16),
            pltpu.VMEM((width, hidden), BF16),
            pltpu.VMEM((hidden, width), BF16),
            pltpu.VMEM((2, width, rows), BF16),
            pltpu.VMEM((rows, hidden), BF16),
            pltpu.VMEM((rows, hidden), BF16),
            pltpu.VMEM((rows, hidden), BF16),
            pltpu.VMEM((hidden, rows), BF16),
            pltpu.VMEM((rows, width), BF16),
            pltpu.VMEM((rows, width), BF16),
            pltpu.VMEM((4, *half), BF16),
            pltpu.SemaphoreType.DMA((3, chunks)),
            pltpu.SemaphoreType.DMA((8,)),
        ],
        compiler_params=pltpu.CompilerParams(vmem_limit_bytes=VMEM_LIMIT),
        cost_estimate=cost(2 * 9 * rows * width * hidden, rows * hidden, 6 * width * hidden),
        name="ffn",
    )(where, normed, normed_t, out_grad, w_gate, w_up, w_down)


ROWS = 256


def tile_of(local):
    return min(local, ROWS)


def in_own_half(core_ref):
    return core_ref[0] == pl.program_id(0) // (pl.num_programs(0) // 2)


def within_half(local, width):
    steps = local // tile_of(local)
    return pl.BlockSpec((tile_of(local), width), lambda i, c: (lax.rem(i, steps), 0))


def normalise(values, gain):
    inverse = lax.rsqrt(jnp.mean(values * values, axis=-1, keepdims=True) + norm_eps)
    return values * inverse * gain


def rms_back(values, gain, grad):
    inverse = lax.rsqrt(jnp.mean(values * values, axis=-1, keepdims=True) + norm_eps)
    scaled = grad * gain
    mean_dot = jnp.mean(values * scaled, axis=-1, keepdims=True)
    unit = values * inverse
    return inverse * (scaled - unit * (inverse * mean_dot))


def project_kernel(scales, core_ref, own_ref, other_ref, gain_ref, *refs):
    count = len(scales)
    w_refs, nt_ref, out_refs = refs[:count], refs[count], refs[count + 1 :]
    values = jnp.where(in_own_half(core_ref), own_ref[...], other_ref[...]).astype(F32)
    normed = normalise(values, gain_ref[...])
    nt_ref[...] = normed.T.astype(BF16)
    low = normed.astype(BF16)
    for scale, w_ref, out_ref in zip(scales, w_refs, out_refs):
        out = dot_nn(low, w_ref[...]).astype(BF16)
        out_ref[...] = out if scale is None else out * BF16(scale)


def own_columns(weight):
    return pl.BlockSpec((weight.shape[0], weight.shape[1] // 2), lambda i, c: (0, c[0]))


def other_columns(weight):
    return pl.BlockSpec((weight.shape[0], weight.shape[1] // 2), lambda i, c: (0, 1 - c[0]))


def own_rows(array):
    return pl.BlockSpec((array.shape[0] // 2, array.shape[1]), lambda i, c: (c[0], 0))


def other_rows(array):
    return pl.BlockSpec((array.shape[0] // 2, array.shape[1]), lambda i, c: (1 - c[0], 0))


def all_of(array):
    return pl.BlockSpec(array.shape, lambda i, c: (0,) * array.ndim)


def half_rows(rows, width):
    return pl.BlockSpec((rows, width), lambda i, c: (i, 0))


def half_columns(width, rows):
    return pl.BlockSpec((width, rows), lambda i, c: (0, i))


def fixed(shape):
    return pl.BlockSpec(shape, lambda i, c: (0,) * len(shape))


def core_call(kernel, steps, core, args, in_specs, out_specs, out_shape, scratch, flops, name):
    return pl.pallas_call(
        kernel,
        grid_spec=pltpu.PrefetchScalarGridSpec(
            num_scalar_prefetch=1,
            grid=(steps,),
            in_specs=in_specs,
            out_specs=out_specs,
            scratch_shapes=scratch,
        ),
        out_shape=out_shape,
        compiler_params=kernel_params(),
        cost_estimate=cost(flops, 0, flops // 400),
        name=name,
    )(core, *args)


def project(core, own, other, gain, weights, scales, name):
    local, width = own.shape
    return core_call(
        functools.partial(project_kernel, scales),
        2 * local // tile_of(local),
        core,
        (own, other, gain, *weights),
        [within_half(local, width)] * 2 + [all_of(gain)] + [own_columns(w) for w in weights],
        [half_columns(width, tile_of(local))] + [half_rows(tile_of(local), w.shape[1] // 2) for w in weights],
        [shape_of((width, 2 * local), BF16)]
        + [shape_of((2 * local, w.shape[1] // 2), BF16) for w in weights],
        [],
        2 * 2 * local * width * sum(w.shape[1] // 2 for w in weights),
        name,
    )


def memory_kernel(parts, core_ref, *refs):
    in_refs = refs[:parts]
    wk_ref, wv_ref = refs[parts : parts + 2]
    mt_refs, (k_ref, v_ref, all_ref) = refs[parts + 2 : -3], refs[-3:]
    rows = in_refs[0].shape[0]
    for i in range(parts):
        all_ref[i * rows : (i + 1) * rows, :] = in_refs[i][...]
    for slot, mt_ref in enumerate(mt_refs):
        mt_ref[...] = all_ref[2 * slot * rows : 2 * (slot + 1) * rows, :].astype(F32).T.astype(BF16)
    k_ref[...] = dot_nn(all_ref[...], wk_ref[...]).astype(BF16)
    v_ref[...] = dot_nn(all_ref[...], wv_ref[...]).astype(BF16)


def project_memory(core, parts, w_key, w_value):
    rows, width = parts[0].shape
    total = rows * len(parts)
    kw = w_key.shape[1] // 2
    return core_call(
        functools.partial(memory_kernel, len(parts)),
        1,
        core,
        (*parts, w_key, w_value),
        [all_of(p) for p in parts] + [own_columns(w_key), own_columns(w_value)],
        [fixed((width, 2 * rows))] * (len(parts) // 2) + [fixed((total, kw)), fixed((total, kw))],
        [shape_of((width, 2 * rows), BF16)] * (len(parts) // 2)
        + [shape_of((total, kw), BF16), shape_of((total, kw), BF16)],
        [pltpu.VMEM((total, width), BF16)],
        2 * total * width * 2 * kw,
        "project_memory",
    )


def join_kernel(low_base, project_next, core_ref, *refs):
    if low_base:
        own_ref, other_ref, refs = refs[0], refs[1], refs[2:]
        base = jnp.where(in_own_half(core_ref), own_ref[...], other_ref[...]).astype(F32)
    else:
        base, refs = refs[0][...], refs[1:]
    mixed_ref, got_ref, w_own_ref, w_other_ref, gain_ref = refs[:5]
    after = base + dot_nn(mixed_ref[...], w_own_ref[...]) + dot_nn(got_ref[...], w_other_ref[...])
    normed = normalise(after, gain_ref[...])
    low = normed.astype(BF16)
    if project_next:
        w_ref, after_ref, nt_ref, out_ref = refs[5:]
        out_ref[...] = dot_nn(low, w_ref[...]).astype(BF16) * BF16(score_scale)
    else:
        after_ref, nt_ref, out_ref = refs[5:]
        out_ref[...] = low
    after_ref[...] = after
    nt_ref[...] = normed.T.astype(BF16)


def join(core, base, mixed, got, w_out, gain, w_next, name):
    rows, half = mixed.shape
    width = w_out.shape[1]
    local = rows // 2
    low_base = isinstance(base, tuple)
    bases = base if low_base else (base,)
    base_specs = [within_half(local, width)] * 2 if low_base else [half_rows(tile_of(local), width)]
    nexts = () if w_next is None else (w_next,)
    out_width = width if w_next is None else w_next.shape[1] // 2
    return core_call(
        functools.partial(join_kernel, low_base, w_next is not None),
        rows // tile_of(local),
        core,
        (*bases, mixed, got, w_out, w_out, gain, *nexts),
        base_specs
        + [half_rows(tile_of(local), half), half_rows(tile_of(local), half), own_rows(w_out), other_rows(w_out), all_of(gain)]
        + [own_columns(w) for w in nexts],
        [half_rows(tile_of(local), width), half_columns(width, tile_of(local)), half_rows(tile_of(local), out_width)],
        [shape_of((rows, width), F32), shape_of((width, rows), BF16), shape_of((rows, out_width), BF16)],
        [],
        2 * rows * width * (width + out_width),
        name,
    )


def back_kernel(low_prior, products, core_ref, *refs):
    if low_prior:
        own_ref, other_ref, refs = refs[0], refs[1], refs[2:]
        prior = jnp.where(in_own_half(core_ref), own_ref[...], other_ref[...]).astype(F32)
    else:
        prior, refs = refs[0][...], refs[1:]
    value_ref, gain_ref, e_ref, got_ref, refs = refs[0], refs[1], refs[2], refs[3], refs[4:]
    if products:
        e = dot_nt(e_ref[...], refs[0][...]) + dot_nt(got_ref[...], refs[1][...])
        refs = refs[2:]
    else:
        e = e_ref[...].astype(F32) + got_ref[...].astype(F32)
    w_ref, grad_ref, half_ref, next_ref = refs
    grad = prior + rms_back(value_ref[...], gain_ref[...], e)
    grad_ref[...] = grad
    low = grad.astype(BF16)
    half = low.shape[1] // 2
    half_ref[...] = jnp.where(core_ref[0] == 0, low[:, :half], low[:, half:])
    next_ref[...] = dot_nt(low, w_ref[...]).astype(BF16)


def back(core, prior, values, gain, e, got, w_in, w_out, name):
    rows, width = values.shape
    local = rows // 2
    low_prior = isinstance(prior, tuple)
    priors = prior if low_prior else (prior,)
    prior_specs = [within_half(local, width)] * 2 if low_prior else [half_rows(tile_of(local), width)]
    ins = () if w_in is None else (w_in, w_in)
    in_specs = [] if w_in is None else [own_columns(w_in), other_columns(w_in)]
    half = w_out.shape[0] // 2
    return core_call(
        functools.partial(back_kernel, low_prior, w_in is not None),
        rows // tile_of(local),
        core,
        (*priors, values, gain, e, got, *ins, w_out),
        prior_specs
        + [half_rows(tile_of(local), width), all_of(gain), half_rows(tile_of(local), e.shape[1]), half_rows(tile_of(local), e.shape[1])]
        + in_specs
        + [own_rows(w_out)],
        [half_rows(tile_of(local), width), half_rows(tile_of(local), width // 2), half_rows(tile_of(local), half)],
        [
            shape_of((rows, width), F32),
            shape_of((rows, width // 2), BF16),
            shape_of((rows, half), BF16),
        ],
        [],
        2 * rows * width * (half + 2 * e.shape[1] * len(ins) // 2),
        name,
    )


def last_kernel(core_ref, prior_ref, base_ref, gain_ref, q_ref, pair_ref, got_ref, *refs):
    wq_own, wq_other, wk_own, wk_other, wv_own, wv_other, grad_ref = refs
    qw = wq_own.shape[1]
    kw = wk_own.shape[1]
    e = dot_nt(q_ref[...], wq_own[...]) + dot_nt(got_ref[:, :qw], wq_other[...])
    for m in range(kw // PAIR):
        c, span = 2 * PAIR * m, slice(PAIR * m, PAIR * (m + 1))
        e = e + dot_nt(pair_ref[:, c : c + PAIR], wk_own[:, span])
        e = e + dot_nt(got_ref[:, qw + c : qw + c + PAIR], wk_other[:, span])
        c = c + PAIR
        e = e + dot_nt(pair_ref[:, c : c + PAIR], wv_own[:, span])
        e = e + dot_nt(got_ref[:, qw + c : qw + c + PAIR], wv_other[:, span])
    grad_ref[...] = prior_ref[...] + rms_back(base_ref[...].astype(F32), gain_ref[...], e)


def last(core, prior, base, gain, grad_q, pair, got, w_query, w_key, w_value):
    local, width = base.shape
    steps = local // tile_of(local)

    def own_tile(array):
        return pl.BlockSpec((tile_of(local), array.shape[1]), lambda i, c: (c[0] * steps + i, 0))

    weights = (w_query, w_query, w_key, w_key, w_value, w_value)
    specs = []
    for w in (w_query, w_key, w_value):
        specs += [own_columns(w), other_columns(w)]
    return core_call(
        last_kernel,
        local // tile_of(local),
        core,
        (prior, base, gain, grad_q, pair, got, *weights),
        [own_tile(prior), half_rows(tile_of(local), width), all_of(gain), own_tile(grad_q), own_tile(pair), half_rows(tile_of(local), got.shape[1])]
        + specs,
        [half_rows(tile_of(local), width)],
        [shape_of((local, width), F32)],
        [],
        2 * local * width * 2 * width,
        "last",
    )


def chip_at(order, p, where):
    masks, core_bit = order
    index = where[2] ^ masks[p]
    return index if core_bit is None else index ^ (where[0] << core_bit)


def outer_kernel(orders, terms, split, count, has_extra, where_ref, *refs):
    lefts = []
    for parts in split:
        lefts.append(refs[:parts])
        refs = refs[parts:]
    right_refs, refs = refs[:count], refs[count:]
    if has_extra:
        extra_ref, refs = refs[0], refs[1:]
    keep_ref, send_ref, sorted_refs = refs[0], refs[1], refs[2:]
    blocks = len(orders[0][0])
    for at, (left, sorted_ref) in enumerate(zip(lefts, sorted_refs)):
        rows = sorted_ref.shape[0] // blocks
        for p in range(blocks):
            index = chip_at(orders[at], p, where_ref)
            if len(left) == 1:
                piece = left[0][pl.ds(pl.multiple_of(index * rows, rows), rows), :]
            else:
                middle = blocks // 2
                first = pl.multiple_of(jnp.minimum(index, middle - 1) * rows, rows)
                second = pl.multiple_of(jnp.maximum(index - middle, 0) * rows, rows)
                piece = jnp.where(
                    index < middle, left[0][pl.ds(first, rows), :], left[1][pl.ds(second, rows), :]
                )
            sorted_ref[p * rows : (p + 1) * rows, :] = piece
    middle = sorted_refs[0].shape[0] // 2
    for out_ref, span in ((send_ref, slice(middle, 2 * middle)), (keep_ref, slice(0, middle))):
        column = 0
        for products in terms:
            total = None
            for left, right, first, start, size in products:
                depth = sorted_refs[left].shape[1]
                factor = right_refs[right][first : first + depth, start : start + size]
                part = dot_nn(sorted_refs[left][span, :], factor)
                total = part if total is None else total + part
            width = total.shape[1]
            out_ref[:, column : column + width] = total.astype(BF16)
            column += width
    if has_extra:
        rows = sorted_refs[0].shape[0] // blocks
        lanes = extra_ref.shape[1]
        row = lax.broadcasted_iota(jnp.int32, (rows, lanes), 0)
        for p in range(blocks):
            index = 2 * chip_at(orders[0], p, where_ref)
            block = jnp.where(row == 0, extra_ref[pl.ds(index, 1), :], 0.0)
            block = jnp.where(row == rows // 2, extra_ref[pl.ds(index + 1, 1), :], block)
            out_ref = keep_ref if p < blocks // 2 else send_ref
            first = p % (blocks // 2) * rows
            out_ref[first : first + rows, column:] = block.astype(BF16)


def outer_halves(where, orders, lefts, rights, terms, extra=None):
    blocks = len(orders[0][0])
    lefts = [v if isinstance(v, tuple) else (v,) for v in lefts]
    totals = [sum(v.shape[0] for v in left) for left in lefts]
    rows = totals[0] // blocks
    if rows % 16:
        joined = [jnp.concatenate(left, axis=0) for left in lefts]
        joined = [
            jnp.concatenate(
                [lax.dynamic_slice_in_dim(v, chip_at(order, p, where) * rows, rows, 0) for p in range(blocks)],
                axis=0,
            )
            for v, order in zip(joined, orders)
        ]
        half = totals[0] // 2
        columns = []
        for products in terms:
            columns.append(
                sum(
                    dot_nn(joined[l], rights[r][first : first + joined[l].shape[1], start : start + size])
                    for l, r, first, start, size in products
                )
            )
        total = jnp.concatenate(columns, axis=1).astype(BF16)
        return total[:half], total[half:]
    width = sum(products[0][4] for products in terms)
    extras = () if extra is None else (extra,)
    if extras:
        width += extra.shape[1]
    half = shape_of((totals[0] // 2, width), BF16)
    flops = 0
    for products in terms:
        for l, _, _, _, size in products:
            flops += 2 * totals[l] * lefts[l][0].shape[1] * size
    whole = pl.BlockSpec(memory_space=pltpu.VMEM)
    flat = [v for left in lefts for v in left]
    return pl.pallas_call(
        functools.partial(outer_kernel, orders, terms, [len(left) for left in lefts], len(rights), bool(extras)),
        in_specs=[pl.BlockSpec(memory_space=pltpu.SMEM)] + [whole] * (len(flat) + len(rights) + len(extras)),
        out_specs=[whole, whole],
        out_shape=[half, half],
        scratch_shapes=[
            pltpu.VMEM((total, left[0].shape[1]), BF16) for total, left in zip(totals, lefts)
        ],
        compiler_params=pltpu.CompilerParams(vmem_limit_bytes=VMEM_LIMIT),
        cost_estimate=cost(flops, 0, flops // 400),
        name="outer_halves",
    )(where, *flat, *rights, *extras)


def pick(value, index, axis):
    return lax.dynamic_index_in_dim(value, index, axis, keepdims=False)


def bits_of(size):
    return (size - 1).bit_length()


class Places:
    def __init__(self):
        self.seq = lax.axis_size("seq")
        self.dp = lax.axis_size("dp")
        self.nx = self.seq // 2
        self.chips = self.dp * self.nx
        place = lax.axis_index("seq")
        self.core = place & 1
        self.x = place >> 1
        self.d = lax.axis_index("dp")
        self.dp_bits = bits_of(self.dp)
        self.x_bits = bits_of(self.nx)
        self.chip = self.d * self.nx + self.x
        self.names = [("dp", b) for b in reversed(range(self.dp_bits))] + [
            ("x", b) for b in reversed(range(self.x_bits))
        ]

    def swap_core(self, value):
        return lax.ppermute(value, "seq", [(s, s ^ 1) for s in range(self.seq)])

    def shift_x(self, value, by):
        pairs = [(s, (s + 2 * by) % self.seq) for s in range(self.seq)]
        return lax.ppermute(value, "seq", pairs)

    def flip(self, value, names):
        d_mask = sum(1 << bit for axis, bit in names if axis == "dp")
        s_mask = sum(2 << bit for axis, bit in names if axis == "x")
        pairs = [
            (d * self.seq + s, (d ^ d_mask) * self.seq + (s ^ s_mask))
            for d in range(self.dp)
            for s in range(self.seq)
        ]
        return lax.ppermute(value, ("dp", "seq"), pairs)

    def by_core(self, own, other, axis):
        first = jnp.concatenate([own, other], axis=axis)
        second = jnp.concatenate([other, own], axis=axis)
        return jnp.where(self.core == 0, first, second)

    def core_rows(self, value, mine):
        half = value.shape[0] // 2
        which = self.core if mine else 1 - self.core
        return lax.dynamic_slice_in_dim(value, which * half, half, 0)

    def stages(self, kind):
        dp0 = [(("dp", 0),)]
        rest = [(("dp", b),) for b in range(1, self.dp_bits)]
        xs = [(("x", b),) for b in range(self.x_bits)]
        at_once = [tuple(one[0] for one in rest)] if len(rest) == 2 else rest
        z1, z2 = rest[:1], rest[1:]
        return {
            "x_y_z1_z2": xs + dp0 + z1 + z2,
            "y_x_z1_z2": dp0 + xs + z1 + z2,
            "y_x_zz": dp0 + xs + at_once,
            "z1_x_wait_z2_y": z1 + xs + [()] + z2 + dp0,
            "x_z1_y_z2": xs + z1 + dp0 + z2,
            "z1_x_y_z2": z1 + xs + dp0 + z2,
        }[kind]

    def block_order(self, kind, core_major=False):
        order = [name for stage in self.stages(kind) for name in stage]
        count = len(order)
        masks = []
        for p in range(self.chips):
            mask = 0
            for k, name in enumerate(order):
                if (p >> (count - 1 - k)) & 1:
                    mask |= 1 << (count - 1 - self.names.index(name))
            masks.append(mask)
        return tuple(masks), count - 1 if core_major else None


class ChipSum:
    def __init__(self, at, kind, kept, sent=None):
        self.at = at
        self.todo = list(at.stages(kind))
        self.rows, self.width = kept.shape
        self.parts = [([kept], 0)]
        self.sent = sent
        if sent is not None:
            self.parts.append(([at.flip(sent, self.todo.pop(0))], 0))

    def result(self):
        return sum(
            box[0][: self.rows, column : column + self.width].astype(F32) for box, column in self.parts
        )


def fold_kernel(plan, count, *refs):
    in_refs, out_refs = refs[:count], refs[count:]
    for sources, (out, out_column), (rows, width) in plan:
        step = 32 if rows % 32 == 0 else 16

        def body(i, carried, sources=sources, out=out, out_column=out_column, width=width, step=step):
            span = pl.ds(pl.multiple_of(i * step, 16), step)
            total = None
            for at, column in sources:
                part = in_refs[at][span, column : column + width].astype(F32)
                total = part if total is None else total + part
            out_refs[out][span, out_column : out_column + width] = total.astype(BF16)
            return carried

        lax.fori_loop(0, rows // step, body, 0)


def fold_arrays(plan, inputs, shapes):
    if all(rows % 16 == 0 for _, _, (rows, _) in plan):
        return pl.pallas_call(
            functools.partial(fold_kernel, plan, len(inputs)),
            grid=(1,),
            in_specs=[
                pl.BlockSpec((rows, array.shape[1]), lambda i, block=block: (block, 0))
                for array, block, rows in inputs
            ],
            out_specs=[pl.BlockSpec(shape, lambda i: (0, 0)) for shape in shapes],
            out_shape=[shape_of(shape, BF16) for shape in shapes],
            compiler_params=kernel_params(),
            cost_estimate=cost(1, 0, 1),
            name="fold",
        )(*[array for array, _, _ in inputs])
    outs = [jnp.zeros(shape, BF16) for shape in shapes]
    for sources, (out, out_column), (rows, width) in plan:
        total = 0.0
        for at, column in sources:
            array, block, size = inputs[at]
            total = total + array[block * size : (block + 1) * size, column : column + width].astype(F32)
        outs[out] = outs[out].at[:, out_column : out_column + width].set(total.astype(BF16))
    return outs


def fold(at, sums, *ties):
    inputs, plan, shapes, sends = [], [], [], {}

    def place_of(array, block, rows):
        for index, known in enumerate(inputs):
            if known[0] is array and known[1:] == (block, rows):
                return index
        inputs.append((array, block, rows))
        return len(inputs) - 1

    for one in sums:
        stage = one.todo.pop(0) if one.todo else ()
        one.rows >>= len(stage)
        for j in range(1, 1 << len(stage)):
            names = tuple(name for k, name in enumerate(stage) if (j >> (len(stage) - 1 - k)) & 1)
            sources = [(place_of(box[0], j, one.rows), column) for box, column in one.parts]
            sends.setdefault((names, one.rows), []).append((one, sources))
    for (names, rows), pieces in sends.items():
        column = 0
        for one, sources in pieces:
            plan.append((sources, (len(shapes), column), (rows, one.width)))
            column += one.width
        shapes.append((rows, column))
    outs = list(fold_arrays(plan, inputs, shapes))
    if ties:
        outs = together(*outs, *ties)
        outs, ties = list(outs[: len(shapes)]), outs[len(shapes) :]
    for out, ((names, rows), pieces) in zip(outs, sends.items()):
        box = [at.flip(out, names)]
        column = 0
        for one, _ in pieces:
            one.sent = out
            one.parts.append((box, column))
            column += one.width
    return ties


def settle(sums, *values):
    boxes = []
    for one in sums:
        for box, _ in one.parts[1:]:
            if not any(box is known for known in boxes):
                boxes.append(box)
    out = together(*[box[0] for box in boxes], *values)
    for box, value in zip(boxes, out):
        box[0] = value
    return out[len(boxes) :]


def finish_sum_kernel(plan, count, where_ref, *refs):
    in_refs, refs = refs[:count], refs[count:]
    out_refs, total_refs = refs[: 2 * len(plan)], refs[2 * len(plan) :]
    for at, ranges in enumerate(plan):
        mine_ref, other_ref, total_ref = out_refs[2 * at], out_refs[2 * at + 1], total_refs[at]
        first = 0
        for sources, width in ranges:
            total = None
            for index, column in sources:
                part = in_refs[index][:, column : column + width].astype(F32)
                total = part if total is None else total + part
            total_ref[:, first : first + width] = total
            first += width
        half = mine_ref.shape[0]
        core = where_ref[0]
        mine_ref[...] = total_ref[pl.ds(pl.multiple_of(core * half, half), half), :]
        other_ref[...] = total_ref[pl.ds(pl.multiple_of((1 - core) * half, half), half), :]


def finish_sums(places, where, groups):
    if any(group[0].rows % 32 and group[0].rows % 16 for group in groups):
        outs = []
        for group in groups:
            total = jnp.concatenate([one.result() for one in group], axis=1)
            outs.append((places.core_rows(total, True), places.core_rows(total, False)))
        return outs
    inputs, plan = [], []

    def place_of(array, rows):
        for index, known in enumerate(inputs):
            if known[0] is array and known[1] == rows:
                return index
        inputs.append((array, rows))
        return len(inputs) - 1

    shapes, scratch = [], []
    for group in groups:
        ranges = []
        for one in group:
            ranges.append(
                ([(place_of(box[0], one.rows), column) for box, column in one.parts], one.width)
            )
        plan.append(ranges)
        width = sum(one.width for one in group)
        shapes += [(group[0].rows // 2, width)] * 2
        scratch.append(pltpu.VMEM((group[0].rows, width), F32))
    outs = core_call(
        functools.partial(finish_sum_kernel, plan, len(inputs)),
        1,
        where,
        [array for array, _ in inputs],
        [pl.BlockSpec((rows, array.shape[1]), lambda i, c: (0, 0)) for array, rows in inputs],
        [fixed(shape) for shape in shapes],
        [shape_of(shape, F32) for shape in shapes],
        scratch,
        16,
        "finish_sums",
    )
    return [(outs[2 * k], outs[2 * k + 1]) for k in range(len(groups))]


def finish_kernel(plan, gains, count, bias_at, where_ref, *refs):
    group_refs, refs = refs[: 2 * count], refs[2 * count :]
    weights = sum(len(pairs) for pairs in gains)
    weight_refs, gain_ref, bias_out, refs = refs[:weights], refs[weights], refs[weights + 1], refs[weights + 2 :]
    out_refs, gain_outs = refs[: len(plan)], refs[len(plan) :]
    span = slice(bias_at, bias_at + bias_out.shape[1])
    bias_out[...] = group_refs[0][0:1, span] + group_refs[1][0:1, span]
    first_core = where_ref[0] == 0
    for (group, column, width), out_ref in zip(plan, out_refs):
        mine = group_refs[2 * group][:, column : column + width]
        got = group_refs[2 * group + 1][:, column : column + width]
        out_ref[:, :width] = jnp.where(first_core, mine, got)
        out_ref[:, width:] = jnp.where(first_core, got, mine)
    at = 0
    for k, (pairs, gain_out) in enumerate(zip(gains, gain_outs)):
        total = None
        for matrix in pairs:
            product = out_refs[matrix][...] * weight_refs[at][...].astype(F32)
            at += 1
            part = product[:, :PAIR]
            for first in range(PAIR, product.shape[1], PAIR):
                part = part + product[:, first : first + PAIR]
            total = part if total is None else total + part
        gain_out[0] = jnp.sum(total.T, axis=0, keepdims=True) / gain_ref[k, 0]


def finish(places, where, joined, plan, gains, gain_rows, bias_at, bias_share):
    half = joined[0][0].shape[0]
    device = 2 * places.chip + places.core
    if half % 16:
        outs = []
        for group, column, width in plan:
            mine, got = joined[group]
            outs.append(places.by_core(mine[:, column : column + width], got[:, column : column + width], 1))
        shares = []
        for gain, pairs in gains:
            total = 0.0
            for matrix, weight in pairs:
                rows = lax.dynamic_slice_in_dim(weight, device * half, half, 0).astype(F32)
                total = total + jnp.sum(rows * outs[matrix], axis=1)
            shares.append(total / pick(gain_rows[gain], device, 0)[0])
        span = slice(bias_at, bias_at + bias_share)
        return outs, shares, joined[0][0][0, span] + joined[0][1][0, span]
    flat = [v for pair in joined for v in pair]
    weights = [weight for _, pairs in gains for _, weight in pairs]
    outs = core_call(
        functools.partial(finish_kernel, plan, [[matrix for matrix, _ in pairs] for _, pairs in gains], len(joined), bias_at),
        1,
        where,
        (*flat, *weights, gain_rows),
        [all_of(v) for v in flat]
        + [pl.BlockSpec((half, w.shape[1]), lambda i, c: (c[1], 0)) for w in weights]
        + [pl.BlockSpec((len(gains), 1, 1, half), lambda i, c: (0, c[1], 0, 0))],
        [fixed((1, bias_share))]
        + [fixed((joined[group][0].shape[0], 2 * width)) for group, _, width in plan]
        + [fixed((1, 1, half)) for _ in gains],
        [shape_of((1, bias_share), F32)]
        + [shape_of((joined[group][0].shape[0], 2 * width), F32) for group, _, width in plan]
        + [shape_of((1, 1, half), F32) for _ in gains],
        [],
        16,
        "finish",
    )
    bias, outs = outs[0].reshape(bias_share), outs[1:]
    return outs[: len(plan)], [v.reshape(half) for v in outs[len(plan) :]], bias


def together(*values):
    return lax.optimization_barrier(values)


def per_device(
    target,
    memory,
    mem_lengths,
    mem_mask,
    distance_buckets,
    norm_self,
    w_query,
    w_key,
    w_value,
    w_out,
    pos_table,
    norm_cross,
    wc_query,
    wc_key,
    wc_value,
    wc_out,
    norm_ffn,
    w_gate,
    w_up,
    w_down,
    out_grad,
):
    at = Places()
    core, nx = at.core, at.nx
    local, width = target.shape[1], target.shape[2]
    mem_local = memory.shape[1]
    rows = 2 * local
    full = distance_buckets.shape[0]
    qw = HEADS * HEAD_DIM // 2
    kw = KV * HEAD_DIM // 2
    head_count = HEADS // 2
    place = at.x.astype(jnp.int32).reshape(1)
    core_arg = core.astype(jnp.int32).reshape(1)
    gain_self = norm_self.reshape(1, width)
    gain_cross = norm_cross.reshape(1, width)
    gain_ffn = norm_ffn.reshape(1, width)

    tokens = target.reshape(local, width)
    far_tokens = [at.shift_x(tokens, s) for s in range(1, nx)]
    tokens_got = at.swap_core(tokens)
    memories = memory.reshape(mem_local, width)
    far_memories = [at.shift_x(memories, s) for s in range(1, nx)]
    memories_got = at.swap_core(memories)
    grads = out_grad.reshape(local, width)
    grads_got = at.swap_core(grads)
    grad_chip = at.by_core(grads, grads_got, 0)

    own_table = lax.dynamic_slice_in_dim(pos_table, core * head_count, head_count, 0)
    onehot = (distance_buckets[:, None] == jnp.arange(BUCKETS, dtype=jnp.int32)[None, :]).astype(F32)
    by_distance = lax.dot_general(
        own_table, onehot, (((1,), (1,)), ((), ())), precision=lax.Precision.HIGHEST
    )
    bias_vec = jnp.pad(by_distance, ((0, 0), (BLK, 0))).reshape(head_count // 2, 2, BLK + full)

    mem_ids = jnp.arange(mem_mask.shape[1], dtype=jnp.int32)
    valid = (mem_ids < mem_lengths[0]) & ((mem_mask[0] == 1) | (mem_ids == 0))
    mask_add = jnp.where(valid, 0.0, big_negative).astype(F32).reshape(2 * nx, mem_local)
    slot_of = jnp.array([s for s in range(nx) for c in range(2)], jnp.int32)
    core_of = jnp.array([c for s in range(nx) for c in range(2)], jnp.int32)
    mask_rows = (((at.x - slot_of + nx) % nx) * 2 + (core ^ core_of))[:, None] == jnp.arange(2 * nx)[None, :]
    mask_col = jnp.sum(jnp.where(mask_rows[:, :, None], mask_add[None], 0.0), axis=1).reshape(-1, 1)

    normed_t, query, keys, values = project(
        core_arg, tokens, tokens_got, gain_self, (w_query, w_key, w_value), (score_scale, None, None), "project"
    )
    grad_half = lax.dynamic_slice_in_dim(grad_chip, core * (width // 2), width // 2, 1)
    where = jnp.stack([core, 2 * at.chip + core, at.chip]).astype(jnp.int32)
    gain_rows = jnp.stack([norm_ffn, norm_cross, norm_self]).reshape(3, 2 * at.chips, 1, -1)
    tied = together(*far_tokens, query, grad_chip, grad_half, bias_vec, mask_col, where, gain_rows)
    far_tokens = list(tied[: nx - 1])
    grad_chip, grad_half, bias_vec, mask_col, where, gain_rows = tied[nx:]
    keys, values, normed_ts = [keys], [values], [normed_t]
    for far in far_tokens:
        far_t, far_k, far_v = project(
            core_arg, far, at.swap_core(far), gain_self, (w_key, w_value), (None, None), "project_far"
        )
        normed_ts.append(far_t)
        keys.append(far_k)
        values.append(far_v)

    mixed, mixed_t, lse_self = self_forward(place, query, keys, values, bias_vec)
    mixed, mixed_t, memories_got, *far_memories = together(mixed, mixed_t, memories_got, *far_memories)
    mem_parts = [memories, memories_got]
    for far in far_memories:
        mem_parts += [far, at.swap_core(far)]
    *mem_ts, mem_keys, mem_values = project_memory(core_arg, mem_parts, wc_key, wc_value)
    mixed_got = at.swap_core(mixed)
    mixed_t_got = at.swap_core(mixed_t)
    after_self, cross_t, cross_query = join(
        core_arg, (tokens, tokens_got), mixed, mixed_got, w_out, gain_cross, wc_query, "join_self"
    )

    crossed, crossed_t, lse_cross = cross_forward(cross_query, mem_keys, mem_values, mask_col)
    crossed_got = at.swap_core(crossed)
    crossed_t_got = at.swap_core(crossed_t)
    after_cross, ffn_t, normed_ffn = join(
        core_arg, after_self, crossed, crossed_got, wc_out, gain_ffn, None, "join_cross"
    )

    hidden_t, e_part, out_mine, out_other, gate_keep, gate_send, up_keep, up_send = ffn(
        where,
        normed_ffn,
        ffn_t,
        grad_chip,
        w_gate,
        w_up,
        w_down,
        [at.block_order("x_y_z1_z2"), at.block_order("y_x_z1_z2")],
    )
    ffn_half = w_gate.shape[1] // 2
    gate_sum = ChipSum(at, "x_y_z1_z2", gate_keep, gate_send)
    up_sum = ChipSum(at, "y_x_z1_z2", up_keep, up_send)
    hidden_t_got = at.swap_core(hidden_t)
    e_got = at.swap_core(e_part)
    out_got = at.swap_core(out_other)
    down_halves = outer_halves(
        where,
        [at.block_order("z1_x_wait_z2_y", True)], [(hidden_t, hidden_t_got)], [grad_half], [[(0, 0, 0, 0, width // 2)]]
    )
    e_part, *down_halves = together(e_part, *down_halves)
    down_sum = ChipSum(at, "z1_x_wait_z2_y", *down_halves)
    grad_after_cross, cross_half, grad_crossed = back(
        core_arg, (grads, grads_got), after_cross, gain_ffn, e_part, e_got, None, wc_out, "back_ffn"
    )

    grad_cq, grad_mem = cross_backward(
        cross_query, mem_keys, mem_values, mask_col, grad_crossed, crossed, lse_cross, nx
    )
    grad_cq_got = at.swap_core(grad_cq)
    wc_out_halves = outer_halves(
        where,
        [at.block_order("z1_x_y_z2", True)],
        [(crossed_t, crossed_t_got)],
        [cross_half],
        [[(0, 0, 0, 0, width // 2)]],
    )
    turns = kw // PAIR
    k_columns = [2 * PAIR * m for m in range(turns)]
    v_columns = [2 * PAIR * m + PAIR for m in range(turns)]
    wc_in_halves = outer_halves(
        where,
        [at.block_order("y_x_z1_z2")] * (1 + nx),
        [cross_t, *mem_ts],
        [grad_cq, *grad_mem],
        [[(0, 0, 0, 0, qw)]] + [[(1 + s, 1 + s, 0, c, PAIR) for s in range(nx)] for c in k_columns + v_columns],
    )
    mem_got = [at.shift_x(grad_mem[s], nx - s) for s in range(1, nx)]

    both = [gate_sum, up_sum]
    tied = settle(both, grad_cq, grad_cq_got, *wc_out_halves)
    grad_cq, grad_cq_got, *wc_out_halves = fold(at, both, *tied)
    grad_after_self, self_half, grad_mixed = back(
        core_arg, grad_after_cross, after_self, gain_cross, grad_cq, grad_cq_got, wc_query, w_out, "back_cross"
    )
    out_halves = outer_halves(
        where,
        [at.block_order("x_z1_y_z2", True)],
        [(mixed_t, mixed_t_got)],
        [self_half],
        [[(0, 0, 0, 0, width // 2)]],
    )
    ffn_sums = [gate_sum, up_sum, down_sum]
    tied = settle(
        ffn_sums,
        grad_mixed,
        grad_after_self,
        out_mine,
        out_got,
        *wc_in_halves,
        *out_halves,
        *wc_out_halves,
        grad_mem[0],
        *mem_got,
    )
    grad_mixed, grad_after_self, out_mine, out_got = tied[:4]
    halves = tied[4:10]
    grad_mem_chip, mem_got = tied[10], tied[11:]

    grad_mixed, *halves = fold(at, ffn_sums, grad_mixed, *halves)
    wc_in_sum = ChipSum(at, "y_x_z1_z2", *halves[:2])
    out_sum = ChipSum(at, "x_z1_y_z2", *halves[2:4])
    wc_out_sum = ChipSum(at, "z1_x_y_z2", *halves[4:])
    early = [*ffn_sums, wc_in_sum, out_sum, wc_out_sum]
    grad_q, grad_pairs, diagonals = self_backward(
        place, query, keys, values, bias_vec, grad_mixed, mixed, lse_self
    )
    tied = settle(early, grad_q, diagonals, out_mine, out_got, grad_mem_chip, *grad_pairs, *mem_got)
    grad_q, diagonals, out_mine, out_got, grad_mem_chip = tied[:5]
    grad_pairs, mem_got = tied[5 : 5 + nx], tied[5 + nx :]
    pair_chip = grad_pairs[0]
    pair_got = [at.shift_x(grad_pairs[s], nx - s) for s in range(1, nx)]

    grad_q, diagonals, grad_mem_chip, out_mine = fold(at, early, grad_q, diagonals, grad_mem_chip, out_mine)

    own_bias = lax.dot_general(
        diagonals.reshape(head_count, -1)[:, BLK:],
        onehot,
        (((1,), (0,)), ((), ())),
        precision=lax.Precision.HIGHEST,
        preferred_element_type=F32,
    )
    table = lax.dynamic_update_slice_in_dim(
        jnp.zeros((HEADS, BUCKETS), F32), own_bias, core * head_count, 0
    ).reshape(2 * at.chips, -1)
    bias_share = table.shape[1]
    in_halves = outer_halves(
        where,
        [at.block_order("y_x_zz")] * nx,
        normed_ts,
        [grad_q, *grad_pairs],
        [[(0, 0, 0, 0, qw)]] + [[(s, 1 + s, 0, c, PAIR) for s in range(nx)] for c in k_columns + v_columns],
        jnp.pad(table, ((0, 0), (0, 128 - bias_share))),
    )
    in_sum = ChipSum(at, "y_x_zz", *in_halves)
    grad_mem_chip, out_mine, *pair_got = together(grad_mem_chip, out_mine, *pair_got)
    for got in pair_got:
        pair_chip = pair_chip + got
    every = [*early, in_sum]

    output = (
        at.core_rows(after_cross, True)
        + out_mine.astype(F32)
        + out_got.astype(F32)
    ).astype(BF16)
    for got in mem_got:
        grad_mem_chip = grad_mem_chip + got
    mem_mine = grad_mem_chip[:mem_local]
    mem_other = at.swap_core(grad_mem_chip[mem_local:])

    def unpaired(columns):
        mine = [mem_mine[:, c : c + PAIR] for c in columns]
        other = [mem_other[:, c : c + PAIR] for c in columns]
        return at.by_core(jnp.concatenate(mine, axis=1), jnp.concatenate(other, axis=1), 1)

    grad_memory = dot_nt(unpaired(k_columns), wc_key) + dot_nt(unpaired(v_columns), wc_value)
    sent = jnp.concatenate([at.core_rows(grad_q, False), at.core_rows(pair_chip, False)], axis=1)
    (grad_target,) = last(
        core_arg,
        grad_after_self,
        tokens,
        gain_self,
        grad_q,
        pair_chip,
        at.swap_core(sent),
        w_query,
        w_key,
        w_value,
    )

    grad_target, grad_memory, output = settle(every, grad_target, grad_memory, output)
    while any(one.todo for one in every):
        fold(at, every)

    sums = [gate_sum, up_sum, wc_in_sum, out_sum, in_sum, wc_out_sum]
    rear, down_rows = finish_sums(at, where, [sums, [down_sum]])
    rear_join = (rear[0], at.swap_core(rear[1]))
    down_join = (down_rows[0], at.swap_core(down_rows[1]))
    wc_at = 2 * ffn_half
    out_at = wc_at + qw + 2 * kw
    in_at = out_at + width // 2
    bias_at = in_at + qw + 2 * kw
    (gate, up, cross_in, cross_key, cross_value, self_out, self_in, self_key, self_value, cross_out, down), gain_grads, bias_out = finish(
        at,
        where,
        [rear_join, down_join],
        [
            (0, 0, ffn_half),
            (0, ffn_half, ffn_half),
            (0, wc_at, qw),
            (0, wc_at + qw, kw),
            (0, wc_at + qw + kw, kw),
            (0, out_at, width // 2),
            (0, in_at, qw),
            (0, in_at + qw, kw),
            (0, in_at + qw + kw, kw),
            (0, in_at + in_sum.width, width // 2),
            (1, 0, width // 2),
        ],
        [
            (0, [(0, w_gate), (1, w_up)]),
            (1, [(2, wc_query)]),
            (2, [(6, w_query), (7, w_key), (8, w_value)]),
        ],
        gain_rows,
        bias_at,
        bias_share,
    )
    gain_ffn_grad, gain_cross_grad, gain_self_grad = gain_grads
    return (
        output.reshape(target.shape),
        grad_target.reshape(target.shape),
        grad_memory.reshape(memory.shape),
        gain_self_grad,
        self_in,
        self_key,
        self_value,
        self_out,
        bias_out,
        gain_cross_grad,
        cross_in,
        cross_key,
        cross_value,
        cross_out,
        gain_ffn_grad,
        gate,
        up,
        down,
    )


def solution(mesh):
    tokens = P("dp", "seq", None)
    row_share = P(("dp", "seq"))
    matrix_share = P(("dp", "seq"), None)
    return jax.shard_map(
        per_device,
        mesh=mesh,
        in_specs=(tokens, tokens, P("dp"), P("dp", None)) + (P(),) * 16 + (tokens,),
        out_specs=(tokens, tokens, tokens, row_share)
        + (matrix_share,) * 4
        + (row_share, row_share)
        + (matrix_share,) * 4
        + (row_share,)
        + (matrix_share,) * 3,
        check_vma=False,
    )
```

```python
import functools

import jax
import jax.numpy as jnp
from jax import lax
from jax.experimental import pallas as pl
from jax.experimental.pallas import tpu as pltpu
from jax.sharding import PartitionSpec as P

HEADS = 16
KV = 8
HEAD_DIM = 64
BUCKETS = 32
BLK = 256
PAIR = 2 * HEAD_DIM

norm_eps = 1e-06
big_negative = -1000000000.0
score_scale = HEAD_DIM ** (-0.5)
F32 = jnp.float32
BF16 = jnp.bfloat16
VMEM_LIMIT = 64 * 1024 * 1024


def dot_nn(a, b):
    return lax.dot_general(a, b, (((1,), (0,)), ((), ())), preferred_element_type=F32)


def dot_nt(a, b):
    return lax.dot_general(a, b, (((1,), (1,)), ((), ())), preferred_element_type=F32)


def dot_tn(a, b):
    return lax.dot_general(a, b, (((0,), (0,)), ((), ())), preferred_element_type=F32)


def lane_pick(source, dest):
    a = lax.broadcasted_iota(jnp.int32, (PAIR, PAIR), 0)
    b = lax.broadcasted_iota(jnp.int32, (PAIR, PAIR), 1)
    keep = (a - source == b - dest) & (b >= dest) & (b < dest + HEAD_DIM)
    return keep.astype(F32).astype(BF16)


def lane_pick_t(source, dest):
    a = lax.broadcasted_iota(jnp.int32, (PAIR, PAIR), 1)
    b = lax.broadcasted_iota(jnp.int32, (PAIR, PAIR), 0)
    keep = (a - source == b - dest) & (b >= dest) & (b < dest + HEAD_DIM)
    return keep.astype(F32).astype(BF16)


def bias_tile(bias_vec_ref, h, delta):
    piece = bias_vec_ref[0, h : h + 1, delta * BLK : delta * BLK + 2 * BLK]
    wide = jnp.broadcast_to(piece, (BLK, 2 * BLK))
    return pltpu.roll(wide, 0, 1, stride=1, stride_axis=0)[:, BLK:]


def tile_plan(row_blocks, slots):
    plan = [(delta, 0) for delta in range(row_blocks)]
    for slot in range(1, slots):
        plan += [(slot * row_blocks + c, slot) for c in range(1 - row_blocks, row_blocks)]
    return plan


def tile_at(row_blocks, rb, kb):
    slot, jb = kb // row_blocks, kb % row_blocks
    if slot == 0:
        return rb - jb, rb - jb
    first = row_blocks + (slot - 1) * (2 * row_blocks - 1)
    return first + rb - jb + row_blocks - 1, slot * row_blocks + rb - jb


def key_blocks(row_blocks, slots, rb):
    return list(range(rb + 1)) + list(range(row_blocks, row_blocks * slots))


def fill_bias(place, bias_vec_ref, tile_ref, row_blocks, slots):
    for at, (delta, slot) in enumerate(tile_plan(row_blocks, slots)):
        for h in range(2):
            tile = bias_tile(bias_vec_ref, h, delta)
            if slot:
                tile = tile + jnp.where(place >= slot, 0.0, big_negative)
            elif delta == 0:
                tile = jnp.where(causal_tile(), tile, big_negative)
            tile_ref[h, at] = tile


def causal_tile():
    key_pos = lax.broadcasted_iota(jnp.int32, (BLK, BLK), 0)
    row_pos = lax.broadcasted_iota(jnp.int32, (BLK, BLK), 1)
    return key_pos <= row_pos


def online_step(carry, scores, value_t):
    highest, total, mixed = carry
    new_high = jnp.maximum(highest, jnp.max(scores, axis=0, keepdims=True))
    fade = jnp.exp(highest - new_high)
    weights = jnp.exp(scores - new_high)
    total = total * fade + jnp.sum(weights, axis=0, keepdims=True)
    mixed = mixed * fade + dot_nn(value_t, weights.astype(BF16))
    return (new_high, total, mixed)


def first_step(scores, value_t):
    highest = jnp.max(scores, axis=0, keepdims=True)
    weights = jnp.exp(scores - highest)
    total = jnp.sum(weights, axis=0, keepdims=True)
    return (highest, total, dot_nn(value_t, weights.astype(BF16)))


def key_spans(row_blocks, slots, rb):
    own, end = (rb + 1) * BLK, row_blocks * slots * BLK
    first_far = row_blocks * BLK
    if slots == 1:
        return [(0, own)]
    if own == first_far:
        return [(0, end)]
    return [(0, own), (first_far, end)]


def self_forward_kernel(slots, place_ref, q_ref, b_ref, *refs):
    k_refs, v_refs = refs[:slots], refs[slots : 2 * slots]
    o_ref, ot_ref, lse_ref, tile_ref, kz_ref, vt_ref, s_ref, p_ref = refs[2 * slots :]
    parity = lax.rem(pl.program_id(0), 2)
    rows_all = q_ref.shape[0]
    row_blocks = rows_all // BLK
    fill_bias(place_ref[0], b_ref, tile_ref, row_blocks, slots)
    for h in range(2):
        for slot in range(slots):
            span = slice(slot * rows_all, (slot + 1) * rows_all)
            pick_k = lane_pick(parity * HEAD_DIM, h * HEAD_DIM)
            pick_v = lane_pick_t(parity * HEAD_DIM, h * HEAD_DIM)
            kz_ref[h, span, :] = dot_nn(k_refs[slot][...], pick_k).astype(BF16)
            vt_ref[h, :, span] = dot_nt(pick_v, v_refs[slot][...]).astype(BF16)
    for rb in range(row_blocks):
        rows = slice(rb * BLK, (rb + 1) * BLK)
        queries = q_ref[rows, :]
        spans = key_spans(row_blocks, slots, rb)
        highest = [None, None]
        for h in range(2):
            for first, end in spans:
                products = dot_nt(kz_ref[h, first:end, :], queries)
                for kb in range(first // BLK, end // BLK):
                    at, _ = tile_at(row_blocks, rb, kb)
                    scores = products[kb * BLK - first : (kb + 1) * BLK - first, :] + tile_ref[h, at]
                    s_ref[h, kb * BLK : (kb + 1) * BLK, :] = scores
                    top = jnp.max(scores, axis=0, keepdims=True)
                    highest[h] = top if highest[h] is None else jnp.maximum(highest[h], top)
        mixed_t = None
        for h in range(2):
            total = None
            part = None
            for first, end in spans:
                weights = jnp.exp(s_ref[h, first:end, :] - highest[h])
                one = jnp.sum(weights, axis=0, keepdims=True)
                total = one if total is None else total + one
                p_ref[h, first:end, :] = weights.astype(BF16)
            for first, end in spans:
                one = dot_nn(vt_ref[h, :, first:end], p_ref[h, first:end, :])
                part = one if part is None else part + one
            part = part / total
            mixed_t = part if mixed_t is None else mixed_t + part
            lse_ref[0, h : h + 1, rows] = highest[h] + jnp.log(total)
        ot_ref[:, rows] = mixed_t.astype(BF16)
        o_ref[rows, :] = mixed_t.T.astype(BF16)


def diagonal_sums(wide):
    rows, lanes = wide.shape
    while rows > 8:
        rows //= 2
        wide = wide[:rows] + pltpu.roll(wide[rows:], lanes - rows, 1)
    row = lax.broadcasted_iota(jnp.int32, (8, lanes), 0)
    total = jnp.where(row == 0, wide, 0.0)
    for b in range(1, 8):
        total = total + jnp.where(row == b, pltpu.roll(wide, lanes - b, 1), 0.0)
    return jnp.sum(total, axis=0, keepdims=True)


def row_products(grad_block, mixed_block):
    turned = (grad_block.astype(F32) * mixed_block.astype(F32)).T
    return [
        jnp.sum(turned[h * HEAD_DIM : (h + 1) * HEAD_DIM], axis=0, keepdims=True) for h in range(2)
    ]


def self_backward_kernel(slots, place_ref, q_ref, b_ref, do_ref, o_ref, lse_ref, *refs):
    k_refs, v_refs = refs[:slots], refs[slots : 2 * slots]
    dq_ref, diag_ref = refs[2 * slots : 2 * slots + 2]
    pair_refs, refs = refs[2 * slots + 2 : 3 * slots + 2], refs[3 * slots + 2 :]
    tile_ref, sum_ref, kz_ref, kt_ref, vz_ref, qp_ref, dop_ref, dk_acc, dv_acc, p_ref, ds_ref = refs
    parity = lax.rem(pl.program_id(0), 2)
    rows_all = q_ref.shape[0]
    row_blocks = rows_all // BLK
    fill_bias(place_ref[0], b_ref, tile_ref, row_blocks, slots)
    for h in range(2):
        in_pick = lane_pick(parity * HEAD_DIM, h * HEAD_DIM)
        out_pick = lane_pick(h * HEAD_DIM, parity * HEAD_DIM)
        pick_t = lane_pick_t(parity * HEAD_DIM, h * HEAD_DIM)
        for slot in range(slots):
            span = slice(slot * rows_all, (slot + 1) * rows_all)
            kz_ref[h, span, :] = dot_nn(k_refs[slot][...], in_pick).astype(BF16)
            kt_ref[h, :, span] = dot_nt(pick_t, k_refs[slot][...]).astype(BF16)
            vz_ref[h, span, :] = dot_nn(v_refs[slot][...], in_pick).astype(BF16)
        side = slice(h * rows_all, (h + 1) * rows_all)
        qp_ref[side, :] = dot_nn(q_ref[...], out_pick).astype(BF16)
        dop_ref[side, :] = dot_nn(do_ref[...], out_pick).astype(BF16)
    seen = set()
    for rb in range(row_blocks):
        rows = slice(rb * BLK, (rb + 1) * BLK)
        spans = key_spans(row_blocks, slots, rb)
        delta_rows = row_products(do_ref[rows, :], o_ref[rows, :])
        for kb in range(rb + 1, row_blocks):
            for h in range(2):
                side = slice(h * rows_all + rb * BLK, h * rows_all + (rb + 1) * BLK)
                keys = slice(kb * BLK, (kb + 1) * BLK)
                p_ref[keys, side] = jnp.zeros((BLK, BLK), BF16)
                ds_ref[keys, side] = jnp.zeros((BLK, BLK), BF16)
        for h in range(2):
            side = slice(h * rows_all + rb * BLK, h * rows_all + (rb + 1) * BLK)
            delta_row = delta_rows[h]
            lse = lse_ref[0, h : h + 1, rows]
            for first, end in spans:
                products = dot_nt(kz_ref[h, first:end, :], q_ref[rows, :])
                grad_products = dot_nt(vz_ref[h, first:end, :], do_ref[rows, :])
                for kb in range(first // BLK, end // BLK):
                    keys = slice(kb * BLK, (kb + 1) * BLK)
                    inner = slice(kb * BLK - first, (kb + 1) * BLK - first)
                    at, delta = tile_at(row_blocks, rb, kb)
                    probs = jnp.exp(products[inner, :] + tile_ref[h, at] - lse)
                    grad_scores = probs * (grad_products[inner, :] - delta_row)
                    p_ref[keys, side] = probs.astype(BF16)
                    ds_ref[keys, side] = grad_scores.astype(BF16)
                    if (h, delta) in seen:
                        sum_ref[h, delta] += grad_scores
                    else:
                        sum_ref[h, delta] = grad_scores
                        seen.add((h, delta))
    grad_v = dot_nn(p_ref[...], dop_ref[...])
    grad_k = dot_nn(ds_ref[...], qp_ref[...])

    @pl.when(parity == 0)
    def first():
        dv_acc[...] = grad_v
        dk_acc[...] = grad_k

    @pl.when(parity == 1)
    def second():
        dv_acc[...] += grad_v
        dk_acc[...] += grad_k

    grad_q = None
    for h in range(2):
        part = dot_nn(kt_ref[h], ds_ref[:, h * rows_all : (h + 1) * rows_all])
        grad_q = part if grad_q is None else grad_q + part
    dq_ref[...] = (grad_q.T * score_scale).astype(BF16)

    diag_ref[...] = jnp.zeros_like(diag_ref)
    for h in range(2):
        for delta in range(row_blocks * slots):
            wide = jnp.concatenate([jnp.zeros((BLK, BLK), F32), sum_ref[h, delta]], axis=1)
            diag_ref[0, h : h + 1, delta * BLK : delta * BLK + 2 * BLK] += diagonal_sums(wide)

    @pl.when(parity == 1)
    def store():
        for slot, pair_ref in enumerate(pair_refs):
            span = slice(slot * rows_all, (slot + 1) * rows_all)
            pair_ref[:, :PAIR] = dk_acc[span, :].astype(BF16)
            pair_ref[:, PAIR:] = dv_acc[span, :].astype(BF16)


def cross_forward_kernel(q_ref, k_ref, v_ref, m_ref, o_ref, ot_ref, lse_ref, kz_ref, vt_ref, s_ref, p_ref):
    parity = lax.rem(pl.program_id(0), 2)
    for h in range(2):
        kz_ref[h] = dot_nn(k_ref[...], lane_pick(parity * HEAD_DIM, h * HEAD_DIM)).astype(BF16)
        vt_ref[h] = dot_nt(lane_pick_t(parity * HEAD_DIM, h * HEAD_DIM), v_ref[...]).astype(BF16)
    for rb in range(q_ref.shape[0] // BLK):
        rows = slice(rb * BLK, (rb + 1) * BLK)
        queries = q_ref[rows, :]
        highest = []
        for h in range(2):
            scores = dot_nt(kz_ref[h], queries) + m_ref[...]
            s_ref[h] = scores
            highest.append(jnp.max(scores, axis=0, keepdims=True))
        mixed_t = None
        for h in range(2):
            weights = jnp.exp(s_ref[h] - highest[h])
            total = jnp.sum(weights, axis=0, keepdims=True)
            p_ref[h] = weights.astype(BF16)
            part = dot_nn(vt_ref[h], p_ref[h]) / total
            mixed_t = part if mixed_t is None else mixed_t + part
            lse_ref[0, h : h + 1, rows] = highest[h] + jnp.log(total)
        ot_ref[:, rows] = mixed_t.astype(BF16)
        o_ref[rows, :] = mixed_t.T.astype(BF16)


def cross_backward_kernel(
    slots,
    q_ref,
    k_ref,
    v_ref,
    m_ref,
    do_ref,
    o_ref,
    lse_ref,
    dq_ref,
    *refs,
):
    pair_refs, refs = refs[:slots], refs[slots:]
    cross_backward_body(slots, pair_refs, q_ref, k_ref, v_ref, m_ref, do_ref, o_ref, lse_ref, dq_ref, *refs)


def cross_backward_body(
    slots,
    pair_refs,
    q_ref,
    k_ref,
    v_ref,
    m_ref,
    do_ref,
    o_ref,
    lse_ref,
    dq_ref,
    kz_ref,
    kt_ref,
    vz_ref,
    qp_ref,
    dop_ref,
    dk_acc,
    dv_acc,
    p_ref,
    ds_ref,
):
    parity = lax.rem(pl.program_id(0), 2)
    rows_all = q_ref.shape[0]
    for h in range(2):
        in_pick = lane_pick(parity * HEAD_DIM, h * HEAD_DIM)
        out_pick = lane_pick(h * HEAD_DIM, parity * HEAD_DIM)
        kz_ref[h] = dot_nn(k_ref[...], in_pick).astype(BF16)
        kt_ref[h] = dot_nt(lane_pick_t(parity * HEAD_DIM, h * HEAD_DIM), k_ref[...]).astype(BF16)
        vz_ref[h] = dot_nn(v_ref[...], in_pick).astype(BF16)
        side = slice(h * rows_all, (h + 1) * rows_all)
        qp_ref[side, :] = dot_nn(q_ref[...], out_pick).astype(BF16)
        dop_ref[side, :] = dot_nn(do_ref[...], out_pick).astype(BF16)
    for rb in range(rows_all // BLK):
        rows = slice(rb * BLK, (rb + 1) * BLK)
        delta_rows = row_products(do_ref[rows, :], o_ref[rows, :])
        for h in range(2):
            side = slice(h * rows_all + rb * BLK, h * rows_all + (rb + 1) * BLK)
            delta_row = delta_rows[h]
            lse = lse_ref[0, h : h + 1, rows]
            probs = jnp.exp(dot_nt(kz_ref[h], q_ref[rows, :]) + m_ref[...] - lse)
            grad_products = dot_nt(vz_ref[h], do_ref[rows, :])
            p_ref[:, side] = probs.astype(BF16)
            ds_ref[:, side] = (probs * (grad_products - delta_row)).astype(BF16)
    grad_v = dot_nn(p_ref[...], dop_ref[...])
    grad_k = dot_nn(ds_ref[...], qp_ref[...])

    @pl.when(parity == 0)
    def first():
        dv_acc[...] = grad_v
        dk_acc[...] = grad_k

    @pl.when(parity == 1)
    def second():
        all_k = (dk_acc[...] + grad_k).astype(BF16)
        all_v = (dv_acc[...] + grad_v).astype(BF16)
        size = all_k.shape[0] // slots
        for slot, pair_ref in enumerate(pair_refs):
            pair_ref[:, :PAIR] = all_k[slot * size : (slot + 1) * size]
            pair_ref[:, PAIR:] = all_v[slot * size : (slot + 1) * size]

    grad_q = None
    for h in range(2):
        part = dot_nn(kt_ref[h], ds_ref[:, h * rows_all : (h + 1) * rows_all])
        grad_q = part if grad_q is None else grad_q + part
    dq_ref[...] = (grad_q.T * score_scale).astype(BF16)


def shape_of(shape, dtype):
    return jax.ShapeDtypeStruct(shape, dtype)


def tile_pair(rows):
    return pl.BlockSpec((rows, PAIR), lambda g: (0, g))


def tile_pair_t(rows):
    return pl.BlockSpec((PAIR, rows), lambda g: (g, 0))


def tile_group(rows):
    return pl.BlockSpec((rows, PAIR), lambda g: (0, g // 2))


def tile_both(rows):
    return pl.BlockSpec((rows, 2 * PAIR), lambda g: (0, g // 2))


def tile_rows(width):
    return pl.BlockSpec((1, 2, width), lambda g: (g, 0, 0))


def kernel_params():
    return pltpu.CompilerParams(
        dimension_semantics=("arbitrary",), vmem_limit_bytes=VMEM_LIMIT
    )


def cost(flops, transcendentals, nbytes):
    return pl.CostEstimate(
        flops=int(flops) // 16, transcendentals=0, bytes_accessed=int(nbytes) // 16
    )


def self_forward(place, q, ks, vs, bias_vec):
    rows, width = q.shape
    slots = len(ks)
    keys = rows * slots
    pairs = width // PAIR
    tiles = len(tile_plan(rows // BLK, slots))
    return pl.pallas_call(
        functools.partial(self_forward_kernel, slots),
        grid=(pairs,),
        in_specs=[pl.BlockSpec(memory_space=pltpu.SMEM), tile_pair(rows), tile_rows(bias_vec.shape[2])]
        + [tile_group(rows)] * (2 * slots),
        out_specs=[tile_pair(rows), tile_pair_t(rows), tile_rows(rows)],
        out_shape=[
            shape_of((rows, width), BF16),
            shape_of((width, rows), BF16),
            shape_of((pairs, 2, rows), F32),
        ],
        scratch_shapes=[
            pltpu.VMEM((2, tiles, BLK, BLK), F32),
            pltpu.VMEM((2, keys, PAIR), BF16),
            pltpu.VMEM((2, PAIR, keys), BF16),
            pltpu.VMEM((2, keys, BLK), F32),
            pltpu.VMEM((2, keys, BLK), BF16),
        ],
        compiler_params=kernel_params(),
        cost_estimate=cost(4 * 2 * rows * keys * width * 2, pairs * 2 * rows * keys, 8 * rows * width),
        name="self_forward",
    )(place, q, bias_vec, *ks, *vs)


def self_backward(place, q, ks, vs, bias_vec, grads, mixed, lse):
    rows, width = q.shape
    kv_width = ks[0].shape[1]
    slots = len(ks)
    keys = rows * slots
    pairs = width // PAIR
    tiles = len(tile_plan(rows // BLK, slots))
    grad_q, diagonals, *pairs_out = pl.pallas_call(
        functools.partial(self_backward_kernel, slots),
        grid=(pairs,),
        in_specs=[
            pl.BlockSpec(memory_space=pltpu.SMEM),
            tile_pair(rows),
            tile_rows(bias_vec.shape[2]),
            tile_pair(rows),
            tile_pair(rows),
            tile_rows(rows),
        ]
        + [tile_group(rows)] * (2 * slots),
        out_specs=[tile_pair(rows), tile_rows(bias_vec.shape[2])] + [tile_both(rows)] * slots,
        out_shape=[shape_of((rows, width), BF16), shape_of(bias_vec.shape, F32)]
        + [shape_of((rows, 2 * kv_width), BF16)] * slots,
        scratch_shapes=[
            pltpu.VMEM((2, tiles, BLK, BLK), F32),
            pltpu.VMEM((2, keys // BLK, BLK, BLK), F32),
            pltpu.VMEM((2, keys, PAIR), BF16),
            pltpu.VMEM((2, PAIR, keys), BF16),
            pltpu.VMEM((2, keys, PAIR), BF16),
            pltpu.VMEM((2 * rows, PAIR), BF16),
            pltpu.VMEM((2 * rows, PAIR), BF16),
            pltpu.VMEM((keys, PAIR), F32),
            pltpu.VMEM((keys, PAIR), F32),
            pltpu.VMEM((keys, 2 * rows), BF16),
            pltpu.VMEM((keys, 2 * rows), BF16),
        ],
        compiler_params=kernel_params(),
        cost_estimate=cost(10 * 2 * rows * keys * width * 2, pairs * 2 * rows * keys, 12 * rows * width),
        name="self_backward",
    )(place, q, bias_vec, grads, mixed, lse, *ks, *vs)
    return grad_q, pairs_out, diagonals


def cross_forward(q, k, v, mask_col):
    rows, width = q.shape
    keys = k.shape[0]
    pairs = width // PAIR
    return pl.pallas_call(
        cross_forward_kernel,
        grid=(pairs,),
        in_specs=[
            tile_pair(rows),
            tile_group(keys),
            tile_group(keys),
            pl.BlockSpec((keys, 1), lambda g: (0, 0)),
        ],
        out_specs=[tile_pair(rows), tile_pair_t(rows), tile_rows(rows)],
        out_shape=[
            shape_of((rows, width), BF16),
            shape_of((width, rows), BF16),
            shape_of((pairs, 2, rows), F32),
        ],
        scratch_shapes=[
            pltpu.VMEM((2, keys, PAIR), BF16),
            pltpu.VMEM((2, PAIR, keys), BF16),
            pltpu.VMEM((2, keys, BLK), F32),
            pltpu.VMEM((2, keys, BLK), BF16),
        ],
        compiler_params=kernel_params(),
        cost_estimate=cost(4 * 2 * rows * keys * width * 2, pairs * 2 * rows * keys, 8 * rows * width),
        name="cross_forward",
    )(q, k, v, mask_col)


def cross_backward(q, k, v, mask_col, grads, mixed, lse, slots):
    rows, width = q.shape
    keys, kv_width = k.shape
    pairs = width // PAIR
    grad_q, *pairs_out = pl.pallas_call(
        functools.partial(cross_backward_kernel, slots),
        grid=(pairs,),
        in_specs=[
            tile_pair(rows),
            tile_group(keys),
            tile_group(keys),
            pl.BlockSpec((keys, 1), lambda g: (0, 0)),
            tile_pair(rows),
            tile_pair(rows),
            tile_rows(rows),
        ],
        out_specs=[tile_pair(rows)] + [tile_both(keys // slots)] * slots,
        out_shape=[shape_of((rows, width), BF16)] + [shape_of((keys // slots, 2 * kv_width), BF16)] * slots,
        scratch_shapes=[
            pltpu.VMEM((2, keys, PAIR), BF16),
            pltpu.VMEM((2, PAIR, keys), BF16),
            pltpu.VMEM((2, keys, PAIR), BF16),
            pltpu.VMEM((2 * rows, PAIR), BF16),
            pltpu.VMEM((2 * rows, PAIR), BF16),
            pltpu.VMEM((keys, PAIR), F32),
            pltpu.VMEM((keys, PAIR), F32),
            pltpu.VMEM((keys, 2 * rows), BF16),
            pltpu.VMEM((keys, 2 * rows), BF16),
        ],
        compiler_params=kernel_params(),
        cost_estimate=cost(10 * 2 * rows * keys * width * 2, pairs * 2 * rows * keys, 12 * rows * width),
        name="cross_backward",
    )(q, k, v, mask_col, grads, mixed, lse)
    return grad_q, pairs_out


FBLK = 256


def ffn_kernel(
    orders,
    where_ref,
    x_ref,
    xt_ref,
    og_ref,
    wg_any,
    wu_any,
    wd_any,
    ht_any,
    e_any,
    out_mine_any,
    out_other_any,
    gate_keep_any,
    gate_send_any,
    up_keep_any,
    up_send_any,
    wg_ref,
    wu_ref,
    wd_ref,
    xs_ref,
    hb_ref,
    gg_ref,
    gu_ref,
    ht_ref,
    e_ref,
    out_ref,
    product_ref,
    in_sems,
    out_sems,
):
    hidden_width = gg_ref.shape[1]
    base = where_ref[0] * hidden_width
    spans = [(first, min(FBLK, hidden_width - first)) for first in range(0, hidden_width, FBLK)]
    loads = []
    for k, (first, size) in enumerate(spans):
        away = pl.ds(pl.multiple_of(base + first, 128), size)
        near = slice(first, first + size)
        loads.append(
            [
                pltpu.make_async_copy(wg_any.at[:, away], wg_ref.at[:, near], in_sems.at[0, k]),
                pltpu.make_async_copy(wu_any.at[:, away], wu_ref.at[:, near], in_sems.at[1, k]),
                pltpu.make_async_copy(wd_any.at[away, :], wd_ref.at[near, :], in_sems.at[2, k]),
            ]
        )
    for group in loads:
        for load in group:
            load.start()
    chips = len(orders[0][0])
    block = xt_ref.shape[0] // chips
    for order in range(2):
        for p in range(chips):
            first = pl.multiple_of(chip_at(orders[order], p, where_ref) * block, block)
            xs_ref[order, p * block : (p + 1) * block, :] = xt_ref[pl.ds(first, block), :]
    factor = (2.0 / jnp.pi) ** 0.5

    def combine(span, gate, up, grad_hidden):
        square = gate * gate
        bend = jnp.tanh(gate * (factor + (factor * 0.044715) * square))
        half = 0.5 + 0.5 * bend
        gelu = gate * half
        slope = half + gelu * (1.0 - bend) * (factor + (factor * 3 * 0.044715) * square)
        hidden = gelu * up
        hb_ref[:, span] = hidden.astype(BF16)
        ht_ref[span, :] = hidden.T.astype(BF16)
        gg_ref[:, span] = (grad_hidden * up * slope).astype(BF16)
        gu_ref[:, span] = (grad_hidden * gelu).astype(BF16)

    waiting = None
    for (first, size), group in zip(spans, loads):
        span = slice(first, first + size)
        for load in group:
            load.wait()
        gate = dot_nn(x_ref[...], wg_ref[:, span])
        up = dot_nn(x_ref[...], wu_ref[:, span])
        grad_hidden = dot_nt(og_ref[...], wd_ref[span, :])
        if waiting is not None:
            combine(*waiting)
        waiting = (span, gate, up, grad_hidden)
    combine(*waiting)
    stores = [pltpu.make_async_copy(ht_ref, ht_any, out_sems.at[0])]
    stores[-1].start()
    e_ref[...] = (dot_nt(gg_ref[...], wg_ref[...]) + dot_nt(gu_ref[...], wu_ref[...])).astype(BF16)
    stores.append(pltpu.make_async_copy(e_ref, e_any, out_sems.at[1]))
    stores[-1].start()
    middle = xt_ref.shape[0] // 2
    outs = [
        (0, gg_ref, middle, gate_send_any),
        (1, gu_ref, middle, up_send_any),
        (0, gg_ref, 0, gate_keep_any),
        (1, gu_ref, 0, up_keep_any),
    ]
    for k, (order, right_ref, first, any_ref) in enumerate(outs):
        product_ref[k] = dot_nn(xs_ref[order, first : first + middle, :], right_ref[...]).astype(BF16)
        stores.append(pltpu.make_async_copy(product_ref.at[k], any_ref, out_sems.at[2 + k]))
        stores[-1].start()
    out_ref[...] = dot_nn(hb_ref[...], wd_ref[...]).astype(BF16)
    half = out_ref.shape[0] // 2
    for k, (which, any_ref) in enumerate(((where_ref[0], out_mine_any), (1 - where_ref[0], out_other_any))):
        source = out_ref.at[pl.ds(pl.multiple_of(which * half, half), half), :]
        stores.append(pltpu.make_async_copy(source, any_ref, out_sems.at[6 + k]))
        stores[-1].start()
    for store in stores:
        store.wait()


def ffn(where, normed, normed_t, out_grad, w_gate, w_up, w_down, orders):
    rows, width = normed.shape
    hidden = w_gate.shape[1] // 2
    chunks = -(-hidden // FBLK)
    whole = pl.BlockSpec(memory_space=pltpu.VMEM)
    anywhere = pl.BlockSpec(memory_space=pl.ANY)
    half = (width // 2, hidden)
    return pl.pallas_call(
        functools.partial(ffn_kernel, orders),
        in_specs=[pl.BlockSpec(memory_space=pltpu.SMEM), whole, whole, whole] + [anywhere] * 3,
        out_specs=[anywhere] * 8,
        out_shape=[
            shape_of((hidden, rows), BF16),
            shape_of((rows, width), BF16),
            shape_of((rows // 2, width), BF16),
            shape_of((rows // 2, width), BF16),
        ]
        + [shape_of(half, BF16)] * 4,
        scratch_shapes=[
            pltpu.VMEM((width, hidden), BF16),
            pltpu.VMEM((width, hidden), BF16),
            pltpu.VMEM((hidden, width), BF16),
            pltpu.VMEM((2, width, rows), BF16),
            pltpu.VMEM((rows, hidden), BF16),
            pltpu.VMEM((rows, hidden), BF16),
            pltpu.VMEM((rows, hidden), BF16),
            pltpu.VMEM((hidden, rows), BF16),
            pltpu.VMEM((rows, width), BF16),
            pltpu.VMEM((rows, width), BF16),
            pltpu.VMEM((4, *half), BF16),
            pltpu.SemaphoreType.DMA((3, chunks)),
            pltpu.SemaphoreType.DMA((8,)),
        ],
        compiler_params=pltpu.CompilerParams(vmem_limit_bytes=VMEM_LIMIT),
        cost_estimate=cost(2 * 9 * rows * width * hidden, rows * hidden, 6 * width * hidden),
        name="ffn",
    )(where, normed, normed_t, out_grad, w_gate, w_up, w_down)


ROWS = 256


def tile_of(local):
    return min(local, ROWS)


def in_own_half(core_ref):
    return core_ref[0] == pl.program_id(0) // (pl.num_programs(0) // 2)


def within_half(local, width):
    steps = local // tile_of(local)
    return pl.BlockSpec((tile_of(local), width), lambda i, c: (lax.rem(i, steps), 0))


def normalise(values, gain):
    inverse = lax.rsqrt(jnp.mean(values * values, axis=-1, keepdims=True) + norm_eps)
    return values * inverse * gain


def rms_back(values, gain, grad):
    inverse = lax.rsqrt(jnp.mean(values * values, axis=-1, keepdims=True) + norm_eps)
    scaled = grad * gain
    mean_dot = jnp.mean(values * scaled, axis=-1, keepdims=True)
    unit = values * inverse
    return inverse * (scaled - unit * (inverse * mean_dot))


def project_kernel(scales, core_ref, own_ref, other_ref, gain_ref, *refs):
    count = len(scales)
    w_refs, nt_ref, out_refs = refs[:count], refs[count], refs[count + 1 :]
    values = jnp.where(in_own_half(core_ref), own_ref[...], other_ref[...]).astype(F32)
    normed = normalise(values, gain_ref[...])
    nt_ref[...] = normed.T.astype(BF16)
    low = normed.astype(BF16)
    for scale, w_ref, out_ref in zip(scales, w_refs, out_refs):
        out = dot_nn(low, w_ref[...]).astype(BF16)
        out_ref[...] = out if scale is None else out * BF16(scale)


def own_columns(weight):
    return pl.BlockSpec((weight.shape[0], weight.shape[1] // 2), lambda i, c: (0, c[0]))


def other_columns(weight):
    return pl.BlockSpec((weight.shape[0], weight.shape[1] // 2), lambda i, c: (0, 1 - c[0]))


def own_rows(array):
    return pl.BlockSpec((array.shape[0] // 2, array.shape[1]), lambda i, c: (c[0], 0))


def other_rows(array):
    return pl.BlockSpec((array.shape[0] // 2, array.shape[1]), lambda i, c: (1 - c[0], 0))


def all_of(array):
    return pl.BlockSpec(array.shape, lambda i, c: (0,) * array.ndim)


def half_rows(rows, width):
    return pl.BlockSpec((rows, width), lambda i, c: (i, 0))


def half_columns(width, rows):
    return pl.BlockSpec((width, rows), lambda i, c: (0, i))


def fixed(shape):
    return pl.BlockSpec(shape, lambda i, c: (0,) * len(shape))


def core_call(kernel, steps, core, args, in_specs, out_specs, out_shape, scratch, flops, name):
    return pl.pallas_call(
        kernel,
        grid_spec=pltpu.PrefetchScalarGridSpec(
            num_scalar_prefetch=1,
            grid=(steps,),
            in_specs=in_specs,
            out_specs=out_specs,
            scratch_shapes=scratch,
        ),
        out_shape=out_shape,
        compiler_params=kernel_params(),
        cost_estimate=cost(flops, 0, flops // 400),
        name=name,
    )(core, *args)


def project(core, own, other, gain, weights, scales, name):
    local, width = own.shape
    return core_call(
        functools.partial(project_kernel, scales),
        2 * local // tile_of(local),
        core,
        (own, other, gain, *weights),
        [within_half(local, width)] * 2 + [all_of(gain)] + [own_columns(w) for w in weights],
        [half_columns(width, tile_of(local))] + [half_rows(tile_of(local), w.shape[1] // 2) for w in weights],
        [shape_of((width, 2 * local), BF16)]
        + [shape_of((2 * local, w.shape[1] // 2), BF16) for w in weights],
        [],
        2 * 2 * local * width * sum(w.shape[1] // 2 for w in weights),
        name,
    )


def memory_kernel(parts, core_ref, *refs):
    in_refs = refs[:parts]
    wk_ref, wv_ref = refs[parts : parts + 2]
    mt_refs, (k_ref, v_ref, all_ref) = refs[parts + 2 : -3], refs[-3:]
    rows = in_refs[0].shape[0]
    for i in range(parts):
        all_ref[i * rows : (i + 1) * rows, :] = in_refs[i][...]
    for slot, mt_ref in enumerate(mt_refs):
        mt_ref[...] = all_ref[2 * slot * rows : 2 * (slot + 1) * rows, :].astype(F32).T.astype(BF16)
    k_ref[...] = dot_nn(all_ref[...], wk_ref[...]).astype(BF16)
    v_ref[...] = dot_nn(all_ref[...], wv_ref[...]).astype(BF16)


def project_memory(core, parts, w_key, w_value):
    rows, width = parts[0].shape
    total = rows * len(parts)
    kw = w_key.shape[1] // 2
    return core_call(
        functools.partial(memory_kernel, len(parts)),
        1,
        core,
        (*parts, w_key, w_value),
        [all_of(p) for p in parts] + [own_columns(w_key), own_columns(w_value)],
        [fixed((width, 2 * rows))] * (len(parts) // 2) + [fixed((total, kw)), fixed((total, kw))],
        [shape_of((width, 2 * rows), BF16)] * (len(parts) // 2)
        + [shape_of((total, kw), BF16), shape_of((total, kw), BF16)],
        [pltpu.VMEM((total, width), BF16)],
        2 * total * width * 2 * kw,
        "project_memory",
    )


def join_kernel(low_base, project_next, core_ref, *refs):
    if low_base:
        own_ref, other_ref, refs = refs[0], refs[1], refs[2:]
        base = jnp.where(in_own_half(core_ref), own_ref[...], other_ref[...]).astype(F32)
    else:
        base, refs = refs[0][...], refs[1:]
    mixed_ref, got_ref, w_own_ref, w_other_ref, gain_ref = refs[:5]
    after = base + dot_nn(mixed_ref[...], w_own_ref[...]) + dot_nn(got_ref[...], w_other_ref[...])
    normed = normalise(after, gain_ref[...])
    low = normed.astype(BF16)
    if project_next:
        w_ref, after_ref, nt_ref, out_ref = refs[5:]
        out_ref[...] = dot_nn(low, w_ref[...]).astype(BF16) * BF16(score_scale)
    else:
        after_ref, nt_ref, out_ref = refs[5:]
        out_ref[...] = low
    after_ref[...] = after
    nt_ref[...] = normed.T.astype(BF16)


def join(core, base, mixed, got, w_out, gain, w_next, name):
    rows, half = mixed.shape
    width = w_out.shape[1]
    local = rows // 2
    low_base = isinstance(base, tuple)
    bases = base if low_base else (base,)
    base_specs = [within_half(local, width)] * 2 if low_base else [half_rows(tile_of(local), width)]
    nexts = () if w_next is None else (w_next,)
    out_width = width if w_next is None else w_next.shape[1] // 2
    return core_call(
        functools.partial(join_kernel, low_base, w_next is not None),
        rows // tile_of(local),
        core,
        (*bases, mixed, got, w_out, w_out, gain, *nexts),
        base_specs
        + [half_rows(tile_of(local), half), half_rows(tile_of(local), half), own_rows(w_out), other_rows(w_out), all_of(gain)]
        + [own_columns(w) for w in nexts],
        [half_rows(tile_of(local), width), half_columns(width, tile_of(local)), half_rows(tile_of(local), out_width)],
        [shape_of((rows, width), F32), shape_of((width, rows), BF16), shape_of((rows, out_width), BF16)],
        [],
        2 * rows * width * (width + out_width),
        name,
    )


def back_kernel(low_prior, products, core_ref, *refs):
    if low_prior:
        own_ref, other_ref, refs = refs[0], refs[1], refs[2:]
        prior = jnp.where(in_own_half(core_ref), own_ref[...], other_ref[...]).astype(F32)
    else:
        prior, refs = refs[0][...], refs[1:]
    value_ref, gain_ref, e_ref, got_ref, refs = refs[0], refs[1], refs[2], refs[3], refs[4:]
    if products:
        e = dot_nt(e_ref[...], refs[0][...]) + dot_nt(got_ref[...], refs[1][...])
        refs = refs[2:]
    else:
        e = e_ref[...].astype(F32) + got_ref[...].astype(F32)
    w_ref, grad_ref, half_ref, next_ref = refs
    grad = prior + rms_back(value_ref[...], gain_ref[...], e)
    grad_ref[...] = grad
    low = grad.astype(BF16)
    half = low.shape[1] // 2
    half_ref[...] = jnp.where(core_ref[0] == 0, low[:, :half], low[:, half:])
    next_ref[...] = dot_nt(low, w_ref[...]).astype(BF16)


def back(core, prior, values, gain, e, got, w_in, w_out, name):
    rows, width = values.shape
    local = rows // 2
    low_prior = isinstance(prior, tuple)
    priors = prior if low_prior else (prior,)
    prior_specs = [within_half(local, width)] * 2 if low_prior else [half_rows(tile_of(local), width)]
    ins = () if w_in is None else (w_in, w_in)
    in_specs = [] if w_in is None else [own_columns(w_in), other_columns(w_in)]
    half = w_out.shape[0] // 2
    return core_call(
        functools.partial(back_kernel, low_prior, w_in is not None),
        rows // tile_of(local),
        core,
        (*priors, values, gain, e, got, *ins, w_out),
        prior_specs
        + [half_rows(tile_of(local), width), all_of(gain), half_rows(tile_of(local), e.shape[1]), half_rows(tile_of(local), e.shape[1])]
        + in_specs
        + [own_rows(w_out)],
        [half_rows(tile_of(local), width), half_rows(tile_of(local), width // 2), half_rows(tile_of(local), half)],
        [
            shape_of((rows, width), F32),
            shape_of((rows, width // 2), BF16),
            shape_of((rows, half), BF16),
        ],
        [],
        2 * rows * width * (half + 2 * e.shape[1] * len(ins) // 2),
        name,
    )


def last_kernel(core_ref, prior_ref, base_ref, gain_ref, q_ref, pair_ref, got_ref, *refs):
    wq_own, wq_other, wk_own, wk_other, wv_own, wv_other, grad_ref = refs
    qw = wq_own.shape[1]
    kw = wk_own.shape[1]
    e = dot_nt(q_ref[...], wq_own[...]) + dot_nt(got_ref[:, :qw], wq_other[...])
    for m in range(kw // PAIR):
        c, span = 2 * PAIR * m, slice(PAIR * m, PAIR * (m + 1))
        e = e + dot_nt(pair_ref[:, c : c + PAIR], wk_own[:, span])
        e = e + dot_nt(got_ref[:, qw + c : qw + c + PAIR], wk_other[:, span])
        c = c + PAIR
        e = e + dot_nt(pair_ref[:, c : c + PAIR], wv_own[:, span])
        e = e + dot_nt(got_ref[:, qw + c : qw + c + PAIR], wv_other[:, span])
    grad_ref[...] = prior_ref[...] + rms_back(base_ref[...].astype(F32), gain_ref[...], e)


def last(core, prior, base, gain, grad_q, pair, got, w_query, w_key, w_value):
    local, width = base.shape
    steps = local // tile_of(local)

    def own_tile(array):
        return pl.BlockSpec((tile_of(local), array.shape[1]), lambda i, c: (c[0] * steps + i, 0))

    weights = (w_query, w_query, w_key, w_key, w_value, w_value)
    specs = []
    for w in (w_query, w_key, w_value):
        specs += [own_columns(w), other_columns(w)]
    return core_call(
        last_kernel,
        local // tile_of(local),
        core,
        (prior, base, gain, grad_q, pair, got, *weights),
        [own_tile(prior), half_rows(tile_of(local), width), all_of(gain), own_tile(grad_q), own_tile(pair), half_rows(tile_of(local), got.shape[1])]
        + specs,
        [half_rows(tile_of(local), width)],
        [shape_of((local, width), F32)],
        [],
        2 * local * width * 2 * width,
        "last",
    )


def chip_at(order, p, where):
    masks, core_bit = order
    index = where[2] ^ masks[p]
    return index if core_bit is None else index ^ (where[0] << core_bit)


def outer_kernel(orders, terms, split, count, has_extra, where_ref, *refs):
    lefts = []
    for parts in split:
        lefts.append(refs[:parts])
        refs = refs[parts:]
    right_refs, refs = refs[:count], refs[count:]
    if has_extra:
        extra_ref, refs = refs[0], refs[1:]
    keep_ref, send_ref, sorted_refs = refs[0], refs[1], refs[2:]
    blocks = len(orders[0][0])
    for at, (left, sorted_ref) in enumerate(zip(lefts, sorted_refs)):
        rows = sorted_ref.shape[0] // blocks
        for p in range(blocks):
            index = chip_at(orders[at], p, where_ref)
            if len(left) == 1:
                piece = left[0][pl.ds(pl.multiple_of(index * rows, rows), rows), :]
            else:
                middle = blocks // 2
                first = pl.multiple_of(jnp.minimum(index, middle - 1) * rows, rows)
                second = pl.multiple_of(jnp.maximum(index - middle, 0) * rows, rows)
                piece = jnp.where(
                    index < middle, left[0][pl.ds(first, rows), :], left[1][pl.ds(second, rows), :]
                )
            sorted_ref[p * rows : (p + 1) * rows, :] = piece
    middle = sorted_refs[0].shape[0] // 2
    for out_ref, span in ((send_ref, slice(middle, 2 * middle)), (keep_ref, slice(0, middle))):
        column = 0
        for products in terms:
            total = None
            for left, right, first, start, size in products:
                depth = sorted_refs[left].shape[1]
                factor = right_refs[right][first : first + depth, start : start + size]
                part = dot_nn(sorted_refs[left][span, :], factor)
                total = part if total is None else total + part
            width = total.shape[1]
            out_ref[:, column : column + width] = total.astype(BF16)
            column += width
    if has_extra:
        rows = sorted_refs[0].shape[0] // blocks
        lanes = extra_ref.shape[1]
        row = lax.broadcasted_iota(jnp.int32, (rows, lanes), 0)
        for p in range(blocks):
            index = 2 * chip_at(orders[0], p, where_ref)
            block = jnp.where(row == 0, extra_ref[pl.ds(index, 1), :], 0.0)
            block = jnp.where(row == rows // 2, extra_ref[pl.ds(index + 1, 1), :], block)
            out_ref = keep_ref if p < blocks // 2 else send_ref
            first = p % (blocks // 2) * rows
            out_ref[first : first + rows, column:] = block.astype(BF16)


def outer_halves(where, orders, lefts, rights, terms, extra=None):
    blocks = len(orders[0][0])
    lefts = [v if isinstance(v, tuple) else (v,) for v in lefts]
    totals = [sum(v.shape[0] for v in left) for left in lefts]
    rows = totals[0] // blocks
    if rows % 16:
        joined = [jnp.concatenate(left, axis=0) for left in lefts]
        joined = [
            jnp.concatenate(
                [lax.dynamic_slice_in_dim(v, chip_at(order, p, where) * rows, rows, 0) for p in range(blocks)],
                axis=0,
            )
            for v, order in zip(joined, orders)
        ]
        half = totals[0] // 2
        columns = []
        for products in terms:
            columns.append(
                sum(
                    dot_nn(joined[l], rights[r][first : first + joined[l].shape[1], start : start + size])
                    for l, r, first, start, size in products
                )
            )
        total = jnp.concatenate(columns, axis=1).astype(BF16)
        return total[:half], total[half:]
    width = sum(products[0][4] for products in terms)
    extras = () if extra is None else (extra,)
    if extras:
        width += extra.shape[1]
    half = shape_of((totals[0] // 2, width), BF16)
    flops = 0
    for products in terms:
        for l, _, _, _, size in products:
            flops += 2 * totals[l] * lefts[l][0].shape[1] * size
    whole = pl.BlockSpec(memory_space=pltpu.VMEM)
    flat = [v for left in lefts for v in left]
    return pl.pallas_call(
        functools.partial(outer_kernel, orders, terms, [len(left) for left in lefts], len(rights), bool(extras)),
        in_specs=[pl.BlockSpec(memory_space=pltpu.SMEM)] + [whole] * (len(flat) + len(rights) + len(extras)),
        out_specs=[whole, whole],
        out_shape=[half, half],
        scratch_shapes=[
            pltpu.VMEM((total, left[0].shape[1]), BF16) for total, left in zip(totals, lefts)
        ],
        compiler_params=pltpu.CompilerParams(vmem_limit_bytes=VMEM_LIMIT),
        cost_estimate=cost(flops, 0, flops // 400),
        name="outer_halves",
    )(where, *flat, *rights, *extras)


def pick(value, index, axis):
    return lax.dynamic_index_in_dim(value, index, axis, keepdims=False)


def bits_of(size):
    return (size - 1).bit_length()


class Places:
    def __init__(self):
        self.seq = lax.axis_size("seq")
        self.dp = lax.axis_size("dp")
        self.nx = self.seq // 2
        self.chips = self.dp * self.nx
        place = lax.axis_index("seq")
        self.core = place & 1
        self.x = place >> 1
        self.d = lax.axis_index("dp")
        self.dp_bits = bits_of(self.dp)
        self.x_bits = bits_of(self.nx)
        self.chip = self.d * self.nx + self.x
        self.names = [("dp", b) for b in reversed(range(self.dp_bits))] + [
            ("x", b) for b in reversed(range(self.x_bits))
        ]

    def swap_core(self, value):
        return lax.ppermute(value, "seq", [(s, s ^ 1) for s in range(self.seq)])

    def shift_x(self, value, by):
        pairs = [(s, (s + 2 * by) % self.seq) for s in range(self.seq)]
        return lax.ppermute(value, "seq", pairs)

    def flip(self, value, names):
        d_mask = sum(1 << bit for axis, bit in names if axis == "dp")
        s_mask = sum(2 << bit for axis, bit in names if axis == "x")
        pairs = [
            (d * self.seq + s, (d ^ d_mask) * self.seq + (s ^ s_mask))
            for d in range(self.dp)
            for s in range(self.seq)
        ]
        return lax.ppermute(value, ("dp", "seq"), pairs)

    def by_core(self, own, other, axis):
        first = jnp.concatenate([own, other], axis=axis)
        second = jnp.concatenate([other, own], axis=axis)
        return jnp.where(self.core == 0, first, second)

    def core_rows(self, value, mine):
        half = value.shape[0] // 2
        which = self.core if mine else 1 - self.core
        return lax.dynamic_slice_in_dim(value, which * half, half, 0)

    def stages(self, kind):
        dp0 = [(("dp", 0),)]
        rest = [(("dp", b),) for b in range(1, self.dp_bits)]
        xs = [(("x", b),) for b in range(self.x_bits)]
        at_once = [tuple(one[0] for one in rest)] if len(rest) == 2 else rest
        z1, z2 = rest[:1], rest[1:]
        return {
            "x_y_z1_z2": xs + dp0 + z1 + z2,
            "y_x_z1_z2": dp0 + xs + z1 + z2,
            "y_x_zz": dp0 + xs + at_once,
            "z1_x_wait_z2_y": z1 + xs + [()] + z2 + dp0,
            "x_z1_y_z2": xs + z1 + dp0 + z2,
            "z1_x_y_z2": z1 + xs + dp0 + z2,
        }[kind]

    def block_order(self, kind, core_major=False):
        order = [name for stage in self.stages(kind) for name in stage]
        count = len(order)
        masks = []
        for p in range(self.chips):
            mask = 0
            for k, name in enumerate(order):
                if (p >> (count - 1 - k)) & 1:
                    mask |= 1 << (count - 1 - self.names.index(name))
            masks.append(mask)
        return tuple(masks), count - 1 if core_major else None


class ChipSum:
    def __init__(self, at, kind, kept, sent=None):
        self.at = at
        self.todo = list(at.stages(kind))
        self.rows, self.width = kept.shape
        self.parts = [([kept], 0)]
        self.sent = sent
        if sent is not None:
            self.parts.append(([at.flip(sent, self.todo.pop(0))], 0))

    def result(self):
        return sum(
            box[0][: self.rows, column : column + self.width].astype(F32) for box, column in self.parts
        )


def fold_kernel(plan, count, *refs):
    in_refs, out_refs = refs[:count], refs[count:]
    for sources, (out, out_column), (rows, width) in plan:
        step = 32 if rows % 32 == 0 else 16

        def body(i, carried, sources=sources, out=out, out_column=out_column, width=width, step=step):
            span = pl.ds(pl.multiple_of(i * step, 16), step)
            total = None
            for at, column in sources:
                part = in_refs[at][span, column : column + width].astype(F32)
                total = part if total is None else total + part
            out_refs[out][span, out_column : out_column + width] = total.astype(BF16)
            return carried

        lax.fori_loop(0, rows // step, body, 0)


def fold_arrays(plan, inputs, shapes):
    if all(rows % 16 == 0 for _, _, (rows, _) in plan):
        return pl.pallas_call(
            functools.partial(fold_kernel, plan, len(inputs)),
            grid=(1,),
            in_specs=[
                pl.BlockSpec((rows, array.shape[1]), lambda i, block=block: (block, 0))
                for array, block, rows in inputs
            ],
            out_specs=[pl.BlockSpec(shape, lambda i: (0, 0)) for shape in shapes],
            out_shape=[shape_of(shape, BF16) for shape in shapes],
            compiler_params=kernel_params(),
            cost_estimate=cost(1, 0, 1),
            name="fold",
        )(*[array for array, _, _ in inputs])
    outs = [jnp.zeros(shape, BF16) for shape in shapes]
    for sources, (out, out_column), (rows, width) in plan:
        total = 0.0
        for at, column in sources:
            array, block, size = inputs[at]
            total = total + array[block * size : (block + 1) * size, column : column + width].astype(F32)
        outs[out] = outs[out].at[:, out_column : out_column + width].set(total.astype(BF16))
    return outs


def fold(at, sums, *ties):
    inputs, plan, shapes, sends = [], [], [], {}

    def place_of(array, block, rows):
        for index, known in enumerate(inputs):
            if known[0] is array and known[1:] == (block, rows):
                return index
        inputs.append((array, block, rows))
        return len(inputs) - 1

    for one in sums:
        stage = one.todo.pop(0) if one.todo else ()
        one.rows >>= len(stage)
        for j in range(1, 1 << len(stage)):
            names = tuple(name for k, name in enumerate(stage) if (j >> (len(stage) - 1 - k)) & 1)
            sources = [(place_of(box[0], j, one.rows), column) for box, column in one.parts]
            sends.setdefault((names, one.rows), []).append((one, sources))
    for (names, rows), pieces in sends.items():
        column = 0
        for one, sources in pieces:
            plan.append((sources, (len(shapes), column), (rows, one.width)))
            column += one.width
        shapes.append((rows, column))
    outs = list(fold_arrays(plan, inputs, shapes))
    if ties:
        outs = together(*outs, *ties)
        outs, ties = list(outs[: len(shapes)]), outs[len(shapes) :]
    for out, ((names, rows), pieces) in zip(outs, sends.items()):
        box = [at.flip(out, names)]
        column = 0
        for one, _ in pieces:
            one.sent = out
            one.parts.append((box, column))
            column += one.width
    return ties


def settle(sums, *values):
    boxes = []
    for one in sums:
        for box, _ in one.parts[1:]:
            if not any(box is known for known in boxes):
                boxes.append(box)
    out = together(*[box[0] for box in boxes], *values)
    for box, value in zip(boxes, out):
        box[0] = value
    return out[len(boxes) :]


def finish_sum_kernel(plan, count, where_ref, *refs):
    in_refs, refs = refs[:count], refs[count:]
    out_refs, total_refs = refs[: 2 * len(plan)], refs[2 * len(plan) :]
    for at, ranges in enumerate(plan):
        mine_ref, other_ref, total_ref = out_refs[2 * at], out_refs[2 * at + 1], total_refs[at]
        first = 0
        for sources, width in ranges:
            total = None
            for index, column in sources:
                part = in_refs[index][:, column : column + width].astype(F32)
                total = part if total is None else total + part
            total_ref[:, first : first + width] = total
            first += width
        half = mine_ref.shape[0]
        core = where_ref[0]
        mine_ref[...] = total_ref[pl.ds(pl.multiple_of(core * half, half), half), :]
        other_ref[...] = total_ref[pl.ds(pl.multiple_of((1 - core) * half, half), half), :]


def finish_sums(places, where, groups):
    if any(group[0].rows % 32 and group[0].rows % 16 for group in groups):
        outs = []
        for group in groups:
            total = jnp.concatenate([one.result() for one in group], axis=1)
            outs.append((places.core_rows(total, True), places.core_rows(total, False)))
        return outs
    inputs, plan = [], []

    def place_of(array, rows):
        for index, known in enumerate(inputs):
            if known[0] is array and known[1] == rows:
                return index
        inputs.append((array, rows))
        return len(inputs) - 1

    shapes, scratch = [], []
    for group in groups:
        ranges = []
        for one in group:
            ranges.append(
                ([(place_of(box[0], one.rows), column) for box, column in one.parts], one.width)
            )
        plan.append(ranges)
        width = sum(one.width for one in group)
        shapes += [(group[0].rows // 2, width)] * 2
        scratch.append(pltpu.VMEM((group[0].rows, width), F32))
    outs = core_call(
        functools.partial(finish_sum_kernel, plan, len(inputs)),
        1,
        where,
        [array for array, _ in inputs],
        [pl.BlockSpec((rows, array.shape[1]), lambda i, c: (0, 0)) for array, rows in inputs],
        [fixed(shape) for shape in shapes],
        [shape_of(shape, F32) for shape in shapes],
        scratch,
        16,
        "finish_sums",
    )
    return [(outs[2 * k], outs[2 * k + 1]) for k in range(len(groups))]


def finish_kernel(plan, gains, count, bias_at, where_ref, *refs):
    group_refs, refs = refs[: 2 * count], refs[2 * count :]
    weights = sum(len(pairs) for pairs in gains)
    weight_refs, gain_ref, bias_out, refs = refs[:weights], refs[weights], refs[weights + 1], refs[weights + 2 :]
    out_refs, gain_outs = refs[: len(plan)], refs[len(plan) :]
    span = slice(bias_at, bias_at + bias_out.shape[1])
    bias_out[...] = group_refs[0][0:1, span] + group_refs[1][0:1, span]
    first_core = where_ref[0] == 0
    for (group, column, width), out_ref in zip(plan, out_refs):
        mine = group_refs[2 * group][:, column : column + width]
        got = group_refs[2 * group + 1][:, column : column + width]
        out_ref[:, :width] = jnp.where(first_core, mine, got)
        out_ref[:, width:] = jnp.where(first_core, got, mine)
    at = 0
    for k, (pairs, gain_out) in enumerate(zip(gains, gain_outs)):
        total = None
        for matrix in pairs:
            product = out_refs[matrix][...] * weight_refs[at][...].astype(F32)
            at += 1
            part = product[:, :PAIR]
            for first in range(PAIR, product.shape[1], PAIR):
                part = part + product[:, first : first + PAIR]
            total = part if total is None else total + part
        gain_out[0] = jnp.sum(total.T, axis=0, keepdims=True) / gain_ref[k, 0]


def finish(places, where, joined, plan, gains, gain_rows, bias_at, bias_share):
    half = joined[0][0].shape[0]
    device = 2 * places.chip + places.core
    if half % 16:
        outs = []
        for group, column, width in plan:
            mine, got = joined[group]
            outs.append(places.by_core(mine[:, column : column + width], got[:, column : column + width], 1))
        shares = []
        for gain, pairs in gains:
            total = 0.0
            for matrix, weight in pairs:
                rows = lax.dynamic_slice_in_dim(weight, device * half, half, 0).astype(F32)
                total = total + jnp.sum(rows * outs[matrix], axis=1)
            shares.append(total / pick(gain_rows[gain], device, 0)[0])
        span = slice(bias_at, bias_at + bias_share)
        return outs, shares, joined[0][0][0, span] + joined[0][1][0, span]
    flat = [v for pair in joined for v in pair]
    weights = [weight for _, pairs in gains for _, weight in pairs]
    outs = core_call(
        functools.partial(finish_kernel, plan, [[matrix for matrix, _ in pairs] for _, pairs in gains], len(joined), bias_at),
        1,
        where,
        (*flat, *weights, gain_rows),
        [all_of(v) for v in flat]
        + [pl.BlockSpec((half, w.shape[1]), lambda i, c: (c[1], 0)) for w in weights]
        + [pl.BlockSpec((len(gains), 1, 1, half), lambda i, c: (0, c[1], 0, 0))],
        [fixed((1, bias_share))]
        + [fixed((joined[group][0].shape[0], 2 * width)) for group, _, width in plan]
        + [fixed((1, 1, half)) for _ in gains],
        [shape_of((1, bias_share), F32)]
        + [shape_of((joined[group][0].shape[0], 2 * width), F32) for group, _, width in plan]
        + [shape_of((1, 1, half), F32) for _ in gains],
        [],
        16,
        "finish",
    )
    bias, outs = outs[0].reshape(bias_share), outs[1:]
    return outs[: len(plan)], [v.reshape(half) for v in outs[len(plan) :]], bias


def together(*values):
    return lax.optimization_barrier(values)


def per_device(
    target,
    memory,
    mem_lengths,
    mem_mask,
    distance_buckets,
    norm_self,
    w_query,
    w_key,
    w_value,
    w_out,
    pos_table,
    norm_cross,
    wc_query,
    wc_key,
    wc_value,
    wc_out,
    norm_ffn,
    w_gate,
    w_up,
    w_down,
    out_grad,
):
    at = Places()
    core, nx = at.core, at.nx
    local, width = target.shape[1], target.shape[2]
    mem_local = memory.shape[1]
    rows = 2 * local
    full = distance_buckets.shape[0]
    qw = HEADS * HEAD_DIM // 2
    kw = KV * HEAD_DIM // 2
    head_count = HEADS // 2
    place = at.x.astype(jnp.int32).reshape(1)
    core_arg = core.astype(jnp.int32).reshape(1)
    gain_self = norm_self.reshape(1, width)
    gain_cross = norm_cross.reshape(1, width)
    gain_ffn = norm_ffn.reshape(1, width)

    tokens = target.reshape(local, width)
    far_tokens = [at.shift_x(tokens, s) for s in range(1, nx)]
    tokens_got = at.swap_core(tokens)
    memories = memory.reshape(mem_local, width)
    far_memories = [at.shift_x(memories, s) for s in range(1, nx)]
    memories_got = at.swap_core(memories)
    grads = out_grad.reshape(local, width)
    grads_got = at.swap_core(grads)

    normed_t, query, keys, values = project(
        core_arg, tokens, tokens_got, gain_self, (w_query, w_key, w_value), (score_scale, None, None), "project"
    )
    query, grads_got, pos_table, distance_buckets, mem_mask = together(
        query, grads_got, pos_table, distance_buckets, mem_mask
    )
    grad_chip = at.by_core(grads, grads_got, 0)

    own_table = lax.dynamic_slice_in_dim(pos_table, core * head_count, head_count, 0)
    onehot = (distance_buckets[:, None] == jnp.arange(BUCKETS, dtype=jnp.int32)[None, :]).astype(F32)
    by_distance = lax.dot_general(
        own_table, onehot, (((1,), (1,)), ((), ())), precision=lax.Precision.HIGHEST
    )
    bias_vec = jnp.pad(by_distance, ((0, 0), (BLK, 0))).reshape(head_count // 2, 2, BLK + full)

    mem_ids = jnp.arange(mem_mask.shape[1], dtype=jnp.int32)
    valid = (mem_ids < mem_lengths[0]) & ((mem_mask[0] == 1) | (mem_ids == 0))
    mask_add = jnp.where(valid, 0.0, big_negative).astype(F32).reshape(2 * nx, mem_local)
    slot_of = jnp.array([s for s in range(nx) for c in range(2)], jnp.int32)
    core_of = jnp.array([c for s in range(nx) for c in range(2)], jnp.int32)
    mask_rows = (((at.x - slot_of + nx) % nx) * 2 + (core ^ core_of))[:, None] == jnp.arange(2 * nx)[None, :]
    mask_col = jnp.sum(jnp.where(mask_rows[:, :, None], mask_add[None], 0.0), axis=1).reshape(-1, 1)

    grad_half = lax.dynamic_slice_in_dim(grad_chip, core * (width // 2), width // 2, 1)
    where = jnp.stack([core, 2 * at.chip + core, at.chip]).astype(jnp.int32)
    tied = together(*far_tokens, query, grad_chip, grad_half, bias_vec, mask_col, where)
    far_tokens = list(tied[: nx - 1])
    grad_chip, grad_half, bias_vec, mask_col, where = tied[nx:]
    keys, values, normed_ts = [keys], [values], [normed_t]
    for far in far_tokens:
        far_t, far_k, far_v = project(
            core_arg, far, at.swap_core(far), gain_self, (w_key, w_value), (None, None), "project_far"
        )
        normed_ts.append(far_t)
        keys.append(far_k)
        values.append(far_v)

    mixed, mixed_t, lse_self = self_forward(place, query, keys, values, bias_vec)
    mixed, mixed_t, memories_got, *far_memories = together(mixed, mixed_t, memories_got, *far_memories)
    mem_parts = [memories, memories_got]
    for far in far_memories:
        mem_parts += [far, at.swap_core(far)]
    *mem_ts, mem_keys, mem_values = project_memory(core_arg, mem_parts, wc_key, wc_value)
    mixed_got = at.swap_core(mixed)
    mixed_t_got = at.swap_core(mixed_t)
    after_self, cross_t, cross_query = join(
        core_arg, (tokens, tokens_got), mixed, mixed_got, w_out, gain_cross, wc_query, "join_self"
    )

    crossed, crossed_t, lse_cross = cross_forward(cross_query, mem_keys, mem_values, mask_col)
    crossed_got = at.swap_core(crossed)
    crossed_t_got = at.swap_core(crossed_t)
    after_cross, ffn_t, normed_ffn = join(
        core_arg, after_self, crossed, crossed_got, wc_out, gain_ffn, None, "join_cross"
    )

    hidden_t, e_part, out_mine, out_other, gate_keep, gate_send, up_keep, up_send = ffn(
        where,
        normed_ffn,
        ffn_t,
        grad_chip,
        w_gate,
        w_up,
        w_down,
        [at.block_order("x_y_z1_z2"), at.block_order("y_x_z1_z2")],
    )
    ffn_half = w_gate.shape[1] // 2
    gate_sum = ChipSum(at, "x_y_z1_z2", gate_keep, gate_send)
    up_sum = ChipSum(at, "y_x_z1_z2", up_keep, up_send)
    hidden_t_got = at.swap_core(hidden_t)
    e_got = at.swap_core(e_part)
    out_got = at.swap_core(out_other)
    down_halves = outer_halves(
        where,
        [at.block_order("z1_x_wait_z2_y", True)], [(hidden_t, hidden_t_got)], [grad_half], [[(0, 0, 0, 0, width // 2)]]
    )
    e_part, *down_halves = together(e_part, *down_halves)
    down_sum = ChipSum(at, "z1_x_wait_z2_y", *down_halves)
    grad_after_cross, cross_half, grad_crossed = back(
        core_arg, (grads, grads_got), after_cross, gain_ffn, e_part, e_got, None, wc_out, "back_ffn"
    )

    grad_cq, grad_mem = cross_backward(
        cross_query, mem_keys, mem_values, mask_col, grad_crossed, crossed, lse_cross, nx
    )
    grad_cq_got = at.swap_core(grad_cq)
    wc_out_halves = outer_halves(
        where,
        [at.block_order("z1_x_y_z2", True)],
        [(crossed_t, crossed_t_got)],
        [cross_half],
        [[(0, 0, 0, 0, width // 2)]],
    )
    turns = kw // PAIR
    k_columns = [2 * PAIR * m for m in range(turns)]
    v_columns = [2 * PAIR * m + PAIR for m in range(turns)]
    wc_in_halves = outer_halves(
        where,
        [at.block_order("y_x_z1_z2")] * (1 + nx),
        [cross_t, *mem_ts],
        [grad_cq, *grad_mem],
        [[(0, 0, 0, 0, qw)]] + [[(1 + s, 1 + s, 0, c, PAIR) for s in range(nx)] for c in k_columns + v_columns],
    )
    mem_got = [at.shift_x(grad_mem[s], nx - s) for s in range(1, nx)]

    both = [gate_sum, up_sum]
    tied = settle(both, grad_cq, grad_cq_got, *wc_out_halves)
    grad_cq, grad_cq_got, *wc_out_halves = fold(at, both, *tied)
    grad_after_self, self_half, grad_mixed = back(
        core_arg, grad_after_cross, after_self, gain_cross, grad_cq, grad_cq_got, wc_query, w_out, "back_cross"
    )
    out_halves = outer_halves(
        where,
        [at.block_order("x_z1_y_z2", True)],
        [(mixed_t, mixed_t_got)],
        [self_half],
        [[(0, 0, 0, 0, width // 2)]],
    )
    ffn_sums = [gate_sum, up_sum, down_sum]
    tied = settle(
        ffn_sums,
        grad_mixed,
        grad_after_self,
        out_mine,
        out_got,
        *wc_in_halves,
        *out_halves,
        *wc_out_halves,
        grad_mem[0],
        *mem_got,
    )
    grad_mixed, grad_after_self, out_mine, out_got = tied[:4]
    halves = tied[4:10]
    grad_mem_chip, mem_got = tied[10], tied[11:]

    grad_mixed, *halves = fold(at, ffn_sums, grad_mixed, *halves)
    wc_in_sum = ChipSum(at, "y_x_z1_z2", *halves[:2])
    out_sum = ChipSum(at, "x_z1_y_z2", *halves[2:4])
    wc_out_sum = ChipSum(at, "z1_x_y_z2", *halves[4:])
    early = [*ffn_sums, wc_in_sum, out_sum, wc_out_sum]
    grad_q, grad_pairs, diagonals = self_backward(
        place, query, keys, values, bias_vec, grad_mixed, mixed, lse_self
    )
    tied = settle(early, grad_q, diagonals, out_mine, out_got, grad_mem_chip, *grad_pairs, *mem_got)
    grad_q, diagonals, out_mine, out_got, grad_mem_chip = tied[:5]
    grad_pairs, mem_got = tied[5 : 5 + nx], tied[5 + nx :]
    pair_chip = grad_pairs[0]
    pair_got = [at.shift_x(grad_pairs[s], nx - s) for s in range(1, nx)]

    grad_q, diagonals, grad_mem_chip, out_mine = fold(at, early, grad_q, diagonals, grad_mem_chip, out_mine)

    own_bias = lax.dot_general(
        diagonals.reshape(head_count, -1)[:, BLK:],
        onehot,
        (((1,), (0,)), ((), ())),
        precision=lax.Precision.HIGHEST,
        preferred_element_type=F32,
    )
    table = lax.dynamic_update_slice_in_dim(
        jnp.zeros((HEADS, BUCKETS), F32), own_bias, core * head_count, 0
    ).reshape(2 * at.chips, -1)
    bias_share = table.shape[1]
    in_halves = outer_halves(
        where,
        [at.block_order("y_x_zz")] * nx,
        normed_ts,
        [grad_q, *grad_pairs],
        [[(0, 0, 0, 0, qw)]] + [[(s, 1 + s, 0, c, PAIR) for s in range(nx)] for c in k_columns + v_columns],
        jnp.pad(table, ((0, 0), (0, 128 - bias_share))),
    )
    in_sum = ChipSum(at, "y_x_zz", *in_halves)
    grad_mem_chip, out_mine, *pair_got = together(grad_mem_chip, out_mine, *pair_got)
    for got in pair_got:
        pair_chip = pair_chip + got
    every = [*early, in_sum]

    output = (
        at.core_rows(after_cross, True)
        + out_mine.astype(F32)
        + out_got.astype(F32)
    ).astype(BF16)
    for got in mem_got:
        grad_mem_chip = grad_mem_chip + got
    mem_mine = grad_mem_chip[:mem_local]
    mem_other = at.swap_core(grad_mem_chip[mem_local:])

    def unpaired(columns):
        mine = [mem_mine[:, c : c + PAIR] for c in columns]
        other = [mem_other[:, c : c + PAIR] for c in columns]
        return at.by_core(jnp.concatenate(mine, axis=1), jnp.concatenate(other, axis=1), 1)

    grad_memory = dot_nt(unpaired(k_columns), wc_key) + dot_nt(unpaired(v_columns), wc_value)
    sent = jnp.concatenate([at.core_rows(grad_q, False), at.core_rows(pair_chip, False)], axis=1)
    (grad_target,) = last(
        core_arg,
        grad_after_self,
        tokens,
        gain_self,
        grad_q,
        pair_chip,
        at.swap_core(sent),
        w_query,
        w_key,
        w_value,
    )

    grad_target, grad_memory, output = settle(every, grad_target, grad_memory, output)
    while any(one.todo for one in every):
        fold(at, every)
    (norm_ffn,) = settle([down_sum], norm_ffn)
    gain_rows = jnp.stack([norm_ffn, norm_cross, norm_self]).reshape(3, 2 * at.chips, 1, -1)
    (gain_rows,) = settle(every, gain_rows)

    sums = [gate_sum, up_sum, wc_in_sum, out_sum, in_sum, wc_out_sum]
    rear, down_rows = finish_sums(at, where, [sums, [down_sum]])
    rear_join = (rear[0], at.swap_core(rear[1]))
    down_join = (down_rows[0], at.swap_core(down_rows[1]))
    wc_at = 2 * ffn_half
    out_at = wc_at + qw + 2 * kw
    in_at = out_at + width // 2
    bias_at = in_at + qw + 2 * kw
    (gate, up, cross_in, cross_key, cross_value, self_out, self_in, self_key, self_value, cross_out, down), gain_grads, bias_out = finish(
        at,
        where,
        [rear_join, down_join],
        [
            (0, 0, ffn_half),
            (0, ffn_half, ffn_half),
            (0, wc_at, qw),
            (0, wc_at + qw, kw),
            (0, wc_at + qw + kw, kw),
            (0, out_at, width // 2),
            (0, in_at, qw),
            (0, in_at + qw, kw),
            (0, in_at + qw + kw, kw),
            (0, in_at + in_sum.width, width // 2),
            (1, 0, width // 2),
        ],
        [
            (0, [(0, w_gate), (1, w_up)]),
            (1, [(2, wc_query)]),
            (2, [(6, w_query), (7, w_key), (8, w_value)]),
        ],
        gain_rows,
        bias_at,
        bias_share,
    )
    gain_ffn_grad, gain_cross_grad, gain_self_grad = gain_grads
    return (
        output.reshape(target.shape),
        grad_target.reshape(target.shape),
        grad_memory.reshape(memory.shape),
        gain_self_grad,
        self_in,
        self_key,
        self_value,
        self_out,
        bias_out,
        gain_cross_grad,
        cross_in,
        cross_key,
        cross_value,
        cross_out,
        gain_ffn_grad,
        gate,
        up,
        down,
    )


def solution(mesh):
    tokens = P("dp", "seq", None)
    row_share = P(("dp", "seq"))
    matrix_share = P(("dp", "seq"), None)
    return jax.shard_map(
        per_device,
        mesh=mesh,
        in_specs=(tokens, tokens, P("dp"), P("dp", None)) + (P(),) * 16 + (tokens,),
        out_specs=(tokens, tokens, tokens, row_share)
        + (matrix_share,) * 4
        + (row_share, row_share)
        + (matrix_share,) * 4
        + (row_share,)
        + (matrix_share,) * 3,
        check_vma=False,
    )
```

```python
import functools

import jax
import jax.numpy as jnp
from jax import lax
from jax.experimental import pallas as pl
from jax.experimental.pallas import tpu as pltpu
from jax.sharding import PartitionSpec as P

HEADS = 16
KV = 8
HEAD_DIM = 64
BUCKETS = 32
BLK = 256
PAIR = 2 * HEAD_DIM

norm_eps = 1e-06
big_negative = -1000000000.0
score_scale = HEAD_DIM ** (-0.5)
F32 = jnp.float32
BF16 = jnp.bfloat16
VMEM_LIMIT = 64 * 1024 * 1024


def dot_nn(a, b):
    return lax.dot_general(a, b, (((1,), (0,)), ((), ())), preferred_element_type=F32)


def dot_nt(a, b):
    return lax.dot_general(a, b, (((1,), (1,)), ((), ())), preferred_element_type=F32)


def dot_tn(a, b):
    return lax.dot_general(a, b, (((0,), (0,)), ((), ())), preferred_element_type=F32)


def lane_pick(source, dest):
    a = lax.broadcasted_iota(jnp.int32, (PAIR, PAIR), 0)
    b = lax.broadcasted_iota(jnp.int32, (PAIR, PAIR), 1)
    keep = (a - source == b - dest) & (b >= dest) & (b < dest + HEAD_DIM)
    return keep.astype(F32).astype(BF16)


def lane_pick_t(source, dest):
    a = lax.broadcasted_iota(jnp.int32, (PAIR, PAIR), 1)
    b = lax.broadcasted_iota(jnp.int32, (PAIR, PAIR), 0)
    keep = (a - source == b - dest) & (b >= dest) & (b < dest + HEAD_DIM)
    return keep.astype(F32).astype(BF16)


def bias_tile(bias_vec_ref, h, delta):
    piece = bias_vec_ref[0, h : h + 1, delta * BLK : delta * BLK + 2 * BLK]
    wide = jnp.broadcast_to(piece, (BLK, 2 * BLK))
    return pltpu.roll(wide, 0, 1, stride=1, stride_axis=0)[:, BLK:]


def tile_plan(row_blocks, slots):
    plan = [(delta, 0) for delta in range(row_blocks)]
    for slot in range(1, slots):
        plan += [(slot * row_blocks + c, slot) for c in range(1 - row_blocks, row_blocks)]
    return plan


def tile_at(row_blocks, rb, kb):
    slot, jb = kb // row_blocks, kb % row_blocks
    if slot == 0:
        return rb - jb, rb - jb
    first = row_blocks + (slot - 1) * (2 * row_blocks - 1)
    return first + rb - jb + row_blocks - 1, slot * row_blocks + rb - jb


def key_blocks(row_blocks, slots, rb):
    return list(range(rb + 1)) + list(range(row_blocks, row_blocks * slots))


def fill_bias(place, bias_vec_ref, tile_ref, row_blocks, slots):
    for at, (delta, slot) in enumerate(tile_plan(row_blocks, slots)):
        for h in range(2):
            tile = bias_tile(bias_vec_ref, h, delta)
            if slot:
                tile = tile + jnp.where(place >= slot, 0.0, big_negative)
            elif delta == 0:
                tile = jnp.where(causal_tile(), tile, big_negative)
            tile_ref[h, at] = tile


def causal_tile():
    key_pos = lax.broadcasted_iota(jnp.int32, (BLK, BLK), 0)
    row_pos = lax.broadcasted_iota(jnp.int32, (BLK, BLK), 1)
    return key_pos <= row_pos


def online_step(carry, scores, value_t):
    highest, total, mixed = carry
    new_high = jnp.maximum(highest, jnp.max(scores, axis=0, keepdims=True))
    fade = jnp.exp(highest - new_high)
    weights = jnp.exp(scores - new_high)
    total = total * fade + jnp.sum(weights, axis=0, keepdims=True)
    mixed = mixed * fade + dot_nn(value_t, weights.astype(BF16))
    return (new_high, total, mixed)


def first_step(scores, value_t):
    highest = jnp.max(scores, axis=0, keepdims=True)
    weights = jnp.exp(scores - highest)
    total = jnp.sum(weights, axis=0, keepdims=True)
    return (highest, total, dot_nn(value_t, weights.astype(BF16)))


def key_spans(row_blocks, slots, rb):
    own, end = (rb + 1) * BLK, row_blocks * slots * BLK
    first_far = row_blocks * BLK
    if slots == 1:
        return [(0, own)]
    if own == first_far:
        return [(0, end)]
    return [(0, own), (first_far, end)]


def self_forward_kernel(slots, place_ref, q_ref, b_ref, *refs):
    k_refs, v_refs = refs[:slots], refs[slots : 2 * slots]
    o_ref, ot_ref, lse_ref, tile_ref, kz_ref, vt_ref, s_ref, p_ref = refs[2 * slots :]
    parity = lax.rem(pl.program_id(0), 2)
    rows_all = q_ref.shape[0]
    row_blocks = rows_all // BLK
    fill_bias(place_ref[0], b_ref, tile_ref, row_blocks, slots)
    for h in range(2):
        for slot in range(slots):
            span = slice(slot * rows_all, (slot + 1) * rows_all)
            pick_k = lane_pick(parity * HEAD_DIM, h * HEAD_DIM)
            pick_v = lane_pick_t(parity * HEAD_DIM, h * HEAD_DIM)
            kz_ref[h, span, :] = dot_nn(k_refs[slot][...], pick_k).astype(BF16)
            vt_ref[h, :, span] = dot_nt(pick_v, v_refs[slot][...]).astype(BF16)
    for rb in range(row_blocks):
        rows = slice(rb * BLK, (rb + 1) * BLK)
        queries = q_ref[rows, :]
        spans = key_spans(row_blocks, slots, rb)
        highest = [None, None]
        for h in range(2):
            for first, end in spans:
                products = dot_nt(kz_ref[h, first:end, :], queries)
                for kb in range(first // BLK, end // BLK):
                    at, _ = tile_at(row_blocks, rb, kb)
                    scores = products[kb * BLK - first : (kb + 1) * BLK - first, :] + tile_ref[h, at]
                    s_ref[h, kb * BLK : (kb + 1) * BLK, :] = scores
                    top = jnp.max(scores, axis=0, keepdims=True)
                    highest[h] = top if highest[h] is None else jnp.maximum(highest[h], top)
        mixed_t = None
        for h in range(2):
            total = None
            part = None
            for first, end in spans:
                weights = jnp.exp(s_ref[h, first:end, :] - highest[h])
                one = jnp.sum(weights, axis=0, keepdims=True)
                total = one if total is None else total + one
                p_ref[h, first:end, :] = weights.astype(BF16)
            for first, end in spans:
                one = dot_nn(vt_ref[h, :, first:end], p_ref[h, first:end, :])
                part = one if part is None else part + one
            part = part / total
            mixed_t = part if mixed_t is None else mixed_t + part
            lse_ref[0, h : h + 1, rows] = highest[h] + jnp.log(total)
        ot_ref[:, rows] = mixed_t.astype(BF16)
        o_ref[rows, :] = mixed_t.T.astype(BF16)


def diagonal_sums(wide):
    rows, lanes = wide.shape
    while rows > 8:
        rows //= 2
        wide = wide[:rows] + pltpu.roll(wide[rows:], lanes - rows, 1)
    row = lax.broadcasted_iota(jnp.int32, (8, lanes), 0)
    total = jnp.where(row == 0, wide, 0.0)
    for b in range(1, 8):
        total = total + jnp.where(row == b, pltpu.roll(wide, lanes - b, 1), 0.0)
    return jnp.sum(total, axis=0, keepdims=True)


def row_products(grad_block, mixed_block):
    turned = (grad_block.astype(F32) * mixed_block.astype(F32)).T
    return [
        jnp.sum(turned[h * HEAD_DIM : (h + 1) * HEAD_DIM], axis=0, keepdims=True) for h in range(2)
    ]


def self_backward_kernel(slots, place_ref, q_ref, b_ref, do_ref, o_ref, lse_ref, *refs):
    k_refs, v_refs = refs[:slots], refs[slots : 2 * slots]
    dq_ref, diag_ref = refs[2 * slots : 2 * slots + 2]
    pair_refs, refs = refs[2 * slots + 2 : 3 * slots + 2], refs[3 * slots + 2 :]
    tile_ref, sum_ref, kz_ref, kt_ref, vz_ref, qp_ref, dop_ref, dk_acc, dv_acc, p_ref, ds_ref = refs
    parity = lax.rem(pl.program_id(0), 2)
    rows_all = q_ref.shape[0]
    row_blocks = rows_all // BLK
    fill_bias(place_ref[0], b_ref, tile_ref, row_blocks, slots)
    for h in range(2):
        in_pick = lane_pick(parity * HEAD_DIM, h * HEAD_DIM)
        out_pick = lane_pick(h * HEAD_DIM, parity * HEAD_DIM)
        pick_t = lane_pick_t(parity * HEAD_DIM, h * HEAD_DIM)
        for slot in range(slots):
            span = slice(slot * rows_all, (slot + 1) * rows_all)
            kz_ref[h, span, :] = dot_nn(k_refs[slot][...], in_pick).astype(BF16)
            kt_ref[h, :, span] = dot_nt(pick_t, k_refs[slot][...]).astype(BF16)
            vz_ref[h, span, :] = dot_nn(v_refs[slot][...], in_pick).astype(BF16)
        side = slice(h * rows_all, (h + 1) * rows_all)
        qp_ref[side, :] = dot_nn(q_ref[...], out_pick).astype(BF16)
        dop_ref[side, :] = dot_nn(do_ref[...], out_pick).astype(BF16)
    seen = set()
    for rb in range(row_blocks):
        rows = slice(rb * BLK, (rb + 1) * BLK)
        spans = key_spans(row_blocks, slots, rb)
        delta_rows = row_products(do_ref[rows, :], o_ref[rows, :])
        for kb in range(rb + 1, row_blocks):
            for h in range(2):
                side = slice(h * rows_all + rb * BLK, h * rows_all + (rb + 1) * BLK)
                keys = slice(kb * BLK, (kb + 1) * BLK)
                p_ref[keys, side] = jnp.zeros((BLK, BLK), BF16)
                ds_ref[keys, side] = jnp.zeros((BLK, BLK), BF16)
        for h in range(2):
            side = slice(h * rows_all + rb * BLK, h * rows_all + (rb + 1) * BLK)
            delta_row = delta_rows[h]
            lse = lse_ref[0, h : h + 1, rows]
            for first, end in spans:
                products = dot_nt(kz_ref[h, first:end, :], q_ref[rows, :])
                grad_products = dot_nt(vz_ref[h, first:end, :], do_ref[rows, :])
                for kb in range(first // BLK, end // BLK):
                    keys = slice(kb * BLK, (kb + 1) * BLK)
                    inner = slice(kb * BLK - first, (kb + 1) * BLK - first)
                    at, delta = tile_at(row_blocks, rb, kb)
                    probs = jnp.exp(products[inner, :] + tile_ref[h, at] - lse)
                    grad_scores = probs * (grad_products[inner, :] - delta_row)
                    p_ref[keys, side] = probs.astype(BF16)
                    ds_ref[keys, side] = grad_scores.astype(BF16)
                    if (h, delta) in seen:
                        sum_ref[h, delta] += grad_scores
                    else:
                        sum_ref[h, delta] = grad_scores
                        seen.add((h, delta))
    grad_v = dot_nn(p_ref[...], dop_ref[...])
    grad_k = dot_nn(ds_ref[...], qp_ref[...])

    @pl.when(parity == 0)
    def first():
        dv_acc[...] = grad_v
        dk_acc[...] = grad_k

    @pl.when(parity == 1)
    def second():
        dv_acc[...] += grad_v
        dk_acc[...] += grad_k

    grad_q = None
    for h in range(2):
        part = dot_nn(kt_ref[h], ds_ref[:, h * rows_all : (h + 1) * rows_all])
        grad_q = part if grad_q is None else grad_q + part
    dq_ref[...] = (grad_q.T * score_scale).astype(BF16)

    diag_ref[...] = jnp.zeros_like(diag_ref)
    for h in range(2):
        for delta in range(row_blocks * slots):
            wide = jnp.concatenate([jnp.zeros((BLK, BLK), F32), sum_ref[h, delta]], axis=1)
            diag_ref[0, h : h + 1, delta * BLK : delta * BLK + 2 * BLK] += diagonal_sums(wide)

    @pl.when(parity == 1)
    def store():
        for slot, pair_ref in enumerate(pair_refs):
            span = slice(slot * rows_all, (slot + 1) * rows_all)
            pair_ref[:, :PAIR] = dk_acc[span, :].astype(BF16)
            pair_ref[:, PAIR:] = dv_acc[span, :].astype(BF16)


def cross_forward_kernel(q_ref, k_ref, v_ref, m_ref, o_ref, ot_ref, lse_ref, kz_ref, vt_ref, s_ref, p_ref):
    parity = lax.rem(pl.program_id(0), 2)
    for h in range(2):
        kz_ref[h] = dot_nn(k_ref[...], lane_pick(parity * HEAD_DIM, h * HEAD_DIM)).astype(BF16)
        vt_ref[h] = dot_nt(lane_pick_t(parity * HEAD_DIM, h * HEAD_DIM), v_ref[...]).astype(BF16)
    for rb in range(q_ref.shape[0] // BLK):
        rows = slice(rb * BLK, (rb + 1) * BLK)
        queries = q_ref[rows, :]
        highest = []
        for h in range(2):
            scores = dot_nt(kz_ref[h], queries) + m_ref[...]
            s_ref[h] = scores
            highest.append(jnp.max(scores, axis=0, keepdims=True))
        mixed_t = None
        for h in range(2):
            weights = jnp.exp(s_ref[h] - highest[h])
            total = jnp.sum(weights, axis=0, keepdims=True)
            p_ref[h] = weights.astype(BF16)
            part = dot_nn(vt_ref[h], p_ref[h]) / total
            mixed_t = part if mixed_t is None else mixed_t + part
            lse_ref[0, h : h + 1, rows] = highest[h] + jnp.log(total)
        ot_ref[:, rows] = mixed_t.astype(BF16)
        o_ref[rows, :] = mixed_t.T.astype(BF16)


def cross_backward_kernel(
    slots,
    q_ref,
    k_ref,
    v_ref,
    m_ref,
    do_ref,
    o_ref,
    lse_ref,
    dq_ref,
    *refs,
):
    pair_refs, refs = refs[:slots], refs[slots:]
    cross_backward_body(slots, pair_refs, q_ref, k_ref, v_ref, m_ref, do_ref, o_ref, lse_ref, dq_ref, *refs)


def cross_backward_body(
    slots,
    pair_refs,
    q_ref,
    k_ref,
    v_ref,
    m_ref,
    do_ref,
    o_ref,
    lse_ref,
    dq_ref,
    kz_ref,
    kt_ref,
    vz_ref,
    qp_ref,
    dop_ref,
    dk_acc,
    dv_acc,
    p_ref,
    ds_ref,
):
    parity = lax.rem(pl.program_id(0), 2)
    rows_all = q_ref.shape[0]
    for h in range(2):
        in_pick = lane_pick(parity * HEAD_DIM, h * HEAD_DIM)
        out_pick = lane_pick(h * HEAD_DIM, parity * HEAD_DIM)
        kz_ref[h] = dot_nn(k_ref[...], in_pick).astype(BF16)
        kt_ref[h] = dot_nt(lane_pick_t(parity * HEAD_DIM, h * HEAD_DIM), k_ref[...]).astype(BF16)
        vz_ref[h] = dot_nn(v_ref[...], in_pick).astype(BF16)
        side = slice(h * rows_all, (h + 1) * rows_all)
        qp_ref[side, :] = dot_nn(q_ref[...], out_pick).astype(BF16)
        dop_ref[side, :] = dot_nn(do_ref[...], out_pick).astype(BF16)
    for rb in range(rows_all // BLK):
        rows = slice(rb * BLK, (rb + 1) * BLK)
        delta_rows = row_products(do_ref[rows, :], o_ref[rows, :])
        for h in range(2):
            side = slice(h * rows_all + rb * BLK, h * rows_all + (rb + 1) * BLK)
            delta_row = delta_rows[h]
            lse = lse_ref[0, h : h + 1, rows]
            probs = jnp.exp(dot_nt(kz_ref[h], q_ref[rows, :]) + m_ref[...] - lse)
            grad_products = dot_nt(vz_ref[h], do_ref[rows, :])
            p_ref[:, side] = probs.astype(BF16)
            ds_ref[:, side] = (probs * (grad_products - delta_row)).astype(BF16)
    grad_v = dot_nn(p_ref[...], dop_ref[...])
    grad_k = dot_nn(ds_ref[...], qp_ref[...])

    @pl.when(parity == 0)
    def first():
        dv_acc[...] = grad_v
        dk_acc[...] = grad_k

    @pl.when(parity == 1)
    def second():
        all_k = (dk_acc[...] + grad_k).astype(BF16)
        all_v = (dv_acc[...] + grad_v).astype(BF16)
        size = all_k.shape[0] // slots
        for slot, pair_ref in enumerate(pair_refs):
            pair_ref[:, :PAIR] = all_k[slot * size : (slot + 1) * size]
            pair_ref[:, PAIR:] = all_v[slot * size : (slot + 1) * size]

    grad_q = None
    for h in range(2):
        part = dot_nn(kt_ref[h], ds_ref[:, h * rows_all : (h + 1) * rows_all])
        grad_q = part if grad_q is None else grad_q + part
    dq_ref[...] = (grad_q.T * score_scale).astype(BF16)


def shape_of(shape, dtype):
    return jax.ShapeDtypeStruct(shape, dtype)


def tile_pair(rows):
    return pl.BlockSpec((rows, PAIR), lambda g: (0, g))


def tile_pair_t(rows):
    return pl.BlockSpec((PAIR, rows), lambda g: (g, 0))


def tile_group(rows):
    return pl.BlockSpec((rows, PAIR), lambda g: (0, g // 2))


def tile_both(rows):
    return pl.BlockSpec((rows, 2 * PAIR), lambda g: (0, g // 2))


def tile_rows(width):
    return pl.BlockSpec((1, 2, width), lambda g: (g, 0, 0))


def kernel_params():
    return pltpu.CompilerParams(
        dimension_semantics=("arbitrary",), vmem_limit_bytes=VMEM_LIMIT
    )


def cost(flops, transcendentals, nbytes):
    return pl.CostEstimate(
        flops=int(flops) // 16, transcendentals=0, bytes_accessed=int(nbytes) // 16
    )


def self_forward(place, q, ks, vs, bias_vec):
    rows, width = q.shape
    slots = len(ks)
    keys = rows * slots
    pairs = width // PAIR
    tiles = len(tile_plan(rows // BLK, slots))
    return pl.pallas_call(
        functools.partial(self_forward_kernel, slots),
        grid=(pairs,),
        in_specs=[pl.BlockSpec(memory_space=pltpu.SMEM), tile_pair(rows), tile_rows(bias_vec.shape[2])]
        + [tile_group(rows)] * (2 * slots),
        out_specs=[tile_pair(rows), tile_pair_t(rows), tile_rows(rows)],
        out_shape=[
            shape_of((rows, width), BF16),
            shape_of((width, rows), BF16),
            shape_of((pairs, 2, rows), F32),
        ],
        scratch_shapes=[
            pltpu.VMEM((2, tiles, BLK, BLK), F32),
            pltpu.VMEM((2, keys, PAIR), BF16),
            pltpu.VMEM((2, PAIR, keys), BF16),
            pltpu.VMEM((2, keys, BLK), F32),
            pltpu.VMEM((2, keys, BLK), BF16),
        ],
        compiler_params=kernel_params(),
        cost_estimate=cost(4 * 2 * rows * keys * width * 2, pairs * 2 * rows * keys, 8 * rows * width),
        name="self_forward",
    )(place, q, bias_vec, *ks, *vs)


def self_backward(place, q, ks, vs, bias_vec, grads, mixed, lse):
    rows, width = q.shape
    kv_width = ks[0].shape[1]
    slots = len(ks)
    keys = rows * slots
    pairs = width // PAIR
    tiles = len(tile_plan(rows // BLK, slots))
    grad_q, diagonals, *pairs_out = pl.pallas_call(
        functools.partial(self_backward_kernel, slots),
        grid=(pairs,),
        in_specs=[
            pl.BlockSpec(memory_space=pltpu.SMEM),
            tile_pair(rows),
            tile_rows(bias_vec.shape[2]),
            tile_pair(rows),
            tile_pair(rows),
            tile_rows(rows),
        ]
        + [tile_group(rows)] * (2 * slots),
        out_specs=[tile_pair(rows), tile_rows(bias_vec.shape[2])] + [tile_both(rows)] * slots,
        out_shape=[shape_of((rows, width), BF16), shape_of(bias_vec.shape, F32)]
        + [shape_of((rows, 2 * kv_width), BF16)] * slots,
        scratch_shapes=[
            pltpu.VMEM((2, tiles, BLK, BLK), F32),
            pltpu.VMEM((2, keys // BLK, BLK, BLK), F32),
            pltpu.VMEM((2, keys, PAIR), BF16),
            pltpu.VMEM((2, PAIR, keys), BF16),
            pltpu.VMEM((2, keys, PAIR), BF16),
            pltpu.VMEM((2 * rows, PAIR), BF16),
            pltpu.VMEM((2 * rows, PAIR), BF16),
            pltpu.VMEM((keys, PAIR), F32),
            pltpu.VMEM((keys, PAIR), F32),
            pltpu.VMEM((keys, 2 * rows), BF16),
            pltpu.VMEM((keys, 2 * rows), BF16),
        ],
        compiler_params=kernel_params(),
        cost_estimate=cost(10 * 2 * rows * keys * width * 2, pairs * 2 * rows * keys, 12 * rows * width),
        name="self_backward",
    )(place, q, bias_vec, grads, mixed, lse, *ks, *vs)
    return grad_q, pairs_out, diagonals


def cross_forward(q, k, v, mask_col):
    rows, width = q.shape
    keys = k.shape[0]
    pairs = width // PAIR
    return pl.pallas_call(
        cross_forward_kernel,
        grid=(pairs,),
        in_specs=[
            tile_pair(rows),
            tile_group(keys),
            tile_group(keys),
            pl.BlockSpec((keys, 1), lambda g: (0, 0)),
        ],
        out_specs=[tile_pair(rows), tile_pair_t(rows), tile_rows(rows)],
        out_shape=[
            shape_of((rows, width), BF16),
            shape_of((width, rows), BF16),
            shape_of((pairs, 2, rows), F32),
        ],
        scratch_shapes=[
            pltpu.VMEM((2, keys, PAIR), BF16),
            pltpu.VMEM((2, PAIR, keys), BF16),
            pltpu.VMEM((2, keys, BLK), F32),
            pltpu.VMEM((2, keys, BLK), BF16),
        ],
        compiler_params=kernel_params(),
        cost_estimate=cost(4 * 2 * rows * keys * width * 2, pairs * 2 * rows * keys, 8 * rows * width),
        name="cross_forward",
    )(q, k, v, mask_col)


def cross_backward(q, k, v, mask_col, grads, mixed, lse, slots):
    rows, width = q.shape
    keys, kv_width = k.shape
    pairs = width // PAIR
    grad_q, *pairs_out = pl.pallas_call(
        functools.partial(cross_backward_kernel, slots),
        grid=(pairs,),
        in_specs=[
            tile_pair(rows),
            tile_group(keys),
            tile_group(keys),
            pl.BlockSpec((keys, 1), lambda g: (0, 0)),
            tile_pair(rows),
            tile_pair(rows),
            tile_rows(rows),
        ],
        out_specs=[tile_pair(rows)] + [tile_both(keys // slots)] * slots,
        out_shape=[shape_of((rows, width), BF16)] + [shape_of((keys // slots, 2 * kv_width), BF16)] * slots,
        scratch_shapes=[
            pltpu.VMEM((2, keys, PAIR), BF16),
            pltpu.VMEM((2, PAIR, keys), BF16),
            pltpu.VMEM((2, keys, PAIR), BF16),
            pltpu.VMEM((2 * rows, PAIR), BF16),
            pltpu.VMEM((2 * rows, PAIR), BF16),
            pltpu.VMEM((keys, PAIR), F32),
            pltpu.VMEM((keys, PAIR), F32),
            pltpu.VMEM((keys, 2 * rows), BF16),
            pltpu.VMEM((keys, 2 * rows), BF16),
        ],
        compiler_params=kernel_params(),
        cost_estimate=cost(10 * 2 * rows * keys * width * 2, pairs * 2 * rows * keys, 12 * rows * width),
        name="cross_backward",
    )(q, k, v, mask_col, grads, mixed, lse)
    return grad_q, pairs_out


FBLK = 256


def ffn_kernel(
    orders,
    where_ref,
    x_ref,
    xt_ref,
    og_ref,
    wg_any,
    wu_any,
    wd_any,
    ht_any,
    e_any,
    out_mine_any,
    out_other_any,
    gate_keep_any,
    gate_send_any,
    up_keep_any,
    up_send_any,
    wg_ref,
    wu_ref,
    wd_ref,
    xs_ref,
    hb_ref,
    gg_ref,
    gu_ref,
    ht_ref,
    e_ref,
    out_ref,
    product_ref,
    in_sems,
    out_sems,
):
    hidden_width = gg_ref.shape[1]
    base = where_ref[0] * hidden_width
    spans = [(first, min(FBLK, hidden_width - first)) for first in range(0, hidden_width, FBLK)]
    loads = []
    for k, (first, size) in enumerate(spans):
        away = pl.ds(pl.multiple_of(base + first, 128), size)
        near = slice(first, first + size)
        loads.append(
            [
                pltpu.make_async_copy(wg_any.at[:, away], wg_ref.at[:, near], in_sems.at[0, k]),
                pltpu.make_async_copy(wu_any.at[:, away], wu_ref.at[:, near], in_sems.at[1, k]),
                pltpu.make_async_copy(wd_any.at[away, :], wd_ref.at[near, :], in_sems.at[2, k]),
            ]
        )
    for group in loads:
        for load in group:
            load.start()
    chips = len(orders[0][0])
    block = xt_ref.shape[0] // chips
    for order in range(2):
        for p in range(chips):
            first = pl.multiple_of(chip_at(orders[order], p, where_ref) * block, block)
            xs_ref[order, p * block : (p + 1) * block, :] = xt_ref[pl.ds(first, block), :]
    factor = (2.0 / jnp.pi) ** 0.5

    def combine(span, gate, up, grad_hidden):
        square = gate * gate
        bend = jnp.tanh(gate * (factor + (factor * 0.044715) * square))
        half = 0.5 + 0.5 * bend
        gelu = gate * half
        slope = half + gelu * (1.0 - bend) * (factor + (factor * 3 * 0.044715) * square)
        hidden = gelu * up
        hb_ref[:, span] = hidden.astype(BF16)
        ht_ref[span, :] = hidden.T.astype(BF16)
        gg_ref[:, span] = (grad_hidden * up * slope).astype(BF16)
        gu_ref[:, span] = (grad_hidden * gelu).astype(BF16)

    waiting = None
    for (first, size), group in zip(spans, loads):
        span = slice(first, first + size)
        for load in group:
            load.wait()
        gate = dot_nn(x_ref[...], wg_ref[:, span])
        up = dot_nn(x_ref[...], wu_ref[:, span])
        grad_hidden = dot_nt(og_ref[...], wd_ref[span, :])
        if waiting is not None:
            combine(*waiting)
        waiting = (span, gate, up, grad_hidden)
    combine(*waiting)
    stores = [pltpu.make_async_copy(ht_ref, ht_any, out_sems.at[0])]
    stores[-1].start()
    e_ref[...] = (dot_nt(gg_ref[...], wg_ref[...]) + dot_nt(gu_ref[...], wu_ref[...])).astype(BF16)
    stores.append(pltpu.make_async_copy(e_ref, e_any, out_sems.at[1]))
    stores[-1].start()
    middle = xt_ref.shape[0] // 2
    outs = [
        (0, gg_ref, middle, gate_send_any),
        (1, gu_ref, middle, up_send_any),
        (0, gg_ref, 0, gate_keep_any),
        (1, gu_ref, 0, up_keep_any),
    ]
    for k, (order, right_ref, first, any_ref) in enumerate(outs):
        product_ref[k] = dot_nn(xs_ref[order, first : first + middle, :], right_ref[...]).astype(BF16)
        stores.append(pltpu.make_async_copy(product_ref.at[k], any_ref, out_sems.at[2 + k]))
        stores[-1].start()
    out_ref[...] = dot_nn(hb_ref[...], wd_ref[...]).astype(BF16)
    half = out_ref.shape[0] // 2
    for k, (which, any_ref) in enumerate(((where_ref[0], out_mine_any), (1 - where_ref[0], out_other_any))):
        source = out_ref.at[pl.ds(pl.multiple_of(which * half, half), half), :]
        stores.append(pltpu.make_async_copy(source, any_ref, out_sems.at[6 + k]))
        stores[-1].start()
    for store in stores:
        store.wait()


def ffn(where, normed, normed_t, out_grad, w_gate, w_up, w_down, orders):
    rows, width = normed.shape
    hidden = w_gate.shape[1] // 2
    chunks = -(-hidden // FBLK)
    whole = pl.BlockSpec(memory_space=pltpu.VMEM)
    anywhere = pl.BlockSpec(memory_space=pl.ANY)
    half = (width // 2, hidden)
    return pl.pallas_call(
        functools.partial(ffn_kernel, orders),
        in_specs=[pl.BlockSpec(memory_space=pltpu.SMEM), whole, whole, whole] + [anywhere] * 3,
        out_specs=[anywhere] * 8,
        out_shape=[
            shape_of((hidden, rows), BF16),
            shape_of((rows, width), BF16),
            shape_of((rows // 2, width), BF16),
            shape_of((rows // 2, width), BF16),
        ]
        + [shape_of(half, BF16)] * 4,
        scratch_shapes=[
            pltpu.VMEM((width, hidden), BF16),
            pltpu.VMEM((width, hidden), BF16),
            pltpu.VMEM((hidden, width), BF16),
            pltpu.VMEM((2, width, rows), BF16),
            pltpu.VMEM((rows, hidden), BF16),
            pltpu.VMEM((rows, hidden), BF16),
            pltpu.VMEM((rows, hidden), BF16),
            pltpu.VMEM((hidden, rows), BF16),
            pltpu.VMEM((rows, width), BF16),
            pltpu.VMEM((rows, width), BF16),
            pltpu.VMEM((4, *half), BF16),
            pltpu.SemaphoreType.DMA((3, chunks)),
            pltpu.SemaphoreType.DMA((8,)),
        ],
        compiler_params=pltpu.CompilerParams(vmem_limit_bytes=VMEM_LIMIT),
        cost_estimate=cost(2 * 9 * rows * width * hidden, rows * hidden, 6 * width * hidden),
        name="ffn",
    )(where, normed, normed_t, out_grad, w_gate, w_up, w_down)


ROWS = 256


def tile_of(local):
    return min(local, ROWS)


def in_own_half(core_ref):
    return core_ref[0] == pl.program_id(0) // (pl.num_programs(0) // 2)


def within_half(local, width):
    steps = local // tile_of(local)
    return pl.BlockSpec((tile_of(local), width), lambda i, c: (lax.rem(i, steps), 0))


def normalise(values, gain):
    inverse = lax.rsqrt(jnp.mean(values * values, axis=-1, keepdims=True) + norm_eps)
    return values * inverse * gain


def rms_back(values, gain, grad):
    inverse = lax.rsqrt(jnp.mean(values * values, axis=-1, keepdims=True) + norm_eps)
    scaled = grad * gain
    mean_dot = jnp.mean(values * scaled, axis=-1, keepdims=True)
    unit = values * inverse
    return inverse * (scaled - unit * (inverse * mean_dot))


def project_kernel(scales, core_ref, own_ref, other_ref, gain_ref, *refs):
    count = len(scales)
    w_refs, nt_ref, out_refs = refs[:count], refs[count], refs[count + 1 :]
    values = jnp.where(in_own_half(core_ref), own_ref[...], other_ref[...]).astype(F32)
    normed = normalise(values, gain_ref[...])
    nt_ref[...] = normed.T.astype(BF16)
    low = normed.astype(BF16)
    for scale, w_ref, out_ref in zip(scales, w_refs, out_refs):
        out = dot_nn(low, w_ref[...]).astype(BF16)
        out_ref[...] = out if scale is None else out * BF16(scale)


def own_columns(weight):
    return pl.BlockSpec((weight.shape[0], weight.shape[1] // 2), lambda i, c: (0, c[0]))


def other_columns(weight):
    return pl.BlockSpec((weight.shape[0], weight.shape[1] // 2), lambda i, c: (0, 1 - c[0]))


def own_rows(array):
    return pl.BlockSpec((array.shape[0] // 2, array.shape[1]), lambda i, c: (c[0], 0))


def other_rows(array):
    return pl.BlockSpec((array.shape[0] // 2, array.shape[1]), lambda i, c: (1 - c[0], 0))


def all_of(array):
    return pl.BlockSpec(array.shape, lambda i, c: (0,) * array.ndim)


def half_rows(rows, width):
    return pl.BlockSpec((rows, width), lambda i, c: (i, 0))


def half_columns(width, rows):
    return pl.BlockSpec((width, rows), lambda i, c: (0, i))


def fixed(shape):
    return pl.BlockSpec(shape, lambda i, c: (0,) * len(shape))


def core_call(kernel, steps, core, args, in_specs, out_specs, out_shape, scratch, flops, name):
    return pl.pallas_call(
        kernel,
        grid_spec=pltpu.PrefetchScalarGridSpec(
            num_scalar_prefetch=1,
            grid=(steps,),
            in_specs=in_specs,
            out_specs=out_specs,
            scratch_shapes=scratch,
        ),
        out_shape=out_shape,
        compiler_params=kernel_params(),
        cost_estimate=cost(flops, 0, flops // 400),
        name=name,
    )(core, *args)


def project(core, own, other, gain, weights, scales, name):
    local, width = own.shape
    return core_call(
        functools.partial(project_kernel, scales),
        2 * local // tile_of(local),
        core,
        (own, other, gain, *weights),
        [within_half(local, width)] * 2 + [all_of(gain)] + [own_columns(w) for w in weights],
        [half_columns(width, tile_of(local))] + [half_rows(tile_of(local), w.shape[1] // 2) for w in weights],
        [shape_of((width, 2 * local), BF16)]
        + [shape_of((2 * local, w.shape[1] // 2), BF16) for w in weights],
        [],
        2 * 2 * local * width * sum(w.shape[1] // 2 for w in weights),
        name,
    )


def memory_kernel(parts, core_ref, *refs):
    in_refs = refs[:parts]
    wk_ref, wv_ref = refs[parts : parts + 2]
    mt_refs, (k_ref, v_ref, all_ref) = refs[parts + 2 : -3], refs[-3:]
    rows = in_refs[0].shape[0]
    for i in range(parts):
        all_ref[i * rows : (i + 1) * rows, :] = in_refs[i][...]
    for slot, mt_ref in enumerate(mt_refs):
        mt_ref[...] = all_ref[2 * slot * rows : 2 * (slot + 1) * rows, :].astype(F32).T.astype(BF16)
    k_ref[...] = dot_nn(all_ref[...], wk_ref[...]).astype(BF16)
    v_ref[...] = dot_nn(all_ref[...], wv_ref[...]).astype(BF16)


def project_memory(core, parts, w_key, w_value):
    rows, width = parts[0].shape
    total = rows * len(parts)
    kw = w_key.shape[1] // 2
    return core_call(
        functools.partial(memory_kernel, len(parts)),
        1,
        core,
        (*parts, w_key, w_value),
        [all_of(p) for p in parts] + [own_columns(w_key), own_columns(w_value)],
        [fixed((width, 2 * rows))] * (len(parts) // 2) + [fixed((total, kw)), fixed((total, kw))],
        [shape_of((width, 2 * rows), BF16)] * (len(parts) // 2)
        + [shape_of((total, kw), BF16), shape_of((total, kw), BF16)],
        [pltpu.VMEM((total, width), BF16)],
        2 * total * width * 2 * kw,
        "project_memory",
    )


def join_kernel(low_base, project_next, core_ref, *refs):
    if low_base:
        own_ref, other_ref, refs = refs[0], refs[1], refs[2:]
        base = jnp.where(in_own_half(core_ref), own_ref[...], other_ref[...]).astype(F32)
    else:
        base, refs = refs[0][...], refs[1:]
    mixed_ref, got_ref, w_own_ref, w_other_ref, gain_ref = refs[:5]
    after = base + dot_nn(mixed_ref[...], w_own_ref[...]) + dot_nn(got_ref[...], w_other_ref[...])
    normed = normalise(after, gain_ref[...])
    low = normed.astype(BF16)
    if project_next:
        w_ref, after_ref, nt_ref, out_ref = refs[5:]
        out_ref[...] = dot_nn(low, w_ref[...]).astype(BF16) * BF16(score_scale)
    else:
        after_ref, nt_ref, out_ref = refs[5:]
        out_ref[...] = low
    after_ref[...] = after
    nt_ref[...] = normed.T.astype(BF16)


def join(core, base, mixed, got, w_out, gain, w_next, name):
    rows, half = mixed.shape
    width = w_out.shape[1]
    local = rows // 2
    low_base = isinstance(base, tuple)
    bases = base if low_base else (base,)
    base_specs = [within_half(local, width)] * 2 if low_base else [half_rows(tile_of(local), width)]
    nexts = () if w_next is None else (w_next,)
    out_width = width if w_next is None else w_next.shape[1] // 2
    return core_call(
        functools.partial(join_kernel, low_base, w_next is not None),
        rows // tile_of(local),
        core,
        (*bases, mixed, got, w_out, w_out, gain, *nexts),
        base_specs
        + [half_rows(tile_of(local), half), half_rows(tile_of(local), half), own_rows(w_out), other_rows(w_out), all_of(gain)]
        + [own_columns(w) for w in nexts],
        [half_rows(tile_of(local), width), half_columns(width, tile_of(local)), half_rows(tile_of(local), out_width)],
        [shape_of((rows, width), F32), shape_of((width, rows), BF16), shape_of((rows, out_width), BF16)],
        [],
        2 * rows * width * (width + out_width),
        name,
    )


def back_kernel(low_prior, products, core_ref, *refs):
    if low_prior:
        own_ref, other_ref, refs = refs[0], refs[1], refs[2:]
        prior = jnp.where(in_own_half(core_ref), own_ref[...], other_ref[...]).astype(F32)
    else:
        prior, refs = refs[0][...], refs[1:]
    value_ref, gain_ref, e_ref, got_ref, refs = refs[0], refs[1], refs[2], refs[3], refs[4:]
    if products:
        e = dot_nt(e_ref[...], refs[0][...]) + dot_nt(got_ref[...], refs[1][...])
        refs = refs[2:]
    else:
        e = e_ref[...].astype(F32) + got_ref[...].astype(F32)
    w_ref, grad_ref, half_ref, next_ref = refs
    grad = prior + rms_back(value_ref[...], gain_ref[...], e)
    grad_ref[...] = grad
    low = grad.astype(BF16)
    half = low.shape[1] // 2
    half_ref[...] = jnp.where(core_ref[0] == 0, low[:, :half], low[:, half:])
    next_ref[...] = dot_nt(low, w_ref[...]).astype(BF16)


def back(core, prior, values, gain, e, got, w_in, w_out, name):
    rows, width = values.shape
    local = rows // 2
    low_prior = isinstance(prior, tuple)
    priors = prior if low_prior else (prior,)
    prior_specs = [within_half(local, width)] * 2 if low_prior else [half_rows(tile_of(local), width)]
    ins = () if w_in is None else (w_in, w_in)
    in_specs = [] if w_in is None else [own_columns(w_in), other_columns(w_in)]
    half = w_out.shape[0] // 2
    return core_call(
        functools.partial(back_kernel, low_prior, w_in is not None),
        rows // tile_of(local),
        core,
        (*priors, values, gain, e, got, *ins, w_out),
        prior_specs
        + [half_rows(tile_of(local), width), all_of(gain), half_rows(tile_of(local), e.shape[1]), half_rows(tile_of(local), e.shape[1])]
        + in_specs
        + [own_rows(w_out)],
        [half_rows(tile_of(local), width), half_rows(tile_of(local), width // 2), half_rows(tile_of(local), half)],
        [
            shape_of((rows, width), F32),
            shape_of((rows, width // 2), BF16),
            shape_of((rows, half), BF16),
        ],
        [],
        2 * rows * width * (half + 2 * e.shape[1] * len(ins) // 2),
        name,
    )


def last_kernel(core_ref, prior_ref, base_ref, gain_ref, q_ref, pair_ref, got_ref, *refs):
    wq_own, wq_other, wk_own, wk_other, wv_own, wv_other, grad_ref = refs
    qw = wq_own.shape[1]
    kw = wk_own.shape[1]
    e = dot_nt(q_ref[...], wq_own[...]) + dot_nt(got_ref[:, :qw], wq_other[...])
    for m in range(kw // PAIR):
        c, span = 2 * PAIR * m, slice(PAIR * m, PAIR * (m + 1))
        e = e + dot_nt(pair_ref[:, c : c + PAIR], wk_own[:, span])
        e = e + dot_nt(got_ref[:, qw + c : qw + c + PAIR], wk_other[:, span])
        c = c + PAIR
        e = e + dot_nt(pair_ref[:, c : c + PAIR], wv_own[:, span])
        e = e + dot_nt(got_ref[:, qw + c : qw + c + PAIR], wv_other[:, span])
    grad_ref[...] = prior_ref[...] + rms_back(base_ref[...].astype(F32), gain_ref[...], e)


def last(core, prior, base, gain, grad_q, pair, got, w_query, w_key, w_value):
    local, width = base.shape
    steps = local // tile_of(local)

    def own_tile(array):
        return pl.BlockSpec((tile_of(local), array.shape[1]), lambda i, c: (c[0] * steps + i, 0))

    weights = (w_query, w_query, w_key, w_key, w_value, w_value)
    specs = []
    for w in (w_query, w_key, w_value):
        specs += [own_columns(w), other_columns(w)]
    return core_call(
        last_kernel,
        local // tile_of(local),
        core,
        (prior, base, gain, grad_q, pair, got, *weights),
        [own_tile(prior), half_rows(tile_of(local), width), all_of(gain), own_tile(grad_q), own_tile(pair), half_rows(tile_of(local), got.shape[1])]
        + specs,
        [half_rows(tile_of(local), width)],
        [shape_of((local, width), F32)],
        [],
        2 * local * width * 2 * width,
        "last",
    )


def chip_at(order, p, where):
    masks, core_bit = order
    index = where[2] ^ masks[p]
    return index if core_bit is None else index ^ (where[0] << core_bit)


def outer_kernel(orders, terms, split, count, has_extra, where_ref, *refs):
    lefts = []
    for parts in split:
        lefts.append(refs[:parts])
        refs = refs[parts:]
    right_refs, refs = refs[:count], refs[count:]
    if has_extra:
        extra_ref, refs = refs[0], refs[1:]
    keep_ref, send_ref, sorted_refs = refs[0], refs[1], refs[2:]
    blocks = len(orders[0][0])
    for at, (left, sorted_ref) in enumerate(zip(lefts, sorted_refs)):
        rows = sorted_ref.shape[0] // blocks
        for p in range(blocks):
            index = chip_at(orders[at], p, where_ref)
            if len(left) == 1:
                piece = left[0][pl.ds(pl.multiple_of(index * rows, rows), rows), :]
            else:
                middle = blocks // 2
                first = pl.multiple_of(jnp.minimum(index, middle - 1) * rows, rows)
                second = pl.multiple_of(jnp.maximum(index - middle, 0) * rows, rows)
                piece = jnp.where(
                    index < middle, left[0][pl.ds(first, rows), :], left[1][pl.ds(second, rows), :]
                )
            sorted_ref[p * rows : (p + 1) * rows, :] = piece
    middle = sorted_refs[0].shape[0] // 2
    for out_ref, span in ((send_ref, slice(middle, 2 * middle)), (keep_ref, slice(0, middle))):
        column = 0
        for products in terms:
            total = None
            for left, right, first, start, size in products:
                depth = sorted_refs[left].shape[1]
                factor = right_refs[right][first : first + depth, start : start + size]
                part = dot_nn(sorted_refs[left][span, :], factor)
                total = part if total is None else total + part
            width = total.shape[1]
            out_ref[:, column : column + width] = total.astype(BF16)
            column += width
    if has_extra:
        rows = sorted_refs[0].shape[0] // blocks
        lanes = extra_ref.shape[1]
        row = lax.broadcasted_iota(jnp.int32, (rows, lanes), 0)
        for p in range(blocks):
            index = 2 * chip_at(orders[0], p, where_ref)
            block = jnp.where(row == 0, extra_ref[pl.ds(index, 1), :], 0.0)
            block = jnp.where(row == rows // 2, extra_ref[pl.ds(index + 1, 1), :], block)
            out_ref = keep_ref if p < blocks // 2 else send_ref
            first = p % (blocks // 2) * rows
            out_ref[first : first + rows, column:] = block.astype(BF16)


def outer_halves(where, orders, lefts, rights, terms, extra=None):
    blocks = len(orders[0][0])
    lefts = [v if isinstance(v, tuple) else (v,) for v in lefts]
    totals = [sum(v.shape[0] for v in left) for left in lefts]
    rows = totals[0] // blocks
    if rows % 16:
        joined = [jnp.concatenate(left, axis=0) for left in lefts]
        joined = [
            jnp.concatenate(
                [lax.dynamic_slice_in_dim(v, chip_at(order, p, where) * rows, rows, 0) for p in range(blocks)],
                axis=0,
            )
            for v, order in zip(joined, orders)
        ]
        half = totals[0] // 2
        columns = []
        for products in terms:
            columns.append(
                sum(
                    dot_nn(joined[l], rights[r][first : first + joined[l].shape[1], start : start + size])
                    for l, r, first, start, size in products
                )
            )
        total = jnp.concatenate(columns, axis=1).astype(BF16)
        return total[:half], total[half:]
    width = sum(products[0][4] for products in terms)
    extras = () if extra is None else (extra,)
    if extras:
        width += extra.shape[1]
    half = shape_of((totals[0] // 2, width), BF16)
    flops = 0
    for products in terms:
        for l, _, _, _, size in products:
            flops += 2 * totals[l] * lefts[l][0].shape[1] * size
    whole = pl.BlockSpec(memory_space=pltpu.VMEM)
    flat = [v for left in lefts for v in left]
    return pl.pallas_call(
        functools.partial(outer_kernel, orders, terms, [len(left) for left in lefts], len(rights), bool(extras)),
        in_specs=[pl.BlockSpec(memory_space=pltpu.SMEM)] + [whole] * (len(flat) + len(rights) + len(extras)),
        out_specs=[whole, whole],
        out_shape=[half, half],
        scratch_shapes=[
            pltpu.VMEM((total, left[0].shape[1]), BF16) for total, left in zip(totals, lefts)
        ],
        compiler_params=pltpu.CompilerParams(vmem_limit_bytes=VMEM_LIMIT),
        cost_estimate=cost(flops, 0, flops // 400),
        name="outer_halves",
    )(where, *flat, *rights, *extras)


def pick(value, index, axis):
    return lax.dynamic_index_in_dim(value, index, axis, keepdims=False)


def bits_of(size):
    return (size - 1).bit_length()


class Places:
    def __init__(self):
        self.seq = lax.axis_size("seq")
        self.dp = lax.axis_size("dp")
        self.nx = self.seq // 2
        self.chips = self.dp * self.nx
        place = lax.axis_index("seq")
        self.core = place & 1
        self.x = place >> 1
        self.d = lax.axis_index("dp")
        self.dp_bits = bits_of(self.dp)
        self.x_bits = bits_of(self.nx)
        self.chip = self.d * self.nx + self.x
        self.names = [("dp", b) for b in reversed(range(self.dp_bits))] + [
            ("x", b) for b in reversed(range(self.x_bits))
        ]

    def swap_core(self, value):
        return lax.ppermute(value, "seq", [(s, s ^ 1) for s in range(self.seq)])

    def shift_x(self, value, by):
        pairs = [(s, (s + 2 * by) % self.seq) for s in range(self.seq)]
        return lax.ppermute(value, "seq", pairs)

    def flip(self, value, names):
        d_mask = sum(1 << bit for axis, bit in names if axis == "dp")
        s_mask = sum(2 << bit for axis, bit in names if axis == "x")
        pairs = [
            (d * self.seq + s, (d ^ d_mask) * self.seq + (s ^ s_mask))
            for d in range(self.dp)
            for s in range(self.seq)
        ]
        return lax.ppermute(value, ("dp", "seq"), pairs)

    def by_core(self, own, other, axis):
        first = jnp.concatenate([own, other], axis=axis)
        second = jnp.concatenate([other, own], axis=axis)
        return jnp.where(self.core == 0, first, second)

    def core_rows(self, value, mine):
        half = value.shape[0] // 2
        which = self.core if mine else 1 - self.core
        return lax.dynamic_slice_in_dim(value, which * half, half, 0)

    def stages(self, kind):
        dp0 = [(("dp", 0),)]
        rest = [(("dp", b),) for b in range(1, self.dp_bits)]
        xs = [(("x", b),) for b in range(self.x_bits)]
        at_once = [tuple(one[0] for one in rest)] if len(rest) == 2 else rest
        z1, z2 = rest[:1], rest[1:]
        return {
            "x_y_z1_z2": xs + dp0 + z1 + z2,
            "y_x_z1_z2": dp0 + xs + z1 + z2,
            "y_x_zz": dp0 + xs + at_once,
            "z1_x_wait_z2_y": z1 + xs + [()] + z2 + dp0,
            "x_z1_y_z2": xs + z1 + dp0 + z2,
            "z1_x_y_z2": z1 + xs + dp0 + z2,
        }[kind]

    def block_order(self, kind, core_major=False):
        order = [name for stage in self.stages(kind) for name in stage]
        count = len(order)
        masks = []
        for p in range(self.chips):
            mask = 0
            for k, name in enumerate(order):
                if (p >> (count - 1 - k)) & 1:
                    mask |= 1 << (count - 1 - self.names.index(name))
            masks.append(mask)
        return tuple(masks), count - 1 if core_major else None


class ChipSum:
    def __init__(self, at, kind, kept, sent=None):
        self.at = at
        self.todo = list(at.stages(kind))
        self.rows, self.width = kept.shape
        self.parts = [([kept], 0)]
        self.sent = sent
        if sent is not None:
            self.parts.append(([at.flip(sent, self.todo.pop(0))], 0))

    def result(self):
        return sum(
            box[0][: self.rows, column : column + self.width].astype(F32) for box, column in self.parts
        )


def fold_kernel(plan, count, *refs):
    in_refs, out_refs = refs[:count], refs[count:]
    for sources, (out, out_column), (rows, width) in plan:
        step = 32 if rows % 32 == 0 else 16

        def body(i, carried, sources=sources, out=out, out_column=out_column, width=width, step=step):
            span = pl.ds(pl.multiple_of(i * step, 16), step)
            total = None
            for at, column in sources:
                part = in_refs[at][span, column : column + width].astype(F32)
                total = part if total is None else total + part
            out_refs[out][span, out_column : out_column + width] = total.astype(BF16)
            return carried

        lax.fori_loop(0, rows // step, body, 0)


def fold_arrays(plan, inputs, shapes):
    if all(rows % 16 == 0 for _, _, (rows, _) in plan):
        return pl.pallas_call(
            functools.partial(fold_kernel, plan, len(inputs)),
            grid=(1,),
            in_specs=[
                pl.BlockSpec((rows, array.shape[1]), lambda i, block=block: (block, 0))
                for array, block, rows in inputs
            ],
            out_specs=[pl.BlockSpec(shape, lambda i: (0, 0)) for shape in shapes],
            out_shape=[shape_of(shape, BF16) for shape in shapes],
            compiler_params=kernel_params(),
            cost_estimate=cost(1, 0, 1),
            name="fold",
        )(*[array for array, _, _ in inputs])
    outs = [jnp.zeros(shape, BF16) for shape in shapes]
    for sources, (out, out_column), (rows, width) in plan:
        total = 0.0
        for at, column in sources:
            array, block, size = inputs[at]
            total = total + array[block * size : (block + 1) * size, column : column + width].astype(F32)
        outs[out] = outs[out].at[:, out_column : out_column + width].set(total.astype(BF16))
    return outs


def fold(at, sums, *ties):
    inputs, plan, shapes, sends = [], [], [], {}

    def place_of(array, block, rows):
        for index, known in enumerate(inputs):
            if known[0] is array and known[1:] == (block, rows):
                return index
        inputs.append((array, block, rows))
        return len(inputs) - 1

    for one in sums:
        stage = one.todo.pop(0) if one.todo else ()
        one.rows >>= len(stage)
        for j in range(1, 1 << len(stage)):
            names = tuple(name for k, name in enumerate(stage) if (j >> (len(stage) - 1 - k)) & 1)
            sources = [(place_of(box[0], j, one.rows), column) for box, column in one.parts]
            sends.setdefault((names, one.rows), []).append((one, sources))
    for (names, rows), pieces in sends.items():
        column = 0
        for one, sources in pieces:
            plan.append((sources, (len(shapes), column), (rows, one.width)))
            column += one.width
        shapes.append((rows, column))
    outs = list(fold_arrays(plan, inputs, shapes))
    if ties:
        outs = together(*outs, *ties)
        outs, ties = list(outs[: len(shapes)]), outs[len(shapes) :]
    for out, ((names, rows), pieces) in zip(outs, sends.items()):
        box = [at.flip(out, names)]
        column = 0
        for one, _ in pieces:
            one.sent = out
            one.parts.append((box, column))
            column += one.width
    return ties


def settle(sums, *values):
    boxes = []
    for one in sums:
        for box, _ in one.parts[1:]:
            if not any(box is known for known in boxes):
                boxes.append(box)
    out = together(*[box[0] for box in boxes], *values)
    for box, value in zip(boxes, out):
        box[0] = value
    return out[len(boxes) :]


def finish_sum_kernel(plan, count, where_ref, *refs):
    in_refs, refs = refs[:count], refs[count:]
    out_refs, total_refs = refs[: 2 * len(plan)], refs[2 * len(plan) :]
    for at, ranges in enumerate(plan):
        mine_ref, other_ref, total_ref = out_refs[2 * at], out_refs[2 * at + 1], total_refs[at]
        first = 0
        for sources, width in ranges:
            total = None
            for index, column in sources:
                part = in_refs[index][:, column : column + width].astype(F32)
                total = part if total is None else total + part
            total_ref[:, first : first + width] = total
            first += width
        half = mine_ref.shape[0]
        core = where_ref[0]
        mine_ref[...] = total_ref[pl.ds(pl.multiple_of(core * half, half), half), :]
        other_ref[...] = total_ref[pl.ds(pl.multiple_of((1 - core) * half, half), half), :]


def finish_sums(places, where, groups):
    if any(group[0].rows % 32 and group[0].rows % 16 for group in groups):
        outs = []
        for group in groups:
            total = jnp.concatenate([one.result() for one in group], axis=1)
            outs.append((places.core_rows(total, True), places.core_rows(total, False)))
        return outs
    inputs, plan = [], []

    def place_of(array, rows):
        for index, known in enumerate(inputs):
            if known[0] is array and known[1] == rows:
                return index
        inputs.append((array, rows))
        return len(inputs) - 1

    shapes, scratch = [], []
    for group in groups:
        ranges = []
        for one in group:
            ranges.append(
                ([(place_of(box[0], one.rows), column) for box, column in one.parts], one.width)
            )
        plan.append(ranges)
        width = sum(one.width for one in group)
        shapes += [(group[0].rows // 2, width)] * 2
        scratch.append(pltpu.VMEM((group[0].rows, width), F32))
    outs = core_call(
        functools.partial(finish_sum_kernel, plan, len(inputs)),
        1,
        where,
        [array for array, _ in inputs],
        [pl.BlockSpec((rows, array.shape[1]), lambda i, c: (0, 0)) for array, rows in inputs],
        [fixed(shape) for shape in shapes],
        [shape_of(shape, F32) for shape in shapes],
        scratch,
        16,
        "finish_sums",
    )
    return [(outs[2 * k], outs[2 * k + 1]) for k in range(len(groups))]


def finish_kernel(plan, gains, count, bias_at, where_ref, *refs):
    group_refs, refs = refs[: 2 * count], refs[2 * count :]
    weights = sum(len(pairs) for pairs in gains)
    weight_refs, gain_ref, bias_out, refs = refs[:weights], refs[weights], refs[weights + 1], refs[weights + 2 :]
    out_refs, gain_outs = refs[: len(plan)], refs[len(plan) :]
    span = slice(bias_at, bias_at + bias_out.shape[1])
    bias_out[...] = group_refs[0][0:1, span] + group_refs[1][0:1, span]
    first_core = where_ref[0] == 0
    for (group, column, width), out_ref in zip(plan, out_refs):
        mine = group_refs[2 * group][:, column : column + width]
        got = group_refs[2 * group + 1][:, column : column + width]
        out_ref[:, :width] = jnp.where(first_core, mine, got)
        out_ref[:, width:] = jnp.where(first_core, got, mine)
    at = 0
    for k, (pairs, gain_out) in enumerate(zip(gains, gain_outs)):
        total = None
        for matrix in pairs:
            product = out_refs[matrix][...] * weight_refs[at][...].astype(F32)
            at += 1
            part = product[:, :PAIR]
            for first in range(PAIR, product.shape[1], PAIR):
                part = part + product[:, first : first + PAIR]
            total = part if total is None else total + part
        gain_out[0] = jnp.sum(total.T, axis=0, keepdims=True) / gain_ref[k, 0]


def finish(places, where, joined, plan, gains, gain_rows, bias_at, bias_share):
    half = joined[0][0].shape[0]
    device = 2 * places.chip + places.core
    if half % 16:
        outs = []
        for group, column, width in plan:
            mine, got = joined[group]
            outs.append(places.by_core(mine[:, column : column + width], got[:, column : column + width], 1))
        shares = []
        for gain, pairs in gains:
            total = 0.0
            for matrix, weight in pairs:
                rows = lax.dynamic_slice_in_dim(weight, device * half, half, 0).astype(F32)
                total = total + jnp.sum(rows * outs[matrix], axis=1)
            shares.append(total / pick(gain_rows[gain], device, 0)[0])
        span = slice(bias_at, bias_at + bias_share)
        return outs, shares, joined[0][0][0, span] + joined[0][1][0, span]
    flat = [v for pair in joined for v in pair]
    weights = [weight for _, pairs in gains for _, weight in pairs]
    outs = core_call(
        functools.partial(finish_kernel, plan, [[matrix for matrix, _ in pairs] for _, pairs in gains], len(joined), bias_at),
        1,
        where,
        (*flat, *weights, gain_rows),
        [all_of(v) for v in flat]
        + [pl.BlockSpec((half, w.shape[1]), lambda i, c: (c[1], 0)) for w in weights]
        + [pl.BlockSpec((len(gains), 1, 1, half), lambda i, c: (0, c[1], 0, 0))],
        [fixed((1, bias_share))]
        + [fixed((joined[group][0].shape[0], 2 * width)) for group, _, width in plan]
        + [fixed((1, 1, half)) for _ in gains],
        [shape_of((1, bias_share), F32)]
        + [shape_of((joined[group][0].shape[0], 2 * width), F32) for group, _, width in plan]
        + [shape_of((1, 1, half), F32) for _ in gains],
        [],
        16,
        "finish",
    )
    bias, outs = outs[0].reshape(bias_share), outs[1:]
    return outs[: len(plan)], [v.reshape(half) for v in outs[len(plan) :]], bias


def together(*values):
    return lax.optimization_barrier(values)


def per_device(
    target,
    memory,
    mem_lengths,
    mem_mask,
    distance_buckets,
    norm_self,
    w_query,
    w_key,
    w_value,
    w_out,
    pos_table,
    norm_cross,
    wc_query,
    wc_key,
    wc_value,
    wc_out,
    norm_ffn,
    w_gate,
    w_up,
    w_down,
    out_grad,
):
    at = Places()
    core, nx = at.core, at.nx
    local, width = target.shape[1], target.shape[2]
    mem_local = memory.shape[1]
    rows = 2 * local
    full = distance_buckets.shape[0]
    qw = HEADS * HEAD_DIM // 2
    kw = KV * HEAD_DIM // 2
    head_count = HEADS // 2
    place = at.x.astype(jnp.int32).reshape(1)
    core_arg = core.astype(jnp.int32).reshape(1)
    gain_self = norm_self.reshape(1, width)
    gain_cross = norm_cross.reshape(1, width)
    gain_ffn = norm_ffn.reshape(1, width)

    tokens = target.reshape(local, width)
    far_tokens = [at.shift_x(tokens, s) for s in range(1, nx)]
    tokens_got = at.swap_core(tokens)
    memories = memory.reshape(mem_local, width)
    far_memories = [at.shift_x(memories, s) for s in range(1, nx)]
    memories_got = at.swap_core(memories)
    grads = out_grad.reshape(local, width)
    grads_got = at.swap_core(grads)

    normed_t, query, keys, values = project(
        core_arg, tokens, tokens_got, gain_self, (w_query, w_key, w_value), (score_scale, None, None), "project"
    )
    query, grads_got, pos_table, distance_buckets, mem_mask = together(
        query, grads_got, pos_table, distance_buckets, mem_mask
    )
    grad_chip = at.by_core(grads, grads_got, 0)

    own_table = lax.dynamic_slice_in_dim(pos_table, core * head_count, head_count, 0)
    onehot = (distance_buckets[:, None] == jnp.arange(BUCKETS, dtype=jnp.int32)[None, :]).astype(F32)
    by_distance = lax.dot_general(
        own_table, onehot, (((1,), (1,)), ((), ())), precision=lax.Precision.HIGHEST
    )
    bias_vec = jnp.pad(by_distance, ((0, 0), (BLK, 0))).reshape(head_count // 2, 2, BLK + full)

    mem_ids = jnp.arange(mem_mask.shape[1], dtype=jnp.int32)
    valid = (mem_ids < mem_lengths[0]) & ((mem_mask[0] == 1) | (mem_ids == 0))
    mask_add = jnp.where(valid, 0.0, big_negative).astype(F32).reshape(2 * nx, mem_local)
    slot_of = jnp.array([s for s in range(nx) for c in range(2)], jnp.int32)
    core_of = jnp.array([c for s in range(nx) for c in range(2)], jnp.int32)
    mask_rows = (((at.x - slot_of + nx) % nx) * 2 + (core ^ core_of))[:, None] == jnp.arange(2 * nx)[None, :]
    mask_col = jnp.sum(jnp.where(mask_rows[:, :, None], mask_add[None], 0.0), axis=1).reshape(-1, 1)

    grad_half = lax.dynamic_slice_in_dim(grad_chip, core * (width // 2), width // 2, 1)
    where = jnp.stack([core, 2 * at.chip + core, at.chip]).astype(jnp.int32)
    tied = together(*far_tokens, query, grad_chip, grad_half, bias_vec, mask_col, where)
    far_tokens = list(tied[: nx - 1])
    grad_chip, grad_half, bias_vec, mask_col, where = tied[nx:]
    keys, values, normed_ts = [keys], [values], [normed_t]
    for far in far_tokens:
        far_t, far_k, far_v = project(
            core_arg, far, at.swap_core(far), gain_self, (w_key, w_value), (None, None), "project_far"
        )
        normed_ts.append(far_t)
        keys.append(far_k)
        values.append(far_v)

    mixed, mixed_t, lse_self = self_forward(place, query, keys, values, bias_vec)
    mixed, mixed_t, memories_got, *far_memories = together(mixed, mixed_t, memories_got, *far_memories)
    mem_parts = [memories, memories_got]
    for far in far_memories:
        mem_parts += [far, at.swap_core(far)]
    *mem_ts, mem_keys, mem_values = project_memory(core_arg, mem_parts, wc_key, wc_value)
    mixed_got = at.swap_core(mixed)
    mixed_t_got = at.swap_core(mixed_t)
    after_self, cross_t, cross_query = join(
        core_arg, (tokens, tokens_got), mixed, mixed_got, w_out, gain_cross, wc_query, "join_self"
    )

    crossed, crossed_t, lse_cross = cross_forward(cross_query, mem_keys, mem_values, mask_col)
    crossed_got = at.swap_core(crossed)
    crossed_t_got = at.swap_core(crossed_t)
    after_cross, ffn_t, normed_ffn = join(
        core_arg, after_self, crossed, crossed_got, wc_out, gain_ffn, None, "join_cross"
    )

    hidden_t, e_part, out_mine, out_other, gate_keep, gate_send, up_keep, up_send = ffn(
        where,
        normed_ffn,
        ffn_t,
        grad_chip,
        w_gate,
        w_up,
        w_down,
        [at.block_order("x_y_z1_z2"), at.block_order("y_x_z1_z2")],
    )
    ffn_half = w_gate.shape[1] // 2
    gate_sum = ChipSum(at, "x_y_z1_z2", gate_keep, gate_send)
    up_sum = ChipSum(at, "y_x_z1_z2", up_keep, up_send)
    hidden_t_got = at.swap_core(hidden_t)
    e_got = at.swap_core(e_part)
    out_got = at.swap_core(out_other)
    down_halves = outer_halves(
        where,
        [at.block_order("z1_x_wait_z2_y", True)], [(hidden_t, hidden_t_got)], [grad_half], [[(0, 0, 0, 0, width // 2)]]
    )
    e_part, *down_halves = together(e_part, *down_halves)
    down_sum = ChipSum(at, "z1_x_wait_z2_y", *down_halves)
    grad_after_cross, cross_half, grad_crossed = back(
        core_arg, (grads, grads_got), after_cross, gain_ffn, e_part, e_got, None, wc_out, "back_ffn"
    )

    grad_cq, grad_mem = cross_backward(
        cross_query, mem_keys, mem_values, mask_col, grad_crossed, crossed, lse_cross, nx
    )
    grad_cq_got = at.swap_core(grad_cq)
    wc_out_halves = outer_halves(
        where,
        [at.block_order("z1_x_y_z2", True)],
        [(crossed_t, crossed_t_got)],
        [cross_half],
        [[(0, 0, 0, 0, width // 2)]],
    )
    turns = kw // PAIR
    k_columns = [2 * PAIR * m for m in range(turns)]
    v_columns = [2 * PAIR * m + PAIR for m in range(turns)]
    wc_in_halves = outer_halves(
        where,
        [at.block_order("y_x_z1_z2")] * (1 + nx),
        [cross_t, *mem_ts],
        [grad_cq, *grad_mem],
        [[(0, 0, 0, 0, qw)]] + [[(1 + s, 1 + s, 0, c, PAIR) for s in range(nx)] for c in k_columns + v_columns],
    )

    both = [gate_sum, up_sum]
    tied = settle(both, grad_cq, grad_cq_got, *wc_out_halves)
    grad_cq, grad_cq_got, *wc_out_halves = fold(at, both, *tied)
    grad_after_self, self_half, grad_mixed = back(
        core_arg, grad_after_cross, after_self, gain_cross, grad_cq, grad_cq_got, wc_query, w_out, "back_cross"
    )
    out_halves = outer_halves(
        where,
        [at.block_order("x_z1_y_z2", True)],
        [(mixed_t, mixed_t_got)],
        [self_half],
        [[(0, 0, 0, 0, width // 2)]],
    )
    ffn_sums = [gate_sum, up_sum, down_sum]
    tied = settle(
        ffn_sums,
        grad_mixed,
        grad_after_self,
        out_mine,
        out_got,
        *wc_in_halves,
        *out_halves,
        *wc_out_halves,
        *grad_mem,
    )
    grad_mixed, grad_after_self, out_mine, out_got = tied[:4]
    halves = tied[4:10]
    grad_mem = tied[10:]

    grad_mixed, *halves = fold(at, ffn_sums, grad_mixed, *halves)
    wc_in_sum = ChipSum(at, "y_x_z1_z2", *halves[:2])
    out_sum = ChipSum(at, "x_z1_y_z2", *halves[2:4])
    wc_out_sum = ChipSum(at, "z1_x_y_z2", *halves[4:])
    early = [*ffn_sums, wc_in_sum, out_sum, wc_out_sum]
    grad_q, grad_pairs, diagonals = self_backward(
        place, query, keys, values, bias_vec, grad_mixed, mixed, lse_self
    )
    tied = settle(early, grad_q, diagonals, out_mine, out_got, *grad_pairs, *grad_mem)
    grad_q, diagonals, out_mine, out_got = tied[:4]
    grad_pairs, grad_mem = tied[4 : 4 + nx], tied[4 + nx :]
    grad_mem_chip = grad_mem[0]
    pair_chip = grad_pairs[0]
    pair_got = [at.shift_x(grad_pairs[s], nx - s) for s in range(1, nx)]
    mem_got = [at.shift_x(grad_mem[s], nx - s) for s in range(1, nx)]

    grad_q, diagonals, grad_mem_chip, out_mine = fold(at, early, grad_q, diagonals, grad_mem_chip, out_mine)

    own_bias = lax.dot_general(
        diagonals.reshape(head_count, -1)[:, BLK:],
        onehot,
        (((1,), (0,)), ((), ())),
        precision=lax.Precision.HIGHEST,
        preferred_element_type=F32,
    )
    table = lax.dynamic_update_slice_in_dim(
        jnp.zeros((HEADS, BUCKETS), F32), own_bias, core * head_count, 0
    ).reshape(2 * at.chips, -1)
    bias_share = table.shape[1]
    in_halves = outer_halves(
        where,
        [at.block_order("y_x_zz")] * nx,
        normed_ts,
        [grad_q, *grad_pairs],
        [[(0, 0, 0, 0, qw)]] + [[(s, 1 + s, 0, c, PAIR) for s in range(nx)] for c in k_columns + v_columns],
        jnp.pad(table, ((0, 0), (0, 128 - bias_share))),
    )
    in_sum = ChipSum(at, "y_x_zz", *in_halves)
    tied = together(grad_mem_chip, out_mine, *pair_got, *mem_got)
    grad_mem_chip, out_mine = tied[:2]
    pair_got, mem_got = tied[2 : 1 + nx], tied[1 + nx :]
    for got in pair_got:
        pair_chip = pair_chip + got
    every = [*early, in_sum]

    output = (
        at.core_rows(after_cross, True)
        + out_mine.astype(F32)
        + out_got.astype(F32)
    ).astype(BF16)
    for got in mem_got:
        grad_mem_chip = grad_mem_chip + got
    mem_mine = grad_mem_chip[:mem_local]
    mem_other = at.swap_core(grad_mem_chip[mem_local:])

    def unpaired(columns):
        mine = [mem_mine[:, c : c + PAIR] for c in columns]
        other = [mem_other[:, c : c + PAIR] for c in columns]
        return at.by_core(jnp.concatenate(mine, axis=1), jnp.concatenate(other, axis=1), 1)

    grad_memory = dot_nt(unpaired(k_columns), wc_key) + dot_nt(unpaired(v_columns), wc_value)
    sent = jnp.concatenate([at.core_rows(grad_q, False), at.core_rows(pair_chip, False)], axis=1)
    (grad_target,) = last(
        core_arg,
        grad_after_self,
        tokens,
        gain_self,
        grad_q,
        pair_chip,
        at.swap_core(sent),
        w_query,
        w_key,
        w_value,
    )

    grad_target, grad_memory, output = settle(every, grad_target, grad_memory, output)
    while any(one.todo for one in every):
        fold(at, every)
    (norm_ffn,) = settle([down_sum], norm_ffn)
    gain_rows = jnp.stack([norm_ffn, norm_cross, norm_self]).reshape(3, 2 * at.chips, 1, -1)
    (gain_rows,) = settle(every, gain_rows)

    sums = [gate_sum, up_sum, wc_in_sum, out_sum, in_sum, wc_out_sum]
    rear, down_rows = finish_sums(at, where, [sums, [down_sum]])
    rear_join = (rear[0], at.swap_core(rear[1]))
    down_join = (down_rows[0], at.swap_core(down_rows[1]))
    wc_at = 2 * ffn_half
    out_at = wc_at + qw + 2 * kw
    in_at = out_at + width // 2
    bias_at = in_at + qw + 2 * kw
    (gate, up, cross_in, cross_key, cross_value, self_out, self_in, self_key, self_value, cross_out, down), gain_grads, bias_out = finish(
        at,
        where,
        [rear_join, down_join],
        [
            (0, 0, ffn_half),
            (0, ffn_half, ffn_half),
            (0, wc_at, qw),
            (0, wc_at + qw, kw),
            (0, wc_at + qw + kw, kw),
            (0, out_at, width // 2),
            (0, in_at, qw),
            (0, in_at + qw, kw),
            (0, in_at + qw + kw, kw),
            (0, in_at + in_sum.width, width // 2),
            (1, 0, width // 2),
        ],
        [
            (0, [(0, w_gate), (1, w_up)]),
            (1, [(2, wc_query)]),
            (2, [(6, w_query), (7, w_key), (8, w_value)]),
        ],
        gain_rows,
        bias_at,
        bias_share,
    )
    gain_ffn_grad, gain_cross_grad, gain_self_grad = gain_grads
    return (
        output.reshape(target.shape),
        grad_target.reshape(target.shape),
        grad_memory.reshape(memory.shape),
        gain_self_grad,
        self_in,
        self_key,
        self_value,
        self_out,
        bias_out,
        gain_cross_grad,
        cross_in,
        cross_key,
        cross_value,
        cross_out,
        gain_ffn_grad,
        gate,
        up,
        down,
    )


def solution(mesh):
    tokens = P("dp", "seq", None)
    row_share = P(("dp", "seq"))
    matrix_share = P(("dp", "seq"), None)
    return jax.shard_map(
        per_device,
        mesh=mesh,
        in_specs=(tokens, tokens, P("dp"), P("dp", None)) + (P(),) * 16 + (tokens,),
        out_specs=(tokens, tokens, tokens, row_share)
        + (matrix_share,) * 4
        + (row_share, row_share)
        + (matrix_share,) * 4
        + (row_share,)
        + (matrix_share,) * 3,
        check_vma=False,
    )
```
